32 devices in a mesh: batch: 8 (over z, core), row: 4 (over y, x).
Axes of the slice: x: 2, y: 2, z: 4, core: 2. Of those that a mesh axis runs over, the one named last changes fastest.
Arguments:
- context_map: bfloat16 [32, 64, 64, 256], P('batch', 'row'), may hold values from -6 to 6
- future_feats: bfloat16 [32, 480, 256], P(('batch', 'row')), may hold values from -6 to 6
- horizon: int32 [32], P(('batch', 'row')), may hold values from 4 to 30, as said below
- cotangent: bfloat16 [32, 736, 768], P(('batch', 'row')), may hold values from -6 to 6
- tile_owner: int32 [124], replicated, may hold values from 0 to 31, as said below
- master_tiles: float32 [256, 256, 256], P(('batch', 'row')), as said below
- moment_first: float32 [256, 256, 256], P(('batch', 'row')), may hold values from -0.00061035156 to 0.00061035156
- moment_second: float32 [256, 256, 256], P(('batch', 'row')), may hold values from 1.2305475e-10 to 4.92219e-10
- norm_gains: float32 [2, 768], replicated, may hold values from 0.5 to 1.5
- gain_first: float32 [2, 768], replicated, may hold values from -0.0024414062 to 0.0024414062
- gain_second: float32 [2, 768], replicated, may hold values from 1.968876e-09 to 7.875504e-09
Outputs:
- block_out: float32 [32, 736, 768], P(('batch', 'row'))
- context_grad: float32 [32, 64, 64, 256], P('batch', 'row')
- future_grad: float32 [32, 480, 256], P(('batch', 'row'))
- new_first: float32 [256, 256, 256], P(('batch', 'row'))
- new_second: float32 [256, 256, 256], P(('batch', 'row'))
- new_master: float32 [256, 256, 256], P(('batch', 'row'))
- new_gain_first: float32 [2, 768], replicated
- new_gain_second: float32 [2, 768], replicated
- new_gains: float32 [2, 768], replicated
- grad_norm: float32 [], replicated
The draws below stay inside these ranges and needn't reach their ends.
Inputs may be any that keep to these rules, and one draw needn't show every extreme that they name: `horizon`: some clip has 30 future frames and some clip has 4. `tile_owner`: owner index counts devices over batch, then row. No device owns more than 8 tiles, and some device owns exactly 8. `master_tiles`: slots that hold no tile carry values that no output reads.
All inputs are finite; a program needn't handle non-finite values.
Results may differ from the reference program's by a relative error of at most 0.017.
The reference program's roundings to bfloat16 on the way count: a program that leaves them out, or rounds other values in their place, can miss the bound.
Values may be sent and summed in bfloat16 or wider, within the bound.
No kernel may reach another device: no remote copies, remote signals or barrier semaphores. Data moves between devices by JAX's collectives and lax.ppermute only.
A program may use at most 448 MiB of HBM per device.

```python
import jax
import jax.numpy as jnp
import numpy as np
from jax import lax

CH = 256
HD = 64
HEADS = 12
D = 768
FF = 3072
TH = 4
IMG = 64
PATCH = 4
FT = 16
FMAX = 30
CTX = 256
NF = 480
SEQ = 736
CLIPS = 32
STEP = 10
TILES = 124
SLOTS = 8
DEVICES = 32


def owner_list(key):
    key_full, key_rest, key_order = jax.random.split(key, 3)
    full_device = jax.random.randint(key_full, (), 0, DEVICES).astype(jnp.int32)
    others = (jax.random.permutation(key_rest, (DEVICES - 1) * SLOTS)[:TILES - SLOTS] // SLOTS).astype(jnp.int32)
    others = others + (others >= full_device).astype(jnp.int32)
    assigned = jnp.concatenate([jnp.zeros((SLOTS,), jnp.int32) + full_device, others])
    shuffle = jax.random.permutation(key_order, TILES)
    return assigned[shuffle].astype(jnp.int32)


def slot_positions(tile_owner):
    ordinal = jnp.arange(TILES)
    earlier = (tile_owner[None, :] == tile_owner[:, None]) & (ordinal[None, :] < ordinal[:, None])
    return (tile_owner * SLOTS + jnp.sum(earlier.astype(jnp.int32), 1)).astype(jnp.int32)


def tile_scales():
    per_model = D // CH
    per_hidden = FF // CH
    scale_list = [(9 * CH) ** (-0.5)] * 9 + [CH ** (-0.5)] * 3 + [8.0 * CH ** (-0.5)]
    scale_list = scale_list + [CH ** (-0.5)] * per_model + [D ** (-0.5)] * (3 * per_model * per_model)
    scale_list = scale_list + [6.0 * D ** (-0.5)] * (per_model * per_model) + [D ** (-0.5)] * (per_model * per_hidden)
    scale_list = scale_list + [2.0 * FF ** (-0.5)] * (per_hidden * per_model)
    return np.array(scale_list, np.float32)


def draw_tile_owner(key, part):
    return owner_list(jax.random.fold_in(key, 7))


def draw_master_tiles(key, part):
    tile_owner = owner_list(jax.random.fold_in(key, 7))
    slot_scale = jnp.full((DEVICES * SLOTS,), 0.05, jnp.float32).at[slot_positions(tile_owner)].set(jnp.asarray(tile_scales()))
    value_key = jax.random.fold_in(key, 11)
    values = jax.random.normal(value_key, (DEVICES * SLOTS, CH, CH), jnp.float32)
    return values * slot_scale[:, None, None]


def draw_horizon(key, part):
    key_all, key_top, key_bottom = jax.random.split(jax.random.fold_in(key, 3), 3)
    frames = jax.random.randint(key_all, (CLIPS,), 4, FMAX + 1)
    top_clip = jax.random.randint(key_top, (), 0, CLIPS)
    bottom_clip = (top_clip + 1 + jax.random.randint(key_bottom, (), 0, CLIPS - 1)) % CLIPS
    return frames.at[top_clip].set(FMAX).at[bottom_clip].set(4).astype(jnp.int32)


def shard_levels(key, shape, cuts, low, largest):
    factor_of = 1.0
    for axis_at, blocks in cuts:
        heights = jax.random.uniform(jax.random.fold_in(jax.random.fold_in(key, 6), axis_at), (blocks,), jnp.float32, low / len(cuts), largest / len(cuts))
        factor_of = factor_of * jnp.repeat(jnp.exp(heights), shape[axis_at] // blocks).reshape((-1,) + (1,) * (len(shape) - 1 - axis_at))
    return factor_of


def scatter_about(rng, dims, scale, most, cuts=(), dtype=jnp.bfloat16):
    values = scale * jax.random.normal(rng, dims, jnp.float32)
    if cuts:
        values = values * shard_levels(rng, dims, cuts, -0.22, 0.18)
    return jnp.clip(values, -most, most).astype(dtype)


def setup_inputs(seed: int = 0) -> dict:
    key_of = jax.random.split(jax.random.key(seed), 12)
    return {
        "context_map": scatter_about(key_of[0], (CLIPS, IMG, IMG, CH), 1.0, 6.0, ((0, 8), (1, 4))),
        "future_feats": scatter_about(key_of[1], (CLIPS, NF, CH), 1.0, 6.0, ((0, 32),)),
        "horizon": draw_horizon(jax.random.fold_in(key_of[11], 71), 0),
        "cotangent": scatter_about(key_of[3], (CLIPS, SEQ, D), 1.0, 6.0, ((0, 32),)),
        "tile_owner": draw_tile_owner(jax.random.fold_in(key_of[11], 71), 0),
        "master_tiles": draw_master_tiles(jax.random.fold_in(key_of[11], 71), 0),
        "moment_first": scatter_about(key_of[6], (DEVICES * SLOTS, CH, CH), (0.111 * (TILES * CH * CH) ** -0.5), 0.00061035156, ((0, 32),), jnp.float32),
        "moment_second": jnp.clip(1.2305474694773721e-10 + 3.6916424084321164e-10 * jax.random.uniform(key_of[7], (DEVICES * SLOTS, CH, CH), jnp.float32) ** shard_levels(key_of[7], (DEVICES * SLOTS, CH, CH), ((0, 32),), -0.2, 0.2), 1.2305474694773721e-10, 4.922189877909489e-10),
        "norm_gains": jnp.clip(1.0 + 0.1 * jax.random.normal(key_of[8], (2, D), jnp.float32), 0.5, 1.5),
        "gain_first": scatter_about(key_of[9], (2, D), (0.444 * (TILES * CH * CH) ** -0.5), 0.0024414062, (), jnp.float32),
        "gain_second": jnp.clip(jax.random.uniform(key_of[10], (2, D), jnp.float32, 1.9688759511637954e-09, 7.875503804655182e-09), 1.9688759511637954e-09, 7.875503804655182e-09),
    }


@jax.custom_vjp
def low(v):
    return lax.optimization_barrier(v.astype(jnp.bfloat16)).astype(jnp.float32)

@jax.custom_vjp
def low_back(v):
    return v

def low_keep(v):
    return (low(v), None)

def low_pass(kept, grad):
    return (grad,)

def back_keep(v):
    return (v, None)

def back_low(kept, grad):
    return (low(grad),)
low.defvjp(low_keep, low_pass)
low_back.defvjp(back_keep, back_low)
best_precision = lax.Precision.HIGHEST
eps_norm = 1e-05
beta_one = 0.9
beta_two = 0.999
learn_rate = 0.02
gain_rate = 0.6
decay_rate = 0.1
adam_eps = 1e-08
clip_level = 1.0
neg_large = -1e+30

def slot_index(tile_owner, slot_count):
    ordinal = jnp.arange(tile_owner.shape[0])
    earlier = (tile_owner[None, :] == tile_owner[:, None]) & (ordinal[None, :] < ordinal[:, None])
    return (tile_owner * slot_count + lax.optimization_barrier(jnp.sum(earlier.astype(jnp.int32), 1))).astype(jnp.int32)

def unpack(tile_stack):
    per_model = D // CH
    per_hidden = FF // CH
    conv_tiles = tile_stack[0:9]
    att_tiles = tile_stack[9:13]
    offset = 13
    matrices = []
    for tile_rows, tile_cols in ((1, per_model), (per_model, 3 * per_model), (per_model, per_model), (per_model, per_hidden), (per_hidden, per_model)):
        amount = tile_rows * tile_cols
        tile_block = tile_stack[offset:offset + amount].reshape(tile_rows, tile_cols, CH, CH)
        matrices.append(tile_block.transpose(0, 2, 1, 3).reshape(tile_rows * CH, tile_cols * CH))
        offset = offset + amount
    return (conv_tiles, att_tiles, matrices)

def rms_norm(values, gain):
    return values * lax.rsqrt(lax.optimization_barrier(jnp.mean(values * values, -1, keepdims=True)) + eps_norm) * gain

def adam_step(weight, grad_now, first, second, rate, decay):
    first_new = beta_one * first + (1.0 - beta_one) * grad_now
    second_new = beta_two * second + (1.0 - beta_two) * grad_now * grad_now
    corr_first = first_new / (1.0 - beta_one ** STEP)
    corr_second = second_new / (1.0 - beta_two ** STEP)
    weight_new = weight - rate * (corr_first / (jnp.sqrt(corr_second) + adam_eps) + decay * weight)
    return (first_new, second_new, weight_new)

def clip_forward(image, feats, clip_horizon, conv_tiles, att_tiles, matrices, gains_now):
    to_query, to_key, to_value, to_out = (att_tiles[0], att_tiles[1], att_tiles[2], att_tiles[3])
    w_emb, w_qkv, w_att, w_up, w_down = matrices
    score_scale = HD ** (-0.5)
    padded = jnp.pad(image, ((1, 1), (1, 1), (0, 0)))
    conv_sum = jnp.zeros((IMG, IMG, CH), jnp.float32)
    for offset_y in range(3):
        for offset_x in range(3):
            window = padded[offset_y:offset_y + IMG, offset_x:offset_x + IMG]
            conv_sum = conv_sum + jnp.einsum('abc,cd->abd', window, conv_tiles[3 * offset_y + offset_x], precision=best_precision)
    conv_out = low_back(conv_sum)
    hidden = image + jax.nn.silu(conv_out)
    keyval = low(low_back(jnp.dot(low(hidden).reshape(IMG * IMG, CH), jnp.concatenate([to_key, to_value], 1), precision=best_precision)))
    pooled = low(low_back(lax.optimization_barrier(jnp.mean(hidden.reshape(IMG // PATCH, PATCH, IMG // PATCH, PATCH, CH), axis=(1, 3))).reshape(CTX, CH)))
    query = low(low_back(jnp.dot(feats, to_query, precision=best_precision))).reshape(NF, TH, HD)
    key_heads = keyval[:, :CH].reshape(IMG * IMG, TH, HD)
    value_heads = keyval[:, CH:].reshape(IMG * IMG, TH, HD)
    cross_scores = low_back(jnp.einsum('qhd,khd->hqk', query, key_heads, precision=best_precision) * score_scale)
    cross_probs = low(jax.nn.softmax(cross_scores, axis=-1))
    cross_mixed = low(low_back(jnp.einsum('hqk,khd->qhd', cross_probs, value_heads, precision=best_precision).reshape(NF, CH)))
    updated = feats + low_back(jnp.dot(cross_mixed, to_out, precision=best_precision))
    seq_in = jnp.concatenate([pooled, low(updated)], 0)
    embed = low_back(jnp.dot(seq_in, w_emb, precision=best_precision))
    normed = low(rms_norm(embed, gains_now[0]))
    qkv = low(low_back(jnp.dot(normed, w_qkv, precision=best_precision)))
    position = jnp.arange(SEQ)
    allowed = (position[None, :] <= position[:, None]) & (position[None, :] < CTX + FT * clip_horizon)
    raw_scores = low_back(jnp.einsum('qhd,khd->hqk', qkv[:, :D].reshape(SEQ, HEADS, HD), qkv[:, D:2 * D].reshape(SEQ, HEADS, HD), precision=best_precision) * score_scale)
    self_probs = low(jax.nn.softmax(jnp.where(allowed[None], raw_scores, neg_large), axis=-1))
    self_mixed = low(low_back(jnp.einsum('hqk,khd->qhd', self_probs, qkv[:, 2 * D:].reshape(SEQ, HEADS, HD), precision=best_precision).reshape(SEQ, D)))
    stream = embed + low_back(jnp.dot(self_mixed, w_att, precision=best_precision))
    normed_two = low(rms_norm(stream, gains_now[1]))
    activated = low(jax.nn.gelu(low_back(jnp.dot(normed_two, w_up, precision=best_precision)), approximate=True))
    return stream + low_back(jnp.dot(activated, w_down, precision=best_precision))

def reference(context_map, future_feats, horizon, cotangent, tile_owner, master_tiles, moment_first, moment_second, norm_gains, gain_first, gain_second):
    slot_of = slot_index(tile_owner, SLOTS)
    position = jnp.arange(SEQ)
    valid = (position[None, :] < CTX + FT * horizon[:, None]).astype(jnp.float32)
    back_rows = cotangent.astype(jnp.float32) * valid[:, :, None]

    def forward(master_now, gains_now, image_all, feats_all):
        tile_stack = low(jnp.take(master_now, slot_of, axis=0))
        conv_tiles, att_tiles, matrices = unpack(tile_stack)

        def one_clip(clip_item):
            return clip_forward(clip_item[0], clip_item[1], clip_item[2], conv_tiles, att_tiles, matrices, gains_now)
        return lax.map(jax.checkpoint(one_clip), (image_all, feats_all, horizon))
    block_out, pullback = jax.vjp(forward, master_tiles, norm_gains, context_map.astype(jnp.float32), future_feats.astype(jnp.float32))
    grad_master, grad_gains, context_grad, future_grad = pullback(back_rows)
    grad_norm = jnp.sqrt(jnp.sum(grad_master * grad_master) + jnp.sum(grad_gains * grad_gains))
    factor = jnp.minimum(1.0, clip_level / (grad_norm + 1e-06))
    used = jnp.zeros((DEVICES * SLOTS,), jnp.float32).at[slot_of].set(1.0)[:, None, None]
    new_first, new_second, new_master = adam_step(master_tiles, grad_master * factor, moment_first, moment_second, learn_rate, decay_rate)
    new_gain_first, new_gain_second, new_gains = adam_step(norm_gains, grad_gains * factor, gain_first, gain_second, gain_rate, 0.0)
    return (block_out, context_grad, future_grad, new_first * used, new_second * used, new_master * used, new_gain_first, new_gain_second, new_gains, grad_norm)
```

```python
import jax
import jax.numpy as jnp
from jax import lax
from jax.sharding import PartitionSpec as P

CH = 256
HD = 64
HEADS = 12
D = 768
FF = 3072
TH = 4
IMG = 64
PATCH = 4
FT = 16
CTX = 256
SEQ = 736
STEP = 10


eps_norm = 1e-05
beta_one = 0.9
beta_two = 0.999
learn_rate = 0.02
gain_rate = 0.6
decay_rate = 0.1
adam_eps = 1e-08
clip_level = 1.0
neg_large = -1e30
AXES = ("z", "c", "y", "x")


def slot_index(tile_owner, slot_count):
    ordinal = jnp.arange(tile_owner.shape[0])
    earlier = (tile_owner[None, :] == tile_owner[:, None]) & (ordinal[None, :] < ordinal[:, None])
    return tile_owner * slot_count + jnp.sum(earlier.astype(jnp.int32), 1)


def unpack(tile_stack):
    per_model = D // CH
    per_hidden = FF // CH
    conv_tiles = tile_stack[0:9]
    att_tiles = tile_stack[9:13]
    offset = 13
    matrices = []
    for tile_rows, tile_cols in (
        (1, per_model),
        (per_model, 3 * per_model),
        (per_model, per_model),
        (per_model, per_hidden),
        (per_hidden, per_model),
    ):
        amount = tile_rows * tile_cols
        tile_block = tile_stack[offset : offset + amount].reshape(tile_rows, tile_cols, CH, CH)
        matrices.append(tile_block.transpose(0, 2, 1, 3).reshape(tile_rows * CH, tile_cols * CH))
        offset = offset + amount
    return (conv_tiles, att_tiles, matrices)


def pack(conv_grad, att_grad, matrices):
    pieces = [conv_grad, att_grad]
    for matrix in matrices:
        tile_rows = matrix.shape[0] // CH
        tile_cols = matrix.shape[1] // CH
        pieces.append(
            matrix.reshape(tile_rows, CH, tile_cols, CH)
            .transpose(0, 2, 1, 3)
            .reshape(tile_rows * tile_cols, CH, CH)
        )
    return jnp.concatenate(pieces, 0)


def rms_norm(values, gain):
    return values * lax.rsqrt(jnp.mean(values * values, -1, keepdims=True) + eps_norm) * gain


def gelu_tanh(values):
    return jax.nn.gelu(values, approximate=True)


def adam_step(weight, grad_now, first, second, rate, decay):
    first_new = beta_one * first + (1.0 - beta_one) * grad_now
    second_new = beta_two * second + (1.0 - beta_two) * grad_now * grad_now
    corr_first = first_new / (1.0 - beta_one**STEP)
    corr_second = second_new / (1.0 - beta_two**STEP)
    weight_new = weight - rate * (corr_first / (jnp.sqrt(corr_second) + adam_eps) + decay * weight)
    return (first_new, second_new, weight_new)


def conv_forward(image, conv_tiles):
    return lax.conv_general_dilated(
        image[None],
        conv_tiles.reshape(3, 3, CH, CH),
        (1, 1),
        [(1, 1), (1, 1)],
        dimension_numbers=("NHWC", "HWIO", "NHWC"),
        preferred_element_type=jnp.float32,
    )[0]


def conv_weight_grad(image, d_conv):
    return lax.conv_general_dilated(
        image[None],
        d_conv[None],
        (1, 1),
        [(1, 1), (1, 1)],
        dimension_numbers=("CHWN", "IHWO", "HWNC"),
        preferred_element_type=jnp.float32,
    ).reshape(9, CH, CH)


def conv_input_grad(d_conv, conv_tiles):
    flipped = conv_tiles[::-1].transpose(0, 2, 1)
    return conv_forward(d_conv, flipped)


def swap_bit(values, axis, bit):
    count = lax.axis_size(axis)
    return lax.ppermute(values, axis, [(i, i ^ bit) for i in range(count)])


def halve(values, axis, dim):
    count = lax.axis_size(axis)
    index = lax.axis_index(axis)
    bit = 1
    while bit < count:
        high = (index // bit) % 2
        shape = values.shape
        parts = values.reshape(
            shape[:dim] + (shape[dim] // 2, 2) + shape[dim + 1 :]
        )
        keep = lax.dynamic_index_in_dim(parts, high, dim + 1, keepdims=False)
        give = lax.dynamic_index_in_dim(parts, 1 - high, dim + 1, keepdims=False)
        got = swap_bit(give, axis, bit)
        values = (keep.astype(jnp.float32) + got.astype(jnp.float32)).astype(values.dtype)
        bit = bit * 2
    return values


def scatter_sum(matrix, order):
    sizes = [lax.axis_size(axis) for axis in AXES]
    values = matrix.astype(jnp.bfloat16).reshape(sizes + [-1, matrix.shape[-1]])
    for axis in order:
        values = halve(values, axis, AXES.index(axis))
    return values.reshape(-1, matrix.shape[-1])


def cross_forward(feats_b, kv_clip, to_query, to_out):
    score_scale = HD ** (-0.5)
    query_b = jnp.dot(feats_b, to_query, preferred_element_type=jnp.float32).astype(jnp.bfloat16)
    key_heads = kv_clip[:, :CH].reshape(-1, TH, HD)
    value_heads = kv_clip[:, CH:].reshape(-1, TH, HD)
    scores = (
        jnp.einsum(
            "qhd,khd->hqk",
            query_b.reshape(-1, TH, HD),
            key_heads,
            preferred_element_type=jnp.float32,
        )
        * score_scale
    )
    row_peak = jnp.max(scores, -1, keepdims=True)
    shifted = jnp.exp(scores - row_peak)
    row_total = jnp.sum(shifted, -1, keepdims=True)
    probs_b = (shifted / row_total).astype(jnp.bfloat16)
    mixed_b = (
        jnp.einsum("hqk,khd->qhd", probs_b, value_heads, preferred_element_type=jnp.float32)
        .reshape(-1, CH)
        .astype(jnp.bfloat16)
    )
    updated = feats_b.astype(jnp.float32) + jnp.dot(
        mixed_b, to_out, preferred_element_type=jnp.float32
    )
    return (query_b, mixed_b, row_peak + jnp.log(row_total), updated)


def cross_backward(feats_b, kv_clip, query_b, mixed_b, log_total, d_updated, to_query, to_out):
    score_scale = HD ** (-0.5)
    d_branch = d_updated.astype(jnp.bfloat16)
    grad_out = jnp.dot(mixed_b.T, d_branch, preferred_element_type=jnp.float32)
    d_mixed = (
        jnp.dot(d_branch, to_out.T, preferred_element_type=jnp.float32)
        .astype(jnp.bfloat16)
        .reshape(-1, TH, HD)
    )
    key_heads = kv_clip[:, :CH].reshape(-1, TH, HD)
    value_heads = kv_clip[:, CH:].reshape(-1, TH, HD)
    query_heads = query_b.reshape(-1, TH, HD)
    scores = (
        jnp.einsum("qhd,khd->hqk", query_heads, key_heads, preferred_element_type=jnp.float32)
        * score_scale
    )
    probs = jnp.exp(scores - log_total)
    d_probs = jnp.einsum("qhd,khd->hqk", d_mixed, value_heads, preferred_element_type=jnp.float32)
    d_values = jnp.einsum(
        "hqk,qhd->khd", probs.astype(jnp.bfloat16), d_mixed, preferred_element_type=jnp.float32
    )
    d_scores = (probs * (d_probs - jnp.sum(probs * d_probs, -1, keepdims=True))).astype(
        jnp.bfloat16
    )
    d_query = (
        (
            jnp.einsum("hqk,khd->qhd", d_scores, key_heads, preferred_element_type=jnp.float32)
            * score_scale
        )
        .reshape(-1, CH)
        .astype(jnp.bfloat16)
    )
    d_keys = (
        jnp.einsum("hqk,qhd->khd", d_scores, query_heads, preferred_element_type=jnp.float32)
        * score_scale
    )
    d_kv = jnp.concatenate([d_keys.reshape(-1, CH), d_values.reshape(-1, CH)], 1).astype(
        jnp.bfloat16
    )
    grad_query = jnp.dot(feats_b.T, d_query, preferred_element_type=jnp.float32)
    d_feats = d_updated + jnp.dot(d_query, to_query.T, preferred_element_type=jnp.float32)
    return (d_kv, d_feats, grad_query, grad_out)


def causal_scores(qkv_b, length):
    position = jnp.arange(qkv_b.shape[0])
    allowed = (position[None, :] <= position[:, None]) & (position[None, :] < length)
    query_heads = qkv_b[:, :D].reshape(-1, HEADS, HD)
    key_heads = qkv_b[:, D : 2 * D].reshape(-1, HEADS, HD)
    raw_scores = jnp.einsum(
        "qhd,khd->hqk", query_heads, key_heads, preferred_element_type=jnp.float32
    ) * HD ** (-0.5)
    return jnp.where(allowed[None], raw_scores, neg_large)


def gpt_forward(seq_in, length, norm_gains, matrices):
    w_emb, w_qkv, w_att, w_up, w_down = matrices
    embed = jnp.dot(seq_in, w_emb, preferred_element_type=jnp.float32)
    normed_b = rms_norm(embed, norm_gains[0]).astype(jnp.bfloat16)
    qkv_b = jnp.dot(normed_b, w_qkv, preferred_element_type=jnp.float32).astype(jnp.bfloat16)
    scores = causal_scores(qkv_b, length)
    row_peak = jnp.max(scores, -1, keepdims=True)
    shifted = jnp.exp(scores - row_peak)
    row_total = jnp.sum(shifted, -1, keepdims=True)
    probs_b = (shifted / row_total).astype(jnp.bfloat16)
    value_heads = qkv_b[:, 2 * D :].reshape(-1, HEADS, HD)
    mixed_b = (
        jnp.einsum("hqk,khd->qhd", probs_b, value_heads, preferred_element_type=jnp.float32)
        .reshape(-1, D)
        .astype(jnp.bfloat16)
    )
    stream = embed + jnp.dot(mixed_b, w_att, preferred_element_type=jnp.float32)
    normed_two = rms_norm(stream, norm_gains[1]).astype(jnp.bfloat16)
    pre_act = jnp.dot(normed_two, w_up, preferred_element_type=jnp.float32)
    act_b = gelu_tanh(pre_act).astype(jnp.bfloat16)
    result = stream + jnp.dot(act_b, w_down, preferred_element_type=jnp.float32)
    return (result, (embed, qkv_b, row_peak + jnp.log(row_total), mixed_b, stream, pre_act))


def gpt_backward(seq_in, length, norm_gains, matrices, kept, d_result):
    w_emb, w_qkv, w_att, w_up, w_down = matrices
    embed, qkv_b, log_total, mixed_b, stream, pre_act = kept
    d_down = d_result.astype(jnp.bfloat16)
    act_b = gelu_tanh(pre_act).astype(jnp.bfloat16)
    grad_down = jnp.dot(act_b.T, d_down, preferred_element_type=jnp.float32)
    d_act = jnp.dot(d_down, w_down.T, preferred_element_type=jnp.float32)
    d_pre = jax.vjp(gelu_tanh, pre_act)[1](d_act)[0].astype(jnp.bfloat16)
    normed_two, norm_back_two = jax.vjp(rms_norm, stream, norm_gains[1])
    grad_up = jnp.dot(normed_two.astype(jnp.bfloat16).T, d_pre, preferred_element_type=jnp.float32)
    d_stream_norm, d_gain_two = norm_back_two(
        jnp.dot(d_pre, w_up.T, preferred_element_type=jnp.float32)
    )
    d_stream = d_result + d_stream_norm
    d_att = d_stream.astype(jnp.bfloat16)
    grad_att = jnp.dot(mixed_b.T, d_att, preferred_element_type=jnp.float32)
    d_mixed = (
        jnp.dot(d_att, w_att.T, preferred_element_type=jnp.float32)
        .astype(jnp.bfloat16)
        .reshape(-1, HEADS, HD)
    )
    probs = jnp.exp(causal_scores(qkv_b, length) - log_total)
    query_heads = qkv_b[:, :D].reshape(-1, HEADS, HD)
    key_heads = qkv_b[:, D : 2 * D].reshape(-1, HEADS, HD)
    value_heads = qkv_b[:, 2 * D :].reshape(-1, HEADS, HD)
    d_probs = jnp.einsum("qhd,khd->hqk", d_mixed, value_heads, preferred_element_type=jnp.float32)
    d_values = jnp.einsum(
        "hqk,qhd->khd", probs.astype(jnp.bfloat16), d_mixed, preferred_element_type=jnp.float32
    )
    d_scores = (probs * (d_probs - jnp.sum(probs * d_probs, -1, keepdims=True))).astype(
        jnp.bfloat16
    )
    d_query = jnp.einsum(
        "hqk,khd->qhd", d_scores, key_heads, preferred_element_type=jnp.float32
    ) * HD ** (-0.5)
    d_keys = jnp.einsum(
        "hqk,qhd->khd", d_scores, query_heads, preferred_element_type=jnp.float32
    ) * HD ** (-0.5)
    d_qkv = jnp.concatenate(
        [d_query.reshape(-1, D), d_keys.reshape(-1, D), d_values.reshape(-1, D)], 1
    ).astype(jnp.bfloat16)
    normed_one, norm_back_one = jax.vjp(rms_norm, embed, norm_gains[0])
    grad_qkv = jnp.dot(normed_one.astype(jnp.bfloat16).T, d_qkv, preferred_element_type=jnp.float32)
    d_embed_norm, d_gain_one = norm_back_one(
        jnp.dot(d_qkv, w_qkv.T, preferred_element_type=jnp.float32)
    )
    d_embed = (d_stream + d_embed_norm).astype(jnp.bfloat16)
    grad_emb = jnp.dot(seq_in.T, d_embed, preferred_element_type=jnp.float32)
    d_seq = jnp.dot(d_embed, w_emb.T, preferred_element_type=jnp.float32)
    return (
        d_seq,
        (grad_emb, grad_qkv, grad_att, grad_up, grad_down),
        jnp.stack([d_gain_one, d_gain_two]),
    )


def local(
    context_map,
    future_feats,
    horizon,
    cotangent,
    tile_owner,
    master_tiles,
    moment_first,
    moment_second,
    norm_gains,
    gain_first,
    gain_second,
):
    slot_count = master_tiles.shape[0]
    slot_of = slot_index(tile_owner, slot_count)
    gathered = lax.all_gather(master_tiles.astype(jnp.bfloat16), AXES, axis=0, tiled=True)
    image = lax.all_to_all(context_map, ("y", "x"), split_axis=0, concat_axis=1, tiled=True)[0]
    tile_stack = gathered.at[slot_of].get(mode="promise_in_bounds")
    conv_tiles, att_tiles, matrices = unpack(tile_stack)
    kv_weight = jnp.concatenate([att_tiles[1], att_tiles[2]], 1)
    conv_out = conv_forward(image, conv_tiles)
    hidden = image.astype(jnp.float32) + jax.nn.silu(conv_out)
    hidden_b = hidden.astype(jnp.bfloat16).reshape(IMG * IMG, CH)
    kv_clip = jnp.dot(hidden_b, kv_weight, preferred_element_type=jnp.float32).astype(jnp.bfloat16)
    side = IMG // PATCH
    pool_clip = (
        jnp.mean(hidden.reshape(side, PATCH, side, PATCH, CH), axis=(1, 3))
        .reshape(CTX, CH)
        .astype(jnp.bfloat16)
    )
    feats_b = future_feats[0]
    length = CTX + FT * horizon[0]
    query_b, mixed_b, cross_total, updated = cross_forward(
        feats_b, kv_clip, att_tiles[0], att_tiles[3]
    )
    seq_in = jnp.concatenate([pool_clip, updated.astype(jnp.bfloat16)], 0)
    block_out, kept = gpt_forward(seq_in, length, norm_gains, matrices)
    position = jnp.arange(SEQ)
    d_result = cotangent[0].astype(jnp.float32) * (position < length).astype(jnp.float32)[:, None]
    d_seq, mat_grads, gain_grad = gpt_backward(
        seq_in, length, norm_gains, matrices, kept, d_result
    )
    grad_emb, grad_qkv, grad_att, grad_up, grad_down = mat_grads
    gain_total = lax.psum(gain_grad, AXES)
    sums = [
        scatter_sum(grad_down, ("c", "x", "y", "z")),
        scatter_sum(grad_up, ("c", "y", "x", "z")),
        scatter_sum(grad_att, ("c", "x", "y", "z")),
        scatter_sum(grad_qkv, ("c", "y", "x", "z")),
        scatter_sum(grad_emb, ("c", "x", "y", "z")),
    ]
    d_pool = d_seq[:CTX].astype(jnp.bfloat16)
    d_kv, d_feats, grad_query, grad_out = cross_backward(
        feats_b, kv_clip, query_b, mixed_b, cross_total, d_seq[CTX:], att_tiles[0], att_tiles[3]
    )
    grad_kv = jnp.dot(hidden_b.T, d_kv, preferred_element_type=jnp.float32)
    d_hidden = jnp.dot(d_kv, kv_weight.T, preferred_element_type=jnp.float32).reshape(IMG, IMG, CH)
    pool_spread = d_pool.astype(jnp.float32).reshape(side, 1, side, 1, CH) * (
        1.0 / (PATCH * PATCH)
    )
    d_hidden = d_hidden + jnp.broadcast_to(pool_spread, (side, PATCH, side, PATCH, CH)).reshape(
        IMG, IMG, CH
    )
    d_conv = jax.vjp(jax.nn.silu, conv_out)[1](d_hidden)[0].astype(jnp.bfloat16)
    grad_conv = conv_weight_grad(image, d_conv)
    context_grad = d_hidden + conv_input_grad(d_conv, conv_tiles)
    rows = lax.all_to_all(
        context_grad.astype(jnp.bfloat16)[None],
        ("y", "x"),
        split_axis=1,
        concat_axis=0,
        tiled=True,
    ).astype(jnp.float32)
    early = jnp.concatenate(
        [
            grad_conv.reshape(9 * CH, CH),
            grad_query,
            grad_kv[:, :CH],
            grad_kv[:, CH:],
            grad_out,
        ],
        0,
    )
    sums.append(scatter_sum(early, ("c", "x", "y", "z")))
    whole = [lax.all_gather(part, AXES, axis=0, tiled=True) for part in sums]
    down_all, up_all, att_all, qkv_all, emb_all, early_all = whole
    tile_grads = pack(
        early_all.reshape(13, CH, CH)[:9],
        early_all.reshape(13, CH, CH)[9:],
        (emb_all, qkv_all, att_all, up_all, down_all),
    )
    square_total = jnp.sum(tile_grads.astype(jnp.float32) ** 2)
    my_slots = lax.axis_index(AXES) * slot_count + jnp.arange(slot_count)
    found = slot_of[None, :] == my_slots[:, None]
    used = jnp.any(found, 1).astype(jnp.float32)[:, None, None]
    my_tiles = jnp.sum(jnp.where(found, jnp.arange(found.shape[1])[None], 0), 1)
    mine = tile_grads.at[my_tiles].get(mode="promise_in_bounds").astype(jnp.float32)
    grad_norm = jnp.sqrt(square_total + jnp.sum(gain_total * gain_total))
    factor = jnp.minimum(1.0, clip_level / (grad_norm + 1e-06))
    new_first, new_second, new_master = adam_step(
        master_tiles, mine * factor, moment_first, moment_second, learn_rate, decay_rate
    )
    new_gain_first, new_gain_second, new_gains = adam_step(
        norm_gains, gain_total * factor, gain_first, gain_second, gain_rate, 0.0
    )
    return (
        block_out[None],
        rows,
        d_feats[None],
        new_first * used,
        new_second * used,
        new_master * used,
        new_gain_first,
        new_gain_second,
        new_gains,
        grad_norm,
    )


def solution(mesh):
    groups, rows = mesh.devices.shape
    fine = jax.sharding.Mesh(mesh.devices.reshape(groups // 2, 2, rows // 2, 2), AXES)
    whole = P(AXES, None, None)
    image = P(("z", "c"), ("y", "x"), None, None)
    in_specs = (image, whole, P(AXES), whole, P(), whole, whole, whole, P(), P(), P())
    out_specs = (whole, image, whole, whole, whole, whole, P(), P(), P(), P())
    return jax.shard_map(local, mesh=fine, in_specs=in_specs, out_specs=out_specs, check_vma=False)
```

```python
import jax
import jax.numpy as jnp
from jax import lax
from jax.experimental import pallas as pl
from jax.experimental.pallas import tpu as pltpu
from jax.sharding import PartitionSpec as P

CH = 256
HD = 64
HEADS = 12
D = 768
FF = 3072
TH = 4
IMG = 64
PATCH = 4
FT = 16
CTX = 256
SEQ = 736
STEP = 10


eps_norm = 1e-05
beta_one = 0.9
beta_two = 0.999
learn_rate = 0.02
gain_rate = 0.6
decay_rate = 0.1
adam_eps = 1e-08
clip_level = 1.0
neg_large = -1e30
AXES = ("z", "c", "y", "x")
CELLS = IMG * IMG
BLOCK = 512
GROUP = 4
EARLY = 13
VMEM_BYTES = 56 * 1024 * 1024
ROW_BLOCKS = ((0, 256), (256, 256), (512, 224))
bf16 = jnp.bfloat16
f32 = jnp.float32


def slot_index(tile_owner, slot_count):
    ordinal = jnp.arange(tile_owner.shape[0])
    earlier = (tile_owner[None, :] == tile_owner[:, None]) & (ordinal[None, :] < ordinal[:, None])
    return tile_owner * slot_count + jnp.sum(earlier.astype(jnp.int32), 1)


def adam_step(weight, grad_now, first, second, rate, decay):
    first_new = beta_one * first + (1.0 - beta_one) * grad_now
    second_new = beta_two * second + (1.0 - beta_two) * grad_now * grad_now
    corr_first = first_new / (1.0 - beta_one**STEP)
    corr_second = second_new / (1.0 - beta_two**STEP)
    weight_new = weight - rate * (corr_first / (jnp.sqrt(corr_second) + adam_eps) + decay * weight)
    return (first_new, second_new, weight_new)


def xor_permute(values, axes, mask):
    count = lax.axis_size(axes)
    return lax.ppermute(values, axes, [(i, i ^ mask) for i in range(count)])


def scatter_axes(values, axes, dim, keep_wide=False):
    count = lax.axis_size(axes)
    mine = lax.axis_index(axes)
    total = lax.dynamic_index_in_dim(values, mine, dim, keepdims=False).astype(f32)
    for mask in range(1, count):
        give = lax.dynamic_index_in_dim(values, mine ^ mask, dim, keepdims=False)
        total = total + xor_permute(give, axes, mask).astype(f32)
    return total if keep_wide else total.astype(values.dtype)


def gather_axes(values, axes):
    pieces = [values]
    for mask in range(1, lax.axis_size(axes)):
        pieces.append(xor_permute(values, axes, mask))
    return jnp.stack(pieces)


def gather_all(values):
    shape = values.shape
    values = gather_axes(values, "z")
    values = gather_axes(values, ("y", "x"))
    values = gather_axes(values, "c")
    cores, rows, depth = values.shape[:3]
    order = jnp.arange(depth * cores * rows)
    z, c, row = order // (cores * rows), (order // rows) % cores, order % rows
    own = lax.axis_index("z"), lax.axis_index("c"), lax.axis_index(("y", "x"))
    at = ((c ^ own[1]) * rows + (row ^ own[2])) * depth + (z ^ own[0])
    return values.reshape((-1,) + shape).at[at].get(mode="promise_in_bounds")


def sum_all(values):
    for axis in ("c", "x", "y", "z"):
        bit = 1
        while bit < lax.axis_size(axis):
            values = values + xor_permute(values, axis, bit)
            bit = bit * 2
    return values


def cut(matrix):
    sizes = [lax.axis_size(axis) for axis in AXES]
    return matrix.astype(bf16).reshape([-1] + sizes + [CH // lax.axis_size(AXES), matrix.shape[-1]])


def sum_core(slices):
    return scatter_axes(slices, "c", 2)


def sum_x(slices):
    return scatter_axes(slices, "x", slices.ndim - 3)


def sum_y(slices):
    return scatter_axes(slices, "y", 2)


def sum_z(slices):
    return scatter_axes(slices, "z", 1, keep_wide=True)


def to_tiles(slices):
    blocks, rows, columns = slices.shape
    return (
        slices.reshape(blocks, rows, columns // CH, CH)
        .transpose(0, 2, 1, 3)
        .reshape(-1, rows, CH)
    )


def dot_nt(a, b):
    return lax.dot_general(a, b, (((1,), (1,)), ((), ())), preferred_element_type=f32)


def dot_nn(a, b):
    return lax.dot_general(a, b, (((1,), (0,)), ((), ())), preferred_element_type=f32)


def dot_tn(a, b):
    return lax.dot_general(a, b, (((0,), (0,)), ((), ())), preferred_element_type=f32)


def head_mask(shape, head):
    return (lax.broadcasted_iota(jnp.int32, shape, len(shape) - 1) // HD) == head


def cost(flops, moved, transcendentals=0):
    return pl.CostEstimate(
        flops=int(flops), bytes_accessed=int(moved), transcendentals=int(transcendentals)
    )


def params():
    return pltpu.CompilerParams(vmem_limit_bytes=VMEM_BYTES)


def cross_forward_kernel(q_ref, k_ref, v_ref, o_ref, l_ref):
    rows = q_ref.shape[0]
    lane = lax.broadcasted_iota(jnp.int32, (rows, 128), 1)
    q = q_ref[...]
    mixed = jnp.zeros((rows, CH), f32)
    stat = jnp.zeros((rows, 128), f32)
    for head in range(TH):
        mask = head_mask((rows, CH), head)
        q_head = jnp.where(mask, q.astype(f32) * 0.125, 0.0).astype(bf16)
        scores = dot_nt(q_head, k_ref[...])
        peak = jnp.max(scores, -1, keepdims=True)
        shifted = jnp.exp(scores - peak)
        total = jnp.sum(shifted, -1, keepdims=True)
        part = dot_nn(shifted.astype(bf16), v_ref[...])
        mixed = jnp.where(mask, part / total, mixed)
        stat = jnp.where(lane == head, peak + jnp.log(total), stat)
    o_ref[...] = mixed.astype(bf16)
    l_ref[...] = stat


def cross_forward(query, kv):
    rows = query.shape[0] // 2
    cells = kv.shape[0]
    return pl.pallas_call(
        cross_forward_kernel,
        grid=(2,),
        in_specs=[
            pl.BlockSpec((rows, CH), lambda i: (i, 0)),
            pl.BlockSpec((cells, CH), lambda i: (0, 0)),
            pl.BlockSpec((cells, CH), lambda i: (0, 1)),
        ],
        out_specs=[
            pl.BlockSpec((rows, CH), lambda i: (i, 0)),
            pl.BlockSpec((rows, 128), lambda i: (i, 0)),
        ],
        out_shape=[
            jax.ShapeDtypeStruct((2 * rows, CH), bf16),
            jax.ShapeDtypeStruct((2 * rows, 128), f32),
        ],
        compiler_params=params(),
        cost_estimate=cost(16 * TH * rows * cells * CH // 2, 8 * cells * CH, 2 * TH * rows * cells),
    )(query, kv, kv)


def delta_rows(d_out, out):
    product = d_out.astype(f32) * out.astype(f32)
    head = lax.broadcasted_iota(jnp.int32, (8, CH), 0)
    lane = lax.broadcasted_iota(jnp.int32, (8, CH), 1)
    pick = ((lane // HD) == head).astype(f32)
    return lax.dot_general(
        pick,
        product,
        (((1,), (1,)), ((), ())),
        precision=lax.Precision.HIGHEST,
        preferred_element_type=f32,
    )


def cross_backward_kernel(
    q_ref, k_ref, v_ref, do_ref, o_ref, l_ref, dq_ref, dkv_ref, q_s, do_s, delta_s, dq_s
):
    step = pl.program_id(0)
    rows = q_ref.shape[0]

    @pl.when(step == 0)
    def _():
        for head in range(TH):
            mask = head_mask((rows, CH), head)
            q_s[head] = jnp.where(mask, q_ref[...].astype(f32) * 0.125, 0.0).astype(bf16)
            do_s[head] = jnp.where(mask, do_ref[...].astype(f32), 0.0).astype(bf16)
        delta_s[...] = delta_rows(do_ref[...], o_ref[...])
        dq_s[...] = jnp.zeros_like(dq_s)

    cells = k_ref.shape[0]
    dk = jnp.zeros((cells, CH), f32)
    dv = jnp.zeros((cells, CH), f32)
    dq = dq_s[...]
    k = k_ref[...]
    for head in range(TH):
        probs = jnp.exp(dot_nt(k, q_s[head]) - l_ref[head : head + 1, :])
        d_probs = dot_nt(v_ref[...], do_s[head])
        d_scores = (probs * (d_probs - delta_s[head : head + 1, :])).astype(bf16)
        dv = dv + dot_nn(probs.astype(bf16), do_s[head])
        dk = dk + dot_nn(d_scores, q_s[head])
        dq = dq + jnp.where(head_mask((rows, CH), head), dot_tn(d_scores, k), 0.0)
    dq_s[...] = dq
    dkv_ref[:, :CH] = dk.astype(bf16)
    dkv_ref[:, CH:] = dv.astype(bf16)

    @pl.when(step == pl.num_programs(0) - 1)
    def _():
        dq_ref[...] = (dq_s[...] * 0.125).astype(bf16)


def cross_backward(query, kv, d_out, out, log_rows):
    rows = query.shape[0]
    cells = kv.shape[0]
    block = 1024
    whole = lambda i: (0, 0)
    return pl.pallas_call(
        cross_backward_kernel,
        grid=(cells // block,),
        in_specs=[
            pl.BlockSpec((rows, CH), whole),
            pl.BlockSpec((block, CH), lambda i: (i, 0)),
            pl.BlockSpec((block, CH), lambda i: (i, 1)),
            pl.BlockSpec((rows, CH), whole),
            pl.BlockSpec((rows, CH), whole),
            pl.BlockSpec((TH, rows), whole),
        ],
        out_specs=[
            pl.BlockSpec((rows, CH), whole),
            pl.BlockSpec((block, 2 * CH), lambda i: (i, 0)),
        ],
        out_shape=[
            jax.ShapeDtypeStruct((rows, CH), bf16),
            jax.ShapeDtypeStruct((cells, 2 * CH), bf16),
        ],
        scratch_shapes=[
            pltpu.VMEM((TH, rows, CH), bf16),
            pltpu.VMEM((TH, rows, CH), bf16),
            pltpu.VMEM((8, rows), f32),
            pltpu.VMEM((rows, CH), f32),
        ],
        compiler_params=params(),
        cost_estimate=cost(10 * TH * rows * cells * CH, 8 * cells * CH, TH * rows * cells),
    )(query, kv, kv, d_out, out, log_rows)


def self_forward_kernel(len_ref, q_ref, k_ref, v_ref, o_ref, l_ref):
    group = pl.program_id(0)
    length = len_ref[0]
    for start, count in ROW_BLOCKS:
        stop = start + count
        q = q_ref[start:stop, :].astype(f32) * 0.125
        row = lax.broadcasted_iota(jnp.int32, (count, 1), 0) + start
        bound = jnp.minimum(row, length - 1)
        allowed = lax.broadcasted_iota(jnp.int32, (count, stop), 1) <= bound
        mixed = jnp.zeros((count, CH), f32)
        stat = l_ref[start:stop, :]
        lane = lax.broadcasted_iota(jnp.int32, (count, 128), 1)
        for head in range(GROUP):
            mask = head_mask((count, CH), head)
            q_head = jnp.where(mask, q, 0.0).astype(bf16)
            scores = jnp.where(allowed, dot_nt(q_head, k_ref[:stop, :]), neg_large)
            peak = jnp.max(scores, -1, keepdims=True)
            shifted = jnp.exp(scores - peak)
            total = jnp.sum(shifted, -1, keepdims=True)
            part = dot_nn(shifted.astype(bf16), v_ref[:stop, :])
            mixed = jnp.where(mask, part / total, mixed)
            stat = jnp.where(lane == group * GROUP + head, peak + jnp.log(total), stat)
        o_ref[start:stop, :] = mixed.astype(bf16)
        l_ref[start:stop, :] = stat


def self_forward(qkv, length):
    groups = D // CH
    return pl.pallas_call(
        self_forward_kernel,
        grid_spec=pltpu.PrefetchScalarGridSpec(
            num_scalar_prefetch=1,
            grid=(groups,),
            in_specs=[
                pl.BlockSpec((SEQ, CH), lambda i, n: (0, i)),
                pl.BlockSpec((SEQ, CH), lambda i, n: (0, groups + i)),
                pl.BlockSpec((SEQ, CH), lambda i, n: (0, 2 * groups + i)),
            ],
            out_specs=[
                pl.BlockSpec((SEQ, CH), lambda i, n: (0, i)),
                pl.BlockSpec((SEQ, 128), lambda i, n: (0, 0)),
            ],
        ),
        out_shape=[
            jax.ShapeDtypeStruct((SEQ, D), bf16),
            jax.ShapeDtypeStruct((SEQ, 128), f32),
        ],
        compiler_params=params(),
        cost_estimate=cost(4 * HEADS * SEQ * SEQ * CH, 8 * SEQ * D, HEADS * SEQ * SEQ),
    )(length, qkv, qkv, qkv)


def self_backward_kernel(
    len_ref, q_ref, k_ref, v_ref, do_ref, o_ref, l_ref, out_ref, dk_s, dv_s
):
    length = len_ref[0]
    dk_s[...] = jnp.zeros_like(dk_s)
    dv_s[...] = jnp.zeros_like(dv_s)
    delta = delta_rows(do_ref[...], o_ref[...])
    for start, count in ROW_BLOCKS:
        stop = start + count
        q = q_ref[start:stop, :].astype(f32) * 0.125
        d_out = do_ref[start:stop, :].astype(f32)
        row = lax.broadcasted_iota(jnp.int32, (1, count), 1) + start
        bound = jnp.minimum(row, length - 1)
        allowed = lax.broadcasted_iota(jnp.int32, (stop, count), 0) <= bound
        dq = jnp.zeros((count, CH), f32)
        k = k_ref[:stop, :]
        v = v_ref[:stop, :]
        dk = dk_s[:stop, :]
        dv = dv_s[:stop, :]
        for head in range(GROUP):
            mask = head_mask((count, CH), head)
            q_head = jnp.where(mask, q, 0.0).astype(bf16)
            d_head = jnp.where(mask, d_out, 0.0).astype(bf16)
            scores = dot_nt(k, q_head)
            logs = l_ref[0, head : head + 1, start:stop]
            probs = jnp.where(allowed, jnp.exp(scores - logs), 0.0)
            d_probs = dot_nt(v, d_head)
            d_scores = (probs * (d_probs - delta[head : head + 1, start:stop])).astype(bf16)
            dv = dv + dot_nn(probs.astype(bf16), d_head)
            dk = dk + dot_nn(d_scores, q_head)
            dq = dq + jnp.where(mask, dot_tn(d_scores, k), 0.0)
        dk_s[:stop, :] = dk
        dv_s[:stop, :] = dv
        out_ref[0, start:stop, :] = (dq * 0.125).astype(bf16)
    out_ref[1] = dk_s[...].astype(bf16)
    out_ref[2] = dv_s[...].astype(bf16)


def self_backward(qkv, d_out, out, log_rows, length):
    groups = D // CH
    at = lambda j: (lambda i, n: (0, j * groups + i))
    return pl.pallas_call(
        self_backward_kernel,
        grid_spec=pltpu.PrefetchScalarGridSpec(
            num_scalar_prefetch=1,
            grid=(groups,),
            in_specs=[
                pl.BlockSpec((SEQ, CH), at(0)),
                pl.BlockSpec((SEQ, CH), at(1)),
                pl.BlockSpec((SEQ, CH), at(2)),
                pl.BlockSpec((SEQ, CH), at(0)),
                pl.BlockSpec((SEQ, CH), at(0)),
                pl.BlockSpec((1, GROUP, SEQ), lambda i, n: (i, 0, 0)),
            ],
            out_specs=pl.BlockSpec((3, SEQ, CH), lambda i, n: (0, 0, i)),
            scratch_shapes=[pltpu.VMEM((SEQ, CH), f32), pltpu.VMEM((SEQ, CH), f32)],
        ),
        out_shape=jax.ShapeDtypeStruct((3, SEQ, D), bf16),
        compiler_params=params(),
        cost_estimate=cost(8 * HEADS * SEQ * SEQ * CH, 16 * SEQ * D, HEADS * SEQ * SEQ),
    )(length, qkv, qkv, qkv, d_out, out, log_rows)


def patch_pick(rows, columns, patch_dim):
    patch = lax.broadcasted_iota(jnp.int32, (rows, columns), patch_dim)
    cell = lax.broadcasted_iota(jnp.int32, (rows, columns), 1 - patch_dim)
    inside = (cell // (PATCH * IMG)) * (IMG // PATCH) + (cell % IMG) // PATCH
    return jnp.where(patch == inside, 1.0 / (PATCH * PATCH), 0.0).astype(bf16)


def image_rows(step, row):
    return pl.ds(pl.multiple_of(step * BLOCK + row * IMG, IMG), BLOCK)


def token_forward_kernel(x_ref, conv_ref, kv_w_ref, slope_ref, hidden_ref, kv_ref, pool_ref):
    step = pl.program_id(0)
    z = jnp.zeros((BLOCK, CH), f32)
    for row in range(3):
        z = z + dot_nn(x_ref[image_rows(step, row), :], conv_ref[row])
    center = x_ref[image_rows(step, 1), CH : 2 * CH].astype(f32)
    gate = 1.0 / (1.0 + jnp.exp(-z))
    hidden = center + z * gate
    slope_ref[...] = (gate * (1.0 + z * (1.0 - gate))).astype(bf16)
    hidden_b = hidden.astype(bf16)
    hidden_ref[...] = hidden_b
    kv_ref[...] = dot_nn(hidden_b, kv_w_ref[...]).astype(bf16)
    rest = (hidden - hidden_b.astype(f32)).astype(bf16)
    pick = patch_pick(pool_ref.shape[0], BLOCK, 0)
    pool_ref[...] = (dot_nn(pick, hidden_b) + dot_nn(pick, rest)).astype(bf16)


def token_forward(wide, conv_rows, kv_weight):
    steps = CELLS // BLOCK
    whole = lambda i: (0, 0)
    block = lambda i: (i, 0)
    return pl.pallas_call(
        token_forward_kernel,
        grid=(steps,),
        in_specs=[
            pl.BlockSpec(wide.shape, whole),
            pl.BlockSpec((3, 3 * CH, CH), lambda i: (0, 0, 0)),
            pl.BlockSpec((CH, 2 * CH), whole),
        ],
        out_specs=[
            pl.BlockSpec((BLOCK, CH), block),
            pl.BlockSpec((BLOCK, CH), block),
            pl.BlockSpec((BLOCK, 2 * CH), block),
            pl.BlockSpec((CTX // steps, CH), block),
        ],
        out_shape=[
            jax.ShapeDtypeStruct((CELLS, CH), bf16),
            jax.ShapeDtypeStruct((CELLS, CH), bf16),
            jax.ShapeDtypeStruct((CELLS, 2 * CH), bf16),
            jax.ShapeDtypeStruct((CTX, CH), bf16),
        ],
        compiler_params=params(),
        cost_estimate=cost(22 * CELLS * CH * CH, 14 * CELLS * CH, CELLS * CH),
    )(wide, conv_rows, kv_weight)


def token_backward_kernel(
    dkv_ref, slope_ref, pool_ref, hidden_ref, x_ref, kv_w_ref,
    d_hidden_ref, gz_ref, conv_ref, kv_g_ref, conv_s, kv_s,
):
    step = pl.program_id(0)

    @pl.when(step == 0)
    def _():
        conv_s[...] = jnp.zeros_like(conv_s)
        kv_s[...] = jnp.zeros_like(kv_s)

    dkv = dkv_ref[...]
    d_hidden = dot_nt(dkv, kv_w_ref[...])
    d_hidden = d_hidden + dot_nn(patch_pick(BLOCK, pool_ref.shape[0], 1), pool_ref[...])
    gz = (d_hidden * slope_ref[...].astype(f32)).astype(bf16)
    d_hidden_ref[...] = d_hidden
    gz_ref[...] = gz
    kv_s[...] += dot_tn(hidden_ref[...], dkv)
    gz_t = gz.T
    for row in range(3):
        conv_s[row] += dot_nn(gz_t, x_ref[image_rows(step, row), :])

    @pl.when(step == pl.num_programs(0) - 1)
    def _():
        for row in range(3):
            for col in range(3):
                conv_ref[3 * row + col] = conv_s[row, :, col * CH : (col + 1) * CH].T.astype(bf16)
        kv_g_ref[0] = kv_s[:, :CH].astype(bf16)
        kv_g_ref[1] = kv_s[:, CH:].astype(bf16)


def token_backward(dkv, slope, d_pool, hidden_b, wide, kv_weight):
    steps = CELLS // BLOCK
    whole = lambda i: (0, 0)
    whole_3 = lambda i: (0, 0, 0)
    block = lambda i: (i, 0)
    return pl.pallas_call(
        token_backward_kernel,
        grid=(steps,),
        in_specs=[
            pl.BlockSpec((BLOCK, 2 * CH), block),
            pl.BlockSpec((BLOCK, CH), block),
            pl.BlockSpec((CTX // steps, CH), block),
            pl.BlockSpec((BLOCK, CH), block),
            pl.BlockSpec(wide.shape, whole),
            pl.BlockSpec((CH, 2 * CH), whole),
        ],
        out_specs=[
            pl.BlockSpec((BLOCK, CH), block),
            pl.BlockSpec((BLOCK, CH), block),
            pl.BlockSpec((9, CH, CH), whole_3),
            pl.BlockSpec((2, CH, CH), whole_3),
        ],
        out_shape=[
            jax.ShapeDtypeStruct((CELLS, CH), f32),
            jax.ShapeDtypeStruct((CELLS, CH), bf16),
            jax.ShapeDtypeStruct((9, CH, CH), bf16),
            jax.ShapeDtypeStruct((2, CH, CH), bf16),
        ],
        scratch_shapes=[pltpu.VMEM((3, CH, 3 * CH), f32), pltpu.VMEM((CH, 2 * CH), f32)],
        compiler_params=params(),
        cost_estimate=cost(26 * CELLS * CH * CH, 20 * CELLS * CH),
    )(dkv, slope, d_pool, hidden_b, wide, kv_weight)


def context_backward_kernel(gz_ref, d_hidden_ref, conv_ref, out_ref, wide_s):
    step = pl.program_id(0)
    steps = pl.num_programs(0)

    def widen(at):
        values = gz_ref[image_rows(at, 0), :].astype(f32)
        col = lax.broadcasted_iota(jnp.int32, (BLOCK, CH), 0) % IMG
        left = jnp.where(col == 0, 0.0, pltpu.roll(values, 1, 0))
        right = jnp.where(col == IMG - 1, 0.0, pltpu.roll(values, BLOCK - 1, 0))
        wide_s[image_rows(at, 1), 0:CH] = left.astype(bf16)
        wide_s[image_rows(at, 1), CH : 2 * CH] = values.astype(bf16)
        wide_s[image_rows(at, 1), 2 * CH :] = right.astype(bf16)

    @pl.when(step == 0)
    def _():
        wide_s[0:IMG, :] = jnp.zeros((IMG, 3 * CH), bf16)
        wide_s[CELLS + IMG :, :] = jnp.zeros((IMG, 3 * CH), bf16)
        widen(0)

    @pl.when(step < steps - 1)
    def _():
        widen(step + 1)

    total = d_hidden_ref[...]
    for row in range(3):
        values = wide_s[image_rows(step, row), :]
        for col in range(3):
            tap = conv_ref[3 * (2 - row) + (2 - col)]
            total = total + dot_nt(values[:, col * CH : (col + 1) * CH], tap)
    out_ref[...] = total.astype(bf16)


def context_backward(gz, d_hidden, conv_tiles):
    block = lambda i: (i, 0)
    return pl.pallas_call(
        context_backward_kernel,
        grid=(CELLS // BLOCK,),
        in_specs=[
            pl.BlockSpec((CELLS, CH), lambda i: (0, 0)),
            pl.BlockSpec((BLOCK, CH), block),
            pl.BlockSpec((9, CH, CH), lambda i: (0, 0, 0)),
        ],
        out_specs=pl.BlockSpec((BLOCK, CH), block),
        out_shape=jax.ShapeDtypeStruct((CELLS, CH), bf16),
        scratch_shapes=[pltpu.VMEM((CELLS + 2 * IMG, 3 * CH), bf16)],
        compiler_params=params(),
        cost_estimate=cost(18 * CELLS * CH * CH, 8 * CELLS * CH),
    )(gz, d_hidden, conv_tiles)


def dot(a, b):
    return jnp.dot(a, b, preferred_element_type=f32)


def gelu_slope(v):
    inner = jnp.sqrt(2.0 / jnp.pi) * (v + 0.044715 * v * v * v)
    bend = jnp.tanh(inner)
    d_inner = jnp.sqrt(2.0 / jnp.pi) * (1.0 + 3.0 * 0.044715 * v * v)
    return 0.5 * (1.0 + bend) + 0.5 * v * (1.0 - bend * bend) * d_inner


def inverse_rms(values):
    return lax.rsqrt(jnp.mean(values * values, -1, keepdims=True) + eps_norm)


def norm_backward(d_normed, values, scale, gain):
    d_gain = jnp.sum(d_normed * values * scale, 0)
    scaled = d_normed * gain
    inner = jnp.mean(scaled * values, -1, keepdims=True)
    return d_gain, scale * scaled - (scale * scale * scale) * values * inner


def local(
    context_map,
    future_feats,
    horizon,
    cotangent,
    tile_owner,
    master_tiles,
    moment_first,
    moment_second,
    norm_gains,
    gain_first,
    gain_second,
):
    slot_count = master_tiles.shape[0]
    devices = lax.axis_size(AXES)
    rows = CH // devices
    slot_of = slot_index(tile_owner, slot_count)

    slices = (
        master_tiles.astype(bf16)
        .reshape(slot_count, devices, rows, CH)
        .transpose(1, 0, 2, 3)
    )
    slices = lax.all_to_all(slices, AXES, split_axis=0, concat_axis=0, tiled=True)
    slices = slices.reshape(devices * slot_count, rows, CH)
    slices = slices.at[slot_of].get(mode="promise_in_bounds")
    early = gather_all(slices[:EARLY]).transpose(1, 0, 2, 3).reshape(EARLY, CH, CH)
    later = slices[EARLY:].reshape(-1, D // CH, rows, CH).transpose(0, 2, 1, 3)
    later = lax.all_gather(later.reshape(-1, D), AXES, axis=0, tiled=True)
    later = later.reshape(devices, -1, rows, D)

    def matrix(start, row_blocks, parts):
        part = later[:, start : start + row_blocks * parts]
        part = part.reshape(devices, row_blocks, parts, rows, D)
        return part.transpose(1, 0, 3, 2, 4).reshape(row_blocks * CH, parts * D)

    image = lax.all_to_all(context_map, ("y", "x"), split_axis=0, concat_axis=1, tiled=True)[0]
    padded = jnp.pad(image, ((1, 1), (1, 1), (0, 0)))
    wide = jnp.concatenate([padded[:, col : col + IMG] for col in range(3)], -1)
    wide = wide.reshape((IMG + 2) * IMG, 3 * CH)

    conv_tiles = early[:9]
    to_query, to_out = early[9], early[12]
    kv_weight = jnp.concatenate([early[10], early[11]], 1)
    w_emb = matrix(0, 1, 1)
    w_qkv = matrix(1, 3, 3)
    w_att = matrix(10, 3, 1)
    w_up = matrix(13, 3, 4)
    w_down = matrix(25, 12, 1)

    slope, hidden_b, kv, pooled = token_forward(wide, conv_tiles.reshape(3, 3 * CH, CH), kv_weight)
    feats_b = future_feats[0]
    length = CTX + FT * horizon
    query = dot(feats_b, to_query).astype(bf16)
    cross_mixed, cross_logs = cross_forward(query, kv)
    updated = feats_b.astype(f32) + dot(cross_mixed, to_out)
    seq = jnp.concatenate([pooled, updated.astype(bf16)], 0)

    gain_one, gain_two = norm_gains[0], norm_gains[1]
    embed = dot(seq, w_emb)
    scale_one = inverse_rms(embed)
    normed_one = (embed * scale_one * gain_one).astype(bf16)
    qkv = dot(normed_one, w_qkv).astype(bf16)
    mixed, logs = self_forward(qkv, length)
    stream = embed + dot(mixed, w_att)
    scale_two = inverse_rms(stream)
    normed_two = (stream * scale_two * gain_two).astype(bf16)
    pre = dot(normed_two, w_up)
    act = jax.nn.gelu(pre, approximate=True).astype(bf16)
    block_out = stream + dot(act, w_down)

    valid = jnp.arange(SEQ) < length[0]
    gd = jnp.where(valid[:, None], cotangent[0], jnp.zeros((), bf16))
    sum_down = cut(dot(act.T, gd))
    gd, sum_down = lax.optimization_barrier((gd, sum_down))
    gpre = (dot(gd, w_down.T) * gelu_slope(pre)).astype(bf16)
    sum_down = sum_core(sum_down)
    sum_up = cut(dot(normed_two.T, gpre))
    gpre, sum_up, sum_down = lax.optimization_barrier((gpre, sum_up, sum_down))
    d_gain_two, d_stream = norm_backward(dot(gpre, w_up.T), stream, scale_two, gain_two)
    d_stream = gd.astype(f32) + d_stream
    ga = d_stream.astype(bf16)
    sum_up = sum_core(sum_up)
    ga, sum_up = lax.optimization_barrier((ga, sum_up))
    sum_down = sum_x(sum_down)
    sum_up = sum_y(sum_up)
    sum_att = cut(dot(mixed.T, ga))
    gog = dot(ga, w_att.T).astype(bf16)
    gog, sum_att = lax.optimization_barrier((gog, sum_att))
    sum_att = sum_core(sum_att)
    log_rows = logs[:, :HEADS].T.reshape(D // CH, GROUP, SEQ)
    gqkv = self_backward(qkv, gog, mixed, log_rows, length)
    gqkv, sum_down, sum_up, sum_att = lax.optimization_barrier((gqkv, sum_down, sum_up, sum_att))
    sum_down = sum_y(sum_down)
    sum_up = sum_x(sum_up)
    sum_att = sum_x(sum_att)
    gqkv = jnp.concatenate([gqkv[0], gqkv[1], gqkv[2]], 1)
    sum_qkv = cut(dot(normed_one.T, gqkv))
    gqkv, sum_qkv = lax.optimization_barrier((gqkv, sum_qkv))
    d_gain_one, d_embed = norm_backward(dot(gqkv, w_qkv.T), embed, scale_one, gain_one)
    gembed = (d_stream + d_embed).astype(bf16)
    sum_qkv = sum_core(sum_qkv)
    sum_emb = cut(dot(seq.T, gembed))
    gseq = dot(gembed, w_emb.T)
    gseq, sum_emb, sum_qkv, sum_down, sum_up, sum_att = lax.optimization_barrier(
        (gseq, sum_emb, sum_qkv, sum_down, sum_up, sum_att)
    )
    sum_down = sum_z(sum_down)
    sum_up = sum_z(sum_up)
    sum_att = sum_y(sum_att)
    sum_emb = sum_core(sum_emb)
    sum_qkv = sum_y(sum_qkv)
    gains = sum_all(jnp.stack([d_gain_one, d_gain_two]))

    gupd = gseq[CTX:]
    gb = gupd.astype(bf16)
    grad_out = dot(cross_mixed.T, gb)
    gox = dot(gb, to_out.T).astype(bf16)
    gq, gkv = cross_backward(query, kv, gox, cross_mixed, cross_logs[:, :TH].T)
    gkv, sum_qkv, sum_emb, sum_down, sum_up, sum_att, gains = lax.optimization_barrier(
        (gkv, sum_qkv, sum_emb, sum_down, sum_up, sum_att, gains)
    )
    grad_query = dot(feats_b.T, gq)
    future_grad = gupd + dot(gq, to_query.T)
    sum_qkv = sum_x(sum_qkv)
    sum_emb = sum_y(sum_emb)
    sum_att = sum_z(sum_att)

    d_hidden, gz, grad_conv, grad_kv = token_backward(
        gkv, slope, gseq[:CTX].astype(bf16), hidden_b, wide, kv_weight
    )
    sum_early = jnp.concatenate(
        [
            grad_conv,
            grad_query.astype(bf16)[None],
            grad_kv,
            grad_out.astype(bf16)[None],
        ],
        0,
    )
    sum_early = cut(sum_early.reshape(EARLY * CH, CH))
    d_hidden, gz, sum_early, sum_qkv, sum_emb = lax.optimization_barrier(
        (d_hidden, gz, sum_early, sum_qkv, sum_emb)
    )
    sum_early = sum_core(sum_early)
    sum_emb = sum_x(sum_emb)
    context_grad = context_backward(gz, d_hidden, conv_tiles)
    sum_qkv = sum_z(sum_qkv)
    sum_emb = sum_z(sum_emb)
    sum_early = scatter_axes(
        sum_early.reshape(sum_early.shape[:2] + (-1,) + sum_early.shape[-2:]), ("y", "x"), 2
    )
    sum_early = sum_z(sum_early)

    sums = [sum_early, sum_emb, sum_qkv, sum_att, sum_up, sum_down]
    sums = jnp.concatenate([to_tiles(part) for part in sums], 0)
    square_total = sum_all(jnp.sum(sums * sums))
    slots = jnp.arange(devices * slot_count)
    found = slot_of[None, :] == slots[:, None]
    tile_of = jnp.sum(jnp.where(found, jnp.arange(found.shape[1])[None], 0), 1)
    mine = sums.astype(bf16).at[tile_of].get(mode="promise_in_bounds")
    mine = mine.reshape(devices, slot_count, rows, CH)
    mine = lax.all_to_all(mine, AXES, split_axis=0, concat_axis=0, tiled=True)
    mine = mine.transpose(1, 0, 2, 3).reshape(slot_count, CH, CH).astype(f32)
    context_rows = lax.all_to_all(
        context_grad.reshape(1, IMG, IMG, CH),
        ("y", "x"),
        split_axis=1,
        concat_axis=0,
        tiled=True,
    ).astype(f32)

    used = jnp.any(found, 1).astype(f32).reshape(devices, slot_count)
    used = lax.dynamic_index_in_dim(used, lax.axis_index(AXES), 0, keepdims=False)[:, None, None]
    grad_norm = jnp.sqrt(square_total + jnp.sum(gains * gains))
    factor = jnp.minimum(1.0, clip_level / (grad_norm + 1e-06))
    new_first, new_second, new_master = adam_step(
        master_tiles, mine * factor, moment_first, moment_second, learn_rate, decay_rate
    )
    new_gain_first, new_gain_second, new_gains = adam_step(
        norm_gains, gains * factor, gain_first, gain_second, gain_rate, 0.0
    )
    return (
        block_out[None],
        context_rows,
        future_grad[None],
        jnp.where(used > 0, new_first, 0.0),
        jnp.where(used > 0, new_second, 0.0),
        jnp.where(used > 0, new_master, 0.0),
        new_gain_first,
        new_gain_second,
        new_gains,
        grad_norm,
    )


def solution(mesh):
    groups, rows = mesh.devices.shape
    fine = jax.sharding.Mesh(mesh.devices.reshape(groups // 2, 2, rows // 2, 2), AXES)
    whole = P(AXES, None, None)
    image = P(("z", "c"), ("y", "x"), None, None)
    in_specs = (image, whole, P(AXES), whole, P(), whole, whole, whole, P(), P(), P())
    out_specs = (whole, image, whole, whole, whole, whole, P(), P(), P(), P())
    return jax.shard_map(local, mesh=fine, in_specs=in_specs, out_specs=out_specs, check_vma=False)
```

```python
import jax
import jax.numpy as jnp
from jax import lax
from jax.experimental import pallas as pl
from jax.experimental.pallas import tpu as pltpu
from jax.sharding import PartitionSpec as P

CH = 256
HD = 64
HEADS = 12
D = 768
FF = 3072
TH = 4
IMG = 64
PATCH = 4
FT = 16
CTX = 256
SEQ = 736
STEP = 10


eps_norm = 1e-05
beta_one = 0.9
beta_two = 0.999
learn_rate = 0.02
gain_rate = 0.6
decay_rate = 0.1
adam_eps = 1e-08
clip_level = 1.0
neg_large = -1e30
AXES = ("z", "c", "y", "x")
CELLS = IMG * IMG
BLOCK = 512
GROUP = 4
EARLY = 13
VMEM_BYTES = 56 * 1024 * 1024
ROW_BLOCKS = ((0, 256), (256, 256), (512, 224))
bf16 = jnp.bfloat16
f32 = jnp.float32


def slot_index(tile_owner, slot_count):
    ordinal = jnp.arange(tile_owner.shape[0])
    earlier = (tile_owner[None, :] == tile_owner[:, None]) & (ordinal[None, :] < ordinal[:, None])
    return tile_owner * slot_count + jnp.sum(earlier.astype(jnp.int32), 1)


def adam_step(weight, grad_now, first, second, rate, decay):
    first_new = beta_one * first + (1.0 - beta_one) * grad_now
    second_new = beta_two * second + (1.0 - beta_two) * grad_now * grad_now
    corr_first = first_new / (1.0 - beta_one**STEP)
    corr_second = second_new / (1.0 - beta_two**STEP)
    weight_new = weight - rate * (corr_first / (jnp.sqrt(corr_second) + adam_eps) + decay * weight)
    return (first_new, second_new, weight_new)


def xor_permute(values, axes, mask):
    count = lax.axis_size(axes)
    return lax.ppermute(values, axes, [(i, i ^ mask) for i in range(count)])


def scatter_axes(values, axes, dim, keep_wide=False):
    count = lax.axis_size(axes)
    mine = lax.axis_index(axes)
    total = lax.dynamic_index_in_dim(values, mine, dim, keepdims=False).astype(f32)
    for mask in range(1, count):
        give = lax.dynamic_index_in_dim(values, mine ^ mask, dim, keepdims=False)
        total = total + xor_permute(give, axes, mask).astype(f32)
    return total if keep_wide else total.astype(values.dtype)


def gather_axes(values, axes):
    pieces = [values]
    for mask in range(1, lax.axis_size(axes)):
        pieces.append(xor_permute(values, axes, mask))
    return jnp.stack(pieces)


def gather_all(values):
    shape = values.shape
    values = gather_axes(values, "z")
    values = gather_axes(values, ("y", "x"))
    values = gather_axes(values, "c")
    cores, rows, depth = values.shape[:3]
    order = jnp.arange(depth * cores * rows)
    z, c, row = order // (cores * rows), (order // rows) % cores, order % rows
    own = lax.axis_index("z"), lax.axis_index("c"), lax.axis_index(("y", "x"))
    at = ((c ^ own[1]) * rows + (row ^ own[2])) * depth + (z ^ own[0])
    return values.reshape((-1,) + shape).at[at].get(mode="promise_in_bounds")


def trade_rows(values):
    count = lax.axis_size(("y", "x"))
    mine = lax.axis_index(("y", "x"))
    pieces = [lax.dynamic_index_in_dim(values, mine, 0, keepdims=False)]
    for mask in range(1, count):
        give = lax.dynamic_index_in_dim(values, mine ^ mask, 0, keepdims=False)
        pieces.append(xor_permute(give, ("y", "x"), mask))
    order = jnp.arange(count) ^ mine
    return jnp.stack(pieces).at[order].get(mode="promise_in_bounds")


def cut(matrix):
    sizes = [lax.axis_size(axis) for axis in AXES]
    return matrix.astype(bf16).reshape([-1] + sizes + [CH // lax.axis_size(AXES), matrix.shape[-1]])


def sum_core(slices):
    return scatter_axes(slices, "c", 2)


def sum_x(slices):
    return scatter_axes(slices, "x", slices.ndim - 3)


def sum_y(slices):
    return scatter_axes(slices, "y", 2)


def sum_z(slices):
    return scatter_axes(slices, "z", 1, keep_wide=True)


def sum_rows(slices):
    merged = slices.reshape(slices.shape[:2] + (-1,) + slices.shape[-2:])
    return scatter_axes(merged, ("y", "x"), 2)


def split_wide(slices):
    parts = slices.shape[-1] // D
    if parts == 1:
        return slices
    cutted = slices.reshape(slices.shape[:-1] + (parts, D))
    cutted = jnp.moveaxis(cutted, -2, 1)
    return cutted.reshape((-1,) + slices.shape[1:-1] + (D,))


tie = lax.optimization_barrier


def to_tiles(slices):
    blocks, rows, columns = slices.shape
    return (
        slices.reshape(blocks, rows, columns // CH, CH)
        .transpose(0, 2, 1, 3)
        .reshape(-1, rows, CH)
    )


def dot_nt(a, b):
    return lax.dot_general(a, b, (((1,), (1,)), ((), ())), preferred_element_type=f32)


def dot_nn(a, b):
    return lax.dot_general(a, b, (((1,), (0,)), ((), ())), preferred_element_type=f32)


def dot_tn(a, b):
    return lax.dot_general(a, b, (((0,), (0,)), ((), ())), preferred_element_type=f32)


def head_mask(shape, head):
    return (lax.broadcasted_iota(jnp.int32, shape, len(shape) - 1) // HD) == head


def cost(flops, moved, transcendentals=0):
    return pl.CostEstimate(
        flops=int(flops), bytes_accessed=int(moved), transcendentals=int(transcendentals)
    )


def params():
    return pltpu.CompilerParams(vmem_limit_bytes=VMEM_BYTES)


def cross_forward_kernel(q_ref, k_ref, v_ref, o_ref, l_ref):
    rows = q_ref.shape[0]
    lane = lax.broadcasted_iota(jnp.int32, (rows, 128), 1)
    q = q_ref[...]
    mixed = jnp.zeros((rows, CH), f32)
    stat = jnp.zeros((rows, 128), f32)
    for head in range(TH):
        mask = head_mask((rows, CH), head)
        q_head = jnp.where(mask, q.astype(f32) * 0.125, 0.0).astype(bf16)
        scores = dot_nt(q_head, k_ref[...])
        peak = jnp.max(scores, -1, keepdims=True)
        shifted = jnp.exp(scores - peak)
        total = jnp.sum(shifted, -1, keepdims=True)
        part = dot_nn(shifted.astype(bf16), v_ref[...])
        mixed = jnp.where(mask, part / total, mixed)
        stat = jnp.where(lane == head, peak + jnp.log(total), stat)
    o_ref[...] = mixed.astype(bf16)
    l_ref[...] = stat


def cross_forward(query, kv):
    rows = query.shape[0] // 2
    cells = kv.shape[0]
    return pl.pallas_call(
        cross_forward_kernel,
        grid=(2,),
        in_specs=[
            pl.BlockSpec((rows, CH), lambda i: (i, 0)),
            pl.BlockSpec((cells, CH), lambda i: (0, 0)),
            pl.BlockSpec((cells, CH), lambda i: (0, 1)),
        ],
        out_specs=[
            pl.BlockSpec((rows, CH), lambda i: (i, 0)),
            pl.BlockSpec((rows, 128), lambda i: (i, 0)),
        ],
        out_shape=[
            jax.ShapeDtypeStruct((2 * rows, CH), bf16),
            jax.ShapeDtypeStruct((2 * rows, 128), f32),
        ],
        compiler_params=params(),
        cost_estimate=cost(16 * TH * rows * cells * CH // 2, 8 * cells * CH, 2 * TH * rows * cells),
    )(query, kv, kv)


def delta_rows(d_out, out):
    product = d_out.astype(f32) * out.astype(f32)
    head = lax.broadcasted_iota(jnp.int32, (8, CH), 0)
    lane = lax.broadcasted_iota(jnp.int32, (8, CH), 1)
    pick = ((lane // HD) == head).astype(f32)
    return lax.dot_general(
        pick,
        product,
        (((1,), (1,)), ((), ())),
        precision=lax.Precision.HIGHEST,
        preferred_element_type=f32,
    )


def cross_backward_kernel(
    q_ref, k_ref, v_ref, do_ref, o_ref, l_ref, dq_ref, dkv_ref, q_s, do_s, delta_s, dq_s
):
    step = pl.program_id(0)
    rows = q_ref.shape[0]

    @pl.when(step == 0)
    def _():
        for head in range(TH):
            mask = head_mask((rows, CH), head)
            q_s[head] = jnp.where(mask, q_ref[...].astype(f32) * 0.125, 0.0).astype(bf16)
            do_s[head] = jnp.where(mask, do_ref[...].astype(f32), 0.0).astype(bf16)
        delta_s[...] = delta_rows(do_ref[...], o_ref[...])
        dq_s[...] = jnp.zeros_like(dq_s)

    cells = k_ref.shape[0]
    dk = jnp.zeros((cells, CH), f32)
    dv = jnp.zeros((cells, CH), f32)
    dq = dq_s[...]
    k = k_ref[...]
    for head in range(TH):
        probs = jnp.exp(dot_nt(k, q_s[head]) - l_ref[head : head + 1, :])
        d_probs = dot_nt(v_ref[...], do_s[head])
        d_scores = (probs * (d_probs - delta_s[head : head + 1, :])).astype(bf16)
        dv = dv + dot_nn(probs.astype(bf16), do_s[head])
        dk = dk + dot_nn(d_scores, q_s[head])
        dq = dq + jnp.where(head_mask((rows, CH), head), dot_tn(d_scores, k), 0.0)
    dq_s[...] = dq
    dkv_ref[:, :CH] = dk.astype(bf16)
    dkv_ref[:, CH:] = dv.astype(bf16)

    @pl.when(step == pl.num_programs(0) - 1)
    def _():
        dq_ref[...] = (dq_s[...] * 0.125).astype(bf16)


def cross_backward(query, kv, d_out, out, log_rows):
    rows = query.shape[0]
    cells = kv.shape[0]
    block = 1024
    whole = lambda i: (0, 0)
    return pl.pallas_call(
        cross_backward_kernel,
        grid=(cells // block,),
        in_specs=[
            pl.BlockSpec((rows, CH), whole),
            pl.BlockSpec((block, CH), lambda i: (i, 0)),
            pl.BlockSpec((block, CH), lambda i: (i, 1)),
            pl.BlockSpec((rows, CH), whole),
            pl.BlockSpec((rows, CH), whole),
            pl.BlockSpec((TH, rows), whole),
        ],
        out_specs=[
            pl.BlockSpec((rows, CH), whole),
            pl.BlockSpec((block, 2 * CH), lambda i: (i, 0)),
        ],
        out_shape=[
            jax.ShapeDtypeStruct((rows, CH), bf16),
            jax.ShapeDtypeStruct((cells, 2 * CH), bf16),
        ],
        scratch_shapes=[
            pltpu.VMEM((TH, rows, CH), bf16),
            pltpu.VMEM((TH, rows, CH), bf16),
            pltpu.VMEM((8, rows), f32),
            pltpu.VMEM((rows, CH), f32),
        ],
        compiler_params=params(),
        cost_estimate=cost(10 * TH * rows * cells * CH, 8 * cells * CH, TH * rows * cells),
    )(query, kv, kv, d_out, out, log_rows)


def self_forward_kernel(len_ref, q_ref, k_ref, v_ref, o_ref, l_ref):
    group = pl.program_id(0)
    length = len_ref[0]
    for start, count in ROW_BLOCKS:
        stop = start + count
        q = q_ref[start:stop, :].astype(f32) * 0.125
        row = lax.broadcasted_iota(jnp.int32, (count, 1), 0) + start
        bound = jnp.minimum(row, length - 1)
        allowed = lax.broadcasted_iota(jnp.int32, (count, stop), 1) <= bound
        mixed = jnp.zeros((count, CH), f32)
        stat = l_ref[start:stop, :]
        lane = lax.broadcasted_iota(jnp.int32, (count, 128), 1)
        for head in range(GROUP):
            mask = head_mask((count, CH), head)
            q_head = jnp.where(mask, q, 0.0).astype(bf16)
            scores = jnp.where(allowed, dot_nt(q_head, k_ref[:stop, :]), neg_large)
            peak = jnp.max(scores, -1, keepdims=True)
            shifted = jnp.exp(scores - peak)
            total = jnp.sum(shifted, -1, keepdims=True)
            part = dot_nn(shifted.astype(bf16), v_ref[:stop, :])
            mixed = jnp.where(mask, part / total, mixed)
            stat = jnp.where(lane == group * GROUP + head, peak + jnp.log(total), stat)
        o_ref[start:stop, :] = mixed.astype(bf16)
        l_ref[start:stop, :] = stat


def self_forward(qkv, length):
    groups = D // CH
    return pl.pallas_call(
        self_forward_kernel,
        grid_spec=pltpu.PrefetchScalarGridSpec(
            num_scalar_prefetch=1,
            grid=(groups,),
            in_specs=[
                pl.BlockSpec((SEQ, CH), lambda i, n: (0, i)),
                pl.BlockSpec((SEQ, CH), lambda i, n: (0, groups + i)),
                pl.BlockSpec((SEQ, CH), lambda i, n: (0, 2 * groups + i)),
            ],
            out_specs=[
                pl.BlockSpec((SEQ, CH), lambda i, n: (0, i)),
                pl.BlockSpec((SEQ, 128), lambda i, n: (0, 0)),
            ],
        ),
        out_shape=[
            jax.ShapeDtypeStruct((SEQ, D), bf16),
            jax.ShapeDtypeStruct((SEQ, 128), f32),
        ],
        compiler_params=params(),
        cost_estimate=cost(4 * HEADS * SEQ * SEQ * CH, 8 * SEQ * D, HEADS * SEQ * SEQ),
    )(length, qkv, qkv, qkv)


def self_backward_kernel(
    len_ref, q_ref, k_ref, v_ref, do_ref, o_ref, l_ref, out_ref, dk_s, dv_s
):
    length = len_ref[0]
    dk_s[...] = jnp.zeros_like(dk_s)
    dv_s[...] = jnp.zeros_like(dv_s)
    delta = delta_rows(do_ref[...], o_ref[...])
    for start, count in ROW_BLOCKS:
        stop = start + count
        q = q_ref[start:stop, :].astype(f32) * 0.125
        d_out = do_ref[start:stop, :].astype(f32)
        row = lax.broadcasted_iota(jnp.int32, (1, count), 1) + start
        bound = jnp.minimum(row, length - 1)
        allowed = lax.broadcasted_iota(jnp.int32, (stop, count), 0) <= bound
        dq = jnp.zeros((count, CH), f32)
        k = k_ref[:stop, :]
        v = v_ref[:stop, :]
        dk = dk_s[:stop, :]
        dv = dv_s[:stop, :]
        for head in range(GROUP):
            mask = head_mask((count, CH), head)
            q_head = jnp.where(mask, q, 0.0).astype(bf16)
            d_head = jnp.where(mask, d_out, 0.0).astype(bf16)
            scores = dot_nt(k, q_head)
            logs = l_ref[0, head : head + 1, start:stop]
            probs = jnp.where(allowed, jnp.exp(scores - logs), 0.0)
            d_probs = dot_nt(v, d_head)
            d_scores = (probs * (d_probs - delta[head : head + 1, start:stop])).astype(bf16)
            dv = dv + dot_nn(probs.astype(bf16), d_head)
            dk = dk + dot_nn(d_scores, q_head)
            dq = dq + jnp.where(mask, dot_tn(d_scores, k), 0.0)
        dk_s[:stop, :] = dk
        dv_s[:stop, :] = dv
        out_ref[0, start:stop, :] = (dq * 0.125).astype(bf16)
    out_ref[1] = dk_s[...].astype(bf16)
    out_ref[2] = dv_s[...].astype(bf16)


def self_backward(qkv, d_out, out, log_rows, length):
    groups = D // CH
    at = lambda j: (lambda i, n: (0, j * groups + i))
    return pl.pallas_call(
        self_backward_kernel,
        grid_spec=pltpu.PrefetchScalarGridSpec(
            num_scalar_prefetch=1,
            grid=(groups,),
            in_specs=[
                pl.BlockSpec((SEQ, CH), at(0)),
                pl.BlockSpec((SEQ, CH), at(1)),
                pl.BlockSpec((SEQ, CH), at(2)),
                pl.BlockSpec((SEQ, CH), at(0)),
                pl.BlockSpec((SEQ, CH), at(0)),
                pl.BlockSpec((1, GROUP, SEQ), lambda i, n: (i, 0, 0)),
            ],
            out_specs=pl.BlockSpec((3, SEQ, CH), lambda i, n: (0, 0, i)),
            scratch_shapes=[pltpu.VMEM((SEQ, CH), f32), pltpu.VMEM((SEQ, CH), f32)],
        ),
        out_shape=jax.ShapeDtypeStruct((3, SEQ, D), bf16),
        compiler_params=params(),
        cost_estimate=cost(8 * HEADS * SEQ * SEQ * CH, 16 * SEQ * D, HEADS * SEQ * SEQ),
    )(length, qkv, qkv, qkv, d_out, out, log_rows)


def patch_pick(rows, columns, patch_dim):
    patch = lax.broadcasted_iota(jnp.int32, (rows, columns), patch_dim)
    cell = lax.broadcasted_iota(jnp.int32, (rows, columns), 1 - patch_dim)
    inside = (cell // (PATCH * IMG)) * (IMG // PATCH) + (cell % IMG) // PATCH
    return jnp.where(patch == inside, 1.0 / (PATCH * PATCH), 0.0).astype(bf16)


def image_rows(step, row):
    return pl.ds(pl.multiple_of(step * BLOCK + row * IMG, IMG), BLOCK)


def token_forward_kernel(x_ref, conv_ref, kv_w_ref, slope_ref, hidden_ref, kv_ref, pool_ref):
    step = pl.program_id(0)
    z = jnp.zeros((BLOCK, CH), f32)
    for row in range(3):
        z = z + dot_nn(x_ref[image_rows(step, row), :], conv_ref[row])
    center = x_ref[image_rows(step, 1), CH : 2 * CH].astype(f32)
    gate = 1.0 / (1.0 + jnp.exp(-z))
    hidden = center + z * gate
    slope_ref[...] = (gate * (1.0 + z * (1.0 - gate))).astype(bf16)
    hidden_b = hidden.astype(bf16)
    hidden_ref[...] = hidden_b
    kv_ref[...] = dot_nn(hidden_b, kv_w_ref[...]).astype(bf16)
    rest = (hidden - hidden_b.astype(f32)).astype(bf16)
    pick = patch_pick(pool_ref.shape[0], BLOCK, 0)
    pool_ref[...] = (dot_nn(pick, hidden_b) + dot_nn(pick, rest)).astype(bf16)


def token_forward(wide, conv_rows, kv_weight):
    steps = CELLS // BLOCK
    whole = lambda i: (0, 0)
    block = lambda i: (i, 0)
    return pl.pallas_call(
        token_forward_kernel,
        grid=(steps,),
        in_specs=[
            pl.BlockSpec(wide.shape, whole),
            pl.BlockSpec((3, 3 * CH, CH), lambda i: (0, 0, 0)),
            pl.BlockSpec((CH, 2 * CH), whole),
        ],
        out_specs=[
            pl.BlockSpec((BLOCK, CH), block),
            pl.BlockSpec((BLOCK, CH), block),
            pl.BlockSpec((BLOCK, 2 * CH), block),
            pl.BlockSpec((CTX // steps, CH), block),
        ],
        out_shape=[
            jax.ShapeDtypeStruct((CELLS, CH), bf16),
            jax.ShapeDtypeStruct((CELLS, CH), bf16),
            jax.ShapeDtypeStruct((CELLS, 2 * CH), bf16),
            jax.ShapeDtypeStruct((CTX, CH), bf16),
        ],
        compiler_params=params(),
        cost_estimate=cost(22 * CELLS * CH * CH, 14 * CELLS * CH, CELLS * CH),
    )(wide, conv_rows, kv_weight)


def token_backward_kernel(
    dkv_ref, slope_ref, pool_ref, hidden_ref, x_ref, kv_w_ref,
    d_hidden_ref, gz_ref, conv_ref, kv_g_ref, conv_s, kv_s,
):
    step = pl.program_id(0)

    @pl.when(step == 0)
    def _():
        conv_s[...] = jnp.zeros_like(conv_s)
        kv_s[...] = jnp.zeros_like(kv_s)

    dkv = dkv_ref[...]
    d_hidden = dot_nt(dkv, kv_w_ref[...])
    d_hidden = d_hidden + dot_nn(patch_pick(BLOCK, pool_ref.shape[0], 1), pool_ref[...])
    gz = (d_hidden * slope_ref[...].astype(f32)).astype(bf16)
    d_hidden_ref[...] = d_hidden
    gz_ref[...] = gz
    kv_s[...] += dot_tn(hidden_ref[...], dkv)
    gz_t = gz.T
    for row in range(3):
        conv_s[row] += dot_nn(gz_t, x_ref[image_rows(step, row), :])

    @pl.when(step == pl.num_programs(0) - 1)
    def _():
        for row in range(3):
            for col in range(3):
                conv_ref[3 * row + col] = conv_s[row, :, col * CH : (col + 1) * CH].T.astype(bf16)
        kv_g_ref[0] = kv_s[:, :CH].astype(bf16)
        kv_g_ref[1] = kv_s[:, CH:].astype(bf16)


def token_backward(dkv, slope, d_pool, hidden_b, wide, kv_weight):
    steps = CELLS // BLOCK
    whole = lambda i: (0, 0)
    whole_3 = lambda i: (0, 0, 0)
    block = lambda i: (i, 0)
    return pl.pallas_call(
        token_backward_kernel,
        grid=(steps,),
        in_specs=[
            pl.BlockSpec((BLOCK, 2 * CH), block),
            pl.BlockSpec((BLOCK, CH), block),
            pl.BlockSpec((CTX // steps, CH), block),
            pl.BlockSpec((BLOCK, CH), block),
            pl.BlockSpec(wide.shape, whole),
            pl.BlockSpec((CH, 2 * CH), whole),
        ],
        out_specs=[
            pl.BlockSpec((BLOCK, CH), block),
            pl.BlockSpec((BLOCK, CH), block),
            pl.BlockSpec((9, CH, CH), whole_3),
            pl.BlockSpec((2, CH, CH), whole_3),
        ],
        out_shape=[
            jax.ShapeDtypeStruct((CELLS, CH), f32),
            jax.ShapeDtypeStruct((CELLS, CH), bf16),
            jax.ShapeDtypeStruct((9, CH, CH), bf16),
            jax.ShapeDtypeStruct((2, CH, CH), bf16),
        ],
        scratch_shapes=[pltpu.VMEM((3, CH, 3 * CH), f32), pltpu.VMEM((CH, 2 * CH), f32)],
        compiler_params=params(),
        cost_estimate=cost(26 * CELLS * CH * CH, 20 * CELLS * CH),
    )(dkv, slope, d_pool, hidden_b, wide, kv_weight)


def context_backward_kernel(gz_ref, d_hidden_ref, conv_ref, out_ref, wide_s):
    step = pl.program_id(0)
    steps = pl.num_programs(0)

    def widen(at):
        values = gz_ref[image_rows(at, 0), :].astype(f32)
        col = lax.broadcasted_iota(jnp.int32, (BLOCK, CH), 0) % IMG
        left = jnp.where(col == 0, 0.0, pltpu.roll(values, 1, 0))
        right = jnp.where(col == IMG - 1, 0.0, pltpu.roll(values, BLOCK - 1, 0))
        wide_s[image_rows(at, 1), 0:CH] = left.astype(bf16)
        wide_s[image_rows(at, 1), CH : 2 * CH] = values.astype(bf16)
        wide_s[image_rows(at, 1), 2 * CH :] = right.astype(bf16)

    @pl.when(step == 0)
    def _():
        wide_s[0:IMG, :] = jnp.zeros((IMG, 3 * CH), bf16)
        wide_s[CELLS + IMG :, :] = jnp.zeros((IMG, 3 * CH), bf16)
        widen(0)

    @pl.when(step < steps - 1)
    def _():
        widen(step + 1)

    total = d_hidden_ref[...]
    for row in range(3):
        values = wide_s[image_rows(step, row), :]
        for col in range(3):
            tap = conv_ref[3 * (2 - row) + (2 - col)]
            total = total + dot_nt(values[:, col * CH : (col + 1) * CH], tap)
    out_ref[...] = total.astype(bf16)


def context_backward(gz, d_hidden, conv_tiles):
    block = lambda i: (i, 0)
    return pl.pallas_call(
        context_backward_kernel,
        grid=(CELLS // BLOCK,),
        in_specs=[
            pl.BlockSpec((CELLS, CH), lambda i: (0, 0)),
            pl.BlockSpec((BLOCK, CH), block),
            pl.BlockSpec((9, CH, CH), lambda i: (0, 0, 0)),
        ],
        out_specs=pl.BlockSpec((BLOCK, CH), block),
        out_shape=jax.ShapeDtypeStruct((CELLS, CH), bf16),
        scratch_shapes=[pltpu.VMEM((CELLS + 2 * IMG, 3 * CH), bf16)],
        compiler_params=params(),
        cost_estimate=cost(18 * CELLS * CH * CH, 8 * CELLS * CH),
    )(gz, d_hidden, conv_tiles)


def dot(a, b):
    return jnp.dot(a, b, preferred_element_type=f32)


def gelu_slope(v):
    inner = jnp.sqrt(2.0 / jnp.pi) * (v + 0.044715 * v * v * v)
    bend = jnp.tanh(inner)
    d_inner = jnp.sqrt(2.0 / jnp.pi) * (1.0 + 3.0 * 0.044715 * v * v)
    return 0.5 * (1.0 + bend) + 0.5 * v * (1.0 - bend * bend) * d_inner


def inverse_rms(values):
    return lax.rsqrt(jnp.mean(values * values, -1, keepdims=True) + eps_norm)


def norm_backward(d_normed, values, scale, gain):
    d_gain = jnp.sum(d_normed * values * scale, 0)
    scaled = d_normed * gain
    inner = jnp.mean(scaled * values, -1, keepdims=True)
    return d_gain, scale * scaled - (scale * scale * scale) * values * inner


def local(
    context_map,
    future_feats,
    horizon,
    cotangent,
    tile_owner,
    master_tiles,
    moment_first,
    moment_second,
    norm_gains,
    gain_first,
    gain_second,
):
    slot_count = master_tiles.shape[0]
    devices = lax.axis_size(AXES)
    rows = CH // devices
    slot_of = slot_index(tile_owner, slot_count)

    image = trade_rows(context_map).reshape(IMG, IMG, CH)

    slices = (
        master_tiles.astype(bf16)
        .reshape(slot_count, devices, rows, CH)
        .transpose(1, 0, 2, 3)
    )
    slices = lax.all_to_all(slices, AXES, split_axis=0, concat_axis=0, tiled=True)
    slices = slices.reshape(devices * slot_count, rows, CH)
    slices = slices.at[slot_of].get(mode="promise_in_bounds")
    early = gather_all(slices[:EARLY]).transpose(1, 0, 2, 3).reshape(EARLY, CH, CH)
    later = slices[EARLY:].reshape(-1, D // CH, rows, CH).transpose(0, 2, 1, 3)
    later = lax.all_gather(later.reshape(-1, D), AXES, axis=0, tiled=True)
    later = later.reshape(devices, -1, rows, D)

    def matrix(start, row_blocks, parts):
        part = later[:, start : start + row_blocks * parts]
        part = part.reshape(devices, row_blocks, parts, rows, D)
        return part.transpose(1, 0, 3, 2, 4).reshape(row_blocks * CH, parts * D)

    padded = jnp.pad(image, ((1, 1), (1, 1), (0, 0)))
    wide = jnp.concatenate([padded[:, col : col + IMG] for col in range(3)], -1)
    wide = wide.reshape((IMG + 2) * IMG, 3 * CH)

    conv_tiles = early[:9]
    to_query, to_out = early[9], early[12]
    kv_weight = jnp.concatenate([early[10], early[11]], 1)
    w_emb = matrix(0, 1, 1)
    w_qkv = matrix(1, 3, 3)
    w_att = matrix(10, 3, 1)
    w_up = matrix(13, 3, 4)
    w_down = matrix(25, 12, 1)

    slope, hidden_b, kv, pooled = token_forward(wide, conv_tiles.reshape(3, 3 * CH, CH), kv_weight)
    feats_b = future_feats[0]
    length = CTX + FT * horizon
    query = dot(feats_b, to_query).astype(bf16)
    cross_mixed, cross_logs = cross_forward(query, kv)
    updated = feats_b.astype(f32) + dot(cross_mixed, to_out)
    seq = jnp.concatenate([pooled, updated.astype(bf16)], 0)

    gain_one, gain_two = norm_gains[0], norm_gains[1]
    embed = dot(seq, w_emb)
    scale_one = inverse_rms(embed)
    normed_one = (embed * scale_one * gain_one).astype(bf16)
    qkv = dot(normed_one, w_qkv).astype(bf16)
    mixed, logs = self_forward(qkv, length)
    stream = embed + dot(mixed, w_att)
    scale_two = inverse_rms(stream)
    normed_two = (stream * scale_two * gain_two).astype(bf16)
    pre = dot(normed_two, w_up)
    act = jax.nn.gelu(pre, approximate=True).astype(bf16)
    block_out = stream + dot(act, w_down)

    valid = jnp.arange(SEQ) < length[0]
    gd = jnp.where(valid[:, None], cotangent[0], jnp.zeros((), bf16))
    sum_down = cut(dot(act.T, gd))
    gd, sum_down = tie((gd, sum_down))
    gpre = (dot(gd, w_down.T) * gelu_slope(pre)).astype(bf16)
    sum_down = sum_core(sum_down)
    sum_up = cut(dot(normed_two.T, gpre))
    gpre, sum_up, sum_down = tie((gpre, sum_up, sum_down))
    d_gain_two, d_stream = norm_backward(dot(gpre, w_up.T), stream, scale_two, gain_two)
    d_stream = gd.astype(f32) + d_stream
    ga = d_stream.astype(bf16)
    sum_up = split_wide(sum_core(sum_up))
    sum_down = sum_x(sum_down)
    ga, sum_up = tie((ga, sum_up))
    sum_up = sum_y(sum_up)
    sum_att = cut(dot(mixed.T, ga))
    gog = dot(ga, w_att.T).astype(bf16)
    log_rows = logs[:, :HEADS].T.reshape(D // CH, GROUP, SEQ)
    gqkv = self_backward(qkv, gog, mixed, log_rows, length)
    gqkv, sum_down, sum_up, sum_att = tie((gqkv, sum_down, sum_up, sum_att))
    sum_down = sum_y(sum_down)
    sum_up = sum_x(sum_up)
    sum_att = sum_core(sum_att)
    gqkv = jnp.concatenate([gqkv[0], gqkv[1], gqkv[2]], 1)
    sum_qkv = cut(dot(normed_one.T, gqkv))
    gqkv, sum_qkv = tie((gqkv, sum_qkv))
    sum_qkv = split_wide(sum_core(sum_qkv))
    d_gain_one, d_embed = norm_backward(dot(gqkv, w_qkv.T), embed, scale_one, gain_one)
    gembed = (d_stream + d_embed).astype(bf16)
    sum_emb = cut(dot(seq.T, gembed))
    gains = jnp.stack([d_gain_one, d_gain_two]).reshape(devices, 1, -1)
    gain_count = gains.shape[-1]
    gains = jnp.pad(gains, ((0, 0), (0, rows - 1), (0, D - gain_count))).astype(bf16)
    sum_emb = jnp.concatenate([sum_emb, gains.reshape((1,) + sum_emb.shape[1:])], 0)
    gseq = dot(gembed, w_emb.T)
    gseq, sum_emb, sum_qkv, sum_down, sum_up, sum_att = tie(
        (gseq, sum_emb, sum_qkv, sum_down, sum_up, sum_att)
    )
    sum_mlp = jnp.concatenate([sum_up, sum_down], 0)
    half = sum_qkv.shape[0] * 2 // 3
    first = sum_qkv[:half]
    second = jnp.concatenate([sum_qkv[half:], sum_att], 0)

    gupd = gseq[CTX:]
    gb = gupd.astype(bf16)
    grad_out = dot(cross_mixed.T, gb)
    gox = dot(gb, to_out.T).astype(bf16)
    gq, gkv = cross_backward(query, kv, gox, cross_mixed, cross_logs[:, :TH].T)
    first = sum_x(first)
    second = sum_y(second)
    sum_mlp = sum_z(sum_mlp)
    sum_emb = sum_core(sum_emb)
    gkv, first, second, sum_mlp, sum_emb = tie((gkv, first, second, sum_mlp, sum_emb))
    grad_query = dot(feats_b.T, gq)

    d_hidden, gz, grad_conv, grad_kv = token_backward(
        gkv, slope, gseq[:CTX].astype(bf16), hidden_b, wide, kv_weight
    )
    first = sum_y(first)
    second = sum_x(second)
    sum_emb = sum_rows(sum_emb)
    sum_early = jnp.concatenate(
        [
            grad_conv,
            grad_query.astype(bf16)[None],
            grad_kv,
            grad_out.astype(bf16)[None],
        ],
        0,
    )
    sum_early = cut(sum_early.reshape(EARLY * CH, CH))
    own_core = lax.axis_index("c")
    keep = lax.dynamic_index_in_dim(sum_early, own_core, 2, keepdims=False)
    give = lax.dynamic_index_in_dim(sum_early, own_core ^ 1, 2, keepdims=False)
    d_hidden, gz, keep, give, first, second, sum_emb = tie(
        (d_hidden, gz, keep, give, first, second, sum_emb)
    )
    sum_early = (keep.astype(f32) + xor_permute(give, "c", 1).astype(f32)).astype(bf16)
    context_grad = context_backward(gz, d_hidden, conv_tiles)
    context_grad, sum_early = tie((context_grad, sum_early))
    sum_att = sum_z(jnp.concatenate([first, second], 0))
    sum_emb = sum_z(sum_emb)
    sum_early = sum_rows(sum_early)
    sum_early = sum_z(sum_early)
    context_rows = trade_rows(context_grad.reshape(context_map.shape))
    future_grad = gupd + dot(gq, to_query.T)

    sums = [sum_early, sum_emb[:1], sum_att, sum_mlp]
    sums = jnp.concatenate([to_tiles(part) for part in sums], 0)
    gains = sum_emb[1, 0, :gain_count]
    square = jnp.sum(sums * sums) + jnp.sum(gains * gains)
    share = jnp.concatenate([square[None], gains])
    share_high = share.astype(bf16)
    share_low = (share - share_high.astype(f32)).astype(bf16)
    share = jnp.pad(
        jnp.stack([share_high, share_low]), ((0, rows - 2), (0, CH - 1 - gain_count))
    )
    slots = jnp.arange(devices * slot_count)
    found = slot_of[None, :] == slots[:, None]
    tile_of = jnp.sum(jnp.where(found, jnp.arange(found.shape[1])[None], 0), 1)
    mine = sums.astype(bf16).at[tile_of].get(mode="promise_in_bounds")
    mine = mine.reshape(devices, slot_count, rows, CH)
    share = jnp.broadcast_to(share[None, None], (devices, 1, rows, CH))
    mine = jnp.concatenate([mine, share], 1)
    mine = lax.all_to_all(mine, AXES, split_axis=0, concat_axis=0, tiled=True)
    shares = mine[:, slot_count, :2].astype(f32)
    shares = shares[:, 0] + shares[:, 1]
    gains = shares[:, 1 : 1 + gain_count].reshape(2, D)
    mine = mine[:, :slot_count].transpose(1, 0, 2, 3).reshape(slot_count, CH, CH).astype(f32)

    used = jnp.any(found, 1).astype(f32).reshape(devices, slot_count)
    used = lax.dynamic_index_in_dim(used, lax.axis_index(AXES), 0, keepdims=False)[:, None, None]
    grad_norm = jnp.sqrt(jnp.sum(shares[:, 0]))
    factor = jnp.minimum(1.0, clip_level / (grad_norm + 1e-06))
    new_first, new_second, new_master = adam_step(
        master_tiles, mine * factor, moment_first, moment_second, learn_rate, decay_rate
    )
    new_gain_first, new_gain_second, new_gains = adam_step(
        norm_gains, gains * factor, gain_first, gain_second, gain_rate, 0.0
    )
    return (
        block_out[None],
        context_rows.reshape(context_map.shape).astype(f32),
        future_grad[None],
        jnp.where(used > 0, new_first, 0.0),
        jnp.where(used > 0, new_second, 0.0),
        jnp.where(used > 0, new_master, 0.0),
        new_gain_first,
        new_gain_second,
        new_gains,
        grad_norm,
    )


def solution(mesh):
    groups, rows = mesh.devices.shape
    fine = jax.sharding.Mesh(mesh.devices.reshape(groups // 2, 2, rows // 2, 2), AXES)
    whole = P(AXES, None, None)
    image = P(("z", "c"), ("y", "x"), None, None)
    in_specs = (image, whole, P(AXES), whole, P(), whole, whole, whole, P(), P(), P())
    out_specs = (whole, image, whole, whole, whole, whole, P(), P(), P(), P())
    return jax.shard_map(local, mesh=fine, in_specs=in_specs, out_specs=out_specs, check_vma=False)
```

```python
import jax
import jax.numpy as jnp
from jax import lax
from jax.experimental import pallas as pl
from jax.experimental.pallas import tpu as pltpu
from jax.sharding import PartitionSpec as P

CH = 256
HD = 64
HEADS = 12
D = 768
FF = 3072
TH = 4
IMG = 64
PATCH = 4
FT = 16
CTX = 256
SEQ = 736
STEP = 10


eps_norm = 1e-05
beta_one = 0.9
beta_two = 0.999
learn_rate = 0.02
gain_rate = 0.6
decay_rate = 0.1
adam_eps = 1e-08
clip_level = 1.0
neg_large = -1e30
AXES = ("z", "c", "y", "x")
CELLS = IMG * IMG
BLOCK = 512
GROUP = 4
EARLY = 13
VMEM_BYTES = 56 * 1024 * 1024
ROW_BLOCKS = ((0, 256), (256, 256), (512, 224))
bf16 = jnp.bfloat16
f32 = jnp.float32


def slot_index(tile_owner, slot_count):
    ordinal = jnp.arange(tile_owner.shape[0])
    earlier = (tile_owner[None, :] == tile_owner[:, None]) & (ordinal[None, :] < ordinal[:, None])
    return tile_owner * slot_count + jnp.sum(earlier.astype(jnp.int32), 1)


def adam_step(weight, grad_now, first, second, rate, decay):
    first_new = beta_one * first + (1.0 - beta_one) * grad_now
    second_new = beta_two * second + (1.0 - beta_two) * grad_now * grad_now
    corr_first = first_new / (1.0 - beta_one**STEP)
    corr_second = second_new / (1.0 - beta_two**STEP)
    weight_new = weight - rate * (corr_first / (jnp.sqrt(corr_second) + adam_eps) + decay * weight)
    return (first_new, second_new, weight_new)


def xor_permute(values, axes, mask):
    count = lax.axis_size(axes)
    return lax.ppermute(values, axes, [(i, i ^ mask) for i in range(count)])


def begin_sum(values, axes, dim):
    mine = lax.axis_index(axes)
    parts = [lax.dynamic_index_in_dim(values, mine, dim, keepdims=False)]
    for mask in range(1, lax.axis_size(axes)):
        give = lax.dynamic_index_in_dim(values, mine ^ mask, dim, keepdims=False)
        parts.append(xor_permute(give, axes, mask))
    return parts


def begin_near(values):
    shape = values.shape
    values = values.reshape((shape[0], shape[1] // 2, 2) + shape[2:])
    mine = lax.axis_index("z") % 2
    keep = lax.dynamic_index_in_dim(values, mine, 2, keepdims=False)
    give = lax.dynamic_index_in_dim(values, 1 - mine, 2, keepdims=False)
    return [keep, xor_permute(give, "z", 1)]


def begin_far(values):
    mine = lax.axis_index("z") // 2
    parts = [lax.dynamic_index_in_dim(values, mine, 1, keepdims=False)]
    for mask in range(1, values.shape[1]):
        give = lax.dynamic_index_in_dim(values, mine ^ mask, 1, keepdims=False)
        parts.append(xor_permute(give, "z", 2 * mask))
    return parts


def end_sum(parts, keep_wide=False):
    total = parts[0].astype(f32)
    for part in parts[1:]:
        total = total + part.astype(f32)
    return total if keep_wide else total.astype(parts[0].dtype)


def hold(values, *sums):
    tied = lax.optimization_barrier((tuple(values), tuple(parts[0] for parts in sums)))
    return tied[0] + tuple([keep] + parts[1:] for keep, parts in zip(tied[1], sums))


def gather_axes(values, axes):
    pieces = [values]
    for mask in range(1, lax.axis_size(axes)):
        pieces.append(xor_permute(values, axes, mask))
    return jnp.stack(pieces)


def gather_all(values):
    shape = values.shape
    values = gather_axes(values, "z")
    values = gather_axes(values, ("y", "x"))
    values = gather_axes(values, "c")
    cores, rows, depth = values.shape[:3]
    order = jnp.arange(depth * cores * rows)
    z, c, row = order // (cores * rows), (order // rows) % cores, order % rows
    own = lax.axis_index("z"), lax.axis_index("c"), lax.axis_index(("y", "x"))
    at = ((c ^ own[1]) * rows + (row ^ own[2])) * depth + (z ^ own[0])
    return values.reshape((-1,) + shape).at[at].get(mode="promise_in_bounds")


def trade_rows(values):
    count = lax.axis_size(("y", "x"))
    mine = lax.axis_index(("y", "x"))
    pieces = [lax.dynamic_index_in_dim(values, mine, 0, keepdims=False)]
    for mask in range(1, count):
        give = lax.dynamic_index_in_dim(values, mine ^ mask, 0, keepdims=False)
        pieces.append(xor_permute(give, ("y", "x"), mask))
    order = jnp.arange(count) ^ mine
    return jnp.stack(pieces).at[order].get(mode="promise_in_bounds")


def cut(matrix):
    sizes = [lax.axis_size(axis) for axis in AXES]
    return matrix.astype(bf16).reshape([-1] + sizes + [CH // lax.axis_size(AXES), matrix.shape[-1]])


tie = lax.optimization_barrier


def to_tiles(slices, parts=1):
    blocks, rows, columns = slices.shape
    return (
        slices.reshape(parts, blocks // parts, rows, columns // CH, CH)
        .transpose(1, 0, 3, 2, 4)
        .reshape(-1, rows, CH)
    )


def from_tiles(tiles, row_blocks, parts):
    rows = tiles.shape[1]
    return (
        tiles.reshape(row_blocks, parts, D // CH, rows, CH)
        .transpose(1, 0, 3, 2, 4)
        .reshape(parts * row_blocks, rows, D)
    )


def dot_nt(a, b):
    return lax.dot_general(a, b, (((1,), (1,)), ((), ())), preferred_element_type=f32)


def dot_nn(a, b):
    return lax.dot_general(a, b, (((1,), (0,)), ((), ())), preferred_element_type=f32)


def dot_tn(a, b):
    return lax.dot_general(a, b, (((0,), (0,)), ((), ())), preferred_element_type=f32)


def head_mask(shape, head):
    return (lax.broadcasted_iota(jnp.int32, shape, len(shape) - 1) // HD) == head


def cost(flops, moved, transcendentals=0):
    return pl.CostEstimate(
        flops=int(flops), bytes_accessed=int(moved), transcendentals=int(transcendentals)
    )


def params():
    return pltpu.CompilerParams(vmem_limit_bytes=VMEM_BYTES)


def cross_forward_kernel(q_ref, k_ref, v_ref, o_ref, l_ref):
    rows = q_ref.shape[0]
    lane = lax.broadcasted_iota(jnp.int32, (rows, 128), 1)
    q = q_ref[...]
    mixed = jnp.zeros((rows, CH), f32)
    stat = jnp.zeros((rows, 128), f32)
    for head in range(TH):
        mask = head_mask((rows, CH), head)
        q_head = jnp.where(mask, q.astype(f32) * 0.125, 0.0).astype(bf16)
        scores = dot_nt(q_head, k_ref[...])
        peak = jnp.max(scores, -1, keepdims=True)
        shifted = jnp.exp(scores - peak)
        total = jnp.sum(shifted, -1, keepdims=True)
        part = dot_nn(shifted.astype(bf16), v_ref[...])
        mixed = jnp.where(mask, part / total, mixed)
        stat = jnp.where(lane == head, peak + jnp.log(total), stat)
    o_ref[...] = mixed.astype(bf16)
    l_ref[0] = stat.T[:8]


def cross_forward(query, kv):
    rows = query.shape[0] // 2
    cells = kv.shape[0]
    return pl.pallas_call(
        cross_forward_kernel,
        grid=(2,),
        in_specs=[
            pl.BlockSpec((rows, CH), lambda i: (i, 0)),
            pl.BlockSpec((cells, CH), lambda i: (0, 0)),
            pl.BlockSpec((cells, CH), lambda i: (0, 1)),
        ],
        out_specs=[
            pl.BlockSpec((rows, CH), lambda i: (i, 0)),
            pl.BlockSpec((1, 8, rows), lambda i: (i, 0, 0)),
        ],
        out_shape=[
            jax.ShapeDtypeStruct((2 * rows, CH), bf16),
            jax.ShapeDtypeStruct((2, 8, rows), f32),
        ],
        compiler_params=params(),
        cost_estimate=cost(16 * TH * rows * cells * CH // 2, 8 * cells * CH, 2 * TH * rows * cells),
    )(query, kv, kv)


def delta_rows(d_out, out):
    product = d_out.astype(f32) * out.astype(f32)
    head = lax.broadcasted_iota(jnp.int32, (8, CH), 0)
    lane = lax.broadcasted_iota(jnp.int32, (8, CH), 1)
    pick = ((lane // HD) == head).astype(f32)
    return lax.dot_general(
        pick,
        product,
        (((1,), (1,)), ((), ())),
        precision=lax.Precision.HIGHEST,
        preferred_element_type=f32,
    )


def cross_backward_kernel(
    q_ref, k_ref, v_ref, do_ref, o_ref, l_ref, dq_ref, dkv_ref, q_s, do_s, delta_s, dq_s
):
    step = pl.program_id(0)
    rows = q_ref.shape[0]

    @pl.when(step == 0)
    def _():
        for head in range(TH):
            mask = head_mask((rows, CH), head)
            q_s[head] = jnp.where(mask, q_ref[...].astype(f32) * 0.125, 0.0).astype(bf16)
            do_s[head] = jnp.where(mask, do_ref[...].astype(f32), 0.0).astype(bf16)
        delta_s[...] = delta_rows(do_ref[...], o_ref[...])
        dq_s[...] = jnp.zeros_like(dq_s)

    cells = k_ref.shape[0]
    dk = jnp.zeros((cells, CH), f32)
    dv = jnp.zeros((cells, CH), f32)
    dq = dq_s[...]
    k = k_ref[...]
    for head in range(TH):
        probs = jnp.exp(dot_nt(k, q_s[head]) - l_ref[head : head + 1, :])
        d_probs = dot_nt(v_ref[...], do_s[head])
        d_scores = (probs * (d_probs - delta_s[head : head + 1, :])).astype(bf16)
        dv = dv + dot_nn(probs.astype(bf16), do_s[head])
        dk = dk + dot_nn(d_scores, q_s[head])
        dq = dq + jnp.where(head_mask((rows, CH), head), dot_tn(d_scores, k), 0.0)
    dq_s[...] = dq
    dkv_ref[:, :CH] = dk.astype(bf16)
    dkv_ref[:, CH:] = dv.astype(bf16)

    @pl.when(step == pl.num_programs(0) - 1)
    def _():
        dq_ref[...] = (dq_s[...] * 0.125).astype(bf16)


def cross_backward(query, kv, d_out, out, log_rows):
    rows = query.shape[0]
    cells = kv.shape[0]
    block = 1024
    whole = lambda i: (0, 0)
    return pl.pallas_call(
        cross_backward_kernel,
        grid=(cells // block,),
        in_specs=[
            pl.BlockSpec((rows, CH), whole),
            pl.BlockSpec((block, CH), lambda i: (i, 0)),
            pl.BlockSpec((block, CH), lambda i: (i, 1)),
            pl.BlockSpec((rows, CH), whole),
            pl.BlockSpec((rows, CH), whole),
            pl.BlockSpec((8, rows), whole),
        ],
        out_specs=[
            pl.BlockSpec((rows, CH), whole),
            pl.BlockSpec((block, 2 * CH), lambda i: (i, 0)),
        ],
        out_shape=[
            jax.ShapeDtypeStruct((rows, CH), bf16),
            jax.ShapeDtypeStruct((cells, 2 * CH), bf16),
        ],
        scratch_shapes=[
            pltpu.VMEM((TH, rows, CH), bf16),
            pltpu.VMEM((TH, rows, CH), bf16),
            pltpu.VMEM((8, rows), f32),
            pltpu.VMEM((rows, CH), f32),
        ],
        compiler_params=params(),
        cost_estimate=cost(10 * TH * rows * cells * CH, 8 * cells * CH, TH * rows * cells),
    )(query, kv, kv, d_out, out, log_rows)


def self_forward_kernel(len_ref, q_ref, k_ref, v_ref, o_ref, l_ref):
    group = pl.program_id(0)
    length = len_ref[0]
    for start, count in ROW_BLOCKS:
        stop = start + count
        q = q_ref[0, start:stop, :].astype(f32) * 0.125
        row = lax.broadcasted_iota(jnp.int32, (count, 1), 0) + start
        bound = jnp.minimum(row, length - 1)
        allowed = lax.broadcasted_iota(jnp.int32, (count, stop), 1) <= bound
        mixed = jnp.zeros((count, CH), f32)
        stat = jnp.zeros((count, 128), f32)
        lane = lax.broadcasted_iota(jnp.int32, (count, 128), 1)
        for head in range(GROUP):
            mask = head_mask((count, CH), head)
            q_head = jnp.where(mask, q, 0.0).astype(bf16)
            scores = jnp.where(allowed, dot_nt(q_head, k_ref[0, :stop, :]), neg_large)
            peak = jnp.max(scores, -1, keepdims=True)
            shifted = jnp.exp(scores - peak)
            total = jnp.sum(shifted, -1, keepdims=True)
            part = dot_nn(shifted.astype(bf16), v_ref[0, :stop, :])
            mixed = jnp.where(mask, part / total, mixed)
            stat = jnp.where(lane == head, peak + jnp.log(total), stat)
        o_ref[start:stop, :] = mixed.astype(bf16)
        l_ref[0, :, start:stop] = stat.T[:8]


def self_forward(qkv, length):
    groups = D // CH
    at = lambda j: (lambda i, n: (j, 0, i))
    return pl.pallas_call(
        self_forward_kernel,
        grid_spec=pltpu.PrefetchScalarGridSpec(
            num_scalar_prefetch=1,
            grid=(groups,),
            in_specs=[pl.BlockSpec((1, SEQ, CH), at(j)) for j in range(3)],
            out_specs=[
                pl.BlockSpec((SEQ, CH), lambda i, n: (0, i)),
                pl.BlockSpec((1, 8, SEQ), lambda i, n: (i, 0, 0)),
            ],
        ),
        out_shape=[
            jax.ShapeDtypeStruct((SEQ, D), bf16),
            jax.ShapeDtypeStruct((groups, 8, SEQ), f32),
        ],
        compiler_params=params(),
        cost_estimate=cost(4 * HEADS * SEQ * SEQ * CH, 8 * SEQ * D, HEADS * SEQ * SEQ),
    )(length, qkv, qkv, qkv)


def self_backward_kernel(
    len_ref, q_ref, k_ref, v_ref, do_ref, o_ref, l_ref, out_ref, dk_s, dv_s
):
    length = len_ref[0]
    dk_s[...] = jnp.zeros_like(dk_s)
    dv_s[...] = jnp.zeros_like(dv_s)
    delta = delta_rows(do_ref[...], o_ref[...])
    for start, count in ROW_BLOCKS:
        stop = start + count
        q = q_ref[0, start:stop, :].astype(f32) * 0.125
        d_out = do_ref[start:stop, :].astype(f32)
        row = lax.broadcasted_iota(jnp.int32, (1, count), 1) + start
        bound = jnp.minimum(row, length - 1)
        allowed = lax.broadcasted_iota(jnp.int32, (stop, count), 0) <= bound
        dq = jnp.zeros((count, CH), f32)
        k = k_ref[0, :stop, :]
        v = v_ref[0, :stop, :]
        dk = dk_s[:stop, :]
        dv = dv_s[:stop, :]
        for head in range(GROUP):
            mask = head_mask((count, CH), head)
            q_head = jnp.where(mask, q, 0.0).astype(bf16)
            d_head = jnp.where(mask, d_out, 0.0).astype(bf16)
            scores = dot_nt(k, q_head)
            logs = l_ref[0, head : head + 1, start:stop]
            probs = jnp.where(allowed, jnp.exp(scores - logs), 0.0)
            d_probs = dot_nt(v, d_head)
            d_scores = (probs * (d_probs - delta[head : head + 1, start:stop])).astype(bf16)
            dv = dv + dot_nn(probs.astype(bf16), d_head)
            dk = dk + dot_nn(d_scores, q_head)
            dq = dq + jnp.where(mask, dot_tn(d_scores, k), 0.0)
        dk_s[:stop, :] = dk
        dv_s[:stop, :] = dv
        out_ref[0, start:stop, :] = (dq * 0.125).astype(bf16)
    out_ref[1] = dk_s[...].astype(bf16)
    out_ref[2] = dv_s[...].astype(bf16)


def self_backward(qkv, d_out, out, log_rows, length):
    groups = D // CH
    at = lambda j: (lambda i, n: (j, 0, i))
    here = lambda i, n: (0, i)
    return pl.pallas_call(
        self_backward_kernel,
        grid_spec=pltpu.PrefetchScalarGridSpec(
            num_scalar_prefetch=1,
            grid=(groups,),
            in_specs=[pl.BlockSpec((1, SEQ, CH), at(j)) for j in range(3)]
            + [
                pl.BlockSpec((SEQ, CH), here),
                pl.BlockSpec((SEQ, CH), here),
                pl.BlockSpec((1, 8, SEQ), lambda i, n: (i, 0, 0)),
            ],
            out_specs=pl.BlockSpec((3, SEQ, CH), lambda i, n: (0, 0, i)),
            scratch_shapes=[pltpu.VMEM((SEQ, CH), f32), pltpu.VMEM((SEQ, CH), f32)],
        ),
        out_shape=jax.ShapeDtypeStruct((3, SEQ, D), bf16),
        compiler_params=params(),
        cost_estimate=cost(8 * HEADS * SEQ * SEQ * CH, 16 * SEQ * D, HEADS * SEQ * SEQ),
    )(length, qkv, qkv, qkv, d_out, out, log_rows)


def full(*shape):
    return pl.BlockSpec(shape, lambda i: (0,) * len(shape))


def part_of(first):
    return pl.BlockSpec((3, CH, D), lambda i: (first + i, 0, 0))


def fixed_part(index):
    return pl.BlockSpec((3, CH, D), lambda i: (index, 0, 0))


def square(ref):
    return ref[...].reshape(D, D)


def row_scale(values):
    return lax.rsqrt(jnp.mean(values * values, -1, keepdims=True) + eps_norm)


def pull_norm(d_normed, values, gain):
    scale = row_scale(values)
    d_gain = jnp.sum(d_normed * values * scale, 0, keepdims=True)
    scaled = d_normed * gain
    inner = jnp.mean(scaled * values, -1, keepdims=True)
    return d_gain, scale * scaled - (scale * scale * scale) * values * inner


def embed_kernel(
    pool_ref, feats_ref, mixed_ref, out_w_ref, emb_ref, w_ref, gain_ref,
    seq_ref, embed_ref, normed_ref, qkv_ref,
):
    @pl.when(pl.program_id(0) == 0)
    def _():
        updated = feats_ref[...].astype(f32) + dot_nn(mixed_ref[...], out_w_ref[...])
        seq_ref[:CTX, :] = pool_ref[...]
        seq_ref[CTX:, :] = updated.astype(bf16)
        embed = dot_nn(seq_ref[...], emb_ref[0])
        embed_ref[...] = embed
        normed_ref[...] = (embed * row_scale(embed) * gain_ref[...]).astype(bf16)

    qkv_ref[0] = dot_nn(normed_ref[...], square(w_ref)).astype(bf16)


def embed_forward(pooled, feats, mixed, to_out, weights, gain):
    last = weights.shape[0] - 1
    return pl.pallas_call(
        embed_kernel,
        grid=(3,),
        in_specs=[
            full(CTX, CH),
            full(SEQ - CTX, CH),
            full(SEQ - CTX, CH),
            full(CH, CH),
            pl.BlockSpec((1, CH, D), lambda i: (last, 0, 0)),
            part_of(0),
            full(1, D),
        ],
        out_specs=[
            full(SEQ, CH),
            full(SEQ, D),
            full(SEQ, D),
            pl.BlockSpec((1, SEQ, D), lambda i: (i, 0, 0)),
        ],
        out_shape=[
            jax.ShapeDtypeStruct((SEQ, CH), bf16),
            jax.ShapeDtypeStruct((SEQ, D), f32),
            jax.ShapeDtypeStruct((SEQ, D), bf16),
            jax.ShapeDtypeStruct((3, SEQ, D), bf16),
        ],
        compiler_params=params(),
        cost_estimate=cost(2 * SEQ * D * (CH + 3 * D), 12 * SEQ * D),
    )(pooled, feats, mixed, to_out, weights, weights, gain)


def up_kernel(
    mixed_ref, embed_ref, att_ref, w_ref, gain_ref,
    stream_ref, normed_ref, act_ref, slope_ref, pre_s,
):
    @pl.when(pl.program_id(0) == 0)
    def _():
        stream = embed_ref[...] + dot_nn(mixed_ref[...], square(att_ref))
        stream_ref[...] = stream
        normed_ref[...] = (stream * row_scale(stream) * gain_ref[...]).astype(bf16)

    pre_s[...] = dot_nn(normed_ref[...], square(w_ref))
    factor = (2.0 / 3.141592653589793) ** 0.5
    cubic = 0.044715 * factor

    def rows_step(index, carry):
        here = pl.ds(pl.multiple_of(index * 16, 16), 16)
        v = pre_s[here, :]
        v2 = v * v
        half = 0.5 + 0.5 * jnp.tanh(v * (factor + cubic * v2))
        act_ref[0, here, :] = (v * half).astype(bf16)
        bend = 2.0 * half * (1.0 - half) * (factor + 3.0 * cubic * v2)
        slope_ref[0, here, :] = (half + v * bend).astype(bf16)
        return carry

    lax.fori_loop(0, SEQ // 16, rows_step, 0, unroll=2)


def up_forward(mixed, embed, weights, gain):
    return pl.pallas_call(
        up_kernel,
        grid=(4,),
        in_specs=[full(SEQ, D), full(SEQ, D), fixed_part(3), part_of(4), full(1, D)],
        out_specs=[
            full(SEQ, D),
            full(SEQ, D),
            pl.BlockSpec((1, SEQ, D), lambda i: (i, 0, 0)),
            pl.BlockSpec((1, SEQ, D), lambda i: (i, 0, 0)),
        ],
        out_shape=[
            jax.ShapeDtypeStruct((SEQ, D), f32),
            jax.ShapeDtypeStruct((SEQ, D), bf16),
            jax.ShapeDtypeStruct((4, SEQ, D), bf16),
            jax.ShapeDtypeStruct((4, SEQ, D), bf16),
        ],
        scratch_shapes=[pltpu.VMEM((SEQ, D), f32)],
        compiler_params=params(),
        cost_estimate=cost(10 * SEQ * D * D, 28 * SEQ * D, 4 * SEQ * D),
    )(mixed, embed, weights, weights, gain)


def down_kernel(act_ref, w_ref, stream_ref, out_ref):
    part = dot_nn(act_ref[0], square(w_ref))

    @pl.when(pl.program_id(0) == 0)
    def _():
        out_ref[...] = stream_ref[...] + part

    @pl.when(pl.program_id(0) > 0)
    def _():
        out_ref[...] += part


def down_forward(act, w_down, stream):
    return pl.pallas_call(
        down_kernel,
        grid=(4,),
        in_specs=[
            pl.BlockSpec((1, SEQ, D), lambda i: (i, 0, 0)),
            part_of(0),
            full(SEQ, D),
        ],
        out_specs=full(SEQ, D),
        out_shape=jax.ShapeDtypeStruct((SEQ, D), f32),
        compiler_params=params(),
        cost_estimate=cost(8 * SEQ * D * D, 24 * SEQ * D),
    )(act, w_down, stream)


def down_grad_kernel(act_ref, gd_ref, out_ref):
    out_ref[...] = dot_tn(act_ref[0], gd_ref[...]).astype(bf16)


def down_grad(act, gd):
    return pl.pallas_call(
        down_grad_kernel,
        grid=(4,),
        in_specs=[pl.BlockSpec((1, SEQ, D), lambda i: (i, 0, 0)), full(SEQ, D)],
        out_specs=pl.BlockSpec((D, D), lambda i: (i, 0)),
        out_shape=jax.ShapeDtypeStruct((4 * D, D), bf16),
        compiler_params=params(),
        cost_estimate=cost(8 * SEQ * D * D, 18 * SEQ * D),
    )(act, gd)


def up_grad_kernel(gd_ref, w_ref, slope_ref, normed_ref, gpre_ref, out_ref, turned_s):
    @pl.when(pl.program_id(0) == 0)
    def _():
        turned_s[...] = normed_ref[...].T

    gpre = (dot_nt(gd_ref[...], square(w_ref)) * slope_ref[0].astype(f32)).astype(bf16)
    gpre_ref[0] = gpre
    out_ref[...] = dot_nn(turned_s[...], gpre).astype(bf16)


def up_grad(gd, w_down, slope, normed):
    part = pl.BlockSpec((1, SEQ, D), lambda i: (i, 0, 0))
    return pl.pallas_call(
        up_grad_kernel,
        grid=(4,),
        in_specs=[full(SEQ, D), part_of(0), part, full(SEQ, D)],
        out_specs=[part, pl.BlockSpec((D, D), lambda i: (i, 0))],
        out_shape=[
            jax.ShapeDtypeStruct((4, SEQ, D), bf16),
            jax.ShapeDtypeStruct((4 * D, D), bf16),
        ],
        scratch_shapes=[pltpu.VMEM((D, SEQ), bf16)],
        compiler_params=params(),
        cost_estimate=cost(16 * SEQ * D * D, 36 * SEQ * D),
    )(gd, w_down, slope, normed)


def att_grad_kernel(
    gpre_ref, w_ref, att_ref, stream_ref, gd_ref, mixed_ref, gain_ref,
    d_stream_ref, gog_ref, att_g_ref, gain_g_ref, total_s,
):
    step = pl.program_id(0)
    part = dot_nt(gpre_ref[0], square(w_ref))

    @pl.when(step == 0)
    def _():
        total_s[...] = part

    @pl.when(step > 0)
    def _():
        total_s[...] += part

    @pl.when(step == pl.num_programs(0) - 1)
    def _():
        d_gain, pulled = pull_norm(total_s[...], stream_ref[...], gain_ref[...])
        gain_g_ref[...] = d_gain
        d_stream = gd_ref[...].astype(f32) + pulled
        d_stream_ref[...] = d_stream
        ga = d_stream.astype(bf16)
        gog_ref[...] = dot_nt(ga, square(att_ref)).astype(bf16)
        att_g_ref[...] = dot_tn(mixed_ref[...], ga).astype(bf16)


def att_grad(gpre, weights, stream, gd, mixed, gain):
    return pl.pallas_call(
        att_grad_kernel,
        grid=(4,),
        in_specs=[
            pl.BlockSpec((1, SEQ, D), lambda i: (i, 0, 0)),
            part_of(4),
            fixed_part(3),
            full(SEQ, D),
            full(SEQ, D),
            full(SEQ, D),
            full(1, D),
        ],
        out_specs=[full(SEQ, D), full(SEQ, D), full(D, D), full(1, D)],
        out_shape=[
            jax.ShapeDtypeStruct((SEQ, D), f32),
            jax.ShapeDtypeStruct((SEQ, D), bf16),
            jax.ShapeDtypeStruct((D, D), bf16),
            jax.ShapeDtypeStruct((1, D), f32),
        ],
        scratch_shapes=[pltpu.VMEM((SEQ, D), f32)],
        compiler_params=params(),
        cost_estimate=cost(12 * SEQ * D * D, 32 * SEQ * D),
    )(gpre, weights, weights, stream, gd, mixed, gain)


def qkv_grad_kernel(normed_ref, g_ref, out_ref, turned_s):
    @pl.when(pl.program_id(0) == 0)
    def _():
        turned_s[...] = normed_ref[...].T

    out_ref[...] = dot_nn(turned_s[...], g_ref[0]).astype(bf16)


def qkv_grad(normed, gqkv):
    return pl.pallas_call(
        qkv_grad_kernel,
        grid=(3,),
        in_specs=[full(SEQ, D), pl.BlockSpec((1, SEQ, D), lambda i: (i, 0, 0))],
        out_specs=pl.BlockSpec((D, D), lambda i: (i, 0)),
        out_shape=jax.ShapeDtypeStruct((3 * D, D), bf16),
        scratch_shapes=[pltpu.VMEM((D, SEQ), bf16)],
        compiler_params=params(),
        cost_estimate=cost(6 * SEQ * D * D, 14 * SEQ * D),
    )(normed, gqkv)


def embed_grad_kernel(
    g_ref, w_ref, emb_ref, embed_ref, d_stream_ref, seq_ref, mixed_ref, out_w_ref, gain_ref,
    emb_g_ref, gupd_ref, pool_g_ref, out_g_ref, gox_ref, gain_g_ref, total_s,
):
    step = pl.program_id(0)
    part = dot_nt(g_ref[0], square(w_ref))

    @pl.when(step == 0)
    def _():
        total_s[...] = part

    @pl.when(step > 0)
    def _():
        total_s[...] += part

    @pl.when(step == pl.num_programs(0) - 1)
    def _():
        d_gain, pulled = pull_norm(total_s[...], embed_ref[...], gain_ref[...])
        gain_g_ref[...] = d_gain
        gembed = (d_stream_ref[...] + pulled).astype(bf16)
        emb_g_ref[...] = dot_tn(seq_ref[...], gembed).astype(bf16)
        gseq = dot_nt(gembed, emb_ref[0])
        gupd = gseq[CTX:]
        gb = gupd.astype(bf16)
        pool_g_ref[...] = gseq[:CTX].astype(bf16)
        gupd_ref[...] = gupd
        out_g_ref[...] = dot_tn(mixed_ref[...], gb).astype(bf16)
        gox_ref[...] = dot_nt(gb, out_w_ref[...]).astype(bf16)


def embed_grad(gqkv, weights, embed, d_stream, seq, mixed, to_out, gain):
    last = weights.shape[0] - 1
    return pl.pallas_call(
        embed_grad_kernel,
        grid=(3,),
        in_specs=[
            pl.BlockSpec((1, SEQ, D), lambda i: (i, 0, 0)),
            part_of(0),
            pl.BlockSpec((1, CH, D), lambda i: (last, 0, 0)),
            full(SEQ, D),
            full(SEQ, D),
            full(SEQ, CH),
            full(SEQ - CTX, CH),
            full(CH, CH),
            full(1, D),
        ],
        out_specs=[
            full(CH, D),
            full(SEQ - CTX, CH),
            full(CTX, CH),
            full(CH, CH),
            full(SEQ - CTX, CH),
            full(1, D),
        ],
        out_shape=[
            jax.ShapeDtypeStruct((CH, D), bf16),
            jax.ShapeDtypeStruct((SEQ - CTX, CH), f32),
            jax.ShapeDtypeStruct((CTX, CH), bf16),
            jax.ShapeDtypeStruct((CH, CH), bf16),
            jax.ShapeDtypeStruct((SEQ - CTX, CH), bf16),
            jax.ShapeDtypeStruct((1, D), f32),
        ],
        scratch_shapes=[pltpu.VMEM((SEQ, D), f32)],
        compiler_params=params(),
        cost_estimate=cost(2 * SEQ * D * (3 * D + 2 * CH), 24 * SEQ * D),
    )(gqkv, weights, weights, embed, d_stream, seq, mixed, to_out, gain)


def patch_pick(rows, columns, patch_dim):
    patch = lax.broadcasted_iota(jnp.int32, (rows, columns), patch_dim)
    cell = lax.broadcasted_iota(jnp.int32, (rows, columns), 1 - patch_dim)
    inside = (cell // (PATCH * IMG)) * (IMG // PATCH) + (cell % IMG) // PATCH
    return jnp.where(patch == inside, 1.0 / (PATCH * PATCH), 0.0).astype(bf16)


def image_rows(step, row):
    return pl.ds(pl.multiple_of(step * BLOCK + row * IMG, IMG), BLOCK)


def token_forward_kernel(x_ref, conv_ref, kv_w_ref, slope_ref, hidden_ref, kv_ref, pool_ref):
    step = pl.program_id(0)
    z = jnp.zeros((BLOCK, CH), f32)
    for row in range(3):
        z = z + dot_nn(x_ref[image_rows(step, row), :], conv_ref[row])
    center = x_ref[image_rows(step, 1), CH : 2 * CH].astype(f32)
    gate = 1.0 / (1.0 + jnp.exp(-z))
    hidden = center + z * gate
    slope_ref[...] = (gate * (1.0 + z * (1.0 - gate))).astype(bf16)
    hidden_b = hidden.astype(bf16)
    hidden_ref[...] = hidden_b
    kv_ref[...] = dot_nn(hidden_b, kv_w_ref[...]).astype(bf16)
    rest = (hidden - hidden_b.astype(f32)).astype(bf16)
    pick = patch_pick(pool_ref.shape[0], BLOCK, 0)
    pool_ref[...] = (dot_nn(pick, hidden_b) + dot_nn(pick, rest)).astype(bf16)


def token_forward(wide, conv_rows, kv_weight):
    steps = CELLS // BLOCK
    whole = lambda i: (0, 0)
    block = lambda i: (i, 0)
    return pl.pallas_call(
        token_forward_kernel,
        grid=(steps,),
        in_specs=[
            pl.BlockSpec(wide.shape, whole),
            pl.BlockSpec((3, 3 * CH, CH), lambda i: (0, 0, 0)),
            pl.BlockSpec((CH, 2 * CH), whole),
        ],
        out_specs=[
            pl.BlockSpec((BLOCK, CH), block),
            pl.BlockSpec((BLOCK, CH), block),
            pl.BlockSpec((BLOCK, 2 * CH), block),
            pl.BlockSpec((CTX // steps, CH), block),
        ],
        out_shape=[
            jax.ShapeDtypeStruct((CELLS, CH), bf16),
            jax.ShapeDtypeStruct((CELLS, CH), bf16),
            jax.ShapeDtypeStruct((CELLS, 2 * CH), bf16),
            jax.ShapeDtypeStruct((CTX, CH), bf16),
        ],
        compiler_params=params(),
        cost_estimate=cost(22 * CELLS * CH * CH, 14 * CELLS * CH, CELLS * CH),
    )(wide, conv_rows, kv_weight)


def token_backward_kernel(
    dkv_ref, slope_ref, pool_ref, hidden_ref, x_ref, kv_w_ref,
    d_hidden_ref, gz_ref, conv_ref, kv_g_ref, conv_s, kv_s,
):
    step = pl.program_id(0)

    @pl.when(step == 0)
    def _():
        conv_s[...] = jnp.zeros_like(conv_s)
        kv_s[...] = jnp.zeros_like(kv_s)

    dkv = dkv_ref[...]
    d_hidden = dot_nt(dkv, kv_w_ref[...])
    d_hidden = d_hidden + dot_nn(patch_pick(BLOCK, pool_ref.shape[0], 1), pool_ref[...])
    gz = (d_hidden * slope_ref[...].astype(f32)).astype(bf16)
    d_hidden_ref[...] = d_hidden
    gz_ref[...] = gz
    kv_s[...] += dot_tn(hidden_ref[...], dkv)
    gz_t = gz.T
    for row in range(3):
        conv_s[row] += dot_nn(gz_t, x_ref[image_rows(step, row), :])

    @pl.when(step == pl.num_programs(0) - 1)
    def _():
        for row in range(3):
            for col in range(3):
                conv_ref[3 * row + col] = conv_s[row, :, col * CH : (col + 1) * CH].T.astype(bf16)
        kv_g_ref[0] = kv_s[:, :CH].astype(bf16)
        kv_g_ref[1] = kv_s[:, CH:].astype(bf16)


def token_backward(dkv, slope, d_pool, hidden_b, wide, kv_weight):
    steps = CELLS // BLOCK
    whole = lambda i: (0, 0)
    whole_3 = lambda i: (0, 0, 0)
    block = lambda i: (i, 0)
    return pl.pallas_call(
        token_backward_kernel,
        grid=(steps,),
        in_specs=[
            pl.BlockSpec((BLOCK, 2 * CH), block),
            pl.BlockSpec((BLOCK, CH), block),
            pl.BlockSpec((CTX // steps, CH), block),
            pl.BlockSpec((BLOCK, CH), block),
            pl.BlockSpec(wide.shape, whole),
            pl.BlockSpec((CH, 2 * CH), whole),
        ],
        out_specs=[
            pl.BlockSpec((BLOCK, CH), block),
            pl.BlockSpec((BLOCK, CH), block),
            pl.BlockSpec((9, CH, CH), whole_3),
            pl.BlockSpec((2, CH, CH), whole_3),
        ],
        out_shape=[
            jax.ShapeDtypeStruct((CELLS, CH), f32),
            jax.ShapeDtypeStruct((CELLS, CH), bf16),
            jax.ShapeDtypeStruct((9, CH, CH), bf16),
            jax.ShapeDtypeStruct((2, CH, CH), bf16),
        ],
        scratch_shapes=[pltpu.VMEM((3, CH, 3 * CH), f32), pltpu.VMEM((CH, 2 * CH), f32)],
        compiler_params=params(),
        cost_estimate=cost(26 * CELLS * CH * CH, 20 * CELLS * CH),
    )(dkv, slope, d_pool, hidden_b, wide, kv_weight)


def context_backward_kernel(gz_ref, d_hidden_ref, conv_ref, out_ref, wide_s):
    step = pl.program_id(0)
    steps = pl.num_programs(0)

    def widen(at):
        values = gz_ref[image_rows(at, 0), :].astype(f32)
        col = lax.broadcasted_iota(jnp.int32, (BLOCK, CH), 0) % IMG
        left = jnp.where(col == 0, 0.0, pltpu.roll(values, 1, 0))
        right = jnp.where(col == IMG - 1, 0.0, pltpu.roll(values, BLOCK - 1, 0))
        wide_s[image_rows(at, 1), 0:CH] = left.astype(bf16)
        wide_s[image_rows(at, 1), CH : 2 * CH] = values.astype(bf16)
        wide_s[image_rows(at, 1), 2 * CH :] = right.astype(bf16)

    @pl.when(step == 0)
    def _():
        wide_s[0:IMG, :] = jnp.zeros((IMG, 3 * CH), bf16)
        wide_s[CELLS + IMG :, :] = jnp.zeros((IMG, 3 * CH), bf16)
        widen(0)

    @pl.when(step < steps - 1)
    def _():
        widen(step + 1)

    total = d_hidden_ref[...]
    for row in range(3):
        values = wide_s[image_rows(step, row), :]
        for col in range(3):
            tap = conv_ref[3 * (2 - row) + (2 - col)]
            total = total + dot_nt(values[:, col * CH : (col + 1) * CH], tap)
    out_ref[...] = total.astype(bf16)


def context_backward(gz, d_hidden, conv_tiles):
    block = lambda i: (i, 0)
    return pl.pallas_call(
        context_backward_kernel,
        grid=(CELLS // BLOCK,),
        in_specs=[
            pl.BlockSpec((CELLS, CH), lambda i: (0, 0)),
            pl.BlockSpec((BLOCK, CH), block),
            pl.BlockSpec((9, CH, CH), lambda i: (0, 0, 0)),
        ],
        out_specs=pl.BlockSpec((BLOCK, CH), block),
        out_shape=jax.ShapeDtypeStruct((CELLS, CH), bf16),
        scratch_shapes=[pltpu.VMEM((CELLS + 2 * IMG, 3 * CH), bf16)],
        compiler_params=params(),
        cost_estimate=cost(18 * CELLS * CH * CH, 8 * CELLS * CH),
    )(gz, d_hidden, conv_tiles)


def local(
    context_map,
    future_feats,
    horizon,
    cotangent,
    tile_owner,
    master_tiles,
    moment_first,
    moment_second,
    norm_gains,
    gain_first,
    gain_second,
):
    slot_count = master_tiles.shape[0]
    devices = lax.axis_size(AXES)
    rows = CH // devices
    slot_of = slot_index(tile_owner, slot_count)

    image = trade_rows(context_map).reshape(IMG, IMG, CH)
    length = CTX + FT * horizon
    valid = jnp.arange(SEQ) < length[0]
    gd = jnp.where(valid[:, None], cotangent[0], jnp.zeros((), bf16))

    slices = (
        master_tiles.astype(bf16)
        .reshape(slot_count, devices, rows, CH)
        .transpose(1, 0, 2, 3)
    )
    slices = lax.all_to_all(slices, AXES, split_axis=0, concat_axis=0, tiled=True)
    slices = slices.reshape(devices * slot_count, rows, CH)
    slices = slices.at[slot_of].get(mode="promise_in_bounds")
    early, emb, qkv, att, up, down = jnp.split(slices, (13, 16, 43, 52, 88))
    weights = jnp.concatenate(
        [
            from_tiles(qkv, 3, 3),
            from_tiles(att, 3, 1),
            from_tiles(up, 3, 4),
            from_tiles(emb, 1, 1),
        ],
        0,
    )
    weights = lax.all_gather(weights, AXES, axis=1, tiled=True)
    w_down = lax.all_gather(from_tiles(down, 12, 1), AXES, axis=1, tiled=True)
    early = gather_all(early).transpose(1, 0, 2, 3).reshape(EARLY, CH, CH)

    padded = jnp.pad(image, ((1, 1), (1, 1), (0, 0)))
    wide = jnp.concatenate([padded[:, col : col + IMG] for col in range(3)], -1)
    wide = wide.reshape((IMG + 2) * IMG, 3 * CH)

    conv_tiles = early[:9]
    to_query, to_out = early[9], early[12]
    kv_weight = jnp.concatenate([early[10], early[11]], 1)

    slope_z, hidden_b, kv, pooled = token_forward(
        wide, conv_tiles.reshape(3, 3 * CH, CH), kv_weight
    )
    feats_b = future_feats[0]
    query = jnp.dot(feats_b, to_query, preferred_element_type=f32).astype(bf16)
    cross_mixed, cross_logs = cross_forward(query, kv)

    gain_one, gain_two = norm_gains[:1], norm_gains[1:]
    seq, embed, normed_one, qkv = embed_forward(
        pooled, feats_b, cross_mixed, to_out, weights, gain_one
    )
    mixed, logs = self_forward(qkv, length)
    stream, normed_two, act, slope = up_forward(mixed, embed, weights, gain_two)

    sum_down = cut(down_grad(act, gd))
    gd, sum_down = tie((gd, sum_down))
    wait_down = begin_sum(sum_down, "c", 2)
    gpre, sum_up = up_grad(gd, w_down, slope, normed_two)
    gpre, sum_up, wait_down = hold((gpre, cut(sum_up)), wait_down)
    wait_up = begin_sum(sum_up, "c", 2)
    wait_down = begin_sum(end_sum(wait_down), "x", 3)
    d_stream, gog, sum_att, gain_g_two = att_grad(gpre, weights, stream, gd, mixed, gain_two)
    gog, sum_att, wait_up = hold((gog, cut(sum_att)), wait_up)
    wait_up = begin_sum(end_sum(wait_up), "y", 2)
    wait_att = begin_sum(sum_att, "c", 2)
    gqkv = self_backward(qkv, gog, mixed, logs, length)
    gqkv, wait_down, wait_up, wait_att = hold((gqkv,), wait_down, wait_up, wait_att)
    wait_down = begin_sum(end_sum(wait_down), "y", 2)
    wait_up = begin_sum(end_sum(wait_up), "x", 2)
    sum_att = end_sum(wait_att)
    sum_qkv = cut(qkv_grad(normed_one, gqkv))
    gqkv, sum_qkv, sum_att = tie((gqkv, sum_qkv, sum_att))
    wait_qkv = begin_sum(sum_qkv, "c", 2)
    emb_g, gupd, pool_g, out_g, gox, gain_g_one = embed_grad(
        gqkv, weights, embed, d_stream, seq, cross_mixed, to_out, gain_one
    )
    gains = jnp.concatenate([gain_g_one, gain_g_two], 0).reshape(devices, 1, -1)
    gain_count = gains.shape[-1]
    gains = jnp.pad(gains, ((0, 0), (0, rows - 1), (0, D - gain_count))).astype(bf16)
    sum_emb = cut(jnp.concatenate([emb_g, gains.reshape(CH, D)], 0))
    gox, gupd, sum_emb, wait_qkv, wait_down, wait_up = hold(
        (gox, gupd, sum_emb), wait_qkv, wait_down, wait_up
    )
    wait_mlp = begin_near(jnp.concatenate([end_sum(wait_up), end_sum(wait_down)], 0))
    sum_qkv = end_sum(wait_qkv)
    wait_first = begin_sum(sum_qkv[:6], "x", 3)
    wait_second = begin_sum(jnp.concatenate([sum_qkv[6:], sum_att], 0), "y", 2)
    wait_emb = begin_sum(sum_emb, "c", 2)

    log_rows = jnp.concatenate([cross_logs[0], cross_logs[1]], 1)
    gq, gkv = cross_backward(query, kv, gox, cross_mixed, log_rows)
    gq, gkv, wait_first, wait_second, wait_mlp, wait_emb = hold(
        (gq, gkv), wait_first, wait_second, wait_mlp, wait_emb
    )
    wait_first = begin_sum(end_sum(wait_first), "y", 2)
    wait_second = begin_sum(end_sum(wait_second), "x", 2)
    wait_mlp = begin_far(end_sum(wait_mlp))
    wait_emb = begin_sum(end_sum(wait_emb), "x", 3)

    d_hidden, gz, conv_g, kv_g = token_backward(gkv, slope_z, pool_g, hidden_b, wide, kv_weight)
    query_g = jnp.dot(feats_b.T, gq, preferred_element_type=f32).astype(bf16)
    sum_early = cut(
        jnp.concatenate([conv_g, query_g[None], kv_g, out_g[None]], 0).reshape(EARLY * CH, CH)
    )
    d_hidden, gz, sum_early, wait_first, wait_second, wait_mlp, wait_emb = hold(
        (d_hidden, gz, sum_early), wait_first, wait_second, wait_mlp, wait_emb
    )
    sum_early = end_sum(begin_sum(sum_early, "c", 2))
    wait_att = begin_near(jnp.concatenate([end_sum(wait_first), end_sum(wait_second)], 0))
    wait_emb = begin_sum(end_sum(wait_emb), "y", 2)
    sum_mlp = end_sum(wait_mlp, keep_wide=True)
    gz, sum_early = tie((gz, sum_early))
    wait_early = begin_sum(
        sum_early.reshape(sum_early.shape[:2] + (-1,) + sum_early.shape[-2:]), ("y", "x"), 2
    )
    context_grad = context_backward(gz, d_hidden, conv_tiles)
    context_grad, wait_early, wait_att, wait_emb = hold(
        (context_grad,), wait_early, wait_att, wait_emb
    )
    wait_early = begin_sum(end_sum(wait_early), "z", 1)
    wait_att = begin_far(end_sum(wait_att))
    wait_emb = begin_sum(end_sum(wait_emb), "z", 1)
    sum_early = end_sum(wait_early, keep_wide=True)
    sum_att = end_sum(wait_att, keep_wide=True)
    sum_emb = end_sum(wait_emb, keep_wide=True)
    context_rows = trade_rows(context_grad.reshape(context_map.shape))
    future_grad = gupd + lax.dot_general(
        gq, to_query, (((1,), (1,)), ((), ())), preferred_element_type=f32
    )

    sums = jnp.concatenate(
        [
            to_tiles(sum_early),
            to_tiles(sum_emb[:1]),
            to_tiles(sum_att[:9], 3),
            to_tiles(sum_att[9:]),
            to_tiles(sum_mlp[:12], 4),
            to_tiles(sum_mlp[12:]),
        ],
        0,
    )
    gains = sum_emb[1, 0, :gain_count]
    share = jnp.concatenate([(jnp.sum(sums * sums) + jnp.sum(gains * gains))[None], gains])
    share_high = share.astype(bf16)
    share_low = (share - share_high.astype(f32)).astype(bf16)
    share = jnp.pad(
        jnp.stack([share_high, share_low]), ((0, rows - 2), (0, CH - 1 - gain_count))
    )
    slots = jnp.arange(devices * slot_count)
    found = slot_of[None, :] == slots[:, None]
    tile_of = jnp.sum(jnp.where(found, jnp.arange(found.shape[1])[None], 0), 1)
    mine = sums.astype(bf16).at[tile_of].get(mode="promise_in_bounds")
    mine = mine.reshape(devices, slot_count, rows, CH)
    share = jnp.broadcast_to(share[None, None], (devices, 1, rows, CH))
    mine = jnp.concatenate([mine, share], 1)
    mine = lax.all_to_all(mine, AXES, split_axis=0, concat_axis=0, tiled=True)
    block_out = down_forward(act, w_down, stream)
    shares = mine[:, slot_count, :2].astype(f32)
    shares = shares[:, 0] + shares[:, 1]
    gains = shares[:, 1 : 1 + gain_count].reshape(2, D)
    mine = mine[:, :slot_count].transpose(1, 0, 2, 3).reshape(slot_count, CH, CH).astype(f32)

    used = jnp.any(found, 1).astype(f32).reshape(devices, slot_count)
    used = lax.dynamic_index_in_dim(used, lax.axis_index(AXES), 0, keepdims=False)[:, None, None]
    grad_norm = jnp.sqrt(jnp.sum(shares[:, 0]))
    factor = jnp.minimum(1.0, clip_level / (grad_norm + 1e-06))
    new_first, new_second, new_master = adam_step(
        master_tiles, mine * factor, moment_first, moment_second, learn_rate, decay_rate
    )
    new_gain_first, new_gain_second, new_gains = adam_step(
        norm_gains, gains * factor, gain_first, gain_second, gain_rate, 0.0
    )
    return (
        block_out[None],
        context_rows.reshape(context_map.shape).astype(f32),
        future_grad[None],
        jnp.where(used > 0, new_first, 0.0),
        jnp.where(used > 0, new_second, 0.0),
        jnp.where(used > 0, new_master, 0.0),
        new_gain_first,
        new_gain_second,
        new_gains,
        grad_norm,
    )


def solution(mesh):
    groups, rows = mesh.devices.shape
    fine = jax.sharding.Mesh(mesh.devices.reshape(groups // 2, 2, rows // 2, 2), AXES)
    whole = P(AXES, None, None)
    image = P(("z", "c"), ("y", "x"), None, None)
    in_specs = (image, whole, P(AXES), whole, P(), whole, whole, whole, P(), P(), P())
    out_specs = (whole, image, whole, whole, whole, whole, P(), P(), P(), P())
    return jax.shard_map(local, mesh=fine, in_specs=in_specs, out_specs=out_specs, check_vma=False)
```

```python
import functools

import jax
import jax.numpy as jnp
from jax import lax
from jax.experimental import pallas as pl
from jax.experimental.pallas import tpu as pltpu
from jax.sharding import PartitionSpec as P

CH = 256
HD = 64
HEADS = 12
D = 768
FF = 3072
TH = 4
IMG = 64
PATCH = 4
FT = 16
CTX = 256
SEQ = 736
STEP = 10


eps_norm = 1e-05
beta_one = 0.9
beta_two = 0.999
learn_rate = 0.02
gain_rate = 0.6
decay_rate = 0.1
adam_eps = 1e-08
clip_level = 1.0
neg_large = -1e30
AXES = ("z", "c", "y", "x")
CELLS = IMG * IMG
BLOCK = 512
GROUP = 4
EARLY = 13
VMEM_BYTES = 56 * 1024 * 1024
ROW_BLOCKS = ((0, 256), (256, 256), (512, 224))
bf16 = jnp.bfloat16
f32 = jnp.float32


def slot_index(tile_owner, slot_count):
    ordinal = jnp.arange(tile_owner.shape[0])
    earlier = (tile_owner[None, :] == tile_owner[:, None]) & (ordinal[None, :] < ordinal[:, None])
    return tile_owner * slot_count + jnp.sum(earlier.astype(jnp.int32), 1)


def adam_step(weight, grad_now, first, second, rate, decay):
    first_new = beta_one * first + (1.0 - beta_one) * grad_now
    second_new = beta_two * second + (1.0 - beta_two) * grad_now * grad_now
    corr_first = first_new / (1.0 - beta_one**STEP)
    corr_second = second_new / (1.0 - beta_two**STEP)
    weight_new = weight - rate * (corr_first / (jnp.sqrt(corr_second) + adam_eps) + decay * weight)
    return (first_new, second_new, weight_new)


def xor_permute(values, axes, mask):
    count = lax.axis_size(axes)
    return lax.ppermute(values, axes, [(i, i ^ mask) for i in range(count)])


def advance(parts, axes, dim):
    mine = lax.axis_index(axes)
    cuts = []
    for mask in range(lax.axis_size(axes)):
        cuts.append(add_up([lax.dynamic_index_in_dim(p, mine ^ mask, dim, False) for p in parts]))
    return cuts


def advance_near(parts):
    mine = lax.axis_index("z") % 2
    shape = parts[0].shape
    parts = [p.reshape((shape[0], shape[1] // 2, 2) + shape[2:]) for p in parts]
    return [
        add_up([lax.dynamic_index_in_dim(p, mine ^ mask, 2, False) for p in parts])
        for mask in range(2)
    ]


def advance_far(parts):
    mine = lax.axis_index("z") // 2
    return [
        add_up([lax.dynamic_index_in_dim(p, mine ^ mask, 1, False) for p in parts])
        for mask in range(parts[0].shape[1])
    ]


def send(cuts, axes, unit=1):
    return [cuts[0]] + [
        xor_permute(cut, axes, unit * mask) for mask, cut in enumerate(cuts) if mask > 0
    ]


def add_up(parts, keep_wide=False):
    total = parts[0].astype(f32)
    for part in parts[1:]:
        total = total + part.astype(f32)
    return total if keep_wide else total.astype(parts[0].dtype)


def hold(values, *sums):
    tied = lax.optimization_barrier((tuple(values), tuple(parts[0] for parts in sums)))
    return tied[0] + tuple([keep] + parts[1:] for keep, parts in zip(tied[1], sums))


def gather_axes(values, axes):
    pieces = [values]
    for mask in range(1, lax.axis_size(axes)):
        pieces.append(xor_permute(values, axes, mask))
    return jnp.stack(pieces)


def gather_all(values):
    shape = values.shape
    values = gather_axes(values, "z")
    values = gather_axes(values, ("y", "x"))
    values = gather_axes(values, "c")
    cores, rows, depth = values.shape[:3]
    order = jnp.arange(depth * cores * rows)
    z, c, row = order // (cores * rows), (order // rows) % cores, order % rows
    own = lax.axis_index("z"), lax.axis_index("c"), lax.axis_index(("y", "x"))
    at = ((c ^ own[1]) * rows + (row ^ own[2])) * depth + (z ^ own[0])
    return values.reshape((-1,) + shape).at[at].get(mode="promise_in_bounds")


def trade_rows(values):
    mine = lax.axis_index(("y", "x"))
    count = lax.axis_size(("y", "x"))
    cuts = [lax.dynamic_index_in_dim(values, mine ^ mask, 0, False) for mask in range(count)]
    return send(cuts, ("y", "x"))


def row_order(pieces):
    order = jnp.arange(len(pieces)) ^ lax.axis_index(("y", "x"))
    return jnp.stack(pieces).at[order].get(mode="promise_in_bounds")


def slice_shape():
    z, c, y, x = [lax.axis_size(axis) for axis in AXES]
    return (z, y, x, CH // (z * c * y * x))


def cut_core(matrix):
    z, y, x, rows = slice_shape()
    parts = matrix.astype(bf16).reshape(-1, z, 2, y, x, rows, matrix.shape[-1])
    own = lax.axis_index("c")
    return [lax.dynamic_index_in_dim(parts, own ^ other, 2, False) for other in range(2)]


def core_parts(parts):
    return [part.reshape((-1,) + slice_shape() + part.shape[-1:]) for part in parts]


tie = lax.optimization_barrier


def to_tiles(slices, parts=1):
    blocks, rows, columns = slices.shape
    return (
        slices.reshape(parts, blocks // parts, rows, columns // CH, CH)
        .transpose(1, 0, 3, 2, 4)
        .reshape(-1, rows, CH)
    )


def from_tiles(tiles, row_blocks, parts):
    rows = tiles.shape[1]
    return (
        tiles.reshape(row_blocks, parts, D // CH, rows, CH)
        .transpose(1, 0, 3, 2, 4)
        .reshape(parts * row_blocks, rows, D)
    )


def dot_nt(a, b):
    return lax.dot_general(a, b, (((1,), (1,)), ((), ())), preferred_element_type=f32)


def dot_nn(a, b):
    return lax.dot_general(a, b, (((1,), (0,)), ((), ())), preferred_element_type=f32)


def dot_tn(a, b):
    return lax.dot_general(a, b, (((0,), (0,)), ((), ())), preferred_element_type=f32)


def head_mask(shape, head):
    return (lax.broadcasted_iota(jnp.int32, shape, len(shape) - 1) // HD) == head


def cost(flops, moved, transcendentals=0):
    return pl.CostEstimate(
        flops=int(flops), bytes_accessed=int(moved), transcendentals=int(transcendentals)
    )


def params():
    return pltpu.CompilerParams(vmem_limit_bytes=VMEM_BYTES)


def cross_forward_kernel(q_ref, k_ref, v_ref, o_ref, l_ref):
    rows = q_ref.shape[0]
    lane = lax.broadcasted_iota(jnp.int32, (rows, 128), 1)
    q = q_ref[...]
    mixed = jnp.zeros((rows, CH), f32)
    stat = jnp.zeros((rows, 128), f32)
    for head in range(TH):
        mask = head_mask((rows, CH), head)
        q_head = jnp.where(mask, q.astype(f32) * 0.125, 0.0).astype(bf16)
        scores = dot_nt(q_head, k_ref[...])
        peak = jnp.max(scores, -1, keepdims=True)
        shifted = jnp.exp(scores - peak)
        total = jnp.sum(shifted, -1, keepdims=True)
        part = dot_nn(shifted.astype(bf16), v_ref[...])
        mixed = jnp.where(mask, part / total, mixed)
        stat = jnp.where(lane == head, peak + jnp.log(total), stat)
    o_ref[...] = mixed.astype(bf16)
    l_ref[0] = stat.T[:8]


def cross_forward(query, kv):
    rows = query.shape[0] // 2
    cells = kv.shape[0]
    return pl.pallas_call(
        cross_forward_kernel,
        grid=(2,),
        in_specs=[
            pl.BlockSpec((rows, CH), lambda i: (i, 0)),
            pl.BlockSpec((cells, CH), lambda i: (0, 0)),
            pl.BlockSpec((cells, CH), lambda i: (0, 1)),
        ],
        out_specs=[
            pl.BlockSpec((rows, CH), lambda i: (i, 0)),
            pl.BlockSpec((1, 8, rows), lambda i: (i, 0, 0)),
        ],
        out_shape=[
            jax.ShapeDtypeStruct((2 * rows, CH), bf16),
            jax.ShapeDtypeStruct((2, 8, rows), f32),
        ],
        compiler_params=params(),
        cost_estimate=cost(16 * TH * rows * cells * CH // 2, 8 * cells * CH, 2 * TH * rows * cells),
    )(query, kv, kv)


def delta_rows(d_out, out):
    product = d_out.astype(f32) * out.astype(f32)
    head = lax.broadcasted_iota(jnp.int32, (8, CH), 0)
    lane = lax.broadcasted_iota(jnp.int32, (8, CH), 1)
    pick = ((lane // HD) == head).astype(f32)
    return lax.dot_general(
        pick,
        product,
        (((1,), (1,)), ((), ())),
        precision=lax.Precision.HIGHEST,
        preferred_element_type=f32,
    )


def cross_backward_kernel(
    q_ref, k_ref, v_ref, do_ref, o_ref, l_ref, dq_ref, dkv_ref, q_s, do_s, delta_s, dq_s
):
    step = pl.program_id(0)
    rows = q_ref.shape[0]

    @pl.when(step == 0)
    def _():
        for head in range(TH):
            mask = head_mask((rows, CH), head)
            q_s[head] = jnp.where(mask, q_ref[...].astype(f32) * 0.125, 0.0).astype(bf16)
            do_s[head] = jnp.where(mask, do_ref[...].astype(f32), 0.0).astype(bf16)
        delta_s[...] = delta_rows(do_ref[...], o_ref[...])
        dq_s[...] = jnp.zeros_like(dq_s)

    cells = k_ref.shape[0]
    dk = jnp.zeros((cells, CH), f32)
    dv = jnp.zeros((cells, CH), f32)
    dq = dq_s[...]
    k = k_ref[...]
    for head in range(TH):
        probs = jnp.exp(dot_nt(k, q_s[head]) - l_ref[head : head + 1, :])
        d_probs = dot_nt(v_ref[...], do_s[head])
        d_scores = (probs * (d_probs - delta_s[head : head + 1, :])).astype(bf16)
        dv = dv + dot_nn(probs.astype(bf16), do_s[head])
        dk = dk + dot_nn(d_scores, q_s[head])
        dq = dq + jnp.where(head_mask((rows, CH), head), dot_tn(d_scores, k), 0.0)
    dq_s[...] = dq
    dkv_ref[:, :CH] = dk.astype(bf16)
    dkv_ref[:, CH:] = dv.astype(bf16)

    @pl.when(step == pl.num_programs(0) - 1)
    def _():
        dq_ref[...] = (dq_s[...] * 0.125).astype(bf16)


def cross_backward(query, kv, d_out, out, log_rows):
    rows = query.shape[0]
    cells = kv.shape[0]
    block = 1024
    whole = lambda i: (0, 0)
    return pl.pallas_call(
        cross_backward_kernel,
        grid=(cells // block,),
        in_specs=[
            pl.BlockSpec((rows, CH), whole),
            pl.BlockSpec((block, CH), lambda i: (i, 0)),
            pl.BlockSpec((block, CH), lambda i: (i, 1)),
            pl.BlockSpec((rows, CH), whole),
            pl.BlockSpec((rows, CH), whole),
            pl.BlockSpec((8, rows), whole),
        ],
        out_specs=[
            pl.BlockSpec((rows, CH), whole),
            pl.BlockSpec((block, 2 * CH), lambda i: (i, 0)),
        ],
        out_shape=[
            jax.ShapeDtypeStruct((rows, CH), bf16),
            jax.ShapeDtypeStruct((cells, 2 * CH), bf16),
        ],
        scratch_shapes=[
            pltpu.VMEM((TH, rows, CH), bf16),
            pltpu.VMEM((TH, rows, CH), bf16),
            pltpu.VMEM((8, rows), f32),
            pltpu.VMEM((rows, CH), f32),
        ],
        compiler_params=params(),
        cost_estimate=cost(10 * TH * rows * cells * CH, 8 * cells * CH, TH * rows * cells),
    )(query, kv, kv, d_out, out, log_rows)


def self_forward_kernel(len_ref, q_ref, k_ref, v_ref, o_ref, l_ref):
    group = pl.program_id(0)
    length = len_ref[0]
    for start, count in ROW_BLOCKS:
        stop = start + count
        q = q_ref[0, start:stop, :].astype(f32) * 0.125
        row = lax.broadcasted_iota(jnp.int32, (count, 1), 0) + start
        bound = jnp.minimum(row, length - 1)
        allowed = lax.broadcasted_iota(jnp.int32, (count, stop), 1) <= bound
        mixed = jnp.zeros((count, CH), f32)
        stat = jnp.zeros((count, 128), f32)
        lane = lax.broadcasted_iota(jnp.int32, (count, 128), 1)
        for head in range(GROUP):
            mask = head_mask((count, CH), head)
            q_head = jnp.where(mask, q, 0.0).astype(bf16)
            scores = jnp.where(allowed, dot_nt(q_head, k_ref[0, :stop, :]), neg_large)
            peak = jnp.max(scores, -1, keepdims=True)
            shifted = jnp.exp(scores - peak)
            total = jnp.sum(shifted, -1, keepdims=True)
            part = dot_nn(shifted.astype(bf16), v_ref[0, :stop, :])
            mixed = jnp.where(mask, part / total, mixed)
            stat = jnp.where(lane == head, peak + jnp.log(total), stat)
        o_ref[start:stop, :] = mixed.astype(bf16)
        l_ref[0, :, start:stop] = stat.T[:8]


def self_forward(qkv, length):
    groups = D // CH
    at = lambda j: (lambda i, n: (j, 0, i))
    return pl.pallas_call(
        self_forward_kernel,
        grid_spec=pltpu.PrefetchScalarGridSpec(
            num_scalar_prefetch=1,
            grid=(groups,),
            in_specs=[pl.BlockSpec((1, SEQ, CH), at(j)) for j in range(3)],
            out_specs=[
                pl.BlockSpec((SEQ, CH), lambda i, n: (0, i)),
                pl.BlockSpec((1, 8, SEQ), lambda i, n: (i, 0, 0)),
            ],
        ),
        out_shape=[
            jax.ShapeDtypeStruct((SEQ, D), bf16),
            jax.ShapeDtypeStruct((groups, 8, SEQ), f32),
        ],
        compiler_params=params(),
        cost_estimate=cost(4 * HEADS * SEQ * SEQ * CH, 8 * SEQ * D, HEADS * SEQ * SEQ),
    )(length, qkv, qkv, qkv)


def self_backward_kernel(
    len_ref, q_ref, k_ref, v_ref, do_ref, o_ref, l_ref, out_ref, dk_s, dv_s
):
    length = len_ref[0]
    dk_s[...] = jnp.zeros_like(dk_s)
    dv_s[...] = jnp.zeros_like(dv_s)
    delta = delta_rows(do_ref[...], o_ref[...])
    for start, count in ROW_BLOCKS:
        stop = start + count
        q = q_ref[0, start:stop, :].astype(f32) * 0.125
        d_out = do_ref[start:stop, :].astype(f32)
        row = lax.broadcasted_iota(jnp.int32, (1, count), 1) + start
        bound = jnp.minimum(row, length - 1)
        allowed = lax.broadcasted_iota(jnp.int32, (stop, count), 0) <= bound
        dq = jnp.zeros((count, CH), f32)
        k = k_ref[0, :stop, :]
        v = v_ref[0, :stop, :]
        dk = dk_s[:stop, :]
        dv = dv_s[:stop, :]
        for head in range(GROUP):
            mask = head_mask((count, CH), head)
            q_head = jnp.where(mask, q, 0.0).astype(bf16)
            d_head = jnp.where(mask, d_out, 0.0).astype(bf16)
            scores = dot_nt(k, q_head)
            logs = l_ref[0, head : head + 1, start:stop]
            probs = jnp.where(allowed, jnp.exp(scores - logs), 0.0)
            d_probs = dot_nt(v, d_head)
            d_scores = (probs * (d_probs - delta[head : head + 1, start:stop])).astype(bf16)
            dv = dv + dot_nn(probs.astype(bf16), d_head)
            dk = dk + dot_nn(d_scores, q_head)
            dq = dq + jnp.where(mask, dot_tn(d_scores, k), 0.0)
        dk_s[:stop, :] = dk
        dv_s[:stop, :] = dv
        out_ref[0, start:stop, :] = (dq * 0.125).astype(bf16)
    out_ref[1] = dk_s[...].astype(bf16)
    out_ref[2] = dv_s[...].astype(bf16)


def self_backward(qkv, d_out, out, log_rows, length):
    groups = D // CH
    at = lambda j: (lambda i, n: (j, 0, i))
    here = lambda i, n: (0, i)
    return pl.pallas_call(
        self_backward_kernel,
        grid_spec=pltpu.PrefetchScalarGridSpec(
            num_scalar_prefetch=1,
            grid=(groups,),
            in_specs=[pl.BlockSpec((1, SEQ, CH), at(j)) for j in range(3)]
            + [
                pl.BlockSpec((SEQ, CH), here),
                pl.BlockSpec((SEQ, CH), here),
                pl.BlockSpec((1, 8, SEQ), lambda i, n: (i, 0, 0)),
            ],
            out_specs=pl.BlockSpec((3, SEQ, CH), lambda i, n: (0, 0, i)),
            scratch_shapes=[pltpu.VMEM((SEQ, CH), f32), pltpu.VMEM((SEQ, CH), f32)],
        ),
        out_shape=jax.ShapeDtypeStruct((3, SEQ, D), bf16),
        compiler_params=params(),
        cost_estimate=cost(8 * HEADS * SEQ * SEQ * CH, 16 * SEQ * D, HEADS * SEQ * SEQ),
    )(length, qkv, qkv, qkv, d_out, out, log_rows)


def full(*shape):
    return pl.BlockSpec(shape, lambda i: (0,) * len(shape))


def part_of(first):
    return pl.BlockSpec((3, CH, D), lambda i: (first + i, 0, 0))


def fixed_part(index):
    return pl.BlockSpec((3, CH, D), lambda i: (index, 0, 0))


def square(ref):
    return ref[...].reshape(D, D)


def write_cores(core, matrix, keep_ref, give_ref, span):
    parts = matrix.reshape(-1, 2, span, matrix.shape[-1])
    first, second = parts[:, 0], parts[:, 1]
    keep = jnp.where(core == 0, first, second)
    give = jnp.where(core == 0, second, first)
    keep_ref[...] = keep.reshape(keep_ref.shape).astype(bf16)
    give_ref[...] = give.reshape(give_ref.shape).astype(bf16)


def core_span():
    return CH // (2 * lax.axis_size("z"))


def core_here():
    return lax.axis_index("c").astype(jnp.int32).reshape(1)


CORE_SPEC = pl.BlockSpec(memory_space=pltpu.SMEM)
HALF = D // 2


def row_scale(values):
    return lax.rsqrt(jnp.mean(values * values, -1, keepdims=True) + eps_norm)


def pull_norm(d_normed, values, gain):
    scale = row_scale(values)
    d_gain = jnp.sum(d_normed * values * scale, 0, keepdims=True)
    scaled = d_normed * gain
    inner = jnp.mean(scaled * values, -1, keepdims=True)
    return d_gain, scale * scaled - (scale * scale * scale) * values * inner


def embed_kernel(
    pool_ref, feats_ref, mixed_ref, out_w_ref, emb_ref, w_ref, gain_ref,
    seq_ref, embed_ref, normed_ref, qkv_ref,
):
    @pl.when(pl.program_id(0) == 0)
    def _():
        updated = feats_ref[...].astype(f32) + dot_nn(mixed_ref[...], out_w_ref[...])
        seq_ref[:CTX, :] = pool_ref[...]
        seq_ref[CTX:, :] = updated.astype(bf16)
        embed = dot_nn(seq_ref[...], emb_ref[0])
        embed_ref[...] = embed
        normed_ref[...] = (embed * row_scale(embed) * gain_ref[...]).astype(bf16)

    qkv_ref[0] = dot_nn(normed_ref[...], square(w_ref)).astype(bf16)


def embed_forward(pooled, feats, mixed, to_out, weights, gain):
    last = weights.shape[0] - 1
    return pl.pallas_call(
        embed_kernel,
        grid=(3,),
        in_specs=[
            full(CTX, CH),
            full(SEQ - CTX, CH),
            full(SEQ - CTX, CH),
            full(CH, CH),
            pl.BlockSpec((1, CH, D), lambda i: (last, 0, 0)),
            part_of(0),
            full(1, D),
        ],
        out_specs=[
            full(SEQ, CH),
            full(SEQ, D),
            full(SEQ, D),
            pl.BlockSpec((1, SEQ, D), lambda i: (i, 0, 0)),
        ],
        out_shape=[
            jax.ShapeDtypeStruct((SEQ, CH), bf16),
            jax.ShapeDtypeStruct((SEQ, D), f32),
            jax.ShapeDtypeStruct((SEQ, D), bf16),
            jax.ShapeDtypeStruct((3, SEQ, D), bf16),
        ],
        compiler_params=params(),
        cost_estimate=cost(2 * SEQ * D * (CH + 3 * D), 12 * SEQ * D),
    )(pooled, feats, mixed, to_out, weights, weights, gain)


def up_kernel(
    mixed_ref, embed_ref, att_ref, w_ref, gain_ref,
    stream_ref, normed_ref, act_ref, slope_ref, pre_s,
):
    @pl.when(pl.program_id(0) == 0)
    def _():
        stream = embed_ref[...] + dot_nn(mixed_ref[...], square(att_ref))
        stream_ref[...] = stream
        normed_ref[...] = (stream * row_scale(stream) * gain_ref[...]).astype(bf16)

    pre_s[...] = dot_nn(normed_ref[...], square(w_ref))
    factor = (2.0 / 3.141592653589793) ** 0.5
    cubic = 0.044715 * factor

    def rows_step(index, carry):
        here = pl.ds(pl.multiple_of(index * 16, 16), 16)
        v = pre_s[here, :]
        v2 = v * v
        half = 0.5 + 0.5 * jnp.tanh(v * (factor + cubic * v2))
        act_ref[0, here, :] = (v * half).astype(bf16)
        bend = 2.0 * half * (1.0 - half) * (factor + 3.0 * cubic * v2)
        slope_ref[0, here, :] = (half + v * bend).astype(bf16)
        return carry

    lax.fori_loop(0, SEQ // 16, rows_step, 0, unroll=2)


def up_forward(mixed, embed, weights, gain):
    return pl.pallas_call(
        up_kernel,
        grid=(4,),
        in_specs=[full(SEQ, D), full(SEQ, D), fixed_part(3), part_of(4), full(1, D)],
        out_specs=[
            full(SEQ, D),
            full(SEQ, D),
            pl.BlockSpec((1, SEQ, D), lambda i: (i, 0, 0)),
            pl.BlockSpec((1, SEQ, D), lambda i: (i, 0, 0)),
        ],
        out_shape=[
            jax.ShapeDtypeStruct((SEQ, D), f32),
            jax.ShapeDtypeStruct((SEQ, D), bf16),
            jax.ShapeDtypeStruct((4, SEQ, D), bf16),
            jax.ShapeDtypeStruct((4, SEQ, D), bf16),
        ],
        scratch_shapes=[pltpu.VMEM((SEQ, D), f32)],
        compiler_params=params(),
        cost_estimate=cost(10 * SEQ * D * D, 28 * SEQ * D, 4 * SEQ * D),
    )(mixed, embed, weights, weights, gain)


def down_kernel(act_ref, w_ref, stream_ref, out_ref):
    part = dot_nn(act_ref[0], square(w_ref))

    @pl.when(pl.program_id(0) == 0)
    def _():
        out_ref[...] = stream_ref[...] + part

    @pl.when(pl.program_id(0) > 0)
    def _():
        out_ref[...] += part


def down_forward(act, w_down, stream):
    return pl.pallas_call(
        down_kernel,
        grid=(4,),
        in_specs=[
            pl.BlockSpec((1, SEQ, D), lambda i: (i, 0, 0)),
            part_of(0),
            full(SEQ, D),
        ],
        out_specs=full(SEQ, D),
        out_shape=jax.ShapeDtypeStruct((SEQ, D), f32),
        compiler_params=params(),
        cost_estimate=cost(8 * SEQ * D * D, 24 * SEQ * D),
    )(act, w_down, stream)


def down_grad_kernel(core_ref, act_ref, gd_ref, keep_ref, give_ref, *, span):
    total = dot_tn(act_ref[0], gd_ref[...])
    write_cores(core_ref[0], total, keep_ref, give_ref, span)


def down_grad(act, gd):
    half = pl.BlockSpec((HALF, D), lambda i: (i, 0))
    return pl.pallas_call(
        functools.partial(down_grad_kernel, span=core_span()),
        grid=(4,),
        in_specs=[CORE_SPEC, pl.BlockSpec((1, SEQ, D), lambda i: (i, 0, 0)), full(SEQ, D)],
        out_specs=[half, half],
        out_shape=[jax.ShapeDtypeStruct((4 * HALF, D), bf16)] * 2,
        compiler_params=params(),
        cost_estimate=cost(8 * SEQ * D * D, 18 * SEQ * D),
    )(core_here(), act, gd)


def up_grad_kernel(
    core_ref, gd_ref, w_ref, slope_ref, normed_ref, gpre_ref, keep_ref, give_ref, turned_s, *, span
):
    @pl.when(pl.program_id(0) == 0)
    def _():
        turned_s[...] = normed_ref[...].T

    gpre = (dot_nt(gd_ref[...], square(w_ref)) * slope_ref[0].astype(f32)).astype(bf16)
    gpre_ref[0] = gpre
    write_cores(core_ref[0], dot_nn(turned_s[...], gpre), keep_ref, give_ref, span)


def up_grad(gd, w_down, slope, normed):
    part = pl.BlockSpec((1, SEQ, D), lambda i: (i, 0, 0))
    half = pl.BlockSpec((HALF, D), lambda i: (i, 0))
    return pl.pallas_call(
        functools.partial(up_grad_kernel, span=core_span()),
        grid=(4,),
        in_specs=[CORE_SPEC, full(SEQ, D), part_of(0), part, full(SEQ, D)],
        out_specs=[part, half, half],
        out_shape=[jax.ShapeDtypeStruct((4, SEQ, D), bf16)]
        + [jax.ShapeDtypeStruct((4 * HALF, D), bf16)] * 2,
        scratch_shapes=[pltpu.VMEM((D, SEQ), bf16)],
        compiler_params=params(),
        cost_estimate=cost(16 * SEQ * D * D, 36 * SEQ * D),
    )(core_here(), gd, w_down, slope, normed)


def att_grad_kernel(
    core_ref, gpre_ref, w_ref, att_ref, stream_ref, gd_ref, mixed_ref, gain_ref,
    d_stream_ref, gog_ref, keep_ref, give_ref, gain_g_ref, total_s, *, span
):
    step = pl.program_id(0)
    part = dot_nt(gpre_ref[0], square(w_ref))

    @pl.when(step == 0)
    def _():
        total_s[...] = part

    @pl.when(step > 0)
    def _():
        total_s[...] += part

    @pl.when(step == pl.num_programs(0) - 1)
    def _():
        d_gain, pulled = pull_norm(total_s[...], stream_ref[...], gain_ref[...])
        gain_g_ref[...] = d_gain
        d_stream = gd_ref[...].astype(f32) + pulled
        d_stream_ref[...] = d_stream
        ga = d_stream.astype(bf16)
        gog_ref[...] = dot_nt(ga, square(att_ref)).astype(bf16)
        write_cores(core_ref[0], dot_tn(mixed_ref[...], ga), keep_ref, give_ref, span)


def att_grad(gpre, weights, stream, gd, mixed, gain):
    return pl.pallas_call(
        functools.partial(att_grad_kernel, span=core_span()),
        grid=(4,),
        in_specs=[
            CORE_SPEC,
            pl.BlockSpec((1, SEQ, D), lambda i: (i, 0, 0)),
            part_of(4),
            fixed_part(3),
            full(SEQ, D),
            full(SEQ, D),
            full(SEQ, D),
            full(1, D),
        ],
        out_specs=[full(SEQ, D), full(SEQ, D), full(HALF, D), full(HALF, D), full(1, D)],
        out_shape=[
            jax.ShapeDtypeStruct((SEQ, D), f32),
            jax.ShapeDtypeStruct((SEQ, D), bf16),
            jax.ShapeDtypeStruct((HALF, D), bf16),
            jax.ShapeDtypeStruct((HALF, D), bf16),
            jax.ShapeDtypeStruct((1, D), f32),
        ],
        scratch_shapes=[pltpu.VMEM((SEQ, D), f32)],
        compiler_params=params(),
        cost_estimate=cost(12 * SEQ * D * D, 32 * SEQ * D),
    )(core_here(), gpre, weights, weights, stream, gd, mixed, gain)


def qkv_grad_kernel(core_ref, normed_ref, g_ref, keep_ref, give_ref, turned_s, *, span):
    @pl.when(pl.program_id(0) == 0)
    def _():
        turned_s[...] = normed_ref[...].T

    write_cores(core_ref[0], dot_nn(turned_s[...], g_ref[0]), keep_ref, give_ref, span)


def qkv_grad(normed, gqkv):
    half = pl.BlockSpec((HALF, D), lambda i: (i, 0))
    return pl.pallas_call(
        functools.partial(qkv_grad_kernel, span=core_span()),
        grid=(3,),
        in_specs=[CORE_SPEC, full(SEQ, D), pl.BlockSpec((1, SEQ, D), lambda i: (i, 0, 0))],
        out_specs=[half, half],
        out_shape=[jax.ShapeDtypeStruct((3 * HALF, D), bf16)] * 2,
        scratch_shapes=[pltpu.VMEM((D, SEQ), bf16)],
        compiler_params=params(),
        cost_estimate=cost(6 * SEQ * D * D, 14 * SEQ * D),
    )(core_here(), normed, gqkv)


def embed_grad_kernel(
    g_ref, w_ref, emb_ref, embed_ref, d_stream_ref, seq_ref, mixed_ref, out_w_ref, gain_ref,
    emb_g_ref, gupd_ref, pool_g_ref, out_g_ref, gox_ref, gain_g_ref, total_s,
):
    step = pl.program_id(0)
    part = dot_nt(g_ref[0], square(w_ref))

    @pl.when(step == 0)
    def _():
        total_s[...] = part

    @pl.when(step > 0)
    def _():
        total_s[...] += part

    @pl.when(step == pl.num_programs(0) - 1)
    def _():
        d_gain, pulled = pull_norm(total_s[...], embed_ref[...], gain_ref[...])
        gain_g_ref[...] = d_gain
        gembed = (d_stream_ref[...] + pulled).astype(bf16)
        emb_g_ref[...] = dot_tn(seq_ref[...], gembed).astype(bf16)
        gseq = dot_nt(gembed, emb_ref[0])
        gupd = gseq[CTX:]
        gb = gupd.astype(bf16)
        pool_g_ref[...] = gseq[:CTX].astype(bf16)
        gupd_ref[...] = gupd
        out_g_ref[...] = dot_tn(mixed_ref[...], gb).astype(bf16)
        gox_ref[...] = dot_nt(gb, out_w_ref[...]).astype(bf16)


def embed_grad(gqkv, weights, embed, d_stream, seq, mixed, to_out, gain):
    last = weights.shape[0] - 1
    return pl.pallas_call(
        embed_grad_kernel,
        grid=(3,),
        in_specs=[
            pl.BlockSpec((1, SEQ, D), lambda i: (i, 0, 0)),
            part_of(0),
            pl.BlockSpec((1, CH, D), lambda i: (last, 0, 0)),
            full(SEQ, D),
            full(SEQ, D),
            full(SEQ, CH),
            full(SEQ - CTX, CH),
            full(CH, CH),
            full(1, D),
        ],
        out_specs=[
            full(CH, D),
            full(SEQ - CTX, CH),
            full(CTX, CH),
            full(CH, CH),
            full(SEQ - CTX, CH),
            full(1, D),
        ],
        out_shape=[
            jax.ShapeDtypeStruct((CH, D), bf16),
            jax.ShapeDtypeStruct((SEQ - CTX, CH), f32),
            jax.ShapeDtypeStruct((CTX, CH), bf16),
            jax.ShapeDtypeStruct((CH, CH), bf16),
            jax.ShapeDtypeStruct((SEQ - CTX, CH), bf16),
            jax.ShapeDtypeStruct((1, D), f32),
        ],
        scratch_shapes=[pltpu.VMEM((SEQ, D), f32)],
        compiler_params=params(),
        cost_estimate=cost(2 * SEQ * D * (3 * D + 2 * CH), 24 * SEQ * D),
    )(gqkv, weights, weights, embed, d_stream, seq, mixed, to_out, gain)


def patch_pick(rows, columns, patch_dim):
    patch = lax.broadcasted_iota(jnp.int32, (rows, columns), patch_dim)
    cell = lax.broadcasted_iota(jnp.int32, (rows, columns), 1 - patch_dim)
    inside = (cell // (PATCH * IMG)) * (IMG // PATCH) + (cell % IMG) // PATCH
    return jnp.where(patch == inside, 1.0 / (PATCH * PATCH), 0.0).astype(bf16)


def image_rows(step, row):
    return pl.ds(pl.multiple_of(step * BLOCK + row * IMG, IMG), BLOCK)


def token_forward_kernel(x_ref, conv_ref, kv_w_ref, slope_ref, hidden_ref, kv_ref, pool_ref):
    step = pl.program_id(0)
    z = jnp.zeros((BLOCK, CH), f32)
    for row in range(3):
        z = z + dot_nn(x_ref[image_rows(step, row), :], conv_ref[row])
    center = x_ref[image_rows(step, 1), CH : 2 * CH].astype(f32)
    gate = 1.0 / (1.0 + jnp.exp(-z))
    hidden = center + z * gate
    slope_ref[...] = (gate * (1.0 + z * (1.0 - gate))).astype(bf16)
    hidden_b = hidden.astype(bf16)
    hidden_ref[...] = hidden_b
    kv_ref[...] = dot_nn(hidden_b, kv_w_ref[...]).astype(bf16)
    rest = (hidden - hidden_b.astype(f32)).astype(bf16)
    pick = patch_pick(pool_ref.shape[0], BLOCK, 0)
    pool_ref[...] = (dot_nn(pick, hidden_b) + dot_nn(pick, rest)).astype(bf16)


def token_forward(wide, conv_rows, kv_weight):
    steps = CELLS // BLOCK
    whole = lambda i: (0, 0)
    block = lambda i: (i, 0)
    return pl.pallas_call(
        token_forward_kernel,
        grid=(steps,),
        in_specs=[
            pl.BlockSpec(wide.shape, whole),
            pl.BlockSpec((3, 3 * CH, CH), lambda i: (0, 0, 0)),
            pl.BlockSpec((CH, 2 * CH), whole),
        ],
        out_specs=[
            pl.BlockSpec((BLOCK, CH), block),
            pl.BlockSpec((BLOCK, CH), block),
            pl.BlockSpec((BLOCK, 2 * CH), block),
            pl.BlockSpec((CTX // steps, CH), block),
        ],
        out_shape=[
            jax.ShapeDtypeStruct((CELLS, CH), bf16),
            jax.ShapeDtypeStruct((CELLS, CH), bf16),
            jax.ShapeDtypeStruct((CELLS, 2 * CH), bf16),
            jax.ShapeDtypeStruct((CTX, CH), bf16),
        ],
        compiler_params=params(),
        cost_estimate=cost(22 * CELLS * CH * CH, 14 * CELLS * CH, CELLS * CH),
    )(wide, conv_rows, kv_weight)


def token_backward_kernel(
    core_ref, dkv_ref, slope_ref, pool_ref, hidden_ref, x_ref, kv_w_ref,
    d_hidden_ref, gz_ref, keep_ref, give_ref, conv_s, kv_s, *, span
):
    step = pl.program_id(0)

    @pl.when(step == 0)
    def _():
        conv_s[...] = jnp.zeros_like(conv_s)
        kv_s[...] = jnp.zeros_like(kv_s)

    dkv = dkv_ref[...]
    d_hidden = dot_nt(dkv, kv_w_ref[...])
    d_hidden = d_hidden + dot_nn(patch_pick(BLOCK, pool_ref.shape[0], 1), pool_ref[...])
    gz = (d_hidden * slope_ref[...].astype(f32)).astype(bf16)
    d_hidden_ref[...] = d_hidden
    gz_ref[...] = gz
    kv_s[...] += dot_tn(hidden_ref[...], dkv)
    gz_t = gz.T
    for row in range(3):
        conv_s[row] += dot_nn(gz_t, x_ref[image_rows(step, row), :])

    @pl.when(step == pl.num_programs(0) - 1)
    def _():
        tiles = []
        for row in range(3):
            for col in range(3):
                tiles.append(conv_s[row, :, col * CH : (col + 1) * CH].T)
        tiles = tiles + [kv_s[:, :CH], kv_s[:, CH:]]
        for at, tile in enumerate(tiles):
            write_cores(core_ref[0], tile, keep_ref.at[at], give_ref.at[at], span)


def token_backward(dkv, slope, d_pool, hidden_b, wide, kv_weight):
    steps = CELLS // BLOCK
    whole = lambda i: (0, 0)
    whole_3 = lambda i: (0, 0, 0)
    block = lambda i: (i, 0)
    return pl.pallas_call(
        functools.partial(token_backward_kernel, span=core_span()),
        grid=(steps,),
        in_specs=[
            CORE_SPEC,
            pl.BlockSpec((BLOCK, 2 * CH), block),
            pl.BlockSpec((BLOCK, CH), block),
            pl.BlockSpec((CTX // steps, CH), block),
            pl.BlockSpec((BLOCK, CH), block),
            pl.BlockSpec(wide.shape, whole),
            pl.BlockSpec((CH, 2 * CH), whole),
        ],
        out_specs=[
            pl.BlockSpec((BLOCK, CH), block),
            pl.BlockSpec((BLOCK, CH), block),
            pl.BlockSpec((11, CH // 2, CH), whole_3),
            pl.BlockSpec((11, CH // 2, CH), whole_3),
        ],
        out_shape=[
            jax.ShapeDtypeStruct((CELLS, CH), f32),
            jax.ShapeDtypeStruct((CELLS, CH), bf16),
            jax.ShapeDtypeStruct((11, CH // 2, CH), bf16),
            jax.ShapeDtypeStruct((11, CH // 2, CH), bf16),
        ],
        scratch_shapes=[pltpu.VMEM((3, CH, 3 * CH), f32), pltpu.VMEM((CH, 2 * CH), f32)],
        compiler_params=params(),
        cost_estimate=cost(26 * CELLS * CH * CH, 20 * CELLS * CH),
    )(core_here(), dkv, slope, d_pool, hidden_b, wide, kv_weight)


def context_backward_kernel(gz_ref, d_hidden_ref, conv_ref, out_ref, wide_s):
    step = pl.program_id(0)
    steps = pl.num_programs(0)

    def widen(at):
        values = gz_ref[image_rows(at, 0), :].astype(f32)
        col = lax.broadcasted_iota(jnp.int32, (BLOCK, CH), 0) % IMG
        left = jnp.where(col == 0, 0.0, pltpu.roll(values, 1, 0))
        right = jnp.where(col == IMG - 1, 0.0, pltpu.roll(values, BLOCK - 1, 0))
        wide_s[image_rows(at, 1), 0:CH] = left.astype(bf16)
        wide_s[image_rows(at, 1), CH : 2 * CH] = values.astype(bf16)
        wide_s[image_rows(at, 1), 2 * CH :] = right.astype(bf16)

    @pl.when(step == 0)
    def _():
        wide_s[0:IMG, :] = jnp.zeros((IMG, 3 * CH), bf16)
        wide_s[CELLS + IMG :, :] = jnp.zeros((IMG, 3 * CH), bf16)
        widen(0)

    @pl.when(step < steps - 1)
    def _():
        widen(step + 1)

    total = d_hidden_ref[...]
    for row in range(3):
        values = wide_s[image_rows(step, row), :]
        for col in range(3):
            tap = conv_ref[3 * (2 - row) + (2 - col)]
            total = total + dot_nt(values[:, col * CH : (col + 1) * CH], tap)
    out_ref[...] = total.astype(bf16)


def context_backward(gz, d_hidden, conv_tiles):
    block = lambda i: (i, 0)
    return pl.pallas_call(
        context_backward_kernel,
        grid=(CELLS // BLOCK,),
        in_specs=[
            pl.BlockSpec((CELLS, CH), lambda i: (0, 0)),
            pl.BlockSpec((BLOCK, CH), block),
            pl.BlockSpec((9, CH, CH), lambda i: (0, 0, 0)),
        ],
        out_specs=pl.BlockSpec((BLOCK, CH), block),
        out_shape=jax.ShapeDtypeStruct((CELLS, CH), bf16),
        scratch_shapes=[pltpu.VMEM((CELLS + 2 * IMG, 3 * CH), bf16)],
        compiler_params=params(),
        cost_estimate=cost(18 * CELLS * CH * CH, 8 * CELLS * CH),
    )(gz, d_hidden, conv_tiles)


def local(
    context_map,
    future_feats,
    horizon,
    cotangent,
    tile_owner,
    master_tiles,
    moment_first,
    moment_second,
    norm_gains,
    gain_first,
    gain_second,
):
    slot_count = master_tiles.shape[0]
    devices = lax.axis_size(AXES)
    rows = CH // devices
    slot_of = slot_index(tile_owner, slot_count)

    pieces = trade_rows(context_map)
    length = CTX + FT * horizon
    valid = jnp.arange(SEQ) < length[0]
    gd = jnp.where(valid[:, None], cotangent[0], jnp.zeros((), bf16))

    slices = (
        master_tiles.astype(bf16)
        .reshape(slot_count, devices, rows, CH)
        .transpose(1, 0, 2, 3)
    )
    slices = lax.all_to_all(slices, AXES, split_axis=0, concat_axis=0, tiled=True)
    slices, pieces, gd = tie((slices, pieces, gd))
    image = row_order(pieces).reshape(IMG, IMG, CH)
    slices = slices.reshape(devices * slot_count, rows, CH)
    slices = slices.at[slot_of].get(mode="promise_in_bounds")
    early, emb, qkv, att, up, down = jnp.split(slices, (13, 16, 43, 52, 88))
    weights = jnp.concatenate(
        [
            from_tiles(qkv, 3, 3),
            from_tiles(att, 3, 1),
            from_tiles(up, 3, 4),
            from_tiles(emb, 1, 1),
        ],
        0,
    )
    weights = lax.all_gather(weights, AXES, axis=1, tiled=True)
    w_down = lax.all_gather(from_tiles(down, 12, 1), AXES, axis=1, tiled=True)
    early = gather_all(early).transpose(1, 0, 2, 3).reshape(EARLY, CH, CH)

    padded = jnp.pad(image, ((1, 1), (1, 1), (0, 0)))
    wide = jnp.concatenate([padded[:, col : col + IMG] for col in range(3)], -1)
    wide = wide.reshape((IMG + 2) * IMG, 3 * CH)

    conv_tiles = early[:9]
    to_query, to_out = early[9], early[12]
    kv_weight = jnp.concatenate([early[10], early[11]], 1)

    slope_z, hidden_b, kv, pooled = token_forward(
        wide, conv_tiles.reshape(3, 3 * CH, CH), kv_weight
    )
    feats_b = future_feats[0]
    query = jnp.dot(feats_b, to_query, preferred_element_type=f32).astype(bf16)
    cross_mixed, cross_logs = cross_forward(query, kv)

    gain_one, gain_two = norm_gains[:1], norm_gains[1:]
    seq, embed, normed_one, qkv = embed_forward(
        pooled, feats_b, cross_mixed, to_out, weights, gain_one
    )
    mixed, logs = self_forward(qkv, length)
    stream, normed_two, act, slope = up_forward(mixed, embed, weights, gain_two)

    down = core_parts(down_grad(act, gd))
    gd, down = tie((gd, down))
    down = send(down, "c")
    gpre, up_keep, up_give = up_grad(gd, w_down, slope, normed_two)
    gpre, up, down = hold((gpre, core_parts([up_keep, up_give])), down)
    down = advance(down, "x", 3)
    gpre, up, down = tie((gpre, up, down))
    up, down = send(up, "c"), send(down, "x")
    d_stream, gog, att_keep, att_give, gain_g_two = att_grad(
        gpre, weights, stream, gd, mixed, gain_two
    )
    gog, att, up = hold((gog, core_parts([att_keep, att_give])), up)
    up = advance(up, "y", 2)
    gog, att, up = tie((gog, att, up))
    up, att = send(up, "y"), send(att, "c")
    gqkv = self_backward(qkv, gog, mixed, logs, length)
    gqkv, down, att = hold((gqkv,), down, att)
    down = advance(down, "y", 2)
    gqkv, down = tie((gqkv, down))
    down = send(down, "y")
    qkv_keep, qkv_give = qkv_grad(normed_one, gqkv)
    gqkv, qkv, up = hold((gqkv, core_parts([qkv_keep, qkv_give])), up)
    up = advance(up, "x", 2)
    gqkv, qkv, up = tie((gqkv, qkv, up))
    qkv, up = send(qkv, "c"), send(up, "x")
    emb_g, gupd, pool_g, out_g, gox, gain_g_one = embed_grad(
        gqkv, weights, embed, d_stream, seq, cross_mixed, to_out, gain_one
    )
    gains = jnp.concatenate([gain_g_one, gain_g_two], 0).reshape(devices, 1, -1)
    gain_count = gains.shape[-1]
    gains = jnp.pad(gains, ((0, 0), (0, rows - 1), (0, D - gain_count))).astype(bf16)
    emb = cut_core(jnp.concatenate([emb_g, gains.reshape(CH, D)], 0))
    gox, gupd, emb, qkv, up, down = hold((gox, gupd, emb), qkv, up, down)
    mlp = advance_near([jnp.concatenate(part, 0) for part in zip(up, down)])
    first = advance([part[:6] for part in qkv], "x", 3)
    second = advance([jnp.concatenate([p[6:], q], 0) for p, q in zip(qkv, att)], "y", 2)
    gox, mlp, first, second, emb = tie((gox, mlp, first, second, emb))
    mlp, emb = send(mlp, "z"), send(emb, "c")
    first, second = send(first, "x"), send(second, "y")

    log_rows = jnp.concatenate([cross_logs[0], cross_logs[1]], 1)
    gq, gkv = cross_backward(query, kv, gox, cross_mixed, log_rows)
    gq, gkv, mlp, first, second, emb = hold((gq, gkv), mlp, first, second, emb)
    mlp, emb = advance_far(mlp), advance(emb, "x", 3)
    first, second = advance(first, "y", 2), advance(second, "x", 2)
    query_g = cut_core(jnp.dot(feats_b.T, gq, preferred_element_type=f32))
    out_g = cut_core(out_g)
    gkv, mlp, first, second, emb, query_g, out_g = tie(
        (gkv, mlp, first, second, emb, query_g, out_g)
    )
    mlp, emb = send(mlp, "z", 2), send(emb, "x")
    first, second = send(first, "y"), send(second, "x")

    d_hidden, gz, token_keep, token_give = token_backward(
        gkv, slope_z, pool_g, hidden_b, wide, kv_weight
    )
    early = [
        jnp.concatenate([token[:9], q.reshape(1, CH // 2, CH), token[9:], o.reshape(1, CH // 2, CH)], 0)
        for token, q, o in zip((token_keep, token_give), query_g, out_g)
    ]
    d_hidden, early, mlp, first, second, emb = hold(
        (d_hidden, core_parts(early)), mlp, first, second, emb
    )
    att = advance_near([jnp.concatenate(part, 0) for part in zip(first, second)])
    emb = advance(emb, "y", 2)
    early, att, emb = tie((early, att, emb))
    early = send(early, "c")
    att, emb = send(att, "z"), send(emb, "y")
    sum_mlp = add_up(mlp, keep_wide=True)
    future_grad = gupd + lax.dot_general(
        gq, to_query, (((1,), (1,)), ((), ())), preferred_element_type=f32
    )
    future_grad, gz, early = hold((future_grad, gz), early)
    shape = early[0].shape
    early = advance([p.reshape(shape[:2] + (-1,) + shape[4:]) for p in early], ("y", "x"), 2)
    gz, early = tie((gz, early))
    early = send(early, ("y", "x"))
    context_grad = context_backward(gz, d_hidden, conv_tiles)
    context_grad, early, att, emb = hold((context_grad,), early, att, emb)
    att = advance_far(att)
    early = advance(early, "z", 1)
    emb = advance(emb, "z", 1)
    early = [jnp.concatenate([e, to_tiles(m)], 0) for e, m in zip(early, emb)]
    context_grad, early, att = tie((context_grad, early, att))
    early, att = send(early, "z"), send(att, "z", 2)
    pieces = trade_rows(context_grad.reshape(context_map.shape))
    sum_early = add_up(early, keep_wide=True)
    sum_att = add_up(att, keep_wide=True)

    sums = jnp.concatenate(
        [
            sum_early[: EARLY + 3],
            to_tiles(sum_att[:9], 3),
            to_tiles(sum_att[9:]),
            to_tiles(sum_mlp[:12], 4),
            to_tiles(sum_mlp[12:]),
        ],
        0,
    )
    gains = sum_early[EARLY + 3, 0, :gain_count]
    share = jnp.concatenate([(jnp.sum(sums * sums) + jnp.sum(gains * gains))[None], gains])
    share_high = share.astype(bf16)
    share_low = (share - share_high.astype(f32)).astype(bf16)
    share = jnp.pad(
        jnp.stack([share_high, share_low]), ((0, rows - 2), (0, CH - 1 - gain_count))
    )
    slots = jnp.arange(devices * slot_count)
    found = slot_of[None, :] == slots[:, None]
    tile_of = jnp.sum(jnp.where(found, jnp.arange(found.shape[1])[None], 0), 1)
    mine = sums.astype(bf16).at[tile_of].get(mode="promise_in_bounds")
    mine = mine.reshape(devices, slot_count, rows, CH)
    share = jnp.broadcast_to(share[None, None], (devices, 1, rows, CH))
    mine = jnp.concatenate([mine, share], 1)
    mine = lax.all_to_all(mine, AXES, split_axis=0, concat_axis=0, tiled=True)
    block_out = down_forward(act, w_down, stream)
    shares = mine[:, slot_count, :2].astype(f32)
    shares = shares[:, 0] + shares[:, 1]
    gains = shares[:, 1 : 1 + gain_count].reshape(2, D)
    mine = mine[:, :slot_count].transpose(1, 0, 2, 3).reshape(slot_count, CH, CH).astype(f32)

    used = jnp.any(found, 1).astype(f32).reshape(devices, slot_count)
    used = lax.dynamic_index_in_dim(used, lax.axis_index(AXES), 0, keepdims=False)[:, None, None]
    grad_norm = jnp.sqrt(jnp.sum(shares[:, 0]))
    factor = jnp.minimum(1.0, clip_level / (grad_norm + 1e-06))
    new_first, new_second, new_master = adam_step(
        master_tiles, mine * factor, moment_first, moment_second, learn_rate, decay_rate
    )
    new_gain_first, new_gain_second, new_gains = adam_step(
        norm_gains, gains * factor, gain_first, gain_second, gain_rate, 0.0
    )
    return (
        block_out[None],
        row_order(pieces).reshape(context_map.shape).astype(f32),
        future_grad[None],
        jnp.where(used > 0, new_first, 0.0),
        jnp.where(used > 0, new_second, 0.0),
        jnp.where(used > 0, new_master, 0.0),
        new_gain_first,
        new_gain_second,
        new_gains,
        grad_norm,
    )


def solution(mesh):
    groups, rows = mesh.devices.shape
    fine = jax.sharding.Mesh(mesh.devices.reshape(groups // 2, 2, rows // 2, 2), AXES)
    whole = P(AXES, None, None)
    image = P(("z", "c"), ("y", "x"), None, None)
    in_specs = (image, whole, P(AXES), whole, P(), whole, whole, whole, P(), P(), P())
    out_specs = (whole, image, whole, whole, whole, whole, P(), P(), P(), P())
    return jax.shard_map(local, mesh=fine, in_specs=in_specs, out_specs=out_specs, check_vma=False)
```

```python
import functools

import jax
import jax.numpy as jnp
from jax import lax
from jax.experimental import pallas as pl
from jax.experimental.pallas import tpu as pltpu
from jax.sharding import PartitionSpec as P

CH = 256
HD = 64
HEADS = 12
D = 768
FF = 3072
TH = 4
IMG = 64
PATCH = 4
FT = 16
CTX = 256
SEQ = 736
STEP = 10


eps_norm = 1e-05
beta_one = 0.9
beta_two = 0.999
learn_rate = 0.02
gain_rate = 0.6
decay_rate = 0.1
adam_eps = 1e-08
clip_level = 1.0
neg_large = -1e30
AXES = ("z", "c", "y", "x")
CELLS = IMG * IMG
BLOCK = 512
GROUP = 4
EARLY = 13
VMEM_BYTES = 56 * 1024 * 1024
ROW_BLOCKS = ((0, 256), (256, 256), (512, 224))
bf16 = jnp.bfloat16
f32 = jnp.float32


def slot_index(tile_owner, slot_count):
    ordinal = jnp.arange(tile_owner.shape[0])
    earlier = (tile_owner[None, :] == tile_owner[:, None]) & (ordinal[None, :] < ordinal[:, None])
    return tile_owner * slot_count + jnp.sum(earlier.astype(jnp.int32), 1)


def adam_step(weight, grad_now, first, second, rate, decay):
    first_new = beta_one * first + (1.0 - beta_one) * grad_now
    second_new = beta_two * second + (1.0 - beta_two) * grad_now * grad_now
    corr_first = first_new / (1.0 - beta_one**STEP)
    corr_second = second_new / (1.0 - beta_two**STEP)
    weight_new = weight - rate * (corr_first / (jnp.sqrt(corr_second) + adam_eps) + decay * weight)
    return (first_new, second_new, weight_new)


def xor_permute(values, axes, mask):
    count = lax.axis_size(axes)
    return lax.ppermute(values, axes, [(i, i ^ mask) for i in range(count)])


def advance(parts, axes, dim):
    mine = lax.axis_index(axes)
    cuts = []
    for mask in range(lax.axis_size(axes)):
        cuts.append(add_up([lax.dynamic_index_in_dim(p, mine ^ mask, dim, False) for p in parts]))
    return cuts


def advance_near(parts):
    mine = lax.axis_index("z") % 2
    shape = parts[0].shape
    parts = [p.reshape((shape[0], shape[1] // 2, 2) + shape[2:]) for p in parts]
    return [
        add_up([lax.dynamic_index_in_dim(p, mine ^ mask, 2, False) for p in parts])
        for mask in range(2)
    ]


def advance_far(parts):
    mine = lax.axis_index("z") // 2
    return [
        add_up([lax.dynamic_index_in_dim(p, mine ^ mask, 1, False) for p in parts])
        for mask in range(parts[0].shape[1])
    ]


def send(cuts, axes, unit=1):
    return [cuts[0]] + [
        xor_permute(cut, axes, unit * mask) for mask, cut in enumerate(cuts) if mask > 0
    ]


def add_up(parts, keep_wide=False):
    total = parts[0].astype(f32)
    for part in parts[1:]:
        total = total + part.astype(f32)
    return total if keep_wide else total.astype(parts[0].dtype)


def hold(values, *sums):
    tied = lax.optimization_barrier((tuple(values), tuple(tuple(parts) for parts in sums)))
    return tied[0] + tuple(list(parts) for parts in tied[1])


def gather_axes(values, axes):
    pieces = [values]
    for mask in range(1, lax.axis_size(axes)):
        pieces.append(xor_permute(values, axes, mask))
    return jnp.stack(pieces)


def gather_all(values):
    shape = values.shape
    values = gather_axes(values, "z")
    values = gather_axes(values, ("y", "x"))
    values = gather_axes(values, "c")
    cores, rows, depth = values.shape[:3]
    order = jnp.arange(depth * cores * rows)
    z, c, row = order // (cores * rows), (order // rows) % cores, order % rows
    own = lax.axis_index("z"), lax.axis_index("c"), lax.axis_index(("y", "x"))
    at = ((c ^ own[1]) * rows + (row ^ own[2])) * depth + (z ^ own[0])
    return values.reshape((-1,) + shape).at[at].get(mode="promise_in_bounds")


def trade_rows(values):
    mine = lax.axis_index(("y", "x"))
    count = lax.axis_size(("y", "x"))
    cuts = [lax.dynamic_index_in_dim(values, mine ^ mask, 0, False) for mask in range(count)]
    return send(cuts, ("y", "x"))


def row_order(pieces):
    order = jnp.arange(len(pieces)) ^ lax.axis_index(("y", "x"))
    return jnp.stack(pieces).at[order].get(mode="promise_in_bounds")


def slice_shape():
    z, c, y, x = [lax.axis_size(axis) for axis in AXES]
    return (z, y, x, CH // (z * c * y * x))


def cut_core(matrix):
    z, y, x, rows = slice_shape()
    parts = matrix.astype(bf16).reshape(-1, z, 2, y, x, rows, matrix.shape[-1])
    own = lax.axis_index("c")
    return [lax.dynamic_index_in_dim(parts, own ^ other, 2, False) for other in range(2)]


def core_parts(parts):
    return [part.reshape((-1,) + slice_shape() + part.shape[-1:]) for part in parts]


tie = lax.optimization_barrier


def to_tiles(slices, parts=1):
    blocks, rows, columns = slices.shape
    return (
        slices.reshape(parts, blocks // parts, rows, columns // CH, CH)
        .transpose(1, 0, 3, 2, 4)
        .reshape(-1, rows, CH)
    )


def from_tiles(tiles, row_blocks, parts):
    rows = tiles.shape[1]
    return (
        tiles.reshape(row_blocks, parts, D // CH, rows, CH)
        .transpose(1, 0, 3, 2, 4)
        .reshape(parts * row_blocks, rows, D)
    )


def dot_nt(a, b):
    return lax.dot_general(a, b, (((1,), (1,)), ((), ())), preferred_element_type=f32)


def dot_nn(a, b):
    return lax.dot_general(a, b, (((1,), (0,)), ((), ())), preferred_element_type=f32)


def dot_tn(a, b):
    return lax.dot_general(a, b, (((0,), (0,)), ((), ())), preferred_element_type=f32)


def head_mask(shape, head):
    return (lax.broadcasted_iota(jnp.int32, shape, len(shape) - 1) // HD) == head


def cost(flops, moved, transcendentals=0):
    return pl.CostEstimate(
        flops=int(flops), bytes_accessed=int(moved), transcendentals=int(transcendentals)
    )


def params():
    return pltpu.CompilerParams(vmem_limit_bytes=VMEM_BYTES)


def cross_forward_kernel(q_ref, k_ref, v_ref, o_ref, l_ref):
    rows = q_ref.shape[0]
    lane = lax.broadcasted_iota(jnp.int32, (rows, 128), 1)
    q = q_ref[...]
    mixed = jnp.zeros((rows, CH), f32)
    stat = jnp.zeros((rows, 128), f32)
    for head in range(TH):
        mask = head_mask((rows, CH), head)
        q_head = jnp.where(mask, q.astype(f32) * 0.125, 0.0).astype(bf16)
        scores = dot_nt(q_head, k_ref[...])
        peak = jnp.max(scores, -1, keepdims=True)
        shifted = jnp.exp(scores - peak)
        total = jnp.sum(shifted, -1, keepdims=True)
        part = dot_nn(shifted.astype(bf16), v_ref[...])
        mixed = jnp.where(mask, part / total, mixed)
        stat = jnp.where(lane == head, peak + jnp.log(total), stat)
    o_ref[...] = mixed.astype(bf16)
    l_ref[0] = stat.T[:8]


def cross_forward(query, kv):
    rows = query.shape[0] // 2
    cells = kv.shape[0]
    return pl.pallas_call(
        cross_forward_kernel,
        grid=(2,),
        in_specs=[
            pl.BlockSpec((rows, CH), lambda i: (i, 0)),
            pl.BlockSpec((cells, CH), lambda i: (0, 0)),
            pl.BlockSpec((cells, CH), lambda i: (0, 1)),
        ],
        out_specs=[
            pl.BlockSpec((rows, CH), lambda i: (i, 0)),
            pl.BlockSpec((1, 8, rows), lambda i: (i, 0, 0)),
        ],
        out_shape=[
            jax.ShapeDtypeStruct((2 * rows, CH), bf16),
            jax.ShapeDtypeStruct((2, 8, rows), f32),
        ],
        compiler_params=params(),
        cost_estimate=cost(16 * TH * rows * cells * CH // 2, 8 * cells * CH, 2 * TH * rows * cells),
    )(query, kv, kv)


def delta_rows(d_out, out):
    product = d_out.astype(f32) * out.astype(f32)
    head = lax.broadcasted_iota(jnp.int32, (8, CH), 0)
    lane = lax.broadcasted_iota(jnp.int32, (8, CH), 1)
    pick = ((lane // HD) == head).astype(f32)
    return lax.dot_general(
        pick,
        product,
        (((1,), (1,)), ((), ())),
        precision=lax.Precision.HIGHEST,
        preferred_element_type=f32,
    )


def cross_backward_kernel(
    q_ref, k_ref, v_ref, do_ref, o_ref, l_ref, dq_ref, dkv_ref, q_s, do_s, delta_s, dq_s
):
    step = pl.program_id(0)
    rows = q_ref.shape[0]

    @pl.when(step == 0)
    def _():
        for head in range(TH):
            mask = head_mask((rows, CH), head)
            q_s[head] = jnp.where(mask, q_ref[...].astype(f32) * 0.125, 0.0).astype(bf16)
            do_s[head] = jnp.where(mask, do_ref[...].astype(f32), 0.0).astype(bf16)
        delta_s[...] = delta_rows(do_ref[...], o_ref[...])
        dq_s[...] = jnp.zeros_like(dq_s)

    cells = k_ref.shape[0]
    dk = jnp.zeros((cells, CH), f32)
    dv = jnp.zeros((cells, CH), f32)
    dq = dq_s[...]
    k = k_ref[...]
    for head in range(TH):
        probs = jnp.exp(dot_nt(k, q_s[head]) - l_ref[head : head + 1, :])
        d_probs = dot_nt(v_ref[...], do_s[head])
        d_scores = (probs * (d_probs - delta_s[head : head + 1, :])).astype(bf16)
        dv = dv + dot_nn(probs.astype(bf16), do_s[head])
        dk = dk + dot_nn(d_scores, q_s[head])
        dq = dq + jnp.where(head_mask((rows, CH), head), dot_tn(d_scores, k), 0.0)
    dq_s[...] = dq
    dkv_ref[:, :CH] = dk.astype(bf16)
    dkv_ref[:, CH:] = dv.astype(bf16)

    @pl.when(step == pl.num_programs(0) - 1)
    def _():
        dq_ref[...] = (dq_s[...] * 0.125).astype(bf16)


def cross_backward(query, kv, d_out, out, log_rows):
    rows = query.shape[0]
    cells = kv.shape[0]
    block = 1024
    whole = lambda i: (0, 0)
    return pl.pallas_call(
        cross_backward_kernel,
        grid=(cells // block,),
        in_specs=[
            pl.BlockSpec((rows, CH), whole),
            pl.BlockSpec((block, CH), lambda i: (i, 0)),
            pl.BlockSpec((block, CH), lambda i: (i, 1)),
            pl.BlockSpec((rows, CH), whole),
            pl.BlockSpec((rows, CH), whole),
            pl.BlockSpec((8, rows), whole),
        ],
        out_specs=[
            pl.BlockSpec((rows, CH), whole),
            pl.BlockSpec((block, 2 * CH), lambda i: (i, 0)),
        ],
        out_shape=[
            jax.ShapeDtypeStruct((rows, CH), bf16),
            jax.ShapeDtypeStruct((cells, 2 * CH), bf16),
        ],
        scratch_shapes=[
            pltpu.VMEM((TH, rows, CH), bf16),
            pltpu.VMEM((TH, rows, CH), bf16),
            pltpu.VMEM((8, rows), f32),
            pltpu.VMEM((rows, CH), f32),
        ],
        compiler_params=params(),
        cost_estimate=cost(10 * TH * rows * cells * CH, 8 * cells * CH, TH * rows * cells),
    )(query, kv, kv, d_out, out, log_rows)


def self_forward_kernel(len_ref, q_ref, k_ref, v_ref, o_ref, l_ref):
    group = pl.program_id(0)
    length = len_ref[0]
    for start, count in ROW_BLOCKS:
        stop = start + count
        q = q_ref[0, start:stop, :].astype(f32) * 0.125
        row = lax.broadcasted_iota(jnp.int32, (count, 1), 0) + start
        bound = jnp.minimum(row, length - 1)
        allowed = lax.broadcasted_iota(jnp.int32, (count, stop), 1) <= bound
        mixed = jnp.zeros((count, CH), f32)
        stat = jnp.zeros((count, 128), f32)
        lane = lax.broadcasted_iota(jnp.int32, (count, 128), 1)
        for head in range(GROUP):
            mask = head_mask((count, CH), head)
            q_head = jnp.where(mask, q, 0.0).astype(bf16)
            scores = jnp.where(allowed, dot_nt(q_head, k_ref[0, :stop, :]), neg_large)
            peak = jnp.max(scores, -1, keepdims=True)
            shifted = jnp.exp(scores - peak)
            total = jnp.sum(shifted, -1, keepdims=True)
            part = dot_nn(shifted.astype(bf16), v_ref[0, :stop, :])
            mixed = jnp.where(mask, part / total, mixed)
            stat = jnp.where(lane == head, peak + jnp.log(total), stat)
        o_ref[start:stop, :] = mixed.astype(bf16)
        l_ref[0, :, start:stop] = stat.T[:8]


def self_forward(qkv, length):
    groups = D // CH
    at = lambda j: (lambda i, n: (j, 0, i))
    return pl.pallas_call(
        self_forward_kernel,
        grid_spec=pltpu.PrefetchScalarGridSpec(
            num_scalar_prefetch=1,
            grid=(groups,),
            in_specs=[pl.BlockSpec((1, SEQ, CH), at(j)) for j in range(3)],
            out_specs=[
                pl.BlockSpec((SEQ, CH), lambda i, n: (0, i)),
                pl.BlockSpec((1, 8, SEQ), lambda i, n: (i, 0, 0)),
            ],
        ),
        out_shape=[
            jax.ShapeDtypeStruct((SEQ, D), bf16),
            jax.ShapeDtypeStruct((groups, 8, SEQ), f32),
        ],
        compiler_params=params(),
        cost_estimate=cost(4 * HEADS * SEQ * SEQ * CH, 8 * SEQ * D, HEADS * SEQ * SEQ),
    )(length, qkv, qkv, qkv)


def self_backward_kernel(
    len_ref, q_ref, k_ref, v_ref, do_ref, o_ref, l_ref, out_ref, dk_s, dv_s
):
    length = len_ref[0]
    dk_s[...] = jnp.zeros_like(dk_s)
    dv_s[...] = jnp.zeros_like(dv_s)
    delta = delta_rows(do_ref[...], o_ref[...])
    for start, count in ROW_BLOCKS:
        stop = start + count
        q = q_ref[0, start:stop, :].astype(f32) * 0.125
        d_out = do_ref[start:stop, :].astype(f32)
        row = lax.broadcasted_iota(jnp.int32, (1, count), 1) + start
        bound = jnp.minimum(row, length - 1)
        allowed = lax.broadcasted_iota(jnp.int32, (stop, count), 0) <= bound
        dq = jnp.zeros((count, CH), f32)
        k = k_ref[0, :stop, :]
        v = v_ref[0, :stop, :]
        dk = dk_s[:stop, :]
        dv = dv_s[:stop, :]
        for head in range(GROUP):
            mask = head_mask((count, CH), head)
            q_head = jnp.where(mask, q, 0.0).astype(bf16)
            d_head = jnp.where(mask, d_out, 0.0).astype(bf16)
            scores = dot_nt(k, q_head)
            logs = l_ref[0, head : head + 1, start:stop]
            probs = jnp.where(allowed, jnp.exp(scores - logs), 0.0)
            d_probs = dot_nt(v, d_head)
            d_scores = (probs * (d_probs - delta[head : head + 1, start:stop])).astype(bf16)
            dv = dv + dot_nn(probs.astype(bf16), d_head)
            dk = dk + dot_nn(d_scores, q_head)
            dq = dq + jnp.where(mask, dot_tn(d_scores, k), 0.0)
        dk_s[:stop, :] = dk
        dv_s[:stop, :] = dv
        out_ref[0, start:stop, :] = (dq * 0.125).astype(bf16)
    out_ref[1] = dk_s[...].astype(bf16)
    out_ref[2] = dv_s[...].astype(bf16)


def self_backward(qkv, d_out, out, log_rows, length):
    groups = D // CH
    at = lambda j: (lambda i, n: (j, 0, i))
    here = lambda i, n: (0, i)
    return pl.pallas_call(
        self_backward_kernel,
        grid_spec=pltpu.PrefetchScalarGridSpec(
            num_scalar_prefetch=1,
            grid=(groups,),
            in_specs=[pl.BlockSpec((1, SEQ, CH), at(j)) for j in range(3)]
            + [
                pl.BlockSpec((SEQ, CH), here),
                pl.BlockSpec((SEQ, CH), here),
                pl.BlockSpec((1, 8, SEQ), lambda i, n: (i, 0, 0)),
            ],
            out_specs=pl.BlockSpec((3, SEQ, CH), lambda i, n: (0, 0, i)),
            scratch_shapes=[pltpu.VMEM((SEQ, CH), f32), pltpu.VMEM((SEQ, CH), f32)],
        ),
        out_shape=jax.ShapeDtypeStruct((3, SEQ, D), bf16),
        compiler_params=params(),
        cost_estimate=cost(8 * HEADS * SEQ * SEQ * CH, 16 * SEQ * D, HEADS * SEQ * SEQ),
    )(length, qkv, qkv, qkv, d_out, out, log_rows)


def full(*shape):
    return pl.BlockSpec(shape, lambda i: (0,) * len(shape))


def part_of(first):
    return pl.BlockSpec((3, CH, D), lambda i: (first + i, 0, 0))


def fixed_part(index):
    return pl.BlockSpec((3, CH, D), lambda i: (index, 0, 0))


def square(ref):
    return ref[...].reshape(D, D)


def write_cores(core, matrix, keep_ref, give_ref, span):
    parts = matrix.reshape(-1, 2, span, matrix.shape[-1])
    first, second = parts[:, 0], parts[:, 1]
    keep = jnp.where(core == 0, first, second)
    give = jnp.where(core == 0, second, first)
    keep_ref[...] = keep.reshape(keep_ref.shape).astype(bf16)
    give_ref[...] = give.reshape(give_ref.shape).astype(bf16)


def core_span():
    return CH // (2 * lax.axis_size("z"))


def core_here():
    return lax.axis_index("c").astype(jnp.int32).reshape(1)


CORE_SPEC = pl.BlockSpec(memory_space=pltpu.SMEM)
HALF = D // 2


def row_scale(values):
    return lax.rsqrt(jnp.mean(values * values, -1, keepdims=True) + eps_norm)


def pull_norm(d_normed, values, gain):
    scale = row_scale(values)
    d_gain = jnp.sum(d_normed * values * scale, 0, keepdims=True)
    scaled = d_normed * gain
    inner = jnp.mean(scaled * values, -1, keepdims=True)
    return d_gain, scale * scaled - (scale * scale * scale) * values * inner


def embed_kernel(
    pool_ref, feats_ref, mixed_ref, out_w_ref, emb_ref, w_ref, gain_ref,
    seq_ref, embed_ref, normed_ref, qkv_ref,
):
    @pl.when(pl.program_id(0) == 0)
    def _():
        updated = feats_ref[...].astype(f32) + dot_nn(mixed_ref[...], out_w_ref[...])
        seq_ref[:CTX, :] = pool_ref[...]
        seq_ref[CTX:, :] = updated.astype(bf16)
        embed = dot_nn(seq_ref[...], emb_ref[0])
        embed_ref[...] = embed
        normed_ref[...] = (embed * row_scale(embed) * gain_ref[...]).astype(bf16)

    qkv_ref[0] = dot_nn(normed_ref[...], square(w_ref)).astype(bf16)


def embed_forward(pooled, feats, mixed, to_out, weights, gain):
    last = weights.shape[0] - 1
    return pl.pallas_call(
        embed_kernel,
        grid=(3,),
        in_specs=[
            full(CTX, CH),
            full(SEQ - CTX, CH),
            full(SEQ - CTX, CH),
            full(CH, CH),
            pl.BlockSpec((1, CH, D), lambda i: (last, 0, 0)),
            part_of(0),
            full(1, D),
        ],
        out_specs=[
            full(SEQ, CH),
            full(SEQ, D),
            full(SEQ, D),
            pl.BlockSpec((1, SEQ, D), lambda i: (i, 0, 0)),
        ],
        out_shape=[
            jax.ShapeDtypeStruct((SEQ, CH), bf16),
            jax.ShapeDtypeStruct((SEQ, D), f32),
            jax.ShapeDtypeStruct((SEQ, D), bf16),
            jax.ShapeDtypeStruct((3, SEQ, D), bf16),
        ],
        compiler_params=params(),
        cost_estimate=cost(2 * SEQ * D * (CH + 3 * D), 12 * SEQ * D),
    )(pooled, feats, mixed, to_out, weights, weights, gain)


def up_kernel(
    mixed_ref, embed_ref, att_ref, w_ref, gain_ref,
    stream_ref, normed_ref, act_ref, slope_ref, pre_s,
):
    @pl.when(pl.program_id(0) == 0)
    def _():
        stream = embed_ref[...] + dot_nn(mixed_ref[...], square(att_ref))
        stream_ref[...] = stream
        normed_ref[...] = (stream * row_scale(stream) * gain_ref[...]).astype(bf16)

    pre_s[...] = dot_nn(normed_ref[...], square(w_ref))
    factor = (2.0 / 3.141592653589793) ** 0.5
    cubic = 0.044715 * factor

    def rows_step(index, carry):
        here = pl.ds(pl.multiple_of(index * 16, 16), 16)
        v = pre_s[here, :]
        v2 = v * v
        half = 0.5 + 0.5 * jnp.tanh(v * (factor + cubic * v2))
        act_ref[0, here, :] = (v * half).astype(bf16)
        bend = 2.0 * half * (1.0 - half) * (factor + 3.0 * cubic * v2)
        slope_ref[0, here, :] = (half + v * bend).astype(bf16)
        return carry

    lax.fori_loop(0, SEQ // 16, rows_step, 0, unroll=2)


def up_forward(mixed, embed, weights, gain):
    return pl.pallas_call(
        up_kernel,
        grid=(4,),
        in_specs=[full(SEQ, D), full(SEQ, D), fixed_part(3), part_of(4), full(1, D)],
        out_specs=[
            full(SEQ, D),
            full(SEQ, D),
            pl.BlockSpec((1, SEQ, D), lambda i: (i, 0, 0)),
            pl.BlockSpec((1, SEQ, D), lambda i: (i, 0, 0)),
        ],
        out_shape=[
            jax.ShapeDtypeStruct((SEQ, D), f32),
            jax.ShapeDtypeStruct((SEQ, D), bf16),
            jax.ShapeDtypeStruct((4, SEQ, D), bf16),
            jax.ShapeDtypeStruct((4, SEQ, D), bf16),
        ],
        scratch_shapes=[pltpu.VMEM((SEQ, D), f32)],
        compiler_params=params(),
        cost_estimate=cost(10 * SEQ * D * D, 28 * SEQ * D, 4 * SEQ * D),
    )(mixed, embed, weights, weights, gain)


def down_kernel(act_ref, w_ref, stream_ref, out_ref):
    part = dot_nn(act_ref[0], square(w_ref))

    @pl.when(pl.program_id(0) == 0)
    def _():
        out_ref[...] = stream_ref[...] + part

    @pl.when(pl.program_id(0) > 0)
    def _():
        out_ref[...] += part


def down_forward(act, w_down, stream):
    return pl.pallas_call(
        down_kernel,
        grid=(4,),
        in_specs=[
            pl.BlockSpec((1, SEQ, D), lambda i: (i, 0, 0)),
            part_of(0),
            full(SEQ, D),
        ],
        out_specs=full(SEQ, D),
        out_shape=jax.ShapeDtypeStruct((SEQ, D), f32),
        compiler_params=params(),
        cost_estimate=cost(8 * SEQ * D * D, 24 * SEQ * D),
    )(act, w_down, stream)


def down_grad_kernel(core_ref, act_ref, gd_ref, keep_ref, give_ref, *, span):
    total = dot_tn(act_ref[0], gd_ref[...])
    write_cores(core_ref[0], total, keep_ref, give_ref, span)


def down_grad(act, gd):
    half = pl.BlockSpec((HALF, D), lambda i: (i, 0))
    return pl.pallas_call(
        functools.partial(down_grad_kernel, span=core_span()),
        grid=(4,),
        in_specs=[CORE_SPEC, pl.BlockSpec((1, SEQ, D), lambda i: (i, 0, 0)), full(SEQ, D)],
        out_specs=[half, half],
        out_shape=[jax.ShapeDtypeStruct((4 * HALF, D), bf16)] * 2,
        compiler_params=params(),
        cost_estimate=cost(8 * SEQ * D * D, 18 * SEQ * D),
    )(core_here(), act, gd)


def up_grad_kernel(
    core_ref, gd_ref, w_ref, slope_ref, normed_ref, gpre_ref, keep_ref, give_ref, turned_s, *, span
):
    @pl.when(pl.program_id(0) == 0)
    def _():
        turned_s[...] = normed_ref[...].T

    gpre = (dot_nt(gd_ref[...], square(w_ref)) * slope_ref[0].astype(f32)).astype(bf16)
    gpre_ref[0] = gpre
    write_cores(core_ref[0], dot_nn(turned_s[...], gpre), keep_ref, give_ref, span)


def up_grad(gd, w_down, slope, normed):
    part = pl.BlockSpec((1, SEQ, D), lambda i: (i, 0, 0))
    half = pl.BlockSpec((HALF, D), lambda i: (i, 0))
    return pl.pallas_call(
        functools.partial(up_grad_kernel, span=core_span()),
        grid=(4,),
        in_specs=[CORE_SPEC, full(SEQ, D), part_of(0), part, full(SEQ, D)],
        out_specs=[part, half, half],
        out_shape=[jax.ShapeDtypeStruct((4, SEQ, D), bf16)]
        + [jax.ShapeDtypeStruct((4 * HALF, D), bf16)] * 2,
        scratch_shapes=[pltpu.VMEM((D, SEQ), bf16)],
        compiler_params=params(),
        cost_estimate=cost(16 * SEQ * D * D, 36 * SEQ * D),
    )(core_here(), gd, w_down, slope, normed)


def att_grad_kernel(
    core_ref, gpre_ref, w_ref, att_ref, stream_ref, gd_ref, mixed_ref, gain_ref,
    d_stream_ref, gog_ref, keep_ref, give_ref, gain_g_ref, total_s, *, span
):
    step = pl.program_id(0)
    part = dot_nt(gpre_ref[0], square(w_ref))

    @pl.when(step == 0)
    def _():
        total_s[...] = part

    @pl.when(step > 0)
    def _():
        total_s[...] += part

    @pl.when(step == pl.num_programs(0) - 1)
    def _():
        d_gain, pulled = pull_norm(total_s[...], stream_ref[...], gain_ref[...])
        gain_g_ref[...] = d_gain
        d_stream = gd_ref[...].astype(f32) + pulled
        d_stream_ref[...] = d_stream
        ga = d_stream.astype(bf16)
        gog_ref[...] = dot_nt(ga, square(att_ref)).astype(bf16)
        write_cores(core_ref[0], dot_tn(mixed_ref[...], ga), keep_ref, give_ref, span)


def att_grad(gpre, weights, stream, gd, mixed, gain):
    return pl.pallas_call(
        functools.partial(att_grad_kernel, span=core_span()),
        grid=(4,),
        in_specs=[
            CORE_SPEC,
            pl.BlockSpec((1, SEQ, D), lambda i: (i, 0, 0)),
            part_of(4),
            fixed_part(3),
            full(SEQ, D),
            full(SEQ, D),
            full(SEQ, D),
            full(1, D),
        ],
        out_specs=[full(SEQ, D), full(SEQ, D), full(HALF, D), full(HALF, D), full(1, D)],
        out_shape=[
            jax.ShapeDtypeStruct((SEQ, D), f32),
            jax.ShapeDtypeStruct((SEQ, D), bf16),
            jax.ShapeDtypeStruct((HALF, D), bf16),
            jax.ShapeDtypeStruct((HALF, D), bf16),
            jax.ShapeDtypeStruct((1, D), f32),
        ],
        scratch_shapes=[pltpu.VMEM((SEQ, D), f32)],
        compiler_params=params(),
        cost_estimate=cost(12 * SEQ * D * D, 32 * SEQ * D),
    )(core_here(), gpre, weights, weights, stream, gd, mixed, gain)


def qkv_grad_kernel(core_ref, normed_ref, g_ref, keep_ref, give_ref, turned_s, *, span):
    @pl.when(pl.program_id(0) == 0)
    def _():
        turned_s[...] = normed_ref[...].T

    write_cores(core_ref[0], dot_nn(turned_s[...], g_ref[0]), keep_ref, give_ref, span)


def qkv_grad(normed, gqkv):
    half = pl.BlockSpec((HALF, D), lambda i: (i, 0))
    return pl.pallas_call(
        functools.partial(qkv_grad_kernel, span=core_span()),
        grid=(3,),
        in_specs=[CORE_SPEC, full(SEQ, D), pl.BlockSpec((1, SEQ, D), lambda i: (i, 0, 0))],
        out_specs=[half, half],
        out_shape=[jax.ShapeDtypeStruct((3 * HALF, D), bf16)] * 2,
        scratch_shapes=[pltpu.VMEM((D, SEQ), bf16)],
        compiler_params=params(),
        cost_estimate=cost(6 * SEQ * D * D, 14 * SEQ * D),
    )(core_here(), normed, gqkv)


def embed_grad_kernel(
    g_ref, w_ref, emb_ref, embed_ref, d_stream_ref, seq_ref, mixed_ref, out_w_ref, gain_ref,
    emb_g_ref, gupd_ref, pool_g_ref, out_g_ref, gox_ref, gain_g_ref, total_s,
):
    step = pl.program_id(0)
    part = dot_nt(g_ref[0], square(w_ref))

    @pl.when(step == 0)
    def _():
        total_s[...] = part

    @pl.when(step > 0)
    def _():
        total_s[...] += part

    @pl.when(step == pl.num_programs(0) - 1)
    def _():
        d_gain, pulled = pull_norm(total_s[...], embed_ref[...], gain_ref[...])
        gain_g_ref[...] = d_gain
        gembed = (d_stream_ref[...] + pulled).astype(bf16)
        emb_g_ref[...] = dot_tn(seq_ref[...], gembed).astype(bf16)
        gseq = dot_nt(gembed, emb_ref[0])
        gupd = gseq[CTX:]
        gb = gupd.astype(bf16)
        pool_g_ref[...] = gseq[:CTX].astype(bf16)
        gupd_ref[...] = gupd
        out_g_ref[...] = dot_tn(mixed_ref[...], gb).astype(bf16)
        gox_ref[...] = dot_nt(gb, out_w_ref[...]).astype(bf16)


def embed_grad(gqkv, weights, embed, d_stream, seq, mixed, to_out, gain):
    last = weights.shape[0] - 1
    return pl.pallas_call(
        embed_grad_kernel,
        grid=(3,),
        in_specs=[
            pl.BlockSpec((1, SEQ, D), lambda i: (i, 0, 0)),
            part_of(0),
            pl.BlockSpec((1, CH, D), lambda i: (last, 0, 0)),
            full(SEQ, D),
            full(SEQ, D),
            full(SEQ, CH),
            full(SEQ - CTX, CH),
            full(CH, CH),
            full(1, D),
        ],
        out_specs=[
            full(CH, D),
            full(SEQ - CTX, CH),
            full(CTX, CH),
            full(CH, CH),
            full(SEQ - CTX, CH),
            full(1, D),
        ],
        out_shape=[
            jax.ShapeDtypeStruct((CH, D), bf16),
            jax.ShapeDtypeStruct((SEQ - CTX, CH), f32),
            jax.ShapeDtypeStruct((CTX, CH), bf16),
            jax.ShapeDtypeStruct((CH, CH), bf16),
            jax.ShapeDtypeStruct((SEQ - CTX, CH), bf16),
            jax.ShapeDtypeStruct((1, D), f32),
        ],
        scratch_shapes=[pltpu.VMEM((SEQ, D), f32)],
        compiler_params=params(),
        cost_estimate=cost(2 * SEQ * D * (3 * D + 2 * CH), 24 * SEQ * D),
    )(gqkv, weights, weights, embed, d_stream, seq, mixed, to_out, gain)


def patch_pick(rows, columns, patch_dim):
    patch = lax.broadcasted_iota(jnp.int32, (rows, columns), patch_dim)
    cell = lax.broadcasted_iota(jnp.int32, (rows, columns), 1 - patch_dim)
    inside = (cell // (PATCH * IMG)) * (IMG // PATCH) + (cell % IMG) // PATCH
    return jnp.where(patch == inside, 1.0 / (PATCH * PATCH), 0.0).astype(bf16)


def image_rows(step, row):
    return pl.ds(pl.multiple_of(step * BLOCK + row * IMG, IMG), BLOCK)


def token_forward_kernel(x_ref, conv_ref, kv_w_ref, slope_ref, hidden_ref, kv_ref, pool_ref):
    step = pl.program_id(0)
    z = jnp.zeros((BLOCK, CH), f32)
    for row in range(3):
        z = z + dot_nn(x_ref[image_rows(step, row), :], conv_ref[row])
    center = x_ref[image_rows(step, 1), CH : 2 * CH].astype(f32)
    gate = 1.0 / (1.0 + jnp.exp(-z))
    hidden = center + z * gate
    slope_ref[...] = (gate * (1.0 + z * (1.0 - gate))).astype(bf16)
    hidden_b = hidden.astype(bf16)
    hidden_ref[...] = hidden_b
    kv_ref[...] = dot_nn(hidden_b, kv_w_ref[...]).astype(bf16)
    rest = (hidden - hidden_b.astype(f32)).astype(bf16)
    pick = patch_pick(pool_ref.shape[0], BLOCK, 0)
    pool_ref[...] = (dot_nn(pick, hidden_b) + dot_nn(pick, rest)).astype(bf16)


def token_forward(wide, conv_rows, kv_weight):
    steps = CELLS // BLOCK
    whole = lambda i: (0, 0)
    block = lambda i: (i, 0)
    return pl.pallas_call(
        token_forward_kernel,
        grid=(steps,),
        in_specs=[
            pl.BlockSpec(wide.shape, whole),
            pl.BlockSpec((3, 3 * CH, CH), lambda i: (0, 0, 0)),
            pl.BlockSpec((CH, 2 * CH), whole),
        ],
        out_specs=[
            pl.BlockSpec((BLOCK, CH), block),
            pl.BlockSpec((BLOCK, CH), block),
            pl.BlockSpec((BLOCK, 2 * CH), block),
            pl.BlockSpec((CTX // steps, CH), block),
        ],
        out_shape=[
            jax.ShapeDtypeStruct((CELLS, CH), bf16),
            jax.ShapeDtypeStruct((CELLS, CH), bf16),
            jax.ShapeDtypeStruct((CELLS, 2 * CH), bf16),
            jax.ShapeDtypeStruct((CTX, CH), bf16),
        ],
        compiler_params=params(),
        cost_estimate=cost(22 * CELLS * CH * CH, 14 * CELLS * CH, CELLS * CH),
    )(wide, conv_rows, kv_weight)


def token_backward_kernel(
    core_ref, dkv_ref, slope_ref, pool_ref, hidden_ref, x_ref, kv_w_ref,
    d_hidden_ref, gz_ref, keep_ref, give_ref, conv_s, kv_s, *, span
):
    step = pl.program_id(0)

    @pl.when(step == 0)
    def _():
        conv_s[...] = jnp.zeros_like(conv_s)
        kv_s[...] = jnp.zeros_like(kv_s)

    dkv = dkv_ref[...]
    d_hidden = dot_nt(dkv, kv_w_ref[...])
    d_hidden = d_hidden + dot_nn(patch_pick(BLOCK, pool_ref.shape[0], 1), pool_ref[...])
    gz = (d_hidden * slope_ref[...].astype(f32)).astype(bf16)
    d_hidden_ref[...] = d_hidden
    gz_ref[...] = gz
    kv_s[...] += dot_tn(hidden_ref[...], dkv)
    gz_t = gz.T
    for row in range(3):
        conv_s[row] += dot_nn(gz_t, x_ref[image_rows(step, row), :])

    @pl.when(step == pl.num_programs(0) - 1)
    def _():
        tiles = []
        for row in range(3):
            for col in range(3):
                tiles.append(conv_s[row, :, col * CH : (col + 1) * CH].T)
        tiles = tiles + [kv_s[:, :CH], kv_s[:, CH:]]
        for at, tile in enumerate(tiles):
            write_cores(core_ref[0], tile, keep_ref.at[at], give_ref.at[at], span)


def token_backward(dkv, slope, d_pool, hidden_b, wide, kv_weight):
    steps = CELLS // BLOCK
    whole = lambda i: (0, 0)
    whole_3 = lambda i: (0, 0, 0)
    block = lambda i: (i, 0)
    return pl.pallas_call(
        functools.partial(token_backward_kernel, span=core_span()),
        grid=(steps,),
        in_specs=[
            CORE_SPEC,
            pl.BlockSpec((BLOCK, 2 * CH), block),
            pl.BlockSpec((BLOCK, CH), block),
            pl.BlockSpec((CTX // steps, CH), block),
            pl.BlockSpec((BLOCK, CH), block),
            pl.BlockSpec(wide.shape, whole),
            pl.BlockSpec((CH, 2 * CH), whole),
        ],
        out_specs=[
            pl.BlockSpec((BLOCK, CH), block),
            pl.BlockSpec((BLOCK, CH), block),
            pl.BlockSpec((11, CH // 2, CH), whole_3),
            pl.BlockSpec((11, CH // 2, CH), whole_3),
        ],
        out_shape=[
            jax.ShapeDtypeStruct((CELLS, CH), f32),
            jax.ShapeDtypeStruct((CELLS, CH), bf16),
            jax.ShapeDtypeStruct((11, CH // 2, CH), bf16),
            jax.ShapeDtypeStruct((11, CH // 2, CH), bf16),
        ],
        scratch_shapes=[pltpu.VMEM((3, CH, 3 * CH), f32), pltpu.VMEM((CH, 2 * CH), f32)],
        compiler_params=params(),
        cost_estimate=cost(26 * CELLS * CH * CH, 20 * CELLS * CH),
    )(core_here(), dkv, slope, d_pool, hidden_b, wide, kv_weight)


def context_backward_kernel(gz_ref, d_hidden_ref, conv_ref, out_ref, wide_s):
    step = pl.program_id(0)
    steps = pl.num_programs(0)

    def widen(at):
        values = gz_ref[image_rows(at, 0), :].astype(f32)
        col = lax.broadcasted_iota(jnp.int32, (BLOCK, CH), 0) % IMG
        left = jnp.where(col == 0, 0.0, pltpu.roll(values, 1, 0))
        right = jnp.where(col == IMG - 1, 0.0, pltpu.roll(values, BLOCK - 1, 0))
        wide_s[image_rows(at, 1), 0:CH] = left.astype(bf16)
        wide_s[image_rows(at, 1), CH : 2 * CH] = values.astype(bf16)
        wide_s[image_rows(at, 1), 2 * CH :] = right.astype(bf16)

    @pl.when(step == 0)
    def _():
        wide_s[0:IMG, :] = jnp.zeros((IMG, 3 * CH), bf16)
        wide_s[CELLS + IMG :, :] = jnp.zeros((IMG, 3 * CH), bf16)
        widen(0)

    @pl.when(step < steps - 1)
    def _():
        widen(step + 1)

    total = d_hidden_ref[...]
    for row in range(3):
        values = wide_s[image_rows(step, row), :]
        for col in range(3):
            tap = conv_ref[3 * (2 - row) + (2 - col)]
            total = total + dot_nt(values[:, col * CH : (col + 1) * CH], tap)
    out_ref[...] = total.astype(bf16)


def context_backward(gz, d_hidden, conv_tiles):
    block = lambda i: (i, 0)
    return pl.pallas_call(
        context_backward_kernel,
        grid=(CELLS // BLOCK,),
        in_specs=[
            pl.BlockSpec((CELLS, CH), lambda i: (0, 0)),
            pl.BlockSpec((BLOCK, CH), block),
            pl.BlockSpec((9, CH, CH), lambda i: (0, 0, 0)),
        ],
        out_specs=pl.BlockSpec((BLOCK, CH), block),
        out_shape=jax.ShapeDtypeStruct((CELLS, CH), bf16),
        scratch_shapes=[pltpu.VMEM((CELLS + 2 * IMG, 3 * CH), bf16)],
        compiler_params=params(),
        cost_estimate=cost(18 * CELLS * CH * CH, 8 * CELLS * CH),
    )(gz, d_hidden, conv_tiles)


def local(
    context_map,
    future_feats,
    horizon,
    cotangent,
    tile_owner,
    master_tiles,
    moment_first,
    moment_second,
    norm_gains,
    gain_first,
    gain_second,
):
    slot_count = master_tiles.shape[0]
    devices = lax.axis_size(AXES)
    rows = CH // devices
    slot_of = slot_index(tile_owner, slot_count)

    pieces = trade_rows(context_map)
    length = CTX + FT * horizon
    valid = jnp.arange(SEQ) < length[0]
    gd = jnp.where(valid[:, None], cotangent[0], jnp.zeros((), bf16))

    slices = (
        master_tiles.astype(bf16)
        .reshape(slot_count, devices, rows, CH)
        .transpose(1, 0, 2, 3)
    )
    slices = lax.all_to_all(slices, AXES, split_axis=0, concat_axis=0, tiled=True)
    slices, pieces, gd = tie((slices, pieces, gd))
    image = row_order(pieces).reshape(IMG, IMG, CH)
    slices = slices.reshape(devices * slot_count, rows, CH)
    slices = slices.at[slot_of].get(mode="promise_in_bounds")
    early, emb, qkv, att, up, down = jnp.split(slices, (13, 16, 43, 52, 88))
    weights = jnp.concatenate(
        [
            from_tiles(qkv, 3, 3),
            from_tiles(att, 3, 1),
            from_tiles(up, 3, 4),
            from_tiles(emb, 1, 1),
        ],
        0,
    )
    weights = lax.all_gather(weights, AXES, axis=1, tiled=True)
    w_down = lax.all_gather(from_tiles(down, 12, 1), AXES, axis=1, tiled=True)
    early = gather_all(early).transpose(1, 0, 2, 3).reshape(EARLY, CH, CH)

    padded = jnp.pad(image, ((1, 1), (1, 1), (0, 0)))
    wide = jnp.concatenate([padded[:, col : col + IMG] for col in range(3)], -1)
    wide = wide.reshape((IMG + 2) * IMG, 3 * CH)

    conv_tiles = early[:9]
    to_query, to_out = early[9], early[12]
    kv_weight = jnp.concatenate([early[10], early[11]], 1)

    slope_z, hidden_b, kv, pooled = token_forward(
        wide, conv_tiles.reshape(3, 3 * CH, CH), kv_weight
    )
    feats_b = future_feats[0]
    query = jnp.dot(feats_b, to_query, preferred_element_type=f32).astype(bf16)
    cross_mixed, cross_logs = cross_forward(query, kv)

    gain_one, gain_two = norm_gains[:1], norm_gains[1:]
    seq, embed, normed_one, qkv = embed_forward(
        pooled, feats_b, cross_mixed, to_out, weights, gain_one
    )
    mixed, logs = self_forward(qkv, length)
    stream, normed_two, act, slope = up_forward(mixed, embed, weights, gain_two)

    down = core_parts(down_grad(act, gd))
    gd, down = tie((gd, down))
    down = send(down, "c")
    gpre, up_keep, up_give = up_grad(gd, w_down, slope, normed_two)
    gpre, up, down = hold((gpre, core_parts([up_keep, up_give])), down)
    down = advance(down, "x", 3)
    gpre, up, down = tie((gpre, up, down))
    up, down = send(up, "c"), send(down, "x")
    d_stream, gog, att_keep, att_give, gain_g_two = att_grad(
        gpre, weights, stream, gd, mixed, gain_two
    )
    gog, att, up = hold((gog, core_parts([att_keep, att_give])), up)
    up = advance(up, "y", 2)
    gog, att, up = tie((gog, att, up))
    up, att = send(up, "y"), send(att, "c")
    gqkv = self_backward(qkv, gog, mixed, logs, length)
    gqkv, down, att = hold((gqkv,), down, att)
    down = advance(down, "y", 2)
    gqkv, down = tie((gqkv, down))
    down = send(down, "y")
    qkv_keep, qkv_give = qkv_grad(normed_one, gqkv)
    gqkv, qkv, up = hold((gqkv, core_parts([qkv_keep, qkv_give])), up)
    up = advance(up, "x", 2)
    gqkv, qkv, up = tie((gqkv, qkv, up))
    qkv, up = send(qkv, "c"), send(up, "x")
    emb_g, gupd, pool_g, out_g, gox, gain_g_one = embed_grad(
        gqkv, weights, embed, d_stream, seq, cross_mixed, to_out, gain_one
    )
    gox, gupd, emb_g, gain_g_one, qkv, up, down = hold(
        (gox, gupd, emb_g, gain_g_one), qkv, up, down
    )
    gains = jnp.concatenate([gain_g_one, gain_g_two], 0).reshape(devices, 1, -1)
    gain_count = gains.shape[-1]
    gains = jnp.pad(gains, ((0, 0), (0, rows - 1), (0, D - gain_count))).astype(bf16)
    emb = cut_core(jnp.concatenate([emb_g, gains.reshape(CH, D)], 0))
    mlp = advance_near([jnp.concatenate(part, 0) for part in zip(up, down)])
    first = advance([part[:6] for part in qkv], "x", 3)
    second = advance([jnp.concatenate([p[6:], q], 0) for p, q in zip(qkv, att)], "y", 2)
    gox, mlp, first, second, emb = tie((gox, mlp, first, second, emb))
    mlp, emb = send(mlp, "z"), send(emb, "c")
    first, second = send(first, "x"), send(second, "y")

    log_rows = jnp.concatenate([cross_logs[0], cross_logs[1]], 1)
    gq, gkv = cross_backward(query, kv, gox, cross_mixed, log_rows)
    gq, gkv, mlp, first, second, emb = hold((gq, gkv), mlp, first, second, emb)
    mlp, emb = advance_far(mlp), advance(emb, "x", 3)
    first, second = advance(first, "y", 2), advance(second, "x", 2)
    query_g = cut_core(jnp.dot(feats_b.T, gq, preferred_element_type=f32))
    out_g = cut_core(out_g)
    gkv, mlp, first, second, emb, query_g, out_g = tie(
        (gkv, mlp, first, second, emb, query_g, out_g)
    )
    mlp, emb = send(mlp, "z", 2), send(emb, "x")
    first, second = send(first, "y"), send(second, "x")

    d_hidden, gz, token_keep, token_give = token_backward(
        gkv, slope_z, pool_g, hidden_b, wide, kv_weight
    )
    d_hidden, token_keep, token_give, mlp, first, second, emb = hold(
        (d_hidden, token_keep, token_give), mlp, first, second, emb
    )
    early = []
    for token, q, o in zip((token_keep, token_give), query_g, out_g):
        q, o = (part.reshape(1, CH // 2, CH) for part in (q, o))
        early.append(jnp.concatenate([token[:9], q, token[9:], o], 0))
    early = core_parts(early)
    att = advance_near([jnp.concatenate(part, 0) for part in zip(first, second)])
    emb = advance(emb, "y", 2)
    early, att, emb = tie((early, att, emb))
    early = send(early, "c")
    att, emb = send(att, "z"), send(emb, "y")
    sum_mlp = add_up(mlp, keep_wide=True)
    future_grad = gupd + lax.dot_general(
        gq, to_query, (((1,), (1,)), ((), ())), preferred_element_type=f32
    )
    future_grad, gz, early = hold((future_grad, gz), early)
    shape = early[0].shape
    early = advance([p.reshape(shape[:2] + (-1,) + shape[4:]) for p in early], ("y", "x"), 2)
    gz, early = tie((gz, early))
    early = send(early, ("y", "x"))
    context_grad = context_backward(gz, d_hidden, conv_tiles)
    context_grad, early, att, emb = hold((context_grad,), early, att, emb)
    att = advance_far(att)
    early = advance(early, "z", 1)
    emb = advance(emb, "z", 1)
    early = [jnp.concatenate([e, to_tiles(m)], 0) for e, m in zip(early, emb)]
    context_grad, early, att = tie((context_grad, early, att))
    early, att = send(early, "z"), send(att, "z", 2)
    pieces = trade_rows(context_grad.reshape(context_map.shape))
    sum_early = add_up(early, keep_wide=True)
    sum_att = add_up(att, keep_wide=True)

    sums = jnp.concatenate(
        [
            sum_early[: EARLY + 3],
            to_tiles(sum_att[:9], 3),
            to_tiles(sum_att[9:]),
            to_tiles(sum_mlp[:12], 4),
            to_tiles(sum_mlp[12:]),
        ],
        0,
    )
    gains = sum_early[EARLY + 3, 0, :gain_count]
    share = jnp.concatenate([(jnp.sum(sums * sums) + jnp.sum(gains * gains))[None], gains])
    share_high = share.astype(bf16)
    share_low = (share - share_high.astype(f32)).astype(bf16)
    share = jnp.pad(
        jnp.stack([share_high, share_low]), ((0, rows - 2), (0, CH - 1 - gain_count))
    )
    slots = jnp.arange(devices * slot_count)
    found = slot_of[None, :] == slots[:, None]
    tile_of = jnp.sum(jnp.where(found, jnp.arange(found.shape[1])[None], 0), 1)
    mine = sums.astype(bf16).at[tile_of].get(mode="promise_in_bounds")
    mine = mine.reshape(devices, slot_count, rows, CH)
    share = jnp.broadcast_to(share[None, None], (devices, 1, rows, CH))
    mine = jnp.concatenate([mine, share], 1)
    mine, act, pieces[-1] = tie((mine, act, pieces[-1]))
    mine = lax.all_to_all(mine, AXES, split_axis=0, concat_axis=0, tiled=True)
    block_out = down_forward(act, w_down, stream)
    shares = mine[:, slot_count, :2].astype(f32)
    shares = shares[:, 0] + shares[:, 1]
    gains = shares[:, 1 : 1 + gain_count].reshape(2, D)
    mine = mine[:, :slot_count].transpose(1, 0, 2, 3).reshape(slot_count, CH, CH).astype(f32)

    used = jnp.any(found, 1).astype(f32).reshape(devices, slot_count)
    used = lax.dynamic_index_in_dim(used, lax.axis_index(AXES), 0, keepdims=False)[:, None, None]
    grad_norm = jnp.sqrt(jnp.sum(shares[:, 0]))
    factor = jnp.minimum(1.0, clip_level / (grad_norm + 1e-06))
    new_first, new_second, new_master = adam_step(
        master_tiles, mine * factor, moment_first, moment_second, learn_rate, decay_rate
    )
    new_gain_first, new_gain_second, new_gains = adam_step(
        norm_gains, gains * factor, gain_first, gain_second, gain_rate, 0.0
    )
    return (
        block_out[None],
        row_order(pieces).reshape(context_map.shape).astype(f32),
        future_grad[None],
        jnp.where(used > 0, new_first, 0.0),
        jnp.where(used > 0, new_second, 0.0),
        jnp.where(used > 0, new_master, 0.0),
        new_gain_first,
        new_gain_second,
        new_gains,
        grad_norm,
    )


def solution(mesh):
    groups, rows = mesh.devices.shape
    fine = jax.sharding.Mesh(mesh.devices.reshape(groups // 2, 2, rows // 2, 2), AXES)
    whole = P(AXES, None, None)
    image = P(("z", "c"), ("y", "x"), None, None)
    in_specs = (image, whole, P(AXES), whole, P(), whole, whole, whole, P(), P(), P())
    out_specs = (whole, image, whole, whole, whole, whole, P(), P(), P(), P())
    return jax.shard_map(local, mesh=fine, in_specs=in_specs, out_specs=out_specs, check_vma=False)
```

```python
import functools

import jax
import jax.numpy as jnp
from jax import lax
from jax.experimental import pallas as pl
from jax.experimental.pallas import tpu as pltpu
from jax.sharding import PartitionSpec as P

CH = 256
HD = 64
HEADS = 12
D = 768
FF = 3072
TH = 4
IMG = 64
PATCH = 4
FT = 16
CTX = 256
SEQ = 736
STEP = 10


eps_norm = 1e-05
beta_one = 0.9
beta_two = 0.999
learn_rate = 0.02
gain_rate = 0.6
decay_rate = 0.1
adam_eps = 1e-08
clip_level = 1.0
neg_large = -1e30
AXES = ("z", "c", "y", "x")
CELLS = IMG * IMG
BLOCK = 512
GROUP = 4
EARLY = 13
VMEM_BYTES = 28 * 1024 * 1024
MLP_BYTES = 44 * 1024 * 1024
ROW_BLOCKS = ((0, 256), (256, 256), (512, 224))
CORE_SPEC = pl.BlockSpec(memory_space=pltpu.SMEM)
bf16 = jnp.bfloat16
f32 = jnp.float32


def slot_index(tile_owner, slot_count):
    ordinal = jnp.arange(tile_owner.shape[0])
    earlier = (tile_owner[None, :] == tile_owner[:, None]) & (ordinal[None, :] < ordinal[:, None])
    return tile_owner * slot_count + jnp.sum(earlier.astype(jnp.int32), 1)


def adam_step(weight, grad_now, first, second, rate, decay):
    first_new = beta_one * first + (1.0 - beta_one) * grad_now
    second_new = beta_two * second + (1.0 - beta_two) * grad_now * grad_now
    corr_first = first_new / (1.0 - beta_one**STEP)
    corr_second = second_new / (1.0 - beta_two**STEP)
    weight_new = weight - rate * (corr_first / (jnp.sqrt(corr_second) + adam_eps) + decay * weight)
    return (first_new, second_new, weight_new)


def xor_permute(values, axes, mask):
    count = lax.axis_size(axes)
    return lax.ppermute(values, axes, [(i, i ^ mask) for i in range(count)])


def pick(parts, index, dim):
    if parts[0].shape[dim] == 2:
        total = add_up(parts)
        first, second = (lax.index_in_dim(total, at, dim, False) for at in range(2))
        return jnp.where(index == 0, first, second)
    return add_up([lax.dynamic_index_in_dim(part, index, dim, False) for part in parts])


def advance(parts, axes, dim):
    mine = lax.axis_index(axes)
    return [pick(parts, mine ^ mask, dim) for mask in range(lax.axis_size(axes))]


def advance_near(parts):
    mine = lax.axis_index("z") % 2
    shape = parts[0].shape
    parts = [p.reshape((shape[0], shape[1] // 2, 2) + shape[2:]) for p in parts]
    return [pick(parts, mine ^ mask, 2) for mask in range(2)]


def advance_far(parts):
    mine = lax.axis_index("z") // 2
    return [pick(parts, mine ^ mask, 1) for mask in range(parts[0].shape[1])]


def send(cuts, axes, unit=1):
    return [cuts[0]] + [
        xor_permute(cut, axes, unit * mask) for mask, cut in enumerate(cuts) if mask > 0
    ]


def add_up(parts, keep_wide=False):
    total = parts[0].astype(f32)
    for part in parts[1:]:
        total = total + part.astype(f32)
    return total if keep_wide else total.astype(parts[0].dtype)


def hold(values, *sums):
    tied = lax.optimization_barrier((tuple(values), tuple(tuple(parts) for parts in sums)))
    return tied[0] + tuple(list(parts) for parts in tied[1])


def gather_axes(values, axes):
    return [values] + [
        xor_permute(values, axes, mask) for mask in range(1, lax.axis_size(axes))
    ]


def joined(pieces):
    return jnp.stack(pieces, 1)


def device_order(values, axes):
    sizes = [lax.axis_size(axis) for axis in AXES]
    own = [lax.axis_index(axis) for axis in AXES]
    places = jnp.unravel_index(jnp.arange(lax.axis_size(AXES)), sizes)
    at = 0
    for axis in axes:
        which = AXES.index(axis)
        at = at * sizes[which] + (places[which] ^ own[which])
    values = values.reshape((values.shape[0], -1) + values.shape[-2:])
    values = values.at[:, at].get(mode="promise_in_bounds")
    return values.reshape(values.shape[0], -1, values.shape[-1])


def place_kernel(own_ref, low_ref, low_other_ref, high_ref, high_other_ref, out_ref, *, half, sizes):
    z_count, c_count, y_count, x_count = sizes
    own_z, own_c, own_y, own_x = (own_ref[axis] for axis in range(4))
    step = pl.program_id(0)

    def place(near_ref, far_ref, x_first):
        for z in range(z_count):
            for y in range(y_count):
                for x in range(x_count):
                    if x_first:
                        at = (x ^ own_x) * y_count + (y ^ own_y)
                    else:
                        at = (y ^ own_y) * x_count + (x ^ own_x)
                    at = at * z_count + (z ^ own_z)
                    near, far = near_ref[0, at], far_ref[0, at]
                    for c in range(c_count):
                        to = ((z * c_count + c) * y_count + y) * x_count + x
                        out_ref[0, to] = jnp.where(own_c == c, near, far)

    @pl.when(step < half)
    def _():
        place(low_ref, low_other_ref, False)

    @pl.when(step >= half)
    def _():
        place(high_ref, high_other_ref, True)


def place_rows(low, high):
    sizes = tuple(lax.axis_size(axis) for axis in AXES)
    half, rows = low[0].shape[0], low[0].shape[-2]
    count = half + high[0].shape[0]
    own = jnp.stack([lax.axis_index(axis) for axis in AXES]).astype(jnp.int32)
    pieces = [part.reshape(part.shape[0], -1, rows, D) for part in low + high]
    block = (1,) + pieces[0].shape[1:]
    early = pl.BlockSpec(block, lambda i: (jnp.minimum(i, half - 1), 0, 0, 0))
    later = pl.BlockSpec(block, lambda i: (jnp.maximum(i - half, 0), 0, 0, 0))
    devices = CH // rows
    out = pl.pallas_call(
        functools.partial(place_kernel, half=half, sizes=sizes),
        grid=(count,),
        in_specs=[CORE_SPEC, early, early, later, later],
        out_specs=pl.BlockSpec((1, devices, rows, D), lambda i: (i, 0, 0, 0)),
        out_shape=jax.ShapeDtypeStruct((count, devices, rows, D), bf16),
        compiler_params=params(),
        cost_estimate=cost(0, 4 * count * CH * D),
    )(own, *pieces)
    return out.reshape(count, CH, D)


def trade_rows(values):
    mine = lax.axis_index(("y", "x"))
    count = lax.axis_size(("y", "x"))
    cuts = [lax.dynamic_index_in_dim(values, mine ^ mask, 0, False) for mask in range(count)]
    return send(cuts, ("y", "x"))


def row_order_kernel(row_ref, *refs):
    at = pl.program_id(0) ^ row_ref[0]
    values = refs[0][...]
    for mask in range(1, len(refs) - 1):
        values = jnp.where(at == mask, refs[mask][...], values)
    refs[-1][0] = values.astype(f32)


def row_order(pieces):
    count = len(pieces)
    cells = pieces[0].size // CH
    return pl.pallas_call(
        row_order_kernel,
        grid=(count,),
        in_specs=[CORE_SPEC] + [pl.BlockSpec((cells, CH), lambda i: (0, 0))] * count,
        out_specs=pl.BlockSpec((1, cells, CH), lambda i: (i, 0, 0)),
        out_shape=jax.ShapeDtypeStruct((count, cells, CH), f32),
        compiler_params=params(),
        cost_estimate=cost(0, 6 * count * cells * CH),
    )(row_here(), *[piece.reshape(cells, CH) for piece in pieces])


def widen_kernel(row_ref, *refs):
    out_ref = refs[-1]
    cells = refs[0].shape[0]
    col = lax.broadcasted_iota(jnp.int32, (cells, CH), 0) % IMG
    out_ref[0:IMG, :] = jnp.zeros((IMG, 3 * CH), bf16)
    out_ref[CELLS + IMG :, :] = jnp.zeros((IMG, 3 * CH), bf16)
    for at in range(len(refs) - 1):
        values = refs[at][...]
        for mask in range(1, len(refs) - 1):
            values = jnp.where(row_ref[0] == mask, refs[at ^ mask][...], values)
        here = slice(IMG + at * cells, IMG + (at + 1) * cells)
        out_ref[here, CH : 2 * CH] = values
        values = values.astype(f32)
        left = jnp.where(col == 0, 0.0, pltpu.roll(values, 1, 0))
        right = jnp.where(col == IMG - 1, 0.0, pltpu.roll(values, cells - 1, 0))
        out_ref[here, 0:CH] = left.astype(bf16)
        out_ref[here, 2 * CH :] = right.astype(bf16)


def widen(pieces):
    cells = pieces[0].size // CH
    vmem = pl.BlockSpec(memory_space=pltpu.VMEM)
    return pl.pallas_call(
        widen_kernel,
        in_specs=[CORE_SPEC] + [vmem] * len(pieces),
        out_specs=vmem,
        out_shape=lasting((CELLS + 2 * IMG, 3 * CH), bf16),
        compiler_params=params(),
        cost_estimate=cost(0, 8 * CELLS * CH),
    )(row_here(), *[piece.reshape(cells, CH) for piece in pieces])


def slice_shape():
    z, c, y, x = [lax.axis_size(axis) for axis in AXES]
    return (z, y, x, CH // (z * c * y * x))


def cut_core(matrix):
    z, y, x, rows = slice_shape()
    parts = matrix.astype(bf16).reshape(-1, z, 2, y, x, rows, matrix.shape[-1])
    own = lax.axis_index("c")
    return [lax.dynamic_index_in_dim(parts, own ^ other, 2, False) for other in range(2)]


def core_parts(parts):
    return [part.reshape((-1,) + slice_shape() + part.shape[-1:]) for part in parts]


tie = lax.optimization_barrier


def to_tiles(slices, parts=1):
    blocks, rows, columns = slices.shape
    return (
        slices.reshape(parts, blocks // parts, rows, columns // CH, CH)
        .transpose(1, 0, 3, 2, 4)
        .reshape(-1, rows, CH)
    )


def from_tiles(tiles, row_blocks, parts):
    rows = tiles.shape[1]
    return (
        tiles.reshape(row_blocks, parts, D // CH, rows, CH)
        .transpose(1, 0, 3, 2, 4)
        .reshape(parts * row_blocks, rows, D)
    )


def dot_nt(a, b):
    return lax.dot_general(a, b, (((1,), (1,)), ((), ())), preferred_element_type=f32)


def dot_nn(a, b):
    return lax.dot_general(a, b, (((1,), (0,)), ((), ())), preferred_element_type=f32)


def dot_tn(a, b):
    return lax.dot_general(a, b, (((0,), (0,)), ((), ())), preferred_element_type=f32)


def head_mask(shape, head):
    return (lax.broadcasted_iota(jnp.int32, shape, len(shape) - 1) // HD) == head


def cost(flops, moved, transcendentals=0):
    return pl.CostEstimate(
        flops=int(flops), bytes_accessed=int(moved), transcendentals=int(transcendentals)
    )


def stay(values):
    return pltpu.with_memory_space_constraint(values, pltpu.HBM)


lasting = pltpu.HBM


def params():
    return pltpu.CompilerParams(vmem_limit_bytes=VMEM_BYTES)


def cross_forward_kernel(q_ref, k_ref, v_ref, o_ref, l_ref):
    rows = q_ref.shape[0]
    lane = lax.broadcasted_iota(jnp.int32, (rows, 128), 1)
    q = q_ref[...]
    mixed = jnp.zeros((rows, CH), f32)
    stat = jnp.zeros((rows, 128), f32)
    for head in range(TH):
        mask = head_mask((rows, CH), head)
        q_head = jnp.where(mask, q.astype(f32) * 0.125, 0.0).astype(bf16)
        scores = dot_nt(q_head, k_ref[...])
        peak = jnp.max(scores, -1, keepdims=True)
        shifted = jnp.exp(scores - peak)
        total = jnp.sum(shifted, -1, keepdims=True)
        part = dot_nn(shifted.astype(bf16), v_ref[...])
        mixed = jnp.where(mask, part / total, mixed)
        stat = jnp.where(lane == head, peak + jnp.log(total), stat)
    o_ref[...] = mixed.astype(bf16)
    l_ref[0] = stat.T[:8]


def cross_forward(query, kv):
    rows = query.shape[0] // 2
    cells = kv.shape[0]
    return pl.pallas_call(
        cross_forward_kernel,
        grid=(2,),
        in_specs=[
            pl.BlockSpec((rows, CH), lambda i: (i, 0)),
            pl.BlockSpec((cells, CH), lambda i: (0, 0)),
            pl.BlockSpec((cells, CH), lambda i: (0, 1)),
        ],
        out_specs=[
            pl.BlockSpec((rows, CH), lambda i: (i, 0)),
            pl.BlockSpec((1, 8, rows), lambda i: (i, 0, 0)),
        ],
        out_shape=[
            jax.ShapeDtypeStruct((2 * rows, CH), bf16),
            jax.ShapeDtypeStruct((2, 8, rows), f32),
        ],
        compiler_params=params(),
        cost_estimate=cost(16 * TH * rows * cells * CH // 2, 8 * cells * CH, 2 * TH * rows * cells),
    )(query, kv, kv)


def delta_rows(d_out, out):
    product = d_out.astype(f32) * out.astype(f32)
    head = lax.broadcasted_iota(jnp.int32, (8, CH), 0)
    lane = lax.broadcasted_iota(jnp.int32, (8, CH), 1)
    pick = ((lane // HD) == head).astype(f32)
    return lax.dot_general(
        pick,
        product,
        (((1,), (1,)), ((), ())),
        precision=lax.Precision.HIGHEST,
        preferred_element_type=f32,
    )


def cross_backward_kernel(
    q_ref, k_ref, v_ref, do_ref, o_ref, l_ref, feats_ref, gupd_ref, query_w_ref,
    dkv_ref, query_g_ref, future_ref, q_s, do_s, delta_s, dq_s,
):
    step = pl.program_id(0)
    rows = q_ref.shape[0]

    @pl.when(step == 0)
    def _():
        for head in range(TH):
            mask = head_mask((rows, CH), head)
            q_s[head] = jnp.where(mask, q_ref[...].astype(f32) * 0.125, 0.0).astype(bf16)
            do_s[head] = jnp.where(mask, do_ref[...].astype(f32), 0.0).astype(bf16)
        delta_s[...] = delta_rows(do_ref[...], o_ref[...])
        dq_s[...] = jnp.zeros_like(dq_s)

    cells = k_ref.shape[0]
    dk = jnp.zeros((cells, CH), f32)
    dv = jnp.zeros((cells, CH), f32)
    dq = dq_s[...]
    k = k_ref[...]
    for head in range(TH):
        probs = jnp.exp(dot_nt(k, q_s[head]) - l_ref[head : head + 1, :])
        d_probs = dot_nt(v_ref[...], do_s[head])
        d_scores = (probs * (d_probs - delta_s[head : head + 1, :])).astype(bf16)
        dv = dv + dot_nn(probs.astype(bf16), do_s[head])
        dk = dk + dot_nn(d_scores, q_s[head])
        dq = dq + jnp.where(head_mask((rows, CH), head), dot_tn(d_scores, k), 0.0)
    dq_s[...] = dq
    dkv_ref[:, :CH] = dk.astype(bf16)
    dkv_ref[:, CH:] = dv.astype(bf16)

    @pl.when(step == pl.num_programs(0) - 1)
    def _():
        gq = (dq_s[...] * 0.125).astype(bf16)
        query_g_ref[...] = dot_tn(feats_ref[...], gq).astype(bf16)
        future_ref[...] = gupd_ref[...] + dot_nt(gq, query_w_ref[...])


def cross_backward(query, kv, d_out, out, log_rows, feats, gupd, to_query):
    rows = query.shape[0]
    cells = kv.shape[0]
    block = 1024
    whole = lambda i: (0, 0)
    return pl.pallas_call(
        cross_backward_kernel,
        grid=(cells // block,),
        in_specs=[
            pl.BlockSpec((rows, CH), whole),
            pl.BlockSpec((block, CH), lambda i: (i, 0)),
            pl.BlockSpec((block, CH), lambda i: (i, 1)),
            pl.BlockSpec((rows, CH), whole),
            pl.BlockSpec((rows, CH), whole),
            pl.BlockSpec((8, rows), whole),
            pl.BlockSpec((rows, CH), whole),
            pl.BlockSpec((rows, CH), whole),
            pl.BlockSpec((CH, CH), whole),
        ],
        out_specs=[
            pl.BlockSpec((block, 2 * CH), lambda i: (i, 0)),
            pl.BlockSpec((CH, CH), whole),
            pl.BlockSpec((rows, CH), whole),
        ],
        out_shape=[
            jax.ShapeDtypeStruct((cells, 2 * CH), bf16),
            jax.ShapeDtypeStruct((CH, CH), bf16),
            jax.ShapeDtypeStruct((rows, CH), f32),
        ],
        scratch_shapes=[
            pltpu.VMEM((TH, rows, CH), bf16),
            pltpu.VMEM((TH, rows, CH), bf16),
            pltpu.VMEM((8, rows), f32),
            pltpu.VMEM((rows, CH), f32),
        ],
        compiler_params=params(),
        cost_estimate=cost(10 * TH * rows * cells * CH, 8 * cells * CH, TH * rows * cells),
    )(query, kv, kv, d_out, out, log_rows, feats, gupd, to_query)


def self_forward_kernel(len_ref, q_ref, k_ref, v_ref, o_ref, l_ref):
    group = pl.program_id(0)
    length = len_ref[0]
    for start, count in ROW_BLOCKS:
        stop = start + count
        q = q_ref[0, start:stop, :].astype(f32) * 0.125
        row = lax.broadcasted_iota(jnp.int32, (count, 1), 0) + start
        bound = jnp.minimum(row, length - 1)
        allowed = lax.broadcasted_iota(jnp.int32, (count, stop), 1) <= bound
        mixed = jnp.zeros((count, CH), f32)
        stat = jnp.zeros((count, 128), f32)
        lane = lax.broadcasted_iota(jnp.int32, (count, 128), 1)
        for head in range(GROUP):
            mask = head_mask((count, CH), head)
            q_head = jnp.where(mask, q, 0.0).astype(bf16)
            scores = jnp.where(allowed, dot_nt(q_head, k_ref[0, :stop, :]), neg_large)
            peak = jnp.max(scores, -1, keepdims=True)
            shifted = jnp.exp(scores - peak)
            total = jnp.sum(shifted, -1, keepdims=True)
            part = dot_nn(shifted.astype(bf16), v_ref[0, :stop, :])
            mixed = jnp.where(mask, part / total, mixed)
            stat = jnp.where(lane == head, peak + jnp.log(total), stat)
        o_ref[start:stop, :] = mixed.astype(bf16)
        l_ref[0, :, start:stop] = stat.T[:8]


def self_forward(qkv, length):
    groups = D // CH
    at = lambda j: (lambda i, n: (j, 0, i))
    return pl.pallas_call(
        self_forward_kernel,
        grid_spec=pltpu.PrefetchScalarGridSpec(
            num_scalar_prefetch=1,
            grid=(groups,),
            in_specs=[pl.BlockSpec((1, SEQ, CH), at(j)) for j in range(3)],
            out_specs=[
                pl.BlockSpec((SEQ, CH), lambda i, n: (0, i)),
                pl.BlockSpec((1, 8, SEQ), lambda i, n: (i, 0, 0)),
            ],
        ),
        out_shape=[
            jax.ShapeDtypeStruct((SEQ, D), bf16),
            jax.ShapeDtypeStruct((groups, 8, SEQ), f32),
        ],
        compiler_params=params(),
        cost_estimate=cost(4 * HEADS * SEQ * SEQ * CH, 8 * SEQ * D, HEADS * SEQ * SEQ),
    )(length, qkv, qkv, qkv)


def self_backward_kernel(
    len_ref, q_ref, k_ref, v_ref, do_ref, o_ref, l_ref, out_ref, dk_s, dv_s
):
    length = len_ref[0]
    dk_s[...] = jnp.zeros_like(dk_s)
    dv_s[...] = jnp.zeros_like(dv_s)
    delta = delta_rows(do_ref[...], o_ref[...])
    for start, count in ROW_BLOCKS:
        stop = start + count
        q = q_ref[0, start:stop, :].astype(f32) * 0.125
        d_out = do_ref[start:stop, :].astype(f32)
        row = lax.broadcasted_iota(jnp.int32, (1, count), 1) + start
        bound = jnp.minimum(row, length - 1)
        allowed = lax.broadcasted_iota(jnp.int32, (stop, count), 0) <= bound
        dq = jnp.zeros((count, CH), f32)
        k = k_ref[0, :stop, :]
        v = v_ref[0, :stop, :]
        dk = dk_s[:stop, :]
        dv = dv_s[:stop, :]
        for head in range(GROUP):
            mask = head_mask((count, CH), head)
            q_head = jnp.where(mask, q, 0.0).astype(bf16)
            d_head = jnp.where(mask, d_out, 0.0).astype(bf16)
            scores = dot_nt(k, q_head)
            logs = l_ref[0, head : head + 1, start:stop]
            probs = jnp.where(allowed, jnp.exp(scores - logs), 0.0)
            d_probs = dot_nt(v, d_head)
            d_scores = (probs * (d_probs - delta[head : head + 1, start:stop])).astype(bf16)
            dv = dv + dot_nn(probs.astype(bf16), d_head)
            dk = dk + dot_nn(d_scores, q_head)
            dq = dq + jnp.where(mask, dot_tn(d_scores, k), 0.0)
        dk_s[:stop, :] = dk
        dv_s[:stop, :] = dv
        out_ref[0, start:stop, :] = (dq * 0.125).astype(bf16)
    out_ref[1] = dk_s[...].astype(bf16)
    out_ref[2] = dv_s[...].astype(bf16)


def self_backward(qkv, d_out, out, log_rows, length):
    groups = D // CH
    at = lambda j: (lambda i, n: (j, 0, i))
    here = lambda i, n: (0, i)
    return pl.pallas_call(
        self_backward_kernel,
        grid_spec=pltpu.PrefetchScalarGridSpec(
            num_scalar_prefetch=1,
            grid=(groups,),
            in_specs=[pl.BlockSpec((1, SEQ, CH), at(j)) for j in range(3)]
            + [
                pl.BlockSpec((SEQ, CH), here),
                pl.BlockSpec((SEQ, CH), here),
                pl.BlockSpec((1, 8, SEQ), lambda i, n: (i, 0, 0)),
            ],
            out_specs=pl.BlockSpec((3, SEQ, CH), lambda i, n: (0, 0, i)),
            scratch_shapes=[pltpu.VMEM((SEQ, CH), f32), pltpu.VMEM((SEQ, CH), f32)],
        ),
        out_shape=jax.ShapeDtypeStruct((3, SEQ, D), bf16),
        compiler_params=params(),
        cost_estimate=cost(8 * HEADS * SEQ * SEQ * CH, 16 * SEQ * D, HEADS * SEQ * SEQ),
    )(length, qkv, qkv, qkv, d_out, out, log_rows)


def full(*shape):
    return pl.BlockSpec(shape, lambda i: (0,) * len(shape))


def part_of(first):
    return pl.BlockSpec((3, CH, D), lambda i: (first + i, 0, 0))


def fixed_part(index):
    return pl.BlockSpec((3, CH, D), lambda i: (index, 0, 0))


def square(ref):
    return ref[...].reshape(D, D)


def write_cores(core, matrix, keep_ref, give_ref, span):
    parts = matrix.reshape(-1, 2, span, matrix.shape[-1])
    first, second = parts[:, 0], parts[:, 1]
    keep = jnp.where(core == 0, first, second)
    give = jnp.where(core == 0, second, first)
    keep_ref[...] = keep.reshape(keep_ref.shape).astype(bf16)
    give_ref[...] = give.reshape(give_ref.shape).astype(bf16)


def core_span():
    return CH // (2 * lax.axis_size("z"))


def row_here():
    return lax.axis_index(("y", "x")).astype(jnp.int32).reshape(1)


def core_here():
    return lax.axis_index("c").astype(jnp.int32).reshape(1)


HALF = D // 2


def row_scale(values):
    return lax.rsqrt(jnp.mean(values * values, -1, keepdims=True) + eps_norm)


def pull_norm(d_normed, values, gain):
    scale = row_scale(values)
    d_gain = jnp.sum(d_normed * values * scale, 0, keepdims=True)
    scaled = d_normed * gain
    inner = jnp.mean(scaled * values, -1, keepdims=True)
    return d_gain, scale * scaled - (scale * scale * scale) * values * inner


def embed_kernel(
    pool_ref, feats_ref, mixed_ref, out_w_ref, emb_ref, w_ref, gain_ref,
    seq_ref, embed_ref, normed_ref, qkv_ref,
):
    @pl.when(pl.program_id(0) == 0)
    def _():
        updated = feats_ref[...].astype(f32) + dot_nn(mixed_ref[...], out_w_ref[...])
        seq_ref[:CTX, :] = pool_ref[...]
        seq_ref[CTX:, :] = updated.astype(bf16)
        embed = dot_nn(seq_ref[...], emb_ref[0])
        embed_ref[...] = embed
        normed_ref[...] = (embed * row_scale(embed) * gain_ref[...]).astype(bf16)

    qkv_ref[0] = dot_nn(normed_ref[...], square(w_ref)).astype(bf16)


def embed_forward(pooled, feats, mixed, to_out, weights, gain):
    last = weights.shape[0] - 1
    return pl.pallas_call(
        embed_kernel,
        grid=(3,),
        in_specs=[
            full(CTX, CH),
            full(SEQ - CTX, CH),
            full(SEQ - CTX, CH),
            full(CH, CH),
            pl.BlockSpec((1, CH, D), lambda i: (last, 0, 0)),
            part_of(0),
            full(1, D),
        ],
        out_specs=[
            full(SEQ, CH),
            full(SEQ, D),
            full(SEQ, D),
            pl.BlockSpec((1, SEQ, D), lambda i: (i, 0, 0)),
        ],
        out_shape=[
            lasting((SEQ, CH), bf16),
            lasting((SEQ, D), f32),
            lasting((SEQ, D), bf16),
            jax.ShapeDtypeStruct((3, SEQ, D), bf16),
        ],
        compiler_params=params(),
        cost_estimate=cost(2 * SEQ * D * (CH + 3 * D), 12 * SEQ * D),
    )(pooled, feats, mixed, to_out, stay(weights), stay(weights), gain)


def mlp_kernel(
    core_ref, mixed_ref, embed_ref, att_ref, up_ref, down_ref, gain_ref, gd_ref,
    out_ref, d_stream_ref, gog_ref, up_keep_ref, up_give_ref, down_keep_ref, down_give_ref,
    att_keep_ref, att_give_ref, gain_g_ref,
    stream_s, normed_s, turned_s, act_s, gpre_s, total_s, *, span
):
    step = pl.program_id(0)
    core = core_ref[0]

    @pl.when(step == 0)
    def _():
        stream = embed_ref[...] + dot_nn(mixed_ref[...], square(att_ref))
        stream_s[...] = stream
        out_ref[...] = stream
        total_s[...] = jnp.zeros_like(total_s)
        normed = stream * row_scale(stream) * gain_ref[...]
        normed_s[...] = normed.astype(bf16)
        turned_s[...] = normed.T.astype(bf16)

    factor = (2.0 / 3.141592653589793) ** 0.5
    cubic = 0.044715 * factor
    rows = SEQ // 4
    for start in range(0, SEQ, rows):
        here = slice(start, start + rows)
        v = dot_nn(normed_s[here, :], square(up_ref))
        v2 = v * v
        half = 0.5 + 0.5 * jnp.tanh(v * (factor + cubic * v2))
        act = (v * half).astype(bf16)
        act_s[here, :] = act
        slope = half + v * (2.0 * half * (1.0 - half) * (factor + 3.0 * cubic * v2))
        gpre = (dot_nt(gd_ref[here, :], square(down_ref)) * slope).astype(bf16)
        gpre_s[here, :] = gpre
        out_ref[here, :] += dot_nn(act, square(down_ref))
        total_s[here, :] += dot_nt(gpre, square(up_ref))
    write_cores(core, dot_tn(act_s[...], gd_ref[...]), down_keep_ref, down_give_ref, span)
    write_cores(core, dot_nn(turned_s[...], gpre_s[...]), up_keep_ref, up_give_ref, span)

    @pl.when(step == pl.num_programs(0) - 1)
    def _():
        d_gain, pulled = pull_norm(total_s[...], stream_s[...], gain_ref[...])
        gain_g_ref[...] = d_gain
        d_stream = gd_ref[...].astype(f32) + pulled
        d_stream_ref[...] = d_stream
        ga = d_stream.astype(bf16)
        gog_ref[...] = dot_nt(ga, square(att_ref)).astype(bf16)
        write_cores(core, dot_tn(mixed_ref[...], ga), att_keep_ref, att_give_ref, span)


def mlp_block(mixed, embed, weights, mlp, gain, gd):
    half = pl.BlockSpec((HALF, D), lambda i: (i, 0))
    return pl.pallas_call(
        functools.partial(mlp_kernel, span=core_span()),
        grid=(4,),
        in_specs=[
            CORE_SPEC,
            full(SEQ, D),
            full(SEQ, D),
            fixed_part(3),
            part_of(0),
            part_of(4),
            full(1, D),
            full(SEQ, D),
        ],
        out_specs=[full(SEQ, D)] * 3 + [half] * 4 + [full(HALF, D)] * 2 + [full(1, D)],
        out_shape=[
            lasting((SEQ, D), f32),
            lasting((SEQ, D), f32),
            jax.ShapeDtypeStruct((SEQ, D), bf16),
        ]
        + [jax.ShapeDtypeStruct((4 * HALF, D), bf16)] * 4
        + [jax.ShapeDtypeStruct((HALF, D), bf16)] * 2
        + [jax.ShapeDtypeStruct((1, D), f32)],
        scratch_shapes=[
            pltpu.VMEM((SEQ, D), f32),
            pltpu.VMEM((SEQ, D), bf16),
            pltpu.VMEM((D, SEQ), bf16),
            pltpu.VMEM((SEQ, D), bf16),
            pltpu.VMEM((SEQ, D), bf16),
            pltpu.VMEM((SEQ, D), f32),
        ],
        compiler_params=pltpu.CompilerParams(vmem_limit_bytes=MLP_BYTES),
        cost_estimate=cost(54 * SEQ * D * D, 60 * SEQ * D, 4 * SEQ * D),
    )(core_here(), mixed, embed, stay(weights), stay(mlp), stay(mlp), gain, gd)


def qkv_grad_kernel(core_ref, normed_ref, g_ref, keep_ref, give_ref, turned_s, *, span):
    @pl.when(pl.program_id(0) == 0)
    def _():
        turned_s[...] = normed_ref[...].T

    write_cores(core_ref[0], dot_nn(turned_s[...], g_ref[0]), keep_ref, give_ref, span)


def qkv_grad(normed, gqkv):
    half = pl.BlockSpec((HALF, D), lambda i: (i, 0))
    return pl.pallas_call(
        functools.partial(qkv_grad_kernel, span=core_span()),
        grid=(3,),
        in_specs=[CORE_SPEC, full(SEQ, D), pl.BlockSpec((1, SEQ, D), lambda i: (i, 0, 0))],
        out_specs=[half, half],
        out_shape=[jax.ShapeDtypeStruct((3 * HALF, D), bf16)] * 2,
        scratch_shapes=[pltpu.VMEM((D, SEQ), bf16)],
        compiler_params=params(),
        cost_estimate=cost(6 * SEQ * D * D, 14 * SEQ * D),
    )(core_here(), normed, gqkv)


def embed_grad_kernel(
    core_ref, g_ref, w_ref, emb_ref, embed_ref, d_stream_ref, seq_ref, mixed_ref, out_w_ref,
    gain_ref, gain_g_ref,
    keep_ref, give_ref, gupd_ref, pool_g_ref, out_g_ref, gox_ref, total_s, *, span, rows
):
    step = pl.program_id(0)
    part = dot_nt(g_ref[0], square(w_ref))

    @pl.when(step == 0)
    def _():
        total_s[...] = part

    @pl.when(step > 0)
    def _():
        total_s[...] += part

    @pl.when(step == pl.num_programs(0) - 1)
    def _():
        d_gain, pulled = pull_norm(total_s[...], embed_ref[...], gain_ref[...])
        gembed = (d_stream_ref[...] + pulled).astype(bf16)
        at = lax.broadcasted_iota(jnp.int32, (CH, D), 0)
        gains = jnp.where(at == 0, d_gain, jnp.where(at == rows, gain_g_ref[...], 0.0))
        for index, values in enumerate((dot_tn(seq_ref[...], gembed), gains)):
            write_cores(core_ref[0], values, keep_ref.at[index], give_ref.at[index], span)
        gseq = dot_nt(gembed, emb_ref[0])
        gupd = gseq[CTX:]
        gb = gupd.astype(bf16)
        pool_g_ref[...] = gseq[:CTX].astype(bf16)
        gupd_ref[...] = gupd
        out_g_ref[...] = dot_tn(mixed_ref[...], gb).astype(bf16)
        gox_ref[...] = dot_nt(gb, out_w_ref[...]).astype(bf16)


def embed_grad(gqkv, weights, embed, d_stream, seq, mixed, to_out, gain, gain_g):
    last = weights.shape[0] - 1
    return pl.pallas_call(
        functools.partial(embed_grad_kernel, span=core_span(), rows=CH // lax.axis_size(AXES)),
        grid=(3,),
        in_specs=[
            CORE_SPEC,
            pl.BlockSpec((1, SEQ, D), lambda i: (i, 0, 0)),
            part_of(0),
            pl.BlockSpec((1, CH, D), lambda i: (last, 0, 0)),
            full(SEQ, D),
            full(SEQ, D),
            full(SEQ, CH),
            full(SEQ - CTX, CH),
            full(CH, CH),
            full(1, D),
            full(1, D),
        ],
        out_specs=[
            full(2, CH // 2, D),
            full(2, CH // 2, D),
            full(SEQ - CTX, CH),
            full(CTX, CH),
            full(CH, CH),
            full(SEQ - CTX, CH),
        ],
        out_shape=[
            jax.ShapeDtypeStruct((2, CH // 2, D), bf16),
            jax.ShapeDtypeStruct((2, CH // 2, D), bf16),
            jax.ShapeDtypeStruct((SEQ - CTX, CH), f32),
            jax.ShapeDtypeStruct((CTX, CH), bf16),
            jax.ShapeDtypeStruct((CH, CH), bf16),
            jax.ShapeDtypeStruct((SEQ - CTX, CH), bf16),
        ],
        scratch_shapes=[pltpu.VMEM((SEQ, D), f32)],
        compiler_params=params(),
        cost_estimate=cost(2 * SEQ * D * (3 * D + 2 * CH), 24 * SEQ * D),
    )(
        core_here(), gqkv, stay(weights), stay(weights), stay(embed), stay(d_stream), stay(seq), stay(mixed), to_out,
        gain, gain_g,
    )


def patch_pick(rows, columns, patch_dim):
    patch = lax.broadcasted_iota(jnp.int32, (rows, columns), patch_dim)
    cell = lax.broadcasted_iota(jnp.int32, (rows, columns), 1 - patch_dim)
    inside = (cell // (PATCH * IMG)) * (IMG // PATCH) + (cell % IMG) // PATCH
    return jnp.where(patch == inside, 1.0 / (PATCH * PATCH), 0.0).astype(bf16)


def image_rows(step, row):
    return pl.ds(pl.multiple_of(step * BLOCK + row * IMG, IMG), BLOCK)


def token_forward_kernel(x_ref, conv_ref, kv_w_ref, slope_ref, hidden_ref, kv_ref, pool_ref):
    step = pl.program_id(0)
    z = jnp.zeros((BLOCK, CH), f32)
    for row in range(3):
        z = z + dot_nn(x_ref[image_rows(step, row), :], conv_ref[row])
    center = x_ref[image_rows(step, 1), CH : 2 * CH].astype(f32)
    gate = 1.0 / (1.0 + jnp.exp(-z))
    hidden = center + z * gate
    slope_ref[...] = (gate * (1.0 + z * (1.0 - gate))).astype(bf16)
    hidden_b = hidden.astype(bf16)
    hidden_ref[...] = hidden_b
    kv_ref[...] = dot_nn(hidden_b, kv_w_ref[...]).astype(bf16)
    rest = (hidden - hidden_b.astype(f32)).astype(bf16)
    pick = patch_pick(pool_ref.shape[0], BLOCK, 0)
    pool_ref[...] = (dot_nn(pick, hidden_b) + dot_nn(pick, rest)).astype(bf16)


def token_forward(wide, conv_rows, kv_weight):
    steps = CELLS // BLOCK
    whole = lambda i: (0, 0)
    block = lambda i: (i, 0)
    return pl.pallas_call(
        token_forward_kernel,
        grid=(steps,),
        in_specs=[
            pl.BlockSpec(wide.shape, whole),
            pl.BlockSpec((3, 3 * CH, CH), lambda i: (0, 0, 0)),
            pl.BlockSpec((CH, 2 * CH), whole),
        ],
        out_specs=[
            pl.BlockSpec((BLOCK, CH), block),
            pl.BlockSpec((BLOCK, CH), block),
            pl.BlockSpec((BLOCK, 2 * CH), block),
            pl.BlockSpec((CTX // steps, CH), block),
        ],
        out_shape=[
            lasting((CELLS, CH), bf16),
            lasting((CELLS, CH), bf16),
            jax.ShapeDtypeStruct((CELLS, 2 * CH), bf16),
            jax.ShapeDtypeStruct((CTX, CH), bf16),
        ],
        compiler_params=params(),
        cost_estimate=cost(22 * CELLS * CH * CH, 14 * CELLS * CH, CELLS * CH),
    )(stay(wide), conv_rows, kv_weight)


def token_backward_kernel(
    core_ref, dkv_ref, slope_ref, pool_ref, hidden_ref, x_ref, kv_w_ref, query_g_ref, out_g_ref,
    d_hidden_ref, gz_ref, keep_ref, give_ref, conv_s, kv_s, *, span
):
    step = pl.program_id(0)

    @pl.when(step == 0)
    def _():
        conv_s[...] = jnp.zeros_like(conv_s)
        kv_s[...] = jnp.zeros_like(kv_s)

    dkv = dkv_ref[...]
    d_hidden = dot_nt(dkv, kv_w_ref[...])
    d_hidden = d_hidden + dot_nn(patch_pick(BLOCK, pool_ref.shape[0], 1), pool_ref[...])
    gz = (d_hidden * slope_ref[...].astype(f32)).astype(bf16)
    d_hidden_ref[...] = d_hidden
    gz_ref[...] = gz
    kv_s[...] += dot_tn(hidden_ref[...], dkv)
    gz_t = gz.T
    for row in range(3):
        conv_s[row] += dot_nn(gz_t, x_ref[image_rows(step, row), :])

    @pl.when(step == pl.num_programs(0) - 1)
    def _():
        tiles = []
        for row in range(3):
            for col in range(3):
                tiles.append(conv_s[row, :, col * CH : (col + 1) * CH].T)
        tiles = tiles + [query_g_ref[...], kv_s[:, :CH], kv_s[:, CH:], out_g_ref[...]]
        for at, tile in enumerate(tiles):
            write_cores(core_ref[0], tile.astype(f32), keep_ref.at[at], give_ref.at[at], span)


def token_backward(dkv, slope, d_pool, hidden_b, wide, kv_weight, query_g, out_g):
    steps = CELLS // BLOCK
    whole = lambda i: (0, 0)
    whole_3 = lambda i: (0, 0, 0)
    block = lambda i: (i, 0)
    return pl.pallas_call(
        functools.partial(token_backward_kernel, span=core_span()),
        grid=(steps,),
        in_specs=[
            CORE_SPEC,
            pl.BlockSpec((BLOCK, 2 * CH), block),
            pl.BlockSpec((BLOCK, CH), block),
            pl.BlockSpec((CTX // steps, CH), block),
            pl.BlockSpec((BLOCK, CH), block),
            pl.BlockSpec(wide.shape, whole),
            pl.BlockSpec((CH, 2 * CH), whole),
            pl.BlockSpec((CH, CH), whole),
            pl.BlockSpec((CH, CH), whole),
        ],
        out_specs=[
            pl.BlockSpec((BLOCK, CH), block),
            pl.BlockSpec((BLOCK, CH), block),
            pl.BlockSpec((EARLY, CH // 2, CH), whole_3),
            pl.BlockSpec((EARLY, CH // 2, CH), whole_3),
        ],
        out_shape=[
            jax.ShapeDtypeStruct((CELLS, CH), f32),
            jax.ShapeDtypeStruct((CELLS, CH), bf16),
            jax.ShapeDtypeStruct((EARLY, CH // 2, CH), bf16),
            jax.ShapeDtypeStruct((EARLY, CH // 2, CH), bf16),
        ],
        scratch_shapes=[pltpu.VMEM((3, CH, 3 * CH), f32), pltpu.VMEM((CH, 2 * CH), f32)],
        compiler_params=params(),
        cost_estimate=cost(26 * CELLS * CH * CH, 20 * CELLS * CH),
    )(core_here(), dkv, stay(slope), d_pool, stay(hidden_b), stay(wide), kv_weight, query_g, out_g)


def context_backward_kernel(gz_ref, d_hidden_ref, conv_ref, out_ref, wide_s):
    step = pl.program_id(0)
    steps = pl.num_programs(0)

    def widen(at):
        values = gz_ref[image_rows(at, 0), :].astype(f32)
        col = lax.broadcasted_iota(jnp.int32, (BLOCK, CH), 0) % IMG
        left = jnp.where(col == 0, 0.0, pltpu.roll(values, 1, 0))
        right = jnp.where(col == IMG - 1, 0.0, pltpu.roll(values, BLOCK - 1, 0))
        wide_s[image_rows(at, 1), 0:CH] = left.astype(bf16)
        wide_s[image_rows(at, 1), CH : 2 * CH] = values.astype(bf16)
        wide_s[image_rows(at, 1), 2 * CH :] = right.astype(bf16)

    @pl.when(step == 0)
    def _():
        wide_s[0:IMG, :] = jnp.zeros((IMG, 3 * CH), bf16)
        wide_s[CELLS + IMG :, :] = jnp.zeros((IMG, 3 * CH), bf16)
        widen(0)

    @pl.when(step < steps - 1)
    def _():
        widen(step + 1)

    total = d_hidden_ref[...]
    for row in range(3):
        values = wide_s[image_rows(step, row), :]
        for col in range(3):
            tap = conv_ref[3 * (2 - row) + (2 - col)]
            total = total + dot_nt(values[:, col * CH : (col + 1) * CH], tap)
    out_ref[...] = total.astype(bf16)


def context_backward(gz, d_hidden, conv_tiles):
    block = lambda i: (i, 0)
    return pl.pallas_call(
        context_backward_kernel,
        grid=(CELLS // BLOCK,),
        in_specs=[
            pl.BlockSpec((CELLS, CH), lambda i: (0, 0)),
            pl.BlockSpec((BLOCK, CH), block),
            pl.BlockSpec((9, CH, CH), lambda i: (0, 0, 0)),
        ],
        out_specs=pl.BlockSpec((BLOCK, CH), block),
        out_shape=jax.ShapeDtypeStruct((CELLS, CH), bf16),
        scratch_shapes=[pltpu.VMEM((CELLS + 2 * IMG, 3 * CH), bf16)],
        compiler_params=params(),
        cost_estimate=cost(18 * CELLS * CH * CH, 8 * CELLS * CH),
    )(gz, d_hidden, conv_tiles)


def local(
    context_map,
    future_feats,
    horizon,
    cotangent,
    tile_owner,
    master_tiles,
    moment_first,
    moment_second,
    norm_gains,
    gain_first,
    gain_second,
):
    slot_count = master_tiles.shape[0]
    devices = lax.axis_size(AXES)
    rows = CH // devices
    slot_of = slot_index(tile_owner, slot_count)

    length = CTX + FT * horizon
    valid = jnp.arange(SEQ) < length[0]
    gd = jnp.where(valid[:, None], cotangent[0], jnp.zeros((), bf16))

    slices = (
        master_tiles.astype(bf16)
        .reshape(slot_count, devices, rows, CH)
        .transpose(1, 0, 2, 3)
    )
    slices = lax.all_to_all(slices, AXES, split_axis=0, concat_axis=0, tiled=True)
    slices, gd = tie((slices, gd))
    slices = slices.reshape(devices * slot_count, rows, CH)
    slices = slices.at[slot_of].get(mode="promise_in_bounds")
    early, emb, qkv, att, up, down = jnp.split(slices, (13, 16, 43, 52, 88))
    mlp = jnp.concatenate([from_tiles(up, 3, 4), from_tiles(down, 12, 1)], 0)
    mlp = lax.all_gather(mlp, AXES, axis=1, tiled=True)
    early = gather_axes(early, "z")
    core = jnp.concatenate([from_tiles(qkv, 3, 3), from_tiles(att, 3, 1), from_tiles(emb, 1, 1)], 0)
    core, early = tie((core, early))
    early = gather_axes(joined(early), ("y", "x"))
    core = gather_axes(core, "z")
    pieces = trade_rows(context_map)
    early = joined(gather_axes(joined(early), "c"))
    early = device_order(early, ("c", "y", "x", "z"))
    wide = widen(pieces)
    core = joined(core)
    low, high = gather_axes(core[:6], "x"), gather_axes(core[6:], "y")

    conv_tiles = early[:9]
    to_query, to_out = early[9], early[12]
    kv_weight = jnp.concatenate([early[10], early[11]], 1)

    wide, low, high = hold((wide,), low, high)
    low, high = joined(low), joined(high)
    wide, low, high = tie((wide, low, high))
    low, high = gather_axes(low, "y"), gather_axes(high, "x")
    slope_z, hidden_b, kv, pooled = token_forward(
        wide, conv_tiles.reshape(3, 3 * CH, CH), kv_weight
    )
    kv, low, high = hold((kv,), low, high)
    low, high = joined(low), joined(high)
    feats_b = future_feats[0]
    query = jnp.dot(feats_b, to_query, preferred_element_type=f32).astype(bf16)
    kv, low, high = tie((kv, low, high))
    low, high = gather_axes(low, "c"), gather_axes(high, "c")
    cross_mixed, cross_logs = cross_forward(query, kv)
    cross_mixed, low, high = hold((cross_mixed,), low, high)
    weights = place_rows(low, high)

    gain_one, gain_two = norm_gains[:1], norm_gains[1:]
    seq, embed, normed_one, qkv = embed_forward(
        pooled, feats_b, cross_mixed, to_out, weights, gain_one
    )
    mixed, logs = self_forward(qkv, length)
    (
        block_out, d_stream, gog, up_keep, up_give, down_keep, down_give, att_keep, att_give,
        gain_g_two,
    ) = mlp_block(mixed, embed, weights, mlp, gain_two, gd)
    gog, up, down, att = tie(
        (
            gog,
            core_parts([up_keep, up_give]),
            core_parts([down_keep, down_give]),
            core_parts([att_keep, att_give]),
        )
    )
    up, down, att = send(up, "c"), send(down, "c"), send(att, "c")
    gqkv = self_backward(qkv, gog, mixed, logs, length)
    gqkv, up, down, att = hold((gqkv,), up, down, att)
    up, down = advance(up, "y", 2), advance(down, "x", 3)
    gqkv, up, down = tie((gqkv, up, down))
    up, down = send(up, "y"), send(down, "x")
    qkv_keep, qkv_give = qkv_grad(normed_one, gqkv)
    gqkv, qkv_keep, qkv_give = tie((gqkv, qkv_keep, qkv_give))
    qkv = send(core_parts([qkv_keep, qkv_give]), "c")
    emb_keep, emb_give, gupd, pool_g, out_g, gox = embed_grad(
        gqkv, weights, embed, d_stream, seq, cross_mixed, to_out, gain_one, gain_g_two
    )
    gox, gupd, emb_keep, emb_give, qkv, up, down = hold(
        (gox, gupd, emb_keep, emb_give), qkv, up, down
    )
    up, down = advance(up, "x", 2), advance(down, "y", 2)
    first = advance([part[:6] for part in qkv], "x", 3)
    second = advance([jnp.concatenate([p[6:], q], 0) for p, q in zip(qkv, att)], "y", 2)
    emb = core_parts([emb_keep, emb_give])
    gox, up, down, first, second, emb = tie((gox, up, down, first, second, emb))
    up, down, emb = send(up, "x"), send(down, "y"), send(emb, "c")
    first, second = send(first, "x"), send(second, "y")

    log_rows = jnp.concatenate([cross_logs[0], cross_logs[1]], 1)
    gkv, query_g, future_grad = cross_backward(
        query, kv, gox, cross_mixed, log_rows, feats_b, gupd, to_query
    )
    gkv, up, down, first, second, emb = hold((gkv,), up, down, first, second, emb)
    mlp = advance_near([jnp.concatenate(part, 0) for part in zip(up, down)])
    emb = advance(emb, "x", 3)
    first, second = advance(first, "y", 2), advance(second, "x", 2)
    gkv, mlp, first, second, emb = tie((gkv, mlp, first, second, emb))
    mlp, emb = send(mlp, "z"), send(emb, "x")
    first, second = send(first, "y"), send(second, "x")

    d_hidden, gz, early_keep, early_give = token_backward(
        gkv, slope_z, pool_g, hidden_b, wide, kv_weight, query_g, out_g
    )
    d_hidden, gz, early_keep, early_give, mlp, first, second, emb = hold(
        (d_hidden, gz, early_keep, early_give), mlp, first, second, emb
    )
    early = core_parts([early_keep, early_give])
    early, mlp, first, second, emb = tie((early, mlp, first, second, emb))
    early = send(early, "c")
    att = advance_near([jnp.concatenate(part, 0) for part in zip(first, second)])
    emb, mlp = advance(emb, "y", 2), advance_far(mlp)
    att, emb, mlp = send(att, "z"), send(emb, "y"), send(mlp, "z", 2)
    gz, early, att, emb = hold((gz,), early, att, emb)
    shape = early[0].shape
    early = advance([p.reshape(shape[:2] + (-1,) + shape[4:]) for p in early], ("y", "x"), 2)
    att = advance_far(att)
    gz, early, att = tie((gz, early, att))
    early, att = send(early, ("y", "x")), send(att, "z", 2)
    context_grad = context_backward(gz, d_hidden, conv_tiles)
    context_grad, early, att, mlp = hold((context_grad,), early, att, mlp)
    early = advance(early, "z", 1)
    emb = advance(emb, "z", 1)
    early = [jnp.concatenate([e, to_tiles(m)], 0) for e, m in zip(early, emb)]
    context_grad, early = tie((context_grad, early))
    early = send(early, "z")
    pieces = trade_rows(context_grad.reshape(context_map.shape))
    sum_mlp = add_up(mlp, keep_wide=True)
    square_mlp = jnp.sum(sum_mlp * sum_mlp)
    half = sum_mlp.shape[0] // 2
    mlp = jnp.concatenate([to_tiles(sum_mlp[:half], 4), to_tiles(sum_mlp[half:])], 0).astype(bf16)
    sum_early = add_up(early, keep_wide=True)
    sum_att = add_up(att, keep_wide=True)

    gains = sum_early[EARLY + 3 :, 0]
    square = square_mlp + jnp.sum(sum_att * sum_att) + jnp.sum(sum_early * sum_early)
    share = jnp.concatenate([gains, jnp.broadcast_to(square, (1, CH))], 0)
    share_high = share.astype(bf16)
    share_low = (share - share_high.astype(f32)).astype(bf16)
    share = jnp.concatenate([share_high, share_low], 0)
    extra = max(1, share.shape[0] // rows)
    share = jnp.pad(share, ((0, extra * rows - share.shape[0]), (0, 0)))
    sums = jnp.concatenate(
        [
            sum_early[: EARLY + 3].astype(bf16),
            to_tiles(sum_att[:9], 3).astype(bf16),
            to_tiles(sum_att[9:]).astype(bf16),
            mlp,
            share.reshape(extra, rows, CH),
        ],
        0,
    )
    slots = jnp.arange(devices * slot_count)
    found = slot_of[None, :] == slots[:, None]
    tiles = found.shape[1]
    tile_of = jnp.sum(jnp.where(found, jnp.arange(tiles)[None], 0), 1)
    tile_of = tile_of.reshape(devices, slot_count)
    shared = jnp.broadcast_to(tiles + jnp.arange(extra)[None], (devices, extra))
    tile_of = jnp.concatenate([tile_of, shared], 1).reshape(-1)
    mine = sums.at[tile_of].get(mode="promise_in_bounds")
    mine = mine.reshape(devices, slot_count + extra, rows, CH)
    mine, pieces[-1] = tie((mine, pieces[-1]))
    mine = lax.all_to_all(mine, AXES, split_axis=0, concat_axis=0, tiled=True)
    shares = mine[:, slot_count:].reshape(devices, -1, CH).astype(f32)
    shares = shares[:, :4] + shares[:, 4:8]
    gains = shares[:2, :3].reshape(2, D)
    mine = mine[:, :slot_count].transpose(1, 0, 2, 3).reshape(slot_count, CH, CH).astype(f32)

    used = jnp.any(found, 1).astype(f32).reshape(devices, slot_count)
    used = lax.dynamic_index_in_dim(used, lax.axis_index(AXES), 0, keepdims=False)[:, None, None]
    grad_norm = jnp.sqrt(jnp.sum(shares[:, 3, 0]))
    factor = jnp.minimum(1.0, clip_level / (grad_norm + 1e-06))
    new_first, new_second, new_master = adam_step(
        master_tiles, mine * factor, moment_first, moment_second, learn_rate, decay_rate
    )
    new_gain_first, new_gain_second, new_gains = adam_step(
        norm_gains, gains * factor, gain_first, gain_second, gain_rate, 0.0
    )
    return (
        block_out[None],
        row_order(pieces).reshape(context_map.shape),
        future_grad[None],
        jnp.where(used > 0, new_first, 0.0),
        jnp.where(used > 0, new_second, 0.0),
        jnp.where(used > 0, new_master, 0.0),
        new_gain_first,
        new_gain_second,
        new_gains,
        grad_norm,
    )


def solution(mesh):
    groups, rows = mesh.devices.shape
    fine = jax.sharding.Mesh(mesh.devices.reshape(groups // 2, 2, rows // 2, 2), AXES)
    whole = P(AXES, None, None)
    image = P(("z", "c"), ("y", "x"), None, None)
    in_specs = (image, whole, P(AXES), whole, P(), whole, whole, whole, P(), P(), P())
    out_specs = (whole, image, whole, whole, whole, whole, P(), P(), P(), P())
    return jax.shard_map(local, mesh=fine, in_specs=in_specs, out_specs=out_specs, check_vma=False)
```

```python
import functools

import jax
import jax.numpy as jnp
from jax import lax
from jax.experimental import pallas as pl
from jax.experimental.pallas import tpu as pltpu
from jax.sharding import PartitionSpec as P

CH = 256
HD = 64
HEADS = 12
D = 768
FF = 3072
TH = 4
IMG = 64
PATCH = 4
FT = 16
CTX = 256
SEQ = 736
STEP = 10


eps_norm = 1e-05
beta_one = 0.9
beta_two = 0.999
learn_rate = 0.02
gain_rate = 0.6
decay_rate = 0.1
adam_eps = 1e-08
clip_level = 1.0
neg_large = -1e30
AXES = ("z", "c", "y", "x")
CELLS = IMG * IMG
BLOCK = 512
GROUP = 4
EARLY = 13
VMEM_BYTES = 28 * 1024 * 1024
MLP_BYTES = 44 * 1024 * 1024
ROW_BLOCKS = ((0, 256), (256, 256), (512, 224))
CORE_SPEC = pl.BlockSpec(memory_space=pltpu.SMEM)
bf16 = jnp.bfloat16
f32 = jnp.float32


def slot_index(tile_owner, slot_count):
    ordinal = jnp.arange(tile_owner.shape[0])
    earlier = (tile_owner[None, :] == tile_owner[:, None]) & (ordinal[None, :] < ordinal[:, None])
    return tile_owner * slot_count + jnp.sum(earlier.astype(jnp.int32), 1)


def adam_step(weight, grad_now, first, second, rate, decay):
    first_new = beta_one * first + (1.0 - beta_one) * grad_now
    second_new = beta_two * second + (1.0 - beta_two) * grad_now * grad_now
    corr_first = first_new / (1.0 - beta_one**STEP)
    corr_second = second_new / (1.0 - beta_two**STEP)
    weight_new = weight - rate * (corr_first / (jnp.sqrt(corr_second) + adam_eps) + decay * weight)
    return (first_new, second_new, weight_new)


def xor_permute(values, axes, mask):
    count = lax.axis_size(axes)
    return lax.ppermute(values, axes, [(i, i ^ mask) for i in range(count)])


def pick(parts, index, dim):
    if parts[0].shape[dim] == 2:
        total = add_up(parts)
        first, second = (lax.index_in_dim(total, at, dim, False) for at in range(2))
        return jnp.where(index == 0, first, second)
    return add_up([lax.dynamic_index_in_dim(part, index, dim, False) for part in parts])


def advance(parts, axes, dim):
    mine = lax.axis_index(axes)
    return [pick(parts, mine ^ mask, dim) for mask in range(lax.axis_size(axes))]


def advance_near(parts):
    mine = lax.axis_index("z") % 2
    shape = parts[0].shape
    parts = [p.reshape((shape[0], shape[1] // 2, 2) + shape[2:]) for p in parts]
    return [pick(parts, mine ^ mask, 2) for mask in range(2)]


def advance_far(parts):
    mine = lax.axis_index("z") // 2
    return [pick(parts, mine ^ mask, 1) for mask in range(parts[0].shape[1])]


def send(cuts, axes, unit=1):
    return [cuts[0]] + [
        xor_permute(cut, axes, unit * mask) for mask, cut in enumerate(cuts) if mask > 0
    ]


def add_up(parts, keep_wide=False):
    total = parts[0].astype(f32)
    for part in parts[1:]:
        total = total + part.astype(f32)
    return total if keep_wide else total.astype(parts[0].dtype)


def hold(values, *sums):
    tied = lax.optimization_barrier((tuple(values), tuple(tuple(parts) for parts in sums)))
    return tied[0] + tuple(list(parts) for parts in tied[1])


def gather_axes(values, axes):
    return [values] + [
        xor_permute(values, axes, mask) for mask in range(1, lax.axis_size(axes))
    ]


def joined(pieces):
    return jnp.stack(pieces, 1)


def device_order(values, axes):
    sizes = [lax.axis_size(axis) for axis in AXES]
    own = [lax.axis_index(axis) for axis in AXES]
    places = jnp.unravel_index(jnp.arange(lax.axis_size(AXES)), sizes)
    at = 0
    for axis in axes:
        which = AXES.index(axis)
        at = at * sizes[which] + (places[which] ^ own[which])
    values = values.reshape((values.shape[0], -1) + values.shape[-2:])
    values = values.at[:, at].get(mode="promise_in_bounds")
    return values.reshape(values.shape[0], -1, values.shape[-1])


def place_kernel(own_ref, low_ref, low_other_ref, high_ref, high_other_ref, out_ref, *, half, sizes):
    z_count, c_count, y_count, x_count = sizes
    own_z, own_c, own_y, own_x = (own_ref[axis] for axis in range(4))
    step = pl.program_id(0)

    def place(near_ref, far_ref, x_first):
        for z in range(z_count):
            for y in range(y_count):
                for x in range(x_count):
                    if x_first:
                        at = (x ^ own_x) * y_count + (y ^ own_y)
                    else:
                        at = (y ^ own_y) * x_count + (x ^ own_x)
                    at = at * z_count + (z ^ own_z)
                    near, far = near_ref[0, at], far_ref[0, at]
                    for c in range(c_count):
                        to = ((z * c_count + c) * y_count + y) * x_count + x
                        out_ref[0, to] = jnp.where(own_c == c, near, far)

    @pl.when(step < half)
    def _():
        place(low_ref, low_other_ref, False)

    @pl.when(step >= half)
    def _():
        place(high_ref, high_other_ref, True)


def place_rows(low, high):
    sizes = tuple(lax.axis_size(axis) for axis in AXES)
    half, rows = low[0].shape[0], low[0].shape[-2]
    count = half + high[0].shape[0]
    own = jnp.stack([lax.axis_index(axis) for axis in AXES]).astype(jnp.int32)
    pieces = [part.reshape(part.shape[0], -1, rows, D) for part in low + high]
    block = (1,) + pieces[0].shape[1:]
    early = pl.BlockSpec(block, lambda i: (jnp.minimum(i, half - 1), 0, 0, 0))
    later = pl.BlockSpec(block, lambda i: (jnp.maximum(i - half, 0), 0, 0, 0))
    devices = CH // rows
    out = pl.pallas_call(
        functools.partial(place_kernel, half=half, sizes=sizes),
        grid=(count,),
        in_specs=[CORE_SPEC, early, early, later, later],
        out_specs=pl.BlockSpec((1, devices, rows, D), lambda i: (i, 0, 0, 0)),
        out_shape=jax.ShapeDtypeStruct((count, devices, rows, D), bf16),
        compiler_params=params(),
        cost_estimate=cost(0, 4 * count * CH * D),
    )(own, *pieces)
    return out.reshape(count, CH, D)


def trade_rows(values):
    mine = lax.axis_index(("y", "x"))
    count = lax.axis_size(("y", "x"))
    cuts = [lax.dynamic_index_in_dim(values, mine ^ mask, 0, False) for mask in range(count)]
    return send(cuts, ("y", "x"))


def row_order_kernel(row_ref, *refs):
    at = pl.program_id(0) ^ row_ref[0]
    values = refs[0][...]
    for mask in range(1, len(refs) - 1):
        values = jnp.where(at == mask, refs[mask][...], values)
    refs[-1][0] = values.astype(f32)


def row_order(pieces):
    count = len(pieces)
    cells = pieces[0].size // CH
    return pl.pallas_call(
        row_order_kernel,
        grid=(count,),
        in_specs=[CORE_SPEC] + [pl.BlockSpec((cells, CH), lambda i: (0, 0))] * count,
        out_specs=pl.BlockSpec((1, cells, CH), lambda i: (i, 0, 0)),
        out_shape=jax.ShapeDtypeStruct((count, cells, CH), f32),
        compiler_params=params(),
        cost_estimate=cost(0, 6 * count * cells * CH),
    )(row_here(), *[piece.reshape(cells, CH) for piece in pieces])


def widen_kernel(row_ref, *refs):
    out_ref = refs[-1]
    cells = refs[0].shape[0]
    col = lax.broadcasted_iota(jnp.int32, (cells, CH), 0) % IMG
    out_ref[0:IMG, :] = jnp.zeros((IMG, 3 * CH), bf16)
    out_ref[CELLS + IMG :, :] = jnp.zeros((IMG, 3 * CH), bf16)
    for at in range(len(refs) - 1):
        values = refs[at][...]
        for mask in range(1, len(refs) - 1):
            values = jnp.where(row_ref[0] == mask, refs[at ^ mask][...], values)
        here = slice(IMG + at * cells, IMG + (at + 1) * cells)
        out_ref[here, CH : 2 * CH] = values
        values = values.astype(f32)
        left = jnp.where(col == 0, 0.0, pltpu.roll(values, 1, 0))
        right = jnp.where(col == IMG - 1, 0.0, pltpu.roll(values, cells - 1, 0))
        out_ref[here, 0:CH] = left.astype(bf16)
        out_ref[here, 2 * CH :] = right.astype(bf16)


def widen(pieces):
    cells = pieces[0].size // CH
    vmem = pl.BlockSpec(memory_space=pltpu.VMEM)
    return pl.pallas_call(
        widen_kernel,
        in_specs=[CORE_SPEC] + [vmem] * len(pieces),
        out_specs=vmem,
        out_shape=lasting((CELLS + 2 * IMG, 3 * CH), bf16),
        compiler_params=params(),
        cost_estimate=cost(0, 8 * CELLS * CH),
    )(row_here(), *[piece.reshape(cells, CH) for piece in pieces])


def slice_shape():
    z, c, y, x = [lax.axis_size(axis) for axis in AXES]
    return (z, y, x, CH // (z * c * y * x))


tie = lax.optimization_barrier


def to_tiles(slices, parts=1):
    blocks, rows, columns = slices.shape
    return (
        slices.reshape(parts, blocks // parts, rows, columns // CH, CH)
        .transpose(1, 0, 3, 2, 4)
        .reshape(-1, rows, CH)
    )


def from_tiles(tiles, row_blocks, parts):
    rows = tiles.shape[1]
    return (
        tiles.reshape(row_blocks, parts, D // CH, rows, CH)
        .transpose(1, 0, 3, 2, 4)
        .reshape(parts * row_blocks, rows, D)
    )


def dot_nt(a, b):
    return lax.dot_general(a, b, (((1,), (1,)), ((), ())), preferred_element_type=f32)


def dot_nn(a, b):
    return lax.dot_general(a, b, (((1,), (0,)), ((), ())), preferred_element_type=f32)


def dot_tn(a, b):
    return lax.dot_general(a, b, (((0,), (0,)), ((), ())), preferred_element_type=f32)


def head_mask(shape, head):
    return (lax.broadcasted_iota(jnp.int32, shape, len(shape) - 1) // HD) == head


def cost(flops, moved, transcendentals=0):
    return pl.CostEstimate(
        flops=int(flops), bytes_accessed=int(moved), transcendentals=int(transcendentals)
    )


def stay(values):
    return pltpu.with_memory_space_constraint(values, pltpu.HBM)


lasting = pltpu.HBM


def params():
    return pltpu.CompilerParams(vmem_limit_bytes=VMEM_BYTES)


def cross_forward_kernel(q_ref, k_ref, v_ref, o_ref, l_ref):
    rows = q_ref.shape[0]
    lane = lax.broadcasted_iota(jnp.int32, (rows, 128), 1)
    q = q_ref[...]
    mixed = jnp.zeros((rows, CH), f32)
    stat = jnp.zeros((rows, 128), f32)
    for head in range(TH):
        mask = head_mask((rows, CH), head)
        q_head = jnp.where(mask, q.astype(f32) * 0.125, 0.0).astype(bf16)
        scores = dot_nt(q_head, k_ref[...])
        peak = jnp.max(scores, -1, keepdims=True)
        shifted = jnp.exp(scores - peak)
        total = jnp.sum(shifted, -1, keepdims=True)
        part = dot_nn(shifted.astype(bf16), v_ref[...])
        mixed = jnp.where(mask, part / total, mixed)
        stat = jnp.where(lane == head, peak + jnp.log(total), stat)
    o_ref[...] = mixed.astype(bf16)
    l_ref[0] = stat.T[:8]


def cross_forward(query, kv):
    rows = query.shape[0] // 2
    cells = kv.shape[0]
    return pl.pallas_call(
        cross_forward_kernel,
        grid=(2,),
        in_specs=[
            pl.BlockSpec((rows, CH), lambda i: (i, 0)),
            pl.BlockSpec((cells, CH), lambda i: (0, 0)),
            pl.BlockSpec((cells, CH), lambda i: (0, 1)),
        ],
        out_specs=[
            pl.BlockSpec((rows, CH), lambda i: (i, 0)),
            pl.BlockSpec((1, 8, rows), lambda i: (i, 0, 0)),
        ],
        out_shape=[
            jax.ShapeDtypeStruct((2 * rows, CH), bf16),
            jax.ShapeDtypeStruct((2, 8, rows), f32),
        ],
        compiler_params=params(),
        cost_estimate=cost(16 * TH * rows * cells * CH // 2, 8 * cells * CH, 2 * TH * rows * cells),
    )(query, kv, kv)


def delta_rows(d_out, out):
    product = d_out.astype(f32) * out.astype(f32)
    head = lax.broadcasted_iota(jnp.int32, (8, CH), 0)
    lane = lax.broadcasted_iota(jnp.int32, (8, CH), 1)
    pick = ((lane // HD) == head).astype(f32)
    return lax.dot_general(
        pick,
        product,
        (((1,), (1,)), ((), ())),
        precision=lax.Precision.HIGHEST,
        preferred_element_type=f32,
    )


def cross_backward_kernel(
    q_ref, k_ref, v_ref, do_ref, o_ref, l_ref, feats_ref, gupd_ref, query_w_ref,
    dkv_ref, query_g_ref, future_ref, q_s, do_s, delta_s, dq_s,
):
    step = pl.program_id(0)
    rows = q_ref.shape[0]

    @pl.when(step == 0)
    def _():
        for head in range(TH):
            mask = head_mask((rows, CH), head)
            q_s[head] = jnp.where(mask, q_ref[...].astype(f32) * 0.125, 0.0).astype(bf16)
            do_s[head] = jnp.where(mask, do_ref[...].astype(f32), 0.0).astype(bf16)
        delta_s[...] = delta_rows(do_ref[...], o_ref[...])
        dq_s[...] = jnp.zeros_like(dq_s)

    cells = k_ref.shape[0]
    dk = jnp.zeros((cells, CH), f32)
    dv = jnp.zeros((cells, CH), f32)
    dq = dq_s[...]
    k = k_ref[...]
    for head in range(TH):
        probs = jnp.exp(dot_nt(k, q_s[head]) - l_ref[head : head + 1, :])
        d_probs = dot_nt(v_ref[...], do_s[head])
        d_scores = (probs * (d_probs - delta_s[head : head + 1, :])).astype(bf16)
        dv = dv + dot_nn(probs.astype(bf16), do_s[head])
        dk = dk + dot_nn(d_scores, q_s[head])
        dq = dq + jnp.where(head_mask((rows, CH), head), dot_tn(d_scores, k), 0.0)
    dq_s[...] = dq
    dkv_ref[:, :CH] = dk.astype(bf16)
    dkv_ref[:, CH:] = dv.astype(bf16)

    @pl.when(step == pl.num_programs(0) - 1)
    def _():
        gq = (dq_s[...] * 0.125).astype(bf16)
        query_g_ref[...] = dot_tn(feats_ref[...], gq).astype(bf16)
        future_ref[...] = gupd_ref[...] + dot_nt(gq, query_w_ref[...])


def cross_backward(query, kv, d_out, out, log_rows, feats, gupd, to_query):
    rows = query.shape[0]
    cells = kv.shape[0]
    block = 1024
    whole = lambda i: (0, 0)
    return pl.pallas_call(
        cross_backward_kernel,
        grid=(cells // block,),
        in_specs=[
            pl.BlockSpec((rows, CH), whole),
            pl.BlockSpec((block, CH), lambda i: (i, 0)),
            pl.BlockSpec((block, CH), lambda i: (i, 1)),
            pl.BlockSpec((rows, CH), whole),
            pl.BlockSpec((rows, CH), whole),
            pl.BlockSpec((8, rows), whole),
            pl.BlockSpec((rows, CH), whole),
            pl.BlockSpec((rows, CH), whole),
            pl.BlockSpec((CH, CH), whole),
        ],
        out_specs=[
            pl.BlockSpec((block, 2 * CH), lambda i: (i, 0)),
            pl.BlockSpec((CH, CH), whole),
            pl.BlockSpec((rows, CH), whole),
        ],
        out_shape=[
            jax.ShapeDtypeStruct((cells, 2 * CH), bf16),
            jax.ShapeDtypeStruct((CH, CH), bf16),
            jax.ShapeDtypeStruct((rows, CH), f32),
        ],
        scratch_shapes=[
            pltpu.VMEM((TH, rows, CH), bf16),
            pltpu.VMEM((TH, rows, CH), bf16),
            pltpu.VMEM((8, rows), f32),
            pltpu.VMEM((rows, CH), f32),
        ],
        compiler_params=params(),
        cost_estimate=cost(10 * TH * rows * cells * CH, 8 * cells * CH, TH * rows * cells),
    )(query, kv, kv, d_out, out, log_rows, feats, gupd, to_query)


def self_forward_kernel(len_ref, q_ref, k_ref, v_ref, o_ref, l_ref):
    group = pl.program_id(0)
    length = len_ref[0]
    for start, count in ROW_BLOCKS:
        stop = start + count
        q = q_ref[0, start:stop, :].astype(f32) * 0.125
        row = lax.broadcasted_iota(jnp.int32, (count, 1), 0) + start
        bound = jnp.minimum(row, length - 1)
        allowed = lax.broadcasted_iota(jnp.int32, (count, stop), 1) <= bound
        mixed = jnp.zeros((count, CH), f32)
        stat = jnp.zeros((count, 128), f32)
        lane = lax.broadcasted_iota(jnp.int32, (count, 128), 1)
        for head in range(GROUP):
            mask = head_mask((count, CH), head)
            q_head = jnp.where(mask, q, 0.0).astype(bf16)
            scores = jnp.where(allowed, dot_nt(q_head, k_ref[0, :stop, :]), neg_large)
            peak = jnp.max(scores, -1, keepdims=True)
            shifted = jnp.exp(scores - peak)
            total = jnp.sum(shifted, -1, keepdims=True)
            part = dot_nn(shifted.astype(bf16), v_ref[0, :stop, :])
            mixed = jnp.where(mask, part / total, mixed)
            stat = jnp.where(lane == head, peak + jnp.log(total), stat)
        o_ref[start:stop, :] = mixed.astype(bf16)
        l_ref[0, :, start:stop] = stat.T[:8]


def self_forward(qkv, length):
    groups = D // CH
    at = lambda j: (lambda i, n: (j, 0, i))
    return pl.pallas_call(
        self_forward_kernel,
        grid_spec=pltpu.PrefetchScalarGridSpec(
            num_scalar_prefetch=1,
            grid=(groups,),
            in_specs=[pl.BlockSpec((1, SEQ, CH), at(j)) for j in range(3)],
            out_specs=[
                pl.BlockSpec((SEQ, CH), lambda i, n: (0, i)),
                pl.BlockSpec((1, 8, SEQ), lambda i, n: (i, 0, 0)),
            ],
        ),
        out_shape=[
            jax.ShapeDtypeStruct((SEQ, D), bf16),
            jax.ShapeDtypeStruct((groups, 8, SEQ), f32),
        ],
        compiler_params=params(),
        cost_estimate=cost(4 * HEADS * SEQ * SEQ * CH, 8 * SEQ * D, HEADS * SEQ * SEQ),
    )(length, qkv, qkv, qkv)


def self_backward_kernel(
    len_ref, q_ref, k_ref, v_ref, do_ref, o_ref, l_ref, out_ref, dk_s, dv_s
):
    length = len_ref[0]
    dk_s[...] = jnp.zeros_like(dk_s)
    dv_s[...] = jnp.zeros_like(dv_s)
    delta = delta_rows(do_ref[...], o_ref[...])
    for start, count in ROW_BLOCKS:
        stop = start + count
        q = q_ref[0, start:stop, :].astype(f32) * 0.125
        d_out = do_ref[start:stop, :].astype(f32)
        row = lax.broadcasted_iota(jnp.int32, (1, count), 1) + start
        bound = jnp.minimum(row, length - 1)
        allowed = lax.broadcasted_iota(jnp.int32, (stop, count), 0) <= bound
        dq = jnp.zeros((count, CH), f32)
        k = k_ref[0, :stop, :]
        v = v_ref[0, :stop, :]
        dk = dk_s[:stop, :]
        dv = dv_s[:stop, :]
        for head in range(GROUP):
            mask = head_mask((count, CH), head)
            q_head = jnp.where(mask, q, 0.0).astype(bf16)
            d_head = jnp.where(mask, d_out, 0.0).astype(bf16)
            scores = dot_nt(k, q_head)
            logs = l_ref[0, head : head + 1, start:stop]
            probs = jnp.where(allowed, jnp.exp(scores - logs), 0.0)
            d_probs = dot_nt(v, d_head)
            d_scores = (probs * (d_probs - delta[head : head + 1, start:stop])).astype(bf16)
            dv = dv + dot_nn(probs.astype(bf16), d_head)
            dk = dk + dot_nn(d_scores, q_head)
            dq = dq + jnp.where(mask, dot_tn(d_scores, k), 0.0)
        dk_s[:stop, :] = dk
        dv_s[:stop, :] = dv
        out_ref[0, start:stop, :] = (dq * 0.125).astype(bf16)
    out_ref[1] = dk_s[...].astype(bf16)
    out_ref[2] = dv_s[...].astype(bf16)


def self_backward(qkv, d_out, out, log_rows, length, count):
    groups = D // CH
    at = lambda j: (lambda i, n: (j, 0, i))
    here = lambda i, n: (0, i)
    return pl.pallas_call(
        self_backward_kernel,
        grid_spec=pltpu.PrefetchScalarGridSpec(
            num_scalar_prefetch=1,
            grid=(count,),
            in_specs=[pl.BlockSpec((1, SEQ, CH), at(j)) for j in range(3)]
            + [
                pl.BlockSpec((SEQ, CH), here),
                pl.BlockSpec((SEQ, CH), here),
                pl.BlockSpec((1, 8, SEQ), lambda i, n: (i, 0, 0)),
            ],
            out_specs=pl.BlockSpec((3, SEQ, CH), lambda i, n: (0, 0, i)),
            scratch_shapes=[pltpu.VMEM((SEQ, CH), f32), pltpu.VMEM((SEQ, CH), f32)],
        ),
        out_shape=jax.ShapeDtypeStruct((3, SEQ, count * CH), bf16),
        compiler_params=params(),
        cost_estimate=cost(
            8 * HEADS * SEQ * SEQ * CH * count // groups, 16 * SEQ * D, HEADS * SEQ * SEQ
        ),
    )(length, stay(qkv), stay(qkv), stay(qkv), d_out, stay(out), log_rows)


def full(*shape):
    return pl.BlockSpec(shape, lambda i: (0,) * len(shape))


def part_of(first):
    return pl.BlockSpec((3, CH, D), lambda i: (first + i, 0, 0))


def fixed_part(index):
    return pl.BlockSpec((3, CH, D), lambda i: (index, 0, 0))


def square(ref):
    return ref[...].reshape(D, D)


def write_cores(core, matrix, keep_refs, sizes, order, at=0):
    z, y, x, rows = sizes
    columns = matrix.shape[-1]
    if rows % 8:
        parts = matrix.reshape(-1, 2, y * x * rows, columns)
    else:
        parts = matrix.reshape(-1, 2, y, x, rows, columns)
    first, second = parts[:, 0], parts[:, 1]
    halves = (jnp.where(core == 0, first, second), jnp.where(core == 0, second, first))
    for ref, half in zip(keep_refs, halves):
        here = slice(at * z, at * z + half.shape[0])
        if rows % 8:
            ref[here] = half.astype(bf16)
            continue
        for row in range(y):
            for col in range(x):
                to = (col, row) if order == "xy" else (row, col)
                ref[to[0], to[1], here] = half[:, row, col].astype(bf16)


def core_shape(count, order, columns=D):
    z, y, x, rows = slice_shape()
    if rows % 8:
        return (count * z, y * x * rows, columns)
    cuts = (x, y) if order == "xy" else (y, x)
    return cuts + (count * z, rows, columns)


def core_block(count, order, at, columns=D):
    shape = core_shape(count, order, columns)
    return pl.BlockSpec(shape, lambda i: (0,) * (len(shape) - 3) + (at(i), 0, 0))


def core_cuts(parts, order):
    z, y, x, rows = slice_shape()
    if rows % 8 == 0:
        return list(parts)
    parts = [part.reshape(-1, y, x, rows, part.shape[-1]) for part in parts]
    dims = (2, 1, 0, 3, 4) if order == "xy" else (1, 2, 0, 3, 4)
    return [part.transpose(dims) for part in parts]


def split_z(slices):
    return slices.reshape((-1, lax.axis_size("z")) + slices.shape[1:])


def row_here():
    return lax.axis_index(("y", "x")).astype(jnp.int32).reshape(1)


def core_here():
    return lax.axis_index("c").astype(jnp.int32).reshape(1)


def row_scale(values):
    return lax.rsqrt(jnp.mean(values * values, -1, keepdims=True) + eps_norm)


def pull_norm(d_normed, values, gain):
    scale = row_scale(values)
    d_gain = jnp.sum(d_normed * values * scale, 0, keepdims=True)
    scaled = d_normed * gain
    inner = jnp.mean(scaled * values, -1, keepdims=True)
    return d_gain, scale * scaled - (scale * scale * scale) * values * inner


def embed_kernel(
    pool_ref, feats_ref, mixed_ref, out_w_ref, emb_ref, w_ref, gain_ref,
    seq_ref, embed_ref, normed_ref, qkv_ref,
):
    @pl.when(pl.program_id(0) == 0)
    def _():
        updated = feats_ref[...].astype(f32) + dot_nn(mixed_ref[...], out_w_ref[...])
        seq_ref[:CTX, :] = pool_ref[...]
        seq_ref[CTX:, :] = updated.astype(bf16)
        embed = dot_nn(seq_ref[...], emb_ref[0])
        embed_ref[...] = embed
        normed_ref[...] = (embed * row_scale(embed) * gain_ref[...]).astype(bf16)

    qkv_ref[0] = dot_nn(normed_ref[...], square(w_ref)).astype(bf16)


def embed_forward(pooled, feats, mixed, to_out, weights, gain):
    last = weights.shape[0] - 1
    return pl.pallas_call(
        embed_kernel,
        grid=(3,),
        in_specs=[
            full(CTX, CH),
            full(SEQ - CTX, CH),
            full(SEQ - CTX, CH),
            full(CH, CH),
            pl.BlockSpec((1, CH, D), lambda i: (last, 0, 0)),
            part_of(0),
            full(1, D),
        ],
        out_specs=[
            full(SEQ, CH),
            full(SEQ, D),
            full(SEQ, D),
            pl.BlockSpec((1, SEQ, D), lambda i: (i, 0, 0)),
        ],
        out_shape=[
            lasting((SEQ, CH), bf16),
            lasting((SEQ, D), f32),
            lasting((SEQ, D), bf16),
            jax.ShapeDtypeStruct((3, SEQ, D), bf16),
        ],
        compiler_params=params(),
        cost_estimate=cost(2 * SEQ * D * (CH + 3 * D), 12 * SEQ * D),
    )(pooled, feats, mixed, to_out, stay(weights), stay(weights), gain)


def mlp_kernel(
    core_ref, mixed_ref, embed_ref, att_ref, up_ref, down_ref, gain_ref, gd_ref,
    out_ref, d_stream_ref, gog_ref, up_keep_ref, up_give_ref, down_keep_ref, down_give_ref,
    att_keep_ref, att_give_ref, gain_g_ref,
    stream_s, normed_s, turned_s, act_s, gpre_s, total_s, *, sizes
):
    step = pl.program_id(0)
    core = core_ref[0]

    @pl.when(step == 0)
    def _():
        stream = embed_ref[...] + dot_nn(mixed_ref[...], square(att_ref))
        stream_s[...] = stream
        out_ref[...] = stream
        total_s[...] = jnp.zeros_like(total_s)
        normed = stream * row_scale(stream) * gain_ref[...]
        normed_s[...] = normed.astype(bf16)
        turned_s[...] = normed.T.astype(bf16)

    factor = (2.0 / 3.141592653589793) ** 0.5
    cubic = 0.044715 * factor
    rows = SEQ // 2
    for start in range(0, SEQ, rows):
        here = slice(start, start + rows)
        v = dot_nn(normed_s[here, :], square(up_ref))
        v2 = v * v
        half = 0.5 + 0.5 * jnp.tanh(v * (factor + cubic * v2))
        act = (v * half).astype(bf16)
        act_s[here, :] = act
        slope = half + v * (2.0 * half * (1.0 - half) * (factor + 3.0 * cubic * v2))
        gpre = (dot_nt(gd_ref[here, :], square(down_ref)) * slope).astype(bf16)
        gpre_s[here, :] = gpre
        out_ref[here, :] += dot_nn(act, square(down_ref))
        total_s[here, :] += dot_nt(gpre, square(up_ref))
    down_refs, up_refs = (down_keep_ref, down_give_ref), (up_keep_ref, up_give_ref)
    write_cores(core, dot_tn(act_s[...], gd_ref[...]), down_refs, sizes, "xy")
    write_cores(core, dot_nn(turned_s[...], gpre_s[...]), up_refs, sizes, "yx")

    @pl.when(step == pl.num_programs(0) - 1)
    def _():
        d_gain, pulled = pull_norm(total_s[...], stream_s[...], gain_ref[...])
        gain_g_ref[...] = d_gain
        d_stream = gd_ref[...].astype(f32) + pulled
        d_stream_ref[...] = d_stream
        ga = d_stream.astype(bf16)
        gog_ref[...] = dot_nt(ga, square(att_ref)).astype(bf16)
        att_refs = (att_keep_ref, att_give_ref)
        write_cores(core, dot_tn(mixed_ref[...], ga), att_refs, sizes, "yx")


def mlp_block(mixed, embed, weights, mlp, gain, gd):
    up_part = core_block(3, "yx", lambda i: i)
    down_part = core_block(3, "xy", lambda i: i)
    att_part = core_block(3, "yx", lambda i: 0)
    return pl.pallas_call(
        functools.partial(mlp_kernel, sizes=slice_shape()),
        grid=(4,),
        in_specs=[
            CORE_SPEC,
            full(SEQ, D),
            full(SEQ, D),
            fixed_part(3),
            part_of(0),
            part_of(4),
            full(1, D),
            full(SEQ, D),
        ],
        out_specs=[full(SEQ, D)] * 3
        + [up_part] * 2
        + [down_part] * 2
        + [att_part] * 2
        + [full(1, D)],
        out_shape=[
            lasting((SEQ, D), f32),
            lasting((SEQ, D), f32),
            jax.ShapeDtypeStruct((SEQ, D), bf16),
        ]
        + [jax.ShapeDtypeStruct(core_shape(12, "yx"), bf16)] * 2
        + [jax.ShapeDtypeStruct(core_shape(12, "xy"), bf16)] * 2
        + [jax.ShapeDtypeStruct(core_shape(3, "yx"), bf16)] * 2
        + [jax.ShapeDtypeStruct((1, D), f32)],
        scratch_shapes=[
            pltpu.VMEM((SEQ, D), f32),
            pltpu.VMEM((SEQ, D), bf16),
            pltpu.VMEM((D, SEQ), bf16),
            pltpu.VMEM((SEQ, D), bf16),
            pltpu.VMEM((SEQ, D), bf16),
            pltpu.VMEM((SEQ, D), f32),
        ],
        compiler_params=pltpu.CompilerParams(vmem_limit_bytes=MLP_BYTES),
        cost_estimate=cost(54 * SEQ * D * D, 60 * SEQ * D, 4 * SEQ * D),
    )(core_here(), mixed, embed, stay(weights), stay(mlp), stay(mlp), gain, gd)


def embed_grad_kernel(
    core_ref, len_ref, q_ref, k_ref, v_ref, do_ref, o_ref, l_ref,
    g_ref, normed_ref, w_ref, emb_ref, embed_ref, d_stream_ref, seq_ref, mixed_ref, out_w_ref,
    gain_ref, gain_g_ref,
    qk_keep_ref, qk_give_ref, v_keep_ref, v_give_ref, keep_ref, give_ref,
    gupd_ref, pool_g_ref, out_g_ref, gox_ref,
    dk_s, dv_s, last_s, turned_s, total_s, *, sizes
):
    step = pl.program_id(0)
    core = core_ref[0]

    @pl.when(step == 0)
    def _():
        self_backward_kernel(
            len_ref, q_ref, k_ref, v_ref, do_ref, o_ref, l_ref, last_s, dk_s, dv_s
        )
        turned_s[...] = normed_ref[...].T
        total_s[...] = jnp.zeros_like(total_s)

    @pl.when(step > 0)
    def _():
        g = jnp.concatenate([g_ref[0], last_s[step - 1]], 1)
        total_s[...] += dot_nt(g, square(w_ref))
        grad = dot_nn(turned_s[...], g)

        @pl.when(step < 3)
        def _():
            write_cores(core, grad, (qk_keep_ref, qk_give_ref), sizes, "xy")

        @pl.when(step == 3)
        def _():
            write_cores(core, grad, (v_keep_ref, v_give_ref), sizes, "yx")

    @pl.when(step == 3)
    def _():
        d_gain, pulled = pull_norm(total_s[...], embed_ref[...], gain_ref[...])
        gembed = (d_stream_ref[...] + pulled).astype(bf16)
        at = lax.broadcasted_iota(jnp.int32, (CH, D), 0)
        gains = jnp.where(at == 0, d_gain, jnp.where(at == sizes[-1], gain_g_ref[...], 0.0))
        for index, values in enumerate((dot_tn(seq_ref[...], gembed), gains)):
            write_cores(core, values, (keep_ref, give_ref), sizes, "xy", index)
        gseq = dot_nt(gembed, emb_ref[0])
        gupd = gseq[CTX:]
        gb = gupd.astype(bf16)
        pool_g_ref[...] = gseq[:CTX].astype(bf16)
        gupd_ref[...] = gupd
        out_g_ref[...] = dot_tn(mixed_ref[...], gb).astype(bf16)
        gox_ref[...] = dot_nt(gb, out_w_ref[...]).astype(bf16)


def embed_grad(
    length, qkv, gog, out, log_rows, gqkv, normed, weights, embed, d_stream, seq, mixed, to_out,
    gain, gain_g,
):
    last = weights.shape[0] - 1
    group = D // CH - 1
    done = gqkv.shape[-1]
    part = lambda i: jnp.maximum(i - 1, 0)
    at = lambda j: pl.BlockSpec((1, SEQ, CH), lambda i: (j, 0, group))
    here = pl.BlockSpec((SEQ, CH), lambda i: (0, group))
    qk_part = core_block(3, "xy", lambda i: jnp.clip(i - 1, 0, 1))
    v_part = core_block(3, "yx", lambda i: 0)
    emb_part = core_block(2, "xy", lambda i: 0)
    return pl.pallas_call(
        functools.partial(embed_grad_kernel, sizes=slice_shape()),
        grid=(4,),
        in_specs=[
            CORE_SPEC,
            CORE_SPEC,
            at(0),
            at(1),
            at(2),
            here,
            here,
            pl.BlockSpec((1, 8, SEQ), lambda i: (group, 0, 0)),
            pl.BlockSpec((1, SEQ, done), lambda i: (part(i), 0, 0)),
            full(SEQ, D),
            pl.BlockSpec((3, CH, D), lambda i: (part(i), 0, 0)),
            pl.BlockSpec((1, CH, D), lambda i: (last, 0, 0)),
            full(SEQ, D),
            full(SEQ, D),
            full(SEQ, CH),
            full(SEQ - CTX, CH),
            full(CH, CH),
            full(1, D),
            full(1, D),
        ],
        out_specs=[
            qk_part,
            qk_part,
            v_part,
            v_part,
            emb_part,
            emb_part,
            full(SEQ - CTX, CH),
            full(CTX, CH),
            full(CH, CH),
            full(SEQ - CTX, CH),
        ],
        out_shape=[jax.ShapeDtypeStruct(core_shape(6, "xy"), bf16)] * 2
        + [jax.ShapeDtypeStruct(core_shape(3, "yx"), bf16)] * 2
        + [jax.ShapeDtypeStruct(core_shape(2, "xy"), bf16)] * 2
        + [
            jax.ShapeDtypeStruct((SEQ - CTX, CH), f32),
            jax.ShapeDtypeStruct((CTX, CH), bf16),
            jax.ShapeDtypeStruct((CH, CH), bf16),
            jax.ShapeDtypeStruct((SEQ - CTX, CH), bf16),
        ],
        scratch_shapes=[
            pltpu.VMEM((SEQ, CH), f32),
            pltpu.VMEM((SEQ, CH), f32),
            pltpu.VMEM((3, SEQ, CH), bf16),
            pltpu.VMEM((D, SEQ), bf16),
            pltpu.VMEM((SEQ, D), f32),
        ],
        compiler_params=pltpu.CompilerParams(vmem_limit_bytes=MLP_BYTES),
        cost_estimate=cost(2 * SEQ * D * (6 * D + 2 * CH) + 32 * SEQ * SEQ * CH, 50 * SEQ * D),
    )(
        core_here(), length, stay(qkv), stay(qkv), stay(qkv), gog, stay(out), log_rows, gqkv, normed, stay(weights),
        stay(weights), stay(embed), stay(d_stream), stay(seq), stay(mixed), to_out, gain, gain_g,
    )


def patch_pick(rows, columns, patch_dim):
    patch = lax.broadcasted_iota(jnp.int32, (rows, columns), patch_dim)
    cell = lax.broadcasted_iota(jnp.int32, (rows, columns), 1 - patch_dim)
    inside = (cell // (PATCH * IMG)) * (IMG // PATCH) + (cell % IMG) // PATCH
    return jnp.where(patch == inside, 1.0 / (PATCH * PATCH), 0.0).astype(bf16)


def image_rows(step, row):
    return pl.ds(pl.multiple_of(step * BLOCK + row * IMG, IMG), BLOCK)


def token_forward_kernel(x_ref, conv_ref, kv_w_ref, slope_ref, hidden_ref, kv_ref, pool_ref):
    step = pl.program_id(0)
    z = jnp.zeros((BLOCK, CH), f32)
    for row in range(3):
        z = z + dot_nn(x_ref[image_rows(step, row), :], conv_ref[row])
    center = x_ref[image_rows(step, 1), CH : 2 * CH].astype(f32)
    gate = 1.0 / (1.0 + jnp.exp(-z))
    hidden = center + z * gate
    slope_ref[...] = (gate * (1.0 + z * (1.0 - gate))).astype(bf16)
    hidden_b = hidden.astype(bf16)
    hidden_ref[...] = hidden_b
    kv_ref[...] = dot_nn(hidden_b, kv_w_ref[...]).astype(bf16)
    rest = (hidden - hidden_b.astype(f32)).astype(bf16)
    pick = patch_pick(pool_ref.shape[0], BLOCK, 0)
    pool_ref[...] = (dot_nn(pick, hidden_b) + dot_nn(pick, rest)).astype(bf16)


def token_forward(wide, conv_rows, kv_weight):
    steps = CELLS // BLOCK
    whole = lambda i: (0, 0)
    block = lambda i: (i, 0)
    return pl.pallas_call(
        token_forward_kernel,
        grid=(steps,),
        in_specs=[
            pl.BlockSpec(wide.shape, whole),
            pl.BlockSpec((3, 3 * CH, CH), lambda i: (0, 0, 0)),
            pl.BlockSpec((CH, 2 * CH), whole),
        ],
        out_specs=[
            pl.BlockSpec((BLOCK, CH), block),
            pl.BlockSpec((BLOCK, CH), block),
            pl.BlockSpec((BLOCK, 2 * CH), block),
            pl.BlockSpec((CTX // steps, CH), block),
        ],
        out_shape=[
            lasting((CELLS, CH), bf16),
            lasting((CELLS, CH), bf16),
            jax.ShapeDtypeStruct((CELLS, 2 * CH), bf16),
            jax.ShapeDtypeStruct((CTX, CH), bf16),
        ],
        compiler_params=params(),
        cost_estimate=cost(22 * CELLS * CH * CH, 14 * CELLS * CH, CELLS * CH),
    )(stay(wide), conv_rows, kv_weight)


def token_backward_kernel(
    core_ref, dkv_ref, slope_ref, pool_ref, hidden_ref, x_ref, kv_w_ref, query_g_ref, out_g_ref,
    d_hidden_ref, gz_ref, keep_ref, give_ref, conv_s, kv_s, *, sizes
):
    step = pl.program_id(0)

    @pl.when(step == 0)
    def _():
        conv_s[...] = jnp.zeros_like(conv_s)
        kv_s[...] = jnp.zeros_like(kv_s)

    dkv = dkv_ref[...]
    d_hidden = dot_nt(dkv, kv_w_ref[...])
    d_hidden = d_hidden + dot_nn(patch_pick(BLOCK, pool_ref.shape[0], 1), pool_ref[...])
    gz = (d_hidden * slope_ref[...].astype(f32)).astype(bf16)
    d_hidden_ref[...] = d_hidden
    gz_ref[...] = gz
    kv_s[...] += dot_tn(hidden_ref[...], dkv)
    gz_t = gz.T
    for row in range(3):
        conv_s[row] += dot_nn(gz_t, x_ref[image_rows(step, row), :])

    @pl.when(step == pl.num_programs(0) - 1)
    def _():
        tiles = []
        for row in range(3):
            for col in range(3):
                tiles.append(conv_s[row, :, col * CH : (col + 1) * CH].T)
        tiles = tiles + [query_g_ref[...], kv_s[:, :CH], kv_s[:, CH:], out_g_ref[...]]
        for at, tile in enumerate(tiles):
            write_cores(core_ref[0], tile.astype(f32), (keep_ref, give_ref), sizes, "yx", at)


def token_backward(dkv, slope, d_pool, hidden_b, wide, kv_weight, query_g, out_g):
    steps = CELLS // BLOCK
    whole = lambda i: (0, 0)
    block = lambda i: (i, 0)
    return pl.pallas_call(
        functools.partial(token_backward_kernel, sizes=slice_shape()),
        grid=(steps,),
        in_specs=[
            CORE_SPEC,
            pl.BlockSpec((BLOCK, 2 * CH), block),
            pl.BlockSpec((BLOCK, CH), block),
            pl.BlockSpec((CTX // steps, CH), block),
            pl.BlockSpec((BLOCK, CH), block),
            pl.BlockSpec(wide.shape, whole),
            pl.BlockSpec((CH, 2 * CH), whole),
            pl.BlockSpec((CH, CH), whole),
            pl.BlockSpec((CH, CH), whole),
        ],
        out_specs=[
            pl.BlockSpec((BLOCK, CH), block),
            pl.BlockSpec((BLOCK, CH), block),
            core_block(EARLY, "yx", lambda i: 0, CH),
            core_block(EARLY, "yx", lambda i: 0, CH),
        ],
        out_shape=[
            jax.ShapeDtypeStruct((CELLS, CH), f32),
            jax.ShapeDtypeStruct((CELLS, CH), bf16),
            jax.ShapeDtypeStruct(core_shape(EARLY, "yx", CH), bf16),
            jax.ShapeDtypeStruct(core_shape(EARLY, "yx", CH), bf16),
        ],
        scratch_shapes=[pltpu.VMEM((3, CH, 3 * CH), f32), pltpu.VMEM((CH, 2 * CH), f32)],
        compiler_params=params(),
        cost_estimate=cost(26 * CELLS * CH * CH, 20 * CELLS * CH),
    )(core_here(), dkv, stay(slope), d_pool, stay(hidden_b), stay(wide), kv_weight, query_g, out_g)


def context_backward_kernel(gz_ref, d_hidden_ref, conv_ref, out_ref, wide_s):
    step = pl.program_id(0)
    steps = pl.num_programs(0)

    def widen(at):
        values = gz_ref[image_rows(at, 0), :].astype(f32)
        col = lax.broadcasted_iota(jnp.int32, (BLOCK, CH), 0) % IMG
        left = jnp.where(col == 0, 0.0, pltpu.roll(values, 1, 0))
        right = jnp.where(col == IMG - 1, 0.0, pltpu.roll(values, BLOCK - 1, 0))
        wide_s[image_rows(at, 1), 0:CH] = left.astype(bf16)
        wide_s[image_rows(at, 1), CH : 2 * CH] = values.astype(bf16)
        wide_s[image_rows(at, 1), 2 * CH :] = right.astype(bf16)

    @pl.when(step == 0)
    def _():
        wide_s[0:IMG, :] = jnp.zeros((IMG, 3 * CH), bf16)
        wide_s[CELLS + IMG :, :] = jnp.zeros((IMG, 3 * CH), bf16)
        widen(0)

    @pl.when(step < steps - 1)
    def _():
        widen(step + 1)

    total = d_hidden_ref[...]
    for row in range(3):
        values = wide_s[image_rows(step, row), :]
        for col in range(3):
            tap = conv_ref[3 * (2 - row) + (2 - col)]
            total = total + dot_nt(values[:, col * CH : (col + 1) * CH], tap)
    out_ref[...] = total.astype(bf16)


def context_backward(gz, d_hidden, conv_tiles):
    block = lambda i: (i, 0)
    return pl.pallas_call(
        context_backward_kernel,
        grid=(CELLS // BLOCK,),
        in_specs=[
            pl.BlockSpec((CELLS, CH), lambda i: (0, 0)),
            pl.BlockSpec((BLOCK, CH), block),
            pl.BlockSpec((9, CH, CH), lambda i: (0, 0, 0)),
        ],
        out_specs=pl.BlockSpec((BLOCK, CH), block),
        out_shape=jax.ShapeDtypeStruct((CELLS, CH), bf16),
        scratch_shapes=[pltpu.VMEM((CELLS + 2 * IMG, 3 * CH), bf16)],
        compiler_params=params(),
        cost_estimate=cost(18 * CELLS * CH * CH, 8 * CELLS * CH),
    )(gz, d_hidden, conv_tiles)


def local(
    context_map,
    future_feats,
    horizon,
    cotangent,
    tile_owner,
    master_tiles,
    moment_first,
    moment_second,
    norm_gains,
    gain_first,
    gain_second,
):
    slot_count = master_tiles.shape[0]
    devices = lax.axis_size(AXES)
    rows = CH // devices
    slot_of = slot_index(tile_owner, slot_count)

    length = CTX + FT * horizon
    valid = jnp.arange(SEQ) < length[0]
    gd = jnp.where(valid[:, None], cotangent[0], jnp.zeros((), bf16))

    slices = (
        master_tiles.astype(bf16)
        .reshape(slot_count, devices, rows, CH)
        .transpose(1, 0, 2, 3)
    )
    slices = lax.all_to_all(slices, AXES, split_axis=0, concat_axis=0, tiled=True)
    extra = max(1, 8 // rows)
    tiles = tile_owner.shape[0]
    span = slot_count + extra
    place = jnp.arange(devices * span)
    device, at = place // span, place % span
    found = slot_of[None, :] == jnp.where(at < slot_count, device * slot_count + at, -1)[:, None]
    tile_of = jnp.sum(jnp.where(found, jnp.arange(tiles)[None], 0), 1)
    tile_of = jnp.where(at < slot_count, tile_of, tiles + at - slot_count)
    mine_at = lax.axis_index(AXES) * slot_count + jnp.arange(slot_count)
    used = jnp.any(slot_of[None, :] == mine_at[:, None], 1).astype(f32)
    slices, gd, tile_of, used = tie((slices, gd, tile_of, used))
    slices = slices.reshape(devices * slot_count, rows, CH)
    slices = slices.at[slot_of].get(mode="promise_in_bounds")
    early, emb, qkv, att, up, down = jnp.split(slices, (13, 16, 43, 52, 88))
    mlp = jnp.concatenate([from_tiles(up, 3, 4), from_tiles(down, 12, 1)], 0)
    mlp = lax.all_gather(mlp, AXES, axis=1, tiled=True)
    early = gather_axes(early, "z")
    core = jnp.concatenate([from_tiles(qkv, 3, 3), from_tiles(att, 3, 1), from_tiles(emb, 1, 1)], 0)
    core, early = tie((core, early))
    early = gather_axes(joined(early), ("y", "x"))
    core = gather_axes(core, "z")
    pieces = trade_rows(context_map)
    early = joined(gather_axes(joined(early), "c"))
    early = device_order(early, ("c", "y", "x", "z"))
    wide = widen(pieces)
    core = joined(core)
    low, high = gather_axes(core[:6], "x"), gather_axes(core[6:], "y")

    conv_tiles = early[:9]
    to_query, to_out = early[9], early[12]
    kv_weight = jnp.concatenate([early[10], early[11]], 1)

    wide, low, high = hold((wide,), low, high)
    low, high = joined(low), joined(high)
    wide, low, high = tie((wide, low, high))
    low, high = gather_axes(low, "y"), gather_axes(high, "x")
    slope_z, hidden_b, kv, pooled = token_forward(
        wide, conv_tiles.reshape(3, 3 * CH, CH), kv_weight
    )
    kv, low, high = hold((kv,), low, high)
    low, high = joined(low), joined(high)
    feats_b = future_feats[0]
    query = jnp.dot(feats_b, to_query, preferred_element_type=f32).astype(bf16)
    kv, low, high = tie((kv, low, high))
    low, high = gather_axes(low, "c"), gather_axes(high, "c")
    cross_mixed, cross_logs = cross_forward(query, kv)
    cross_mixed, low, high = hold((cross_mixed,), low, high)
    weights = place_rows(low, high)

    gain_one, gain_two = norm_gains[:1], norm_gains[1:]
    seq, embed, normed_one, qkv = embed_forward(
        pooled, feats_b, cross_mixed, to_out, weights, gain_one
    )
    mixed, logs = self_forward(qkv, length)
    (
        block_out, d_stream, gog, up_keep, up_give, down_keep, down_give, att_keep, att_give,
        gain_g_two,
    ) = mlp_block(mixed, embed, weights, mlp, gain_two, gd)
    up = core_cuts([up_keep, up_give], "yx")
    down = core_cuts([down_keep, down_give], "xy")
    att = core_cuts([att_keep, att_give], "yx")
    gog, up, down, att = tie((gog, up, down, att))
    up, down, att = send(up, "c"), send(down, "c"), send(att, "c")
    gqkv = self_backward(qkv, gog, mixed, logs, length, 2)
    gqkv, up, down, att = hold((gqkv,), up, down, att)
    up, down = advance(up, "y", 0), advance(down, "x", 0)
    gqkv, up, down = tie((gqkv, up, down))
    up, down = send(up, "y"), send(down, "x")
    (
        qk_keep, qk_give, v_keep, v_give, emb_keep, emb_give, gupd, pool_g, out_g, gox,
    ) = embed_grad(
        length, qkv, gog, mixed, logs, gqkv, normed_one, weights, embed, d_stream, seq,
        cross_mixed, to_out, gain_one, gain_g_two,
    )
    first = core_cuts([qk_keep, qk_give], "xy")
    second = core_cuts([v_keep, v_give], "yx")
    emb = core_cuts([emb_keep, emb_give], "xy")
    gox, gupd, first, second, emb, up, down = hold((gox, gupd, first, second, emb), up, down)
    up, down = advance(up, "x", 0), advance(down, "y", 0)
    gox, up, down, first, second, emb = tie((gox, up, down, first, second, emb))
    up, down, emb = send(up, "x"), send(down, "y"), send(emb, "c")
    first, second = send(first, "c"), send(second, "c")

    log_rows = jnp.concatenate([cross_logs[0], cross_logs[1]], 1)
    gkv, query_g, future_grad = cross_backward(
        query, kv, gox, cross_mixed, log_rows, feats_b, gupd, to_query
    )
    gkv, up, down, first, second, emb = hold((gkv,), up, down, first, second, emb)
    mlp = advance_near([split_z(jnp.concatenate(part, 0)) for part in zip(up, down)])
    emb = advance(emb, "x", 0)
    second = [jnp.concatenate([p, q], 2) for p, q in zip(second, att)]
    first, second = advance(first, "x", 0), advance(second, "y", 0)
    gkv, mlp, first, second, emb = tie((gkv, mlp, first, second, emb))
    mlp, emb = send(mlp, "z"), send(emb, "x")
    first, second = send(first, "x"), send(second, "y")

    d_hidden, gz, early_keep, early_give = token_backward(
        gkv, slope_z, pool_g, hidden_b, wide, kv_weight, query_g, out_g
    )
    d_hidden, gz, early_keep, early_give, mlp, first, second, emb = hold(
        (d_hidden, gz, early_keep, early_give), mlp, first, second, emb
    )
    early = core_cuts([early_keep, early_give], "yx")
    early, mlp, first, second, emb = tie((early, mlp, first, second, emb))
    early = send(early, "c")
    first, second = advance(first, "y", 0), advance(second, "x", 0)
    emb, mlp = advance(emb, "y", 0), advance_far(mlp)
    first, second = send(first, "y"), send(second, "x")
    emb, mlp = send(emb, "y"), send(mlp, "z", 2)
    gz, early, first, second, emb = hold((gz,), early, first, second, emb)
    early = advance([p.reshape((-1,) + p.shape[2:]) for p in early], ("y", "x"), 0)
    att = advance_near([split_z(jnp.concatenate(part, 0)) for part in zip(first, second)])
    gz, early, att = tie((gz, early, att))
    early, att = send(early, ("y", "x")), send(att, "z")
    context_grad = context_backward(gz, d_hidden, conv_tiles)
    context_grad, early, att, mlp = hold((context_grad,), early, att, mlp)
    early = advance([split_z(part) for part in early], "z", 1)
    emb = advance([split_z(part) for part in emb], "z", 1)
    early = [jnp.concatenate([e, to_tiles(m)], 0) for e, m in zip(early, emb)]
    att = advance_far(att)
    context_grad, early, att = tie((context_grad, early, att))
    early, att = send(early, "z"), send(att, "z", 2)
    pieces = trade_rows(context_grad.reshape(context_map.shape))
    sum_mlp = add_up(mlp, keep_wide=True)
    square_mlp = jnp.sum(sum_mlp * sum_mlp)
    half = sum_mlp.shape[0] // 2
    mlp = jnp.concatenate([to_tiles(sum_mlp[:half], 4), to_tiles(sum_mlp[half:])], 0).astype(bf16)
    sum_early = add_up(early, keep_wide=True)
    sum_att = add_up(att, keep_wide=True)

    gains = sum_early[EARLY + 3 :, 0]
    square = square_mlp + jnp.sum(sum_att * sum_att) + jnp.sum(sum_early * sum_early)
    share = jnp.concatenate([gains, jnp.broadcast_to(square, (1, CH))], 0)
    share_high = share.astype(bf16)
    share_low = (share - share_high.astype(f32)).astype(bf16)
    share = jnp.concatenate([share_high, share_low], 0)
    share = jnp.pad(share, ((0, extra * rows - share.shape[0]), (0, 0)))
    sums = jnp.concatenate(
        [
            sum_early[: EARLY + 3].astype(bf16),
            to_tiles(sum_att[:9], 3).astype(bf16),
            to_tiles(sum_att[9:]).astype(bf16),
            mlp,
            share.reshape(extra, rows, CH),
        ],
        0,
    )
    mine = sums.at[tile_of].get(mode="promise_in_bounds")
    mine = mine.reshape(devices, slot_count + extra, rows, CH)
    mine, pieces[-1] = tie((mine, pieces[-1]))
    mine = lax.all_to_all(mine, AXES, split_axis=0, concat_axis=0, tiled=True)
    shares = mine[:, slot_count:].reshape(devices, -1, CH).astype(f32)
    shares = shares[:, :4] + shares[:, 4:8]
    gains = shares[:2, :3].reshape(2, D)
    mine = mine[:, :slot_count].transpose(1, 0, 2, 3).reshape(slot_count, CH, CH).astype(f32)

    used = used[:, None, None]
    grad_norm = jnp.sqrt(jnp.sum(shares[:, 3, 0]))
    factor = jnp.minimum(1.0, clip_level / (grad_norm + 1e-06))
    new_first, new_second, new_master = adam_step(
        master_tiles, mine * factor, moment_first, moment_second, learn_rate, decay_rate
    )
    new_gain_first, new_gain_second, new_gains = adam_step(
        norm_gains, gains * factor, gain_first, gain_second, gain_rate, 0.0
    )
    return (
        block_out[None],
        row_order(pieces).reshape(context_map.shape),
        future_grad[None],
        jnp.where(used > 0, new_first, 0.0),
        jnp.where(used > 0, new_second, 0.0),
        jnp.where(used > 0, new_master, 0.0),
        new_gain_first,
        new_gain_second,
        new_gains,
        grad_norm,
    )


def solution(mesh):
    groups, rows = mesh.devices.shape
    fine = jax.sharding.Mesh(mesh.devices.reshape(groups // 2, 2, rows // 2, 2), AXES)
    whole = P(AXES, None, None)
    image = P(("z", "c"), ("y", "x"), None, None)
    in_specs = (image, whole, P(AXES), whole, P(), whole, whole, whole, P(), P(), P())
    out_specs = (whole, image, whole, whole, whole, whole, P(), P(), P(), P())
    return jax.shard_map(local, mesh=fine, in_specs=in_specs, out_specs=out_specs, check_vma=False)
```

```python
import functools

import jax
import jax.numpy as jnp
from jax import lax
from jax.experimental import pallas as pl
from jax.experimental.pallas import tpu as pltpu
from jax.sharding import PartitionSpec as P

CH = 256
HD = 64
HEADS = 12
D = 768
FF = 3072
TH = 4
IMG = 64
PATCH = 4
FT = 16
CTX = 256
SEQ = 736
STEP = 10


eps_norm = 1e-05
beta_one = 0.9
beta_two = 0.999
learn_rate = 0.02
gain_rate = 0.6
decay_rate = 0.1
adam_eps = 1e-08
clip_level = 1.0
neg_large = -1e30
AXES = ("z", "c", "y", "x")
CELLS = IMG * IMG
BLOCK = 512
GROUP = 4
EARLY = 13
VMEM_BYTES = 28 * 1024 * 1024
MLP_BYTES = 44 * 1024 * 1024
ROW_BLOCKS = ((0, 256), (256, 256), (512, 224))
CORE_SPEC = pl.BlockSpec(memory_space=pltpu.SMEM)
bf16 = jnp.bfloat16
f32 = jnp.float32


def slot_index(tile_owner, slot_count):
    ordinal = jnp.arange(tile_owner.shape[0])
    earlier = (tile_owner[None, :] == tile_owner[:, None]) & (ordinal[None, :] < ordinal[:, None])
    return tile_owner * slot_count + jnp.sum(earlier.astype(jnp.int32), 1)


def adam_step(weight, grad_now, first, second, rate, decay):
    first_new = beta_one * first + (1.0 - beta_one) * grad_now
    second_new = beta_two * second + (1.0 - beta_two) * grad_now * grad_now
    corr_first = first_new / (1.0 - beta_one**STEP)
    corr_second = second_new / (1.0 - beta_two**STEP)
    weight_new = weight - rate * (corr_first / (jnp.sqrt(corr_second) + adam_eps) + decay * weight)
    return (first_new, second_new, weight_new)


def xor_permute(values, axes, mask):
    count = lax.axis_size(axes)
    return lax.ppermute(values, axes, [(i, i ^ mask) for i in range(count)])


def pick(parts, index, dim):
    if parts[0].shape[dim] == 2:
        total = add_up(parts)
        first, second = (lax.index_in_dim(total, at, dim, False) for at in range(2))
        return jnp.where(index == 0, first, second)
    return add_up([lax.dynamic_index_in_dim(part, index, dim, False) for part in parts])


def advance(parts, axes, dim):
    mine = lax.axis_index(axes)
    return [pick(parts, mine ^ mask, dim) for mask in range(lax.axis_size(axes))]


def advance_near(parts):
    mine = lax.axis_index("z") % 2
    shape = parts[0].shape
    parts = [p.reshape((shape[0], shape[1] // 2, 2) + shape[2:]) for p in parts]
    return [pick(parts, mine ^ mask, 2) for mask in range(2)]


def advance_far(parts):
    mine = lax.axis_index("z") // 2
    return [pick(parts, mine ^ mask, 1) for mask in range(parts[0].shape[1])]


def send(cuts, axes, unit=1):
    return [cuts[0]] + [
        xor_permute(cut, axes, unit * mask) for mask, cut in enumerate(cuts) if mask > 0
    ]


def add_up(parts, keep_wide=False):
    total = parts[0].astype(f32)
    for part in parts[1:]:
        total = total + part.astype(f32)
    return total if keep_wide else total.astype(parts[0].dtype)


def hold(values, *sums):
    tied = lax.optimization_barrier((tuple(values), tuple(tuple(parts) for parts in sums)))
    return tied[0] + tuple(list(parts) for parts in tied[1])


def gather_axes(values, axes):
    return [values] + [
        xor_permute(values, axes, mask) for mask in range(1, lax.axis_size(axes))
    ]


def joined(pieces):
    return jnp.stack(pieces, 1)


def device_order(values, axes):
    sizes = [lax.axis_size(axis) for axis in AXES]
    own = [lax.axis_index(axis) for axis in AXES]
    places = jnp.unravel_index(jnp.arange(lax.axis_size(AXES)), sizes)
    at = 0
    for axis in axes:
        which = AXES.index(axis)
        at = at * sizes[which] + (places[which] ^ own[which])
    values = values.reshape((values.shape[0], -1) + values.shape[-2:])
    values = values.at[:, at].get(mode="promise_in_bounds")
    return values.reshape(values.shape[0], -1, values.shape[-1])


def place_kernel(own_ref, low_ref, low_other_ref, high_ref, high_other_ref, out_ref, *, half, sizes):
    z_count, c_count, y_count, x_count = sizes
    own_z, own_c, own_y, own_x = (own_ref[axis] for axis in range(4))
    step = pl.program_id(0)

    def place(near_ref, far_ref, x_first):
        for z in range(z_count):
            for y in range(y_count):
                for x in range(x_count):
                    if x_first:
                        at = (x ^ own_x) * y_count + (y ^ own_y)
                    else:
                        at = (y ^ own_y) * x_count + (x ^ own_x)
                    at = at * z_count + (z ^ own_z)
                    near, far = near_ref[0, at], far_ref[0, at]
                    for c in range(c_count):
                        to = ((z * c_count + c) * y_count + y) * x_count + x
                        out_ref[0, to] = jnp.where(own_c == c, near, far)

    @pl.when(step < half)
    def _():
        place(low_ref, low_other_ref, False)

    @pl.when(step >= half)
    def _():
        place(high_ref, high_other_ref, True)


def place_rows(low, high):
    sizes = tuple(lax.axis_size(axis) for axis in AXES)
    half, rows = low[0].shape[0], low[0].shape[-2]
    count = half + high[0].shape[0]
    own = jnp.stack([lax.axis_index(axis) for axis in AXES]).astype(jnp.int32)
    pieces = [part.reshape(part.shape[0], -1, rows, D) for part in low + high]
    block = (1,) + pieces[0].shape[1:]
    early = pl.BlockSpec(block, lambda i: (jnp.minimum(i, half - 1), 0, 0, 0))
    later = pl.BlockSpec(block, lambda i: (jnp.maximum(i - half, 0), 0, 0, 0))
    devices = CH // rows
    out = pl.pallas_call(
        functools.partial(place_kernel, half=half, sizes=sizes),
        grid=(count,),
        in_specs=[CORE_SPEC, early, early, later, later],
        out_specs=pl.BlockSpec((1, devices, rows, D), lambda i: (i, 0, 0, 0)),
        out_shape=jax.ShapeDtypeStruct((count, devices, rows, D), bf16),
        compiler_params=params(),
        cost_estimate=cost(0, 4 * count * CH * D),
    )(own, *pieces)
    return out.reshape(count, CH, D)


def trade_rows(values):
    mine = lax.axis_index(("y", "x"))
    count = lax.axis_size(("y", "x"))
    cuts = [lax.dynamic_index_in_dim(values, mine ^ mask, 0, False) for mask in range(count)]
    return send(cuts, ("y", "x"))


def row_order_kernel(row_ref, *refs):
    at = pl.program_id(0) ^ row_ref[0]
    values = refs[0][...]
    for mask in range(1, len(refs) - 1):
        values = jnp.where(at == mask, refs[mask][...], values)
    refs[-1][0] = values.astype(f32)


def row_order(pieces):
    count = len(pieces)
    cells = pieces[0].size // CH
    return pl.pallas_call(
        row_order_kernel,
        grid=(count,),
        in_specs=[CORE_SPEC] + [pl.BlockSpec((cells, CH), lambda i: (0, 0))] * count,
        out_specs=pl.BlockSpec((1, cells, CH), lambda i: (i, 0, 0)),
        out_shape=jax.ShapeDtypeStruct((count, cells, CH), f32),
        compiler_params=params(),
        cost_estimate=cost(0, 6 * count * cells * CH),
    )(row_here(), *[piece.reshape(cells, CH) for piece in pieces])


def widen_kernel(row_ref, *refs):
    out_ref = refs[-1]
    cells = refs[0].shape[0]
    col = lax.broadcasted_iota(jnp.int32, (cells, CH), 0) % IMG
    out_ref[0:IMG, :] = jnp.zeros((IMG, 3 * CH), bf16)
    out_ref[CELLS + IMG :, :] = jnp.zeros((IMG, 3 * CH), bf16)
    for at in range(len(refs) - 1):
        values = refs[at][...]
        for mask in range(1, len(refs) - 1):
            values = jnp.where(row_ref[0] == mask, refs[at ^ mask][...], values)
        here = slice(IMG + at * cells, IMG + (at + 1) * cells)
        out_ref[here, CH : 2 * CH] = values
        values = values.astype(f32)
        left = jnp.where(col == 0, 0.0, pltpu.roll(values, 1, 0))
        right = jnp.where(col == IMG - 1, 0.0, pltpu.roll(values, cells - 1, 0))
        out_ref[here, 0:CH] = left.astype(bf16)
        out_ref[here, 2 * CH :] = right.astype(bf16)


def widen(pieces):
    cells = pieces[0].size // CH
    vmem = pl.BlockSpec(memory_space=pltpu.VMEM)
    return pl.pallas_call(
        widen_kernel,
        in_specs=[CORE_SPEC] + [vmem] * len(pieces),
        out_specs=vmem,
        out_shape=lasting((CELLS + 2 * IMG, 3 * CH), bf16),
        compiler_params=params(),
        cost_estimate=cost(0, 8 * CELLS * CH),
    )(row_here(), *[piece.reshape(cells, CH) for piece in pieces])


def slice_shape():
    z, c, y, x = [lax.axis_size(axis) for axis in AXES]
    return (z, y, x, CH // (z * c * y * x))


tie = lax.optimization_barrier


def to_tiles(slices, parts=1):
    blocks, rows, columns = slices.shape
    return (
        slices.reshape(parts, blocks // parts, rows, columns // CH, CH)
        .transpose(1, 0, 3, 2, 4)
        .reshape(-1, rows, CH)
    )


def from_tiles(tiles, row_blocks, parts):
    rows = tiles.shape[1]
    return (
        tiles.reshape(row_blocks, parts, D // CH, rows, CH)
        .transpose(1, 0, 3, 2, 4)
        .reshape(parts * row_blocks, rows, D)
    )


def dot_nt(a, b):
    return lax.dot_general(a, b, (((1,), (1,)), ((), ())), preferred_element_type=f32)


def dot_nn(a, b):
    return lax.dot_general(a, b, (((1,), (0,)), ((), ())), preferred_element_type=f32)


def dot_tn(a, b):
    return lax.dot_general(a, b, (((0,), (0,)), ((), ())), preferred_element_type=f32)


def head_mask(shape, head):
    return (lax.broadcasted_iota(jnp.int32, shape, len(shape) - 1) // HD) == head


def cost(flops, moved, transcendentals=0):
    return pl.CostEstimate(
        flops=int(flops), bytes_accessed=int(moved), transcendentals=int(transcendentals)
    )


def stay(values):
    return pltpu.with_memory_space_constraint(values, pltpu.HBM)


lasting = pltpu.HBM


def params():
    return pltpu.CompilerParams(vmem_limit_bytes=VMEM_BYTES)


def cross_forward_kernel(q_ref, k_ref, v_ref, o_ref, l_ref):
    rows = q_ref.shape[0]
    lane = lax.broadcasted_iota(jnp.int32, (rows, 128), 1)
    q = q_ref[...]
    mixed = jnp.zeros((rows, CH), f32)
    stat = jnp.zeros((rows, 128), f32)
    for head in range(TH):
        mask = head_mask((rows, CH), head)
        q_head = jnp.where(mask, q.astype(f32) * 0.125, 0.0).astype(bf16)
        scores = dot_nt(q_head, k_ref[...])
        peak = jnp.max(scores, -1, keepdims=True)
        shifted = jnp.exp(scores - peak)
        total = jnp.sum(shifted, -1, keepdims=True)
        part = dot_nn(shifted.astype(bf16), v_ref[...])
        mixed = jnp.where(mask, part / total, mixed)
        stat = jnp.where(lane == head, peak + jnp.log(total), stat)
    o_ref[...] = mixed.astype(bf16)
    l_ref[0] = stat.T[:8]


def cross_forward(query, kv):
    rows = query.shape[0] // 2
    cells = kv.shape[0]
    return pl.pallas_call(
        cross_forward_kernel,
        grid=(2,),
        in_specs=[
            pl.BlockSpec((rows, CH), lambda i: (i, 0)),
            pl.BlockSpec((cells, CH), lambda i: (0, 0)),
            pl.BlockSpec((cells, CH), lambda i: (0, 1)),
        ],
        out_specs=[
            pl.BlockSpec((rows, CH), lambda i: (i, 0)),
            pl.BlockSpec((1, 8, rows), lambda i: (i, 0, 0)),
        ],
        out_shape=[
            jax.ShapeDtypeStruct((2 * rows, CH), bf16),
            jax.ShapeDtypeStruct((2, 8, rows), f32),
        ],
        compiler_params=params(),
        cost_estimate=cost(16 * TH * rows * cells * CH // 2, 8 * cells * CH, 2 * TH * rows * cells),
    )(query, kv, kv)


def delta_rows(d_out, out):
    product = d_out.astype(f32) * out.astype(f32)
    head = lax.broadcasted_iota(jnp.int32, (8, CH), 0)
    lane = lax.broadcasted_iota(jnp.int32, (8, CH), 1)
    pick = ((lane // HD) == head).astype(f32)
    return lax.dot_general(
        pick,
        product,
        (((1,), (1,)), ((), ())),
        precision=lax.Precision.HIGHEST,
        preferred_element_type=f32,
    )


def cross_backward_kernel(
    q_ref, k_ref, v_ref, do_ref, o_ref, l_ref, feats_ref, gupd_ref, query_w_ref,
    dkv_ref, query_g_ref, future_ref, q_s, do_s, delta_s, dq_s,
):
    step = pl.program_id(0)
    rows = q_ref.shape[0]

    @pl.when(step == 0)
    def _():
        for head in range(TH):
            mask = head_mask((rows, CH), head)
            q_s[head] = jnp.where(mask, q_ref[...].astype(f32) * 0.125, 0.0).astype(bf16)
            do_s[head] = jnp.where(mask, do_ref[...].astype(f32), 0.0).astype(bf16)
        delta_s[...] = delta_rows(do_ref[...], o_ref[...])
        dq_s[...] = jnp.zeros_like(dq_s)

    cells = k_ref.shape[0]
    dk = jnp.zeros((cells, CH), f32)
    dv = jnp.zeros((cells, CH), f32)
    dq = dq_s[...]
    k = k_ref[...]
    for head in range(TH):
        probs = jnp.exp(dot_nt(k, q_s[head]) - l_ref[head : head + 1, :])
        d_probs = dot_nt(v_ref[...], do_s[head])
        d_scores = (probs * (d_probs - delta_s[head : head + 1, :])).astype(bf16)
        dv = dv + dot_nn(probs.astype(bf16), do_s[head])
        dk = dk + dot_nn(d_scores, q_s[head])
        dq = dq + jnp.where(head_mask((rows, CH), head), dot_tn(d_scores, k), 0.0)
    dq_s[...] = dq
    dkv_ref[:, :CH] = dk.astype(bf16)
    dkv_ref[:, CH:] = dv.astype(bf16)

    @pl.when(step == pl.num_programs(0) - 1)
    def _():
        gq = (dq_s[...] * 0.125).astype(bf16)
        query_g_ref[...] = dot_tn(feats_ref[...], gq).astype(bf16)
        future_ref[...] = gupd_ref[...] + dot_nt(gq, query_w_ref[...])


def cross_backward(query, kv, d_out, out, log_rows, feats, gupd, to_query):
    rows = query.shape[0]
    cells = kv.shape[0]
    block = 1024
    whole = lambda i: (0, 0)
    return pl.pallas_call(
        cross_backward_kernel,
        grid=(cells // block,),
        in_specs=[
            pl.BlockSpec((rows, CH), whole),
            pl.BlockSpec((block, CH), lambda i: (i, 0)),
            pl.BlockSpec((block, CH), lambda i: (i, 1)),
            pl.BlockSpec((rows, CH), whole),
            pl.BlockSpec((rows, CH), whole),
            pl.BlockSpec((8, rows), whole),
            pl.BlockSpec((rows, CH), whole),
            pl.BlockSpec((rows, CH), whole),
            pl.BlockSpec((CH, CH), whole),
        ],
        out_specs=[
            pl.BlockSpec((block, 2 * CH), lambda i: (i, 0)),
            pl.BlockSpec((CH, CH), whole),
            pl.BlockSpec((rows, CH), whole),
        ],
        out_shape=[
            jax.ShapeDtypeStruct((cells, 2 * CH), bf16),
            jax.ShapeDtypeStruct((CH, CH), bf16),
            jax.ShapeDtypeStruct((rows, CH), f32),
        ],
        scratch_shapes=[
            pltpu.VMEM((TH, rows, CH), bf16),
            pltpu.VMEM((TH, rows, CH), bf16),
            pltpu.VMEM((8, rows), f32),
            pltpu.VMEM((rows, CH), f32),
        ],
        compiler_params=params(),
        cost_estimate=cost(10 * TH * rows * cells * CH, 8 * cells * CH, TH * rows * cells),
    )(query, kv, kv, d_out, out, log_rows, feats, gupd, to_query)


def self_forward_kernel(len_ref, q_ref, k_ref, v_ref, o_ref, l_ref):
    group = pl.program_id(0)
    length = len_ref[0]
    for start, count in ROW_BLOCKS:
        stop = start + count
        q = q_ref[0, start:stop, :].astype(f32) * 0.125
        row = lax.broadcasted_iota(jnp.int32, (count, 1), 0) + start
        bound = jnp.minimum(row, length - 1)
        allowed = lax.broadcasted_iota(jnp.int32, (count, stop), 1) <= bound
        mixed = jnp.zeros((count, CH), f32)
        stat = jnp.zeros((count, 128), f32)
        lane = lax.broadcasted_iota(jnp.int32, (count, 128), 1)
        for head in range(GROUP):
            mask = head_mask((count, CH), head)
            q_head = jnp.where(mask, q, 0.0).astype(bf16)
            scores = jnp.where(allowed, dot_nt(q_head, k_ref[0, :stop, :]), neg_large)
            peak = jnp.max(scores, -1, keepdims=True)
            shifted = jnp.exp(scores - peak)
            total = jnp.sum(shifted, -1, keepdims=True)
            part = dot_nn(shifted.astype(bf16), v_ref[0, :stop, :])
            mixed = jnp.where(mask, part / total, mixed)
            stat = jnp.where(lane == head, peak + jnp.log(total), stat)
        o_ref[start:stop, :] = mixed.astype(bf16)
        l_ref[0, :, start:stop] = stat.T[:8]


def self_forward(qkv, length):
    groups = D // CH
    at = lambda j: (lambda i, n: (j, 0, i))
    return pl.pallas_call(
        self_forward_kernel,
        grid_spec=pltpu.PrefetchScalarGridSpec(
            num_scalar_prefetch=1,
            grid=(groups,),
            in_specs=[pl.BlockSpec((1, SEQ, CH), at(j)) for j in range(3)],
            out_specs=[
                pl.BlockSpec((SEQ, CH), lambda i, n: (0, i)),
                pl.BlockSpec((1, 8, SEQ), lambda i, n: (i, 0, 0)),
            ],
        ),
        out_shape=[
            lasting((SEQ, D), bf16),
            jax.ShapeDtypeStruct((groups, 8, SEQ), f32),
        ],
        compiler_params=params(),
        cost_estimate=cost(4 * HEADS * SEQ * SEQ * CH, 8 * SEQ * D, HEADS * SEQ * SEQ),
    )(length, qkv, qkv, qkv)


def self_backward_kernel(
    len_ref, q_ref, k_ref, v_ref, do_ref, o_ref, l_ref, out_ref, dk_s, dv_s
):
    length = len_ref[0]
    dk_s[...] = jnp.zeros_like(dk_s)
    dv_s[...] = jnp.zeros_like(dv_s)
    delta = delta_rows(do_ref[...], o_ref[...])
    for start, count in ROW_BLOCKS:
        stop = start + count
        q = q_ref[0, start:stop, :].astype(f32) * 0.125
        d_out = do_ref[start:stop, :].astype(f32)
        row = lax.broadcasted_iota(jnp.int32, (1, count), 1) + start
        bound = jnp.minimum(row, length - 1)
        allowed = lax.broadcasted_iota(jnp.int32, (stop, count), 0) <= bound
        dq = jnp.zeros((count, CH), f32)
        k = k_ref[0, :stop, :]
        v = v_ref[0, :stop, :]
        dk = dk_s[:stop, :]
        dv = dv_s[:stop, :]
        for head in range(GROUP):
            mask = head_mask((count, CH), head)
            q_head = jnp.where(mask, q, 0.0).astype(bf16)
            d_head = jnp.where(mask, d_out, 0.0).astype(bf16)
            scores = dot_nt(k, q_head)
            logs = l_ref[0, head : head + 1, start:stop]
            probs = jnp.where(allowed, jnp.exp(scores - logs), 0.0)
            d_probs = dot_nt(v, d_head)
            d_scores = (probs * (d_probs - delta[head : head + 1, start:stop])).astype(bf16)
            dv = dv + dot_nn(probs.astype(bf16), d_head)
            dk = dk + dot_nn(d_scores, q_head)
            dq = dq + jnp.where(mask, dot_tn(d_scores, k), 0.0)
        dk_s[:stop, :] = dk
        dv_s[:stop, :] = dv
        out_ref[0, start:stop, :] = (dq * 0.125).astype(bf16)
    out_ref[1] = dk_s[...].astype(bf16)
    out_ref[2] = dv_s[...].astype(bf16)


def self_backward(qkv, d_out, out, log_rows, length, count):
    groups = D // CH
    at = lambda j: (lambda i, n: (j, 0, i))
    here = lambda i, n: (0, i)
    return pl.pallas_call(
        self_backward_kernel,
        grid_spec=pltpu.PrefetchScalarGridSpec(
            num_scalar_prefetch=1,
            grid=(count,),
            in_specs=[pl.BlockSpec((1, SEQ, CH), at(j)) for j in range(3)]
            + [
                pl.BlockSpec((SEQ, CH), here),
                pl.BlockSpec((SEQ, CH), here),
                pl.BlockSpec((1, 8, SEQ), lambda i, n: (i, 0, 0)),
            ],
            out_specs=pl.BlockSpec((3, SEQ, CH), lambda i, n: (0, 0, i)),
            scratch_shapes=[pltpu.VMEM((SEQ, CH), f32), pltpu.VMEM((SEQ, CH), f32)],
        ),
        out_shape=jax.ShapeDtypeStruct((3, SEQ, count * CH), bf16),
        compiler_params=params(),
        cost_estimate=cost(
            8 * HEADS * SEQ * SEQ * CH * count // groups, 16 * SEQ * D, HEADS * SEQ * SEQ
        ),
    )(length, stay(qkv), stay(qkv), stay(qkv), stay(d_out), stay(out), log_rows)


def full(*shape):
    return pl.BlockSpec(shape, lambda i: (0,) * len(shape))


def part_of(first):
    return pl.BlockSpec((3, CH, D), lambda i: (first + i, 0, 0))


def fixed_part(index):
    return pl.BlockSpec((3, CH, D), lambda i: (index, 0, 0))


def square(ref):
    return ref[...].reshape(D, D)


def write_cores(core, matrix, keep_refs, sizes, order, at=0):
    z, y, x, rows = sizes
    columns = matrix.shape[-1]
    if rows % 8:
        parts = matrix.reshape(-1, 2, y * x * rows, columns)
    else:
        parts = matrix.reshape(-1, 2, y, x, rows, columns)
    first, second = parts[:, 0], parts[:, 1]
    halves = (jnp.where(core == 0, first, second), jnp.where(core == 0, second, first))
    for ref, half in zip(keep_refs, halves):
        here = slice(at * z, at * z + half.shape[0])
        if rows % 8:
            ref[here] = half.astype(bf16)
            continue
        for row in range(y):
            for col in range(x):
                to = (col, row) if order == "xy" else (row, col)
                ref[to[0], to[1], here] = half[:, row, col].astype(bf16)


def core_shape(count, order, columns=D):
    z, y, x, rows = slice_shape()
    if rows % 8:
        return (count * z, y * x * rows, columns)
    cuts = (x, y) if order == "xy" else (y, x)
    return cuts + (count * z, rows, columns)


def core_block(count, order, at, columns=D):
    shape = core_shape(count, order, columns)
    return pl.BlockSpec(shape, lambda i: (0,) * (len(shape) - 3) + (at(i), 0, 0))


def core_cuts(parts, order):
    z, y, x, rows = slice_shape()
    if rows % 8 == 0:
        return list(parts)
    parts = [part.reshape(-1, y, x, rows, part.shape[-1]) for part in parts]
    dims = (2, 1, 0, 3, 4) if order == "xy" else (1, 2, 0, 3, 4)
    return [part.transpose(dims) for part in parts]


def split_z(slices):
    return slices.reshape((-1, lax.axis_size("z")) + slices.shape[1:])


def row_here():
    return lax.axis_index(("y", "x")).astype(jnp.int32).reshape(1)


def core_here():
    return lax.axis_index("c").astype(jnp.int32).reshape(1)


def row_scale(values):
    return lax.rsqrt(jnp.mean(values * values, -1, keepdims=True) + eps_norm)


def pull_norm(d_normed, values, gain):
    scale = row_scale(values)
    d_gain = jnp.sum(d_normed * values * scale, 0, keepdims=True)
    scaled = d_normed * gain
    inner = jnp.mean(scaled * values, -1, keepdims=True)
    return d_gain, scale * scaled - (scale * scale * scale) * values * inner


def embed_kernel(
    pool_ref, feats_ref, mixed_ref, out_w_ref, emb_ref, w_ref, gain_ref,
    seq_ref, embed_ref, normed_ref, qkv_ref,
):
    @pl.when(pl.program_id(0) == 0)
    def _():
        updated = feats_ref[...].astype(f32) + dot_nn(mixed_ref[...], out_w_ref[...])
        seq_ref[:CTX, :] = pool_ref[...]
        seq_ref[CTX:, :] = updated.astype(bf16)
        embed = dot_nn(seq_ref[...], emb_ref[0])
        embed_ref[...] = embed
        normed_ref[...] = (embed * row_scale(embed) * gain_ref[...]).astype(bf16)

    qkv_ref[0] = dot_nn(normed_ref[...], square(w_ref)).astype(bf16)


def embed_forward(pooled, feats, mixed, to_out, weights, gain):
    last = weights.shape[0] - 1
    return pl.pallas_call(
        embed_kernel,
        grid=(3,),
        in_specs=[
            full(CTX, CH),
            full(SEQ - CTX, CH),
            full(SEQ - CTX, CH),
            full(CH, CH),
            pl.BlockSpec((1, CH, D), lambda i: (last, 0, 0)),
            part_of(0),
            full(1, D),
        ],
        out_specs=[
            full(SEQ, CH),
            full(SEQ, D),
            full(SEQ, D),
            pl.BlockSpec((1, SEQ, D), lambda i: (i, 0, 0)),
        ],
        out_shape=[
            lasting((SEQ, CH), bf16),
            lasting((SEQ, D), f32),
            lasting((SEQ, D), bf16),
            lasting((3, SEQ, D), bf16),
        ],
        compiler_params=params(),
        cost_estimate=cost(2 * SEQ * D * (CH + 3 * D), 12 * SEQ * D),
    )(pooled, feats, mixed, to_out, stay(weights), stay(weights), gain)


def mlp_kernel(
    core_ref, mixed_ref, embed_ref, att_ref, up_ref, down_ref, gain_ref, gd_ref,
    out_ref, d_stream_ref, gog_ref, up_keep_ref, up_give_ref, down_keep_ref, down_give_ref,
    att_keep_ref, att_give_ref, gain_g_ref,
    stream_s, normed_s, turned_s, act_s, gpre_s, total_s, *, sizes
):
    step = pl.program_id(0)
    core = core_ref[0]

    @pl.when(step == 0)
    def _():
        stream = embed_ref[...] + dot_nn(mixed_ref[...], square(att_ref))
        stream_s[...] = stream
        out_ref[...] = stream
        total_s[...] = jnp.zeros_like(total_s)
        normed = stream * row_scale(stream) * gain_ref[...]
        normed_s[...] = normed.astype(bf16)
        turned_s[...] = normed.T.astype(bf16)

    factor = (2.0 / 3.141592653589793) ** 0.5
    cubic = 0.044715 * factor
    rows = SEQ // 2
    for start in range(0, SEQ, rows):
        here = slice(start, start + rows)
        v = dot_nn(normed_s[here, :], square(up_ref))
        v2 = v * v
        half = 0.5 + 0.5 * jnp.tanh(v * (factor + cubic * v2))
        act = (v * half).astype(bf16)
        act_s[here, :] = act
        slope = half + v * (2.0 * half * (1.0 - half) * (factor + 3.0 * cubic * v2))
        gpre = (dot_nt(gd_ref[here, :], square(down_ref)) * slope).astype(bf16)
        gpre_s[here, :] = gpre
        out_ref[here, :] += dot_nn(act, square(down_ref))
        total_s[here, :] += dot_nt(gpre, square(up_ref))
    down_refs, up_refs = (down_keep_ref, down_give_ref), (up_keep_ref, up_give_ref)
    write_cores(core, dot_tn(act_s[...], gd_ref[...]), down_refs, sizes, "xy")
    write_cores(core, dot_nn(turned_s[...], gpre_s[...]), up_refs, sizes, "yx")

    @pl.when(step == pl.num_programs(0) - 1)
    def _():
        d_gain, pulled = pull_norm(total_s[...], stream_s[...], gain_ref[...])
        gain_g_ref[...] = d_gain
        d_stream = gd_ref[...].astype(f32) + pulled
        d_stream_ref[...] = d_stream
        ga = d_stream.astype(bf16)
        gog_ref[...] = dot_nt(ga, square(att_ref)).astype(bf16)
        att_refs = (att_keep_ref, att_give_ref)
        write_cores(core, dot_tn(mixed_ref[...], ga), att_refs, sizes, "yx")


def mlp_block(mixed, embed, weights, mlp, gain, gd):
    up_part = core_block(3, "yx", lambda i: i)
    down_part = core_block(3, "xy", lambda i: i)
    att_part = core_block(3, "yx", lambda i: 0)
    return pl.pallas_call(
        functools.partial(mlp_kernel, sizes=slice_shape()),
        grid=(4,),
        in_specs=[
            CORE_SPEC,
            full(SEQ, D),
            full(SEQ, D),
            fixed_part(3),
            part_of(0),
            part_of(4),
            full(1, D),
            full(SEQ, D),
        ],
        out_specs=[full(SEQ, D)] * 3
        + [up_part] * 2
        + [down_part] * 2
        + [att_part] * 2
        + [full(1, D)],
        out_shape=[
            lasting((SEQ, D), f32),
            lasting((SEQ, D), f32),
            lasting((SEQ, D), bf16),
        ]
        + [jax.ShapeDtypeStruct(core_shape(12, "yx"), bf16)] * 2
        + [jax.ShapeDtypeStruct(core_shape(12, "xy"), bf16)] * 2
        + [lasting(core_shape(3, "yx"), bf16)] * 2
        + [jax.ShapeDtypeStruct((1, D), f32)],
        scratch_shapes=[
            pltpu.VMEM((SEQ, D), f32),
            pltpu.VMEM((SEQ, D), bf16),
            pltpu.VMEM((D, SEQ), bf16),
            pltpu.VMEM((SEQ, D), bf16),
            pltpu.VMEM((SEQ, D), bf16),
            pltpu.VMEM((SEQ, D), f32),
        ],
        compiler_params=pltpu.CompilerParams(vmem_limit_bytes=MLP_BYTES),
        cost_estimate=cost(54 * SEQ * D * D, 60 * SEQ * D, 4 * SEQ * D),
    )(
        core_here(), stay(mixed), stay(embed), stay(weights), stay(mlp), stay(mlp), gain, stay(gd)
    )


def embed_grad_kernel(
    core_ref, len_ref, q_ref, k_ref, v_ref, do_ref, o_ref, l_ref,
    g_ref, normed_ref, w_ref, emb_ref, embed_ref, d_stream_ref, seq_ref, mixed_ref, out_w_ref,
    gain_ref, gain_g_ref,
    qk_keep_ref, qk_give_ref, v_keep_ref, v_give_ref, keep_ref, give_ref,
    gupd_ref, pool_g_ref, out_g_ref, gox_ref,
    dk_s, dv_s, last_s, turned_s, total_s, *, sizes
):
    step = pl.program_id(0)
    core = core_ref[0]

    @pl.when(step == 0)
    def _():
        self_backward_kernel(
            len_ref, q_ref, k_ref, v_ref, do_ref, o_ref, l_ref, last_s, dk_s, dv_s
        )
        turned_s[...] = normed_ref[...].T
        total_s[...] = jnp.zeros_like(total_s)

    @pl.when(step > 0)
    def _():
        g = jnp.concatenate([g_ref[0], last_s[step - 1]], 1)
        total_s[...] += dot_nt(g, square(w_ref))
        grad = dot_nn(turned_s[...], g)

        @pl.when(step < 3)
        def _():
            write_cores(core, grad, (qk_keep_ref, qk_give_ref), sizes, "xy")

        @pl.when(step == 3)
        def _():
            write_cores(core, grad, (v_keep_ref, v_give_ref), sizes, "yx")

    @pl.when(step == 3)
    def _():
        d_gain, pulled = pull_norm(total_s[...], embed_ref[...], gain_ref[...])
        gembed = (d_stream_ref[...] + pulled).astype(bf16)
        at = lax.broadcasted_iota(jnp.int32, (CH, D), 0)
        gains = jnp.where(at == 0, d_gain, jnp.where(at == sizes[-1], gain_g_ref[...], 0.0))
        for index, values in enumerate((dot_tn(seq_ref[...], gembed), gains)):
            write_cores(core, values, (keep_ref, give_ref), sizes, "xy", index)
        gseq = dot_nt(gembed, emb_ref[0])
        gupd = gseq[CTX:]
        gb = gupd.astype(bf16)
        pool_g_ref[...] = gseq[:CTX].astype(bf16)
        gupd_ref[...] = gupd
        out_g_ref[...] = dot_tn(mixed_ref[...], gb).astype(bf16)
        gox_ref[...] = dot_nt(gb, out_w_ref[...]).astype(bf16)


def embed_grad(
    length, qkv, gog, out, log_rows, gqkv, normed, weights, embed, d_stream, seq, mixed, to_out,
    gain, gain_g,
):
    last = weights.shape[0] - 1
    group = D // CH - 1
    done = gqkv.shape[-1]
    part = lambda i: jnp.maximum(i - 1, 0)
    at = lambda j: pl.BlockSpec((1, SEQ, CH), lambda i: (j, 0, group))
    here = pl.BlockSpec((SEQ, CH), lambda i: (0, group))
    qk_part = core_block(3, "xy", lambda i: jnp.clip(i - 1, 0, 1))
    v_part = core_block(3, "yx", lambda i: 0)
    emb_part = core_block(2, "xy", lambda i: 0)
    return pl.pallas_call(
        functools.partial(embed_grad_kernel, sizes=slice_shape()),
        grid=(4,),
        in_specs=[
            CORE_SPEC,
            CORE_SPEC,
            at(0),
            at(1),
            at(2),
            here,
            here,
            pl.BlockSpec((1, 8, SEQ), lambda i: (group, 0, 0)),
            pl.BlockSpec((1, SEQ, done), lambda i: (part(i), 0, 0)),
            full(SEQ, D),
            pl.BlockSpec((3, CH, D), lambda i: (part(i), 0, 0)),
            pl.BlockSpec((1, CH, D), lambda i: (last, 0, 0)),
            full(SEQ, D),
            full(SEQ, D),
            full(SEQ, CH),
            full(SEQ - CTX, CH),
            full(CH, CH),
            full(1, D),
            full(1, D),
        ],
        out_specs=[
            qk_part,
            qk_part,
            v_part,
            v_part,
            emb_part,
            emb_part,
            full(SEQ - CTX, CH),
            full(CTX, CH),
            full(CH, CH),
            full(SEQ - CTX, CH),
        ],
        out_shape=[jax.ShapeDtypeStruct(core_shape(6, "xy"), bf16)] * 2
        + [jax.ShapeDtypeStruct(core_shape(3, "yx"), bf16)] * 2
        + [jax.ShapeDtypeStruct(core_shape(2, "xy"), bf16)] * 2
        + [
            jax.ShapeDtypeStruct((SEQ - CTX, CH), f32),
            jax.ShapeDtypeStruct((CTX, CH), bf16),
            jax.ShapeDtypeStruct((CH, CH), bf16),
            jax.ShapeDtypeStruct((SEQ - CTX, CH), bf16),
        ],
        scratch_shapes=[
            pltpu.VMEM((SEQ, CH), f32),
            pltpu.VMEM((SEQ, CH), f32),
            pltpu.VMEM((3, SEQ, CH), bf16),
            pltpu.VMEM((D, SEQ), bf16),
            pltpu.VMEM((SEQ, D), f32),
        ],
        compiler_params=pltpu.CompilerParams(vmem_limit_bytes=MLP_BYTES),
        cost_estimate=cost(2 * SEQ * D * (6 * D + 2 * CH) + 32 * SEQ * SEQ * CH, 50 * SEQ * D),
    )(
        core_here(), length, stay(qkv), stay(qkv), stay(qkv), stay(gog), stay(out), log_rows, gqkv, normed, stay(weights),
        stay(weights), stay(embed), stay(d_stream), stay(seq), stay(mixed), to_out, gain, gain_g,
    )


def patch_pick(rows, columns, patch_dim):
    patch = lax.broadcasted_iota(jnp.int32, (rows, columns), patch_dim)
    cell = lax.broadcasted_iota(jnp.int32, (rows, columns), 1 - patch_dim)
    inside = (cell // (PATCH * IMG)) * (IMG // PATCH) + (cell % IMG) // PATCH
    return jnp.where(patch == inside, 1.0 / (PATCH * PATCH), 0.0).astype(bf16)


def image_rows(step, row):
    return pl.ds(pl.multiple_of(step * BLOCK + row * IMG, IMG), BLOCK)


def token_forward_kernel(x_ref, conv_ref, kv_w_ref, slope_ref, hidden_ref, kv_ref, pool_ref):
    step = pl.program_id(0)
    z = jnp.zeros((BLOCK, CH), f32)
    for row in range(3):
        z = z + dot_nn(x_ref[image_rows(step, row), :], conv_ref[row])
    center = x_ref[image_rows(step, 1), CH : 2 * CH].astype(f32)
    gate = 1.0 / (1.0 + jnp.exp(-z))
    hidden = center + z * gate
    slope_ref[...] = (gate * (1.0 + z * (1.0 - gate))).astype(bf16)
    hidden_b = hidden.astype(bf16)
    hidden_ref[...] = hidden_b
    kv_ref[...] = dot_nn(hidden_b, kv_w_ref[...]).astype(bf16)
    rest = (hidden - hidden_b.astype(f32)).astype(bf16)
    pick = patch_pick(pool_ref.shape[0], BLOCK, 0)
    pool_ref[...] = (dot_nn(pick, hidden_b) + dot_nn(pick, rest)).astype(bf16)


def token_forward(wide, conv_rows, kv_weight):
    steps = CELLS // BLOCK
    whole = lambda i: (0, 0)
    block = lambda i: (i, 0)
    return pl.pallas_call(
        token_forward_kernel,
        grid=(steps,),
        in_specs=[
            pl.BlockSpec(wide.shape, whole),
            pl.BlockSpec((3, 3 * CH, CH), lambda i: (0, 0, 0)),
            pl.BlockSpec((CH, 2 * CH), whole),
        ],
        out_specs=[
            pl.BlockSpec((BLOCK, CH), block),
            pl.BlockSpec((BLOCK, CH), block),
            pl.BlockSpec((BLOCK, 2 * CH), block),
            pl.BlockSpec((CTX // steps, CH), block),
        ],
        out_shape=[
            lasting((CELLS, CH), bf16),
            lasting((CELLS, CH), bf16),
            jax.ShapeDtypeStruct((CELLS, 2 * CH), bf16),
            jax.ShapeDtypeStruct((CTX, CH), bf16),
        ],
        compiler_params=params(),
        cost_estimate=cost(22 * CELLS * CH * CH, 14 * CELLS * CH, CELLS * CH),
    )(stay(wide), conv_rows, kv_weight)


def token_backward_kernel(
    core_ref, dkv_ref, slope_ref, pool_ref, hidden_ref, x_ref, kv_w_ref, query_g_ref, out_g_ref,
    d_hidden_ref, gz_ref, keep_ref, give_ref, conv_s, kv_s, *, sizes
):
    step = pl.program_id(0)

    @pl.when(step == 0)
    def _():
        conv_s[...] = jnp.zeros_like(conv_s)
        kv_s[...] = jnp.zeros_like(kv_s)

    dkv = dkv_ref[...]
    d_hidden = dot_nt(dkv, kv_w_ref[...])
    d_hidden = d_hidden + dot_nn(patch_pick(BLOCK, pool_ref.shape[0], 1), pool_ref[...])
    gz = (d_hidden * slope_ref[...].astype(f32)).astype(bf16)
    d_hidden_ref[...] = d_hidden
    gz_ref[...] = gz
    kv_s[...] += dot_tn(hidden_ref[...], dkv)
    gz_t = gz.T
    for row in range(3):
        conv_s[row] += dot_nn(gz_t, x_ref[image_rows(step, row), :])

    @pl.when(step == pl.num_programs(0) - 1)
    def _():
        tiles = []
        for row in range(3):
            for col in range(3):
                tiles.append(conv_s[row, :, col * CH : (col + 1) * CH].T)
        tiles = tiles + [query_g_ref[...], kv_s[:, :CH], kv_s[:, CH:], out_g_ref[...]]
        for at, tile in enumerate(tiles):
            write_cores(core_ref[0], tile.astype(f32), (keep_ref, give_ref), sizes, "yx", at)


def token_backward(dkv, slope, d_pool, hidden_b, wide, kv_weight, query_g, out_g):
    steps = CELLS // BLOCK
    whole = lambda i: (0, 0)
    block = lambda i: (i, 0)
    return pl.pallas_call(
        functools.partial(token_backward_kernel, sizes=slice_shape()),
        grid=(steps,),
        in_specs=[
            CORE_SPEC,
            pl.BlockSpec((BLOCK, 2 * CH), block),
            pl.BlockSpec((BLOCK, CH), block),
            pl.BlockSpec((CTX // steps, CH), block),
            pl.BlockSpec((BLOCK, CH), block),
            pl.BlockSpec(wide.shape, whole),
            pl.BlockSpec((CH, 2 * CH), whole),
            pl.BlockSpec((CH, CH), whole),
            pl.BlockSpec((CH, CH), whole),
        ],
        out_specs=[
            pl.BlockSpec((BLOCK, CH), block),
            pl.BlockSpec((BLOCK, CH), block),
            core_block(EARLY, "yx", lambda i: 0, CH),
            core_block(EARLY, "yx", lambda i: 0, CH),
        ],
        out_shape=[
            jax.ShapeDtypeStruct((CELLS, CH), f32),
            jax.ShapeDtypeStruct((CELLS, CH), bf16),
            jax.ShapeDtypeStruct(core_shape(EARLY, "yx", CH), bf16),
            jax.ShapeDtypeStruct(core_shape(EARLY, "yx", CH), bf16),
        ],
        scratch_shapes=[pltpu.VMEM((3, CH, 3 * CH), f32), pltpu.VMEM((CH, 2 * CH), f32)],
        compiler_params=params(),
        cost_estimate=cost(26 * CELLS * CH * CH, 20 * CELLS * CH),
    )(core_here(), dkv, stay(slope), d_pool, stay(hidden_b), stay(wide), kv_weight, query_g, out_g)


def context_backward_kernel(gz_ref, d_hidden_ref, conv_ref, out_ref, wide_s):
    step = pl.program_id(0)
    steps = pl.num_programs(0)

    def widen(at):
        values = gz_ref[image_rows(at, 0), :].astype(f32)
        col = lax.broadcasted_iota(jnp.int32, (BLOCK, CH), 0) % IMG
        left = jnp.where(col == 0, 0.0, pltpu.roll(values, 1, 0))
        right = jnp.where(col == IMG - 1, 0.0, pltpu.roll(values, BLOCK - 1, 0))
        wide_s[image_rows(at, 1), 0:CH] = left.astype(bf16)
        wide_s[image_rows(at, 1), CH : 2 * CH] = values.astype(bf16)
        wide_s[image_rows(at, 1), 2 * CH :] = right.astype(bf16)

    @pl.when(step == 0)
    def _():
        wide_s[0:IMG, :] = jnp.zeros((IMG, 3 * CH), bf16)
        wide_s[CELLS + IMG :, :] = jnp.zeros((IMG, 3 * CH), bf16)
        widen(0)

    @pl.when(step < steps - 1)
    def _():
        widen(step + 1)

    total = d_hidden_ref[...]
    for row in range(3):
        values = wide_s[image_rows(step, row), :]
        for col in range(3):
            tap = conv_ref[3 * (2 - row) + (2 - col)]
            total = total + dot_nt(values[:, col * CH : (col + 1) * CH], tap)
    out_ref[...] = total.astype(bf16)


def context_backward(gz, d_hidden, conv_tiles):
    block = lambda i: (i, 0)
    return pl.pallas_call(
        context_backward_kernel,
        grid=(CELLS // BLOCK,),
        in_specs=[
            pl.BlockSpec((CELLS, CH), lambda i: (0, 0)),
            pl.BlockSpec((BLOCK, CH), block),
            pl.BlockSpec((9, CH, CH), lambda i: (0, 0, 0)),
        ],
        out_specs=pl.BlockSpec((BLOCK, CH), block),
        out_shape=jax.ShapeDtypeStruct((CELLS, CH), bf16),
        scratch_shapes=[pltpu.VMEM((CELLS + 2 * IMG, 3 * CH), bf16)],
        compiler_params=params(),
        cost_estimate=cost(18 * CELLS * CH * CH, 8 * CELLS * CH),
    )(gz, d_hidden, conv_tiles)


def local(
    context_map,
    future_feats,
    horizon,
    cotangent,
    tile_owner,
    master_tiles,
    moment_first,
    moment_second,
    norm_gains,
    gain_first,
    gain_second,
):
    slot_count = master_tiles.shape[0]
    devices = lax.axis_size(AXES)
    rows = CH // devices
    slot_of = slot_index(tile_owner, slot_count)

    length = CTX + FT * horizon
    valid = jnp.arange(SEQ) < length[0]
    gd = jnp.where(valid[:, None], cotangent[0], jnp.zeros((), bf16))

    slices = (
        master_tiles.astype(bf16)
        .reshape(slot_count, devices, rows, CH)
        .transpose(1, 0, 2, 3)
    )
    slices = lax.all_to_all(slices, AXES, split_axis=0, concat_axis=0, tiled=True)
    extra = max(1, 8 // rows)
    tiles = tile_owner.shape[0]
    span = slot_count + extra
    place = jnp.arange(devices * span)
    device, at = place // span, place % span
    found = slot_of[None, :] == jnp.where(at < slot_count, device * slot_count + at, -1)[:, None]
    tile_of = jnp.sum(jnp.where(found, jnp.arange(tiles)[None], 0), 1)
    tile_of = jnp.where(at < slot_count, tile_of, tiles + at - slot_count)
    mine_at = lax.axis_index(AXES) * slot_count + jnp.arange(slot_count)
    used = jnp.any(slot_of[None, :] == mine_at[:, None], 1).astype(f32)
    slices, gd, tile_of, used = tie((slices, gd, tile_of, used))
    slices = slices.reshape(devices * slot_count, rows, CH)
    slices = slices.at[slot_of].get(mode="promise_in_bounds")
    early, emb, qkv, att, up, down = jnp.split(slices, (13, 16, 43, 52, 88))
    mlp = jnp.concatenate([from_tiles(up, 3, 4), from_tiles(down, 12, 1)], 0)
    early = gather_axes(early, "z")
    core = jnp.concatenate([from_tiles(qkv, 3, 3), from_tiles(att, 3, 1), from_tiles(emb, 1, 1)], 0)
    core, early = tie((core, early))
    early = gather_axes(joined(early), ("y", "x"))
    core = gather_axes(core, "z")
    pieces = trade_rows(context_map)
    early = joined(gather_axes(joined(early), "c"))
    early = device_order(early, ("c", "y", "x", "z"))
    wide = widen(pieces)
    core = joined(core)
    low, high = gather_axes(core[:6], "x"), gather_axes(core[6:], "y")

    conv_tiles = early[:9]
    to_query, to_out = early[9], early[12]
    kv_weight = jnp.concatenate([early[10], early[11]], 1)

    wide, mlp, low, high = hold((wide, mlp), low, high)
    mlp = lax.all_gather(mlp, AXES, axis=1, tiled=True)
    low, high = joined(low), joined(high)
    wide, low, high = tie((wide, low, high))
    low, high = gather_axes(low, "y"), gather_axes(high, "x")
    slope_z, hidden_b, kv, pooled = token_forward(
        wide, conv_tiles.reshape(3, 3 * CH, CH), kv_weight
    )
    kv, low, high = hold((kv,), low, high)
    low, high = joined(low), joined(high)
    feats_b = future_feats[0]
    query = jnp.dot(feats_b, to_query, preferred_element_type=f32).astype(bf16)
    kv, low, high = tie((kv, low, high))
    low, high = gather_axes(low, "c"), gather_axes(high, "c")
    cross_mixed, cross_logs = cross_forward(query, kv)
    cross_mixed, low, high = hold((cross_mixed,), low, high)
    weights = place_rows(low, high)

    gain_one, gain_two = norm_gains[:1], norm_gains[1:]
    seq, embed, normed_one, qkv = embed_forward(
        pooled, feats_b, cross_mixed, to_out, weights, gain_one
    )
    mixed, logs = self_forward(qkv, length)
    (
        block_out, d_stream, gog, up_keep, up_give, down_keep, down_give, att_keep, att_give,
        gain_g_two,
    ) = mlp_block(mixed, embed, weights, mlp, gain_two, gd)
    up = core_cuts([up_keep, up_give], "yx")
    down = core_cuts([down_keep, down_give], "xy")
    att = core_cuts([att_keep, att_give], "yx")
    gog, up, down, att = tie((gog, up, down, att))
    up, down, att = send(up, "c"), send(down, "c"), send(att, "c")
    gqkv = self_backward(qkv, gog, mixed, logs, length, 2)
    gqkv, up, down, att = hold((gqkv,), up, down, att)
    up, down = advance(up, "y", 0), advance(down, "x", 0)
    gqkv, up, down = tie((gqkv, up, down))
    up, down = send(up, "y"), send(down, "x")
    (
        qk_keep, qk_give, v_keep, v_give, emb_keep, emb_give, gupd, pool_g, out_g, gox,
    ) = embed_grad(
        length, qkv, gog, mixed, logs, gqkv, normed_one, weights, embed, d_stream, seq,
        cross_mixed, to_out, gain_one, gain_g_two,
    )
    first = core_cuts([qk_keep, qk_give], "xy")
    second = core_cuts([v_keep, v_give], "yx")
    emb = core_cuts([emb_keep, emb_give], "xy")
    gox, gupd, first, second, emb, up, down = hold((gox, gupd, first, second, emb), up, down)
    up, down = advance(up, "x", 0), advance(down, "y", 0)
    gox, up, down, first, second, emb = tie((gox, up, down, first, second, emb))
    up, down, emb = send(up, "x"), send(down, "y"), send(emb, "c")
    first, second = send(first, "c"), send(second, "c")

    log_rows = jnp.concatenate([cross_logs[0], cross_logs[1]], 1)
    gkv, query_g, future_grad = cross_backward(
        query, kv, gox, cross_mixed, log_rows, feats_b, gupd, to_query
    )
    gkv, up, down, first, second, emb = hold((gkv,), up, down, first, second, emb)
    mlp = advance_near([split_z(jnp.concatenate(part, 0)) for part in zip(up, down)])
    emb = advance(emb, "x", 0)
    second = [jnp.concatenate([p, q], 2) for p, q in zip(second, att)]
    first, second = advance(first, "x", 0), advance(second, "y", 0)
    gkv, mlp, first, second, emb = tie((gkv, mlp, first, second, emb))
    mlp, emb = send(mlp, "z"), send(emb, "x")
    first, second = send(first, "x"), send(second, "y")

    d_hidden, gz, early_keep, early_give = token_backward(
        gkv, slope_z, pool_g, hidden_b, wide, kv_weight, query_g, out_g
    )
    d_hidden, gz, early_keep, early_give, mlp, first, second, emb = hold(
        (d_hidden, gz, early_keep, early_give), mlp, first, second, emb
    )
    early = core_cuts([early_keep, early_give], "yx")
    early, mlp, first, second, emb = tie((early, mlp, first, second, emb))
    early = send(early, "c")
    first, second = advance(first, "y", 0), advance(second, "x", 0)
    emb, mlp = advance(emb, "y", 0), advance_far(mlp)
    first, second = send(first, "y"), send(second, "x")
    emb, mlp = send(emb, "y"), send(mlp, "z", 2)
    gz, early, first, second, emb = hold((gz,), early, first, second, emb)
    early = advance([p.reshape((-1,) + p.shape[2:]) for p in early], ("y", "x"), 0)
    att = advance_near([split_z(jnp.concatenate(part, 0)) for part in zip(first, second)])
    gz, early, att = tie((gz, early, att))
    early, att = send(early, ("y", "x")), send(att, "z")
    context_grad = context_backward(gz, d_hidden, conv_tiles)
    context_grad, early, att, mlp = hold((context_grad,), early, att, mlp)
    early = advance([split_z(part) for part in early], "z", 1)
    emb = advance([split_z(part) for part in emb], "z", 1)
    early = [jnp.concatenate([e, to_tiles(m)], 0) for e, m in zip(early, emb)]
    att = advance_far(att)
    context_grad, early, att = tie((context_grad, early, att))
    early, att = send(early, "z"), send(att, "z", 2)
    pieces = trade_rows(context_grad.reshape(context_map.shape))
    sum_mlp = add_up(mlp, keep_wide=True)
    square_mlp = jnp.sum(sum_mlp * sum_mlp)
    half = sum_mlp.shape[0] // 2
    mlp = jnp.concatenate([to_tiles(sum_mlp[:half], 4), to_tiles(sum_mlp[half:])], 0).astype(bf16)
    sum_early = add_up(early, keep_wide=True)
    sum_att = add_up(att, keep_wide=True)

    gains = sum_early[EARLY + 3 :, 0]
    square = square_mlp + jnp.sum(sum_att * sum_att) + jnp.sum(sum_early * sum_early)
    share = jnp.concatenate([gains, jnp.broadcast_to(square, (1, CH))], 0)
    share_high = share.astype(bf16)
    share_low = (share - share_high.astype(f32)).astype(bf16)
    share = jnp.concatenate([share_high, share_low], 0)
    share = jnp.pad(share, ((0, extra * rows - share.shape[0]), (0, 0)))
    sums = jnp.concatenate(
        [
            sum_early[: EARLY + 3].astype(bf16),
            to_tiles(sum_att[:9], 3).astype(bf16),
            to_tiles(sum_att[9:]).astype(bf16),
            mlp,
            share.reshape(extra, rows, CH),
        ],
        0,
    )
    mine = sums.at[tile_of].get(mode="promise_in_bounds")
    mine = mine.reshape(devices, slot_count + extra, rows, CH)
    mine, pieces[-1] = tie((mine, pieces[-1]))
    mine = lax.all_to_all(mine, AXES, split_axis=0, concat_axis=0, tiled=True)
    shares = mine[:, slot_count:].reshape(devices, -1, CH).astype(f32)
    shares = shares[:, :4] + shares[:, 4:8]
    gains = shares[:2, :3].reshape(2, D)
    mine = mine[:, :slot_count].transpose(1, 0, 2, 3).reshape(slot_count, CH, CH).astype(f32)

    used = used[:, None, None]
    grad_norm = jnp.sqrt(jnp.sum(shares[:, 3, 0]))
    factor = jnp.minimum(1.0, clip_level / (grad_norm + 1e-06))
    new_first, new_second, new_master = adam_step(
        master_tiles, mine * factor, moment_first, moment_second, learn_rate, decay_rate
    )
    new_gain_first, new_gain_second, new_gains = adam_step(
        norm_gains, gains * factor, gain_first, gain_second, gain_rate, 0.0
    )
    return (
        block_out[None],
        row_order(pieces).reshape(context_map.shape),
        future_grad[None],
        jnp.where(used > 0, new_first, 0.0),
        jnp.where(used > 0, new_second, 0.0),
        jnp.where(used > 0, new_master, 0.0),
        new_gain_first,
        new_gain_second,
        new_gains,
        grad_norm,
    )


def solution(mesh):
    groups, rows = mesh.devices.shape
    fine = jax.sharding.Mesh(mesh.devices.reshape(groups // 2, 2, rows // 2, 2), AXES)
    whole = P(AXES, None, None)
    image = P(("z", "c"), ("y", "x"), None, None)
    in_specs = (image, whole, P(AXES), whole, P(), whole, whole, whole, P(), P(), P())
    out_specs = (whole, image, whole, whole, whole, whole, P(), P(), P(), P())
    return jax.shard_map(local, mesh=fine, in_specs=in_specs, out_specs=out_specs, check_vma=False)
```

```python
import functools

import jax
import jax.numpy as jnp
from jax import lax
from jax.experimental import pallas as pl
from jax.experimental.pallas import tpu as pltpu
from jax.sharding import PartitionSpec as P

CH = 256
HD = 64
HEADS = 12
D = 768
FF = 3072
TH = 4
IMG = 64
PATCH = 4
FT = 16
CTX = 256
SEQ = 736
STEP = 10


eps_norm = 1e-05
beta_one = 0.9
beta_two = 0.999
learn_rate = 0.02
gain_rate = 0.6
decay_rate = 0.1
adam_eps = 1e-08
clip_level = 1.0
neg_large = -1e30
AXES = ("z", "c", "y", "x")
CELLS = IMG * IMG
BLOCK = 512
GROUP = 4
EARLY = 13
VMEM_BYTES = 28 * 1024 * 1024
MLP_BYTES = 40 * 1024 * 1024
ROW_BLOCKS = ((0, 256), (256, 256), (512, 224))
CORE_SPEC = pl.BlockSpec(memory_space=pltpu.SMEM)
bf16 = jnp.bfloat16
f32 = jnp.float32


def slot_index(tile_owner, slot_count):
    ordinal = jnp.arange(tile_owner.shape[0])
    earlier = (tile_owner[None, :] == tile_owner[:, None]) & (ordinal[None, :] < ordinal[:, None])
    return tile_owner * slot_count + jnp.sum(earlier.astype(jnp.int32), 1)


def adam_step(weight, grad_now, first, second, rate, decay):
    first_new = beta_one * first + (1.0 - beta_one) * grad_now
    second_new = beta_two * second + (1.0 - beta_two) * grad_now * grad_now
    corr_first = first_new / (1.0 - beta_one**STEP)
    corr_second = second_new / (1.0 - beta_two**STEP)
    weight_new = weight - rate * (corr_first / (jnp.sqrt(corr_second) + adam_eps) + decay * weight)
    return (first_new, second_new, weight_new)


def xor_permute(values, axes, mask):
    count = lax.axis_size(axes)
    return lax.ppermute(values, axes, [(i, i ^ mask) for i in range(count)])


def pick(parts, index, dim):
    if parts[0].shape[dim] == 2:
        total = add_up(parts)
        first, second = (lax.index_in_dim(total, at, dim, False) for at in range(2))
        return jnp.where(index == 0, first, second)
    return add_up([lax.dynamic_index_in_dim(part, index, dim, False) for part in parts])


def advance(parts, axes, dim):
    mine = lax.axis_index(axes)
    return [pick(parts, mine ^ mask, dim) for mask in range(lax.axis_size(axes))]


def advance_near(parts):
    mine = lax.axis_index("z") % 2
    shape = parts[0].shape
    parts = [p.reshape((shape[0], shape[1] // 2, 2) + shape[2:]) for p in parts]
    return [pick(parts, mine ^ mask, 2) for mask in range(2)]


def advance_far(parts):
    mine = lax.axis_index("z") // 2
    return [pick(parts, mine ^ mask, 1) for mask in range(parts[0].shape[1])]


def send(cuts, axes, unit=1):
    return [cuts[0]] + [
        xor_permute(cut, axes, unit * mask) for mask, cut in enumerate(cuts) if mask > 0
    ]


def add_up(parts, keep_wide=False):
    total = parts[0].astype(f32)
    for part in parts[1:]:
        total = total + part.astype(f32)
    return total if keep_wide else total.astype(parts[0].dtype)


def hold(values, *sums):
    tied = lax.optimization_barrier((tuple(values), tuple(tuple(parts) for parts in sums)))
    return tied[0] + tuple(list(parts) for parts in tied[1])


def gather_axes(values, axes):
    return [values] + [
        xor_permute(values, axes, mask) for mask in range(1, lax.axis_size(axes))
    ]


def joined(pieces):
    return jnp.stack(pieces, 1)


def device_order(values, axes):
    sizes = [lax.axis_size(axis) for axis in AXES]
    own = [lax.axis_index(axis) for axis in AXES]
    places = jnp.unravel_index(jnp.arange(lax.axis_size(AXES)), sizes)
    at = 0
    for axis in axes:
        which = AXES.index(axis)
        at = at * sizes[which] + (places[which] ^ own[which])
    values = values.reshape((values.shape[0], -1) + values.shape[-2:])
    values = values.at[:, at].get(mode="promise_in_bounds")
    return values.reshape(values.shape[0], -1, values.shape[-1])


def place_kernel(own_ref, low_ref, low_other_ref, high_ref, high_other_ref, out_ref, *, half, sizes):
    z_count, c_count, y_count, x_count = sizes
    own_z, own_c, own_y, own_x = (own_ref[axis] for axis in range(4))
    step = pl.program_id(0)

    def place(near_ref, far_ref, x_first):
        for z in range(z_count):
            for y in range(y_count):
                for x in range(x_count):
                    if x_first:
                        at = (x ^ own_x) * y_count + (y ^ own_y)
                    else:
                        at = (y ^ own_y) * x_count + (x ^ own_x)
                    at = at * z_count + (z ^ own_z)
                    near, far = near_ref[0, at], far_ref[0, at]
                    for c in range(c_count):
                        to = ((z * c_count + c) * y_count + y) * x_count + x
                        out_ref[0, to] = jnp.where(own_c == c, near, far)

    @pl.when(step < half)
    def _():
        place(low_ref, low_other_ref, False)

    @pl.when(step >= half)
    def _():
        place(high_ref, high_other_ref, True)


def place_rows(low, high):
    sizes = tuple(lax.axis_size(axis) for axis in AXES)
    half, rows = low[0].shape[0], low[0].shape[-2]
    count = half + high[0].shape[0]
    own = jnp.stack([lax.axis_index(axis) for axis in AXES]).astype(jnp.int32)
    pieces = [part.reshape(part.shape[0], -1, rows, D) for part in low + high]
    block = (1,) + pieces[0].shape[1:]
    early = pl.BlockSpec(block, lambda i: (jnp.minimum(i, half - 1), 0, 0, 0))
    later = pl.BlockSpec(block, lambda i: (jnp.maximum(i - half, 0), 0, 0, 0))
    devices = CH // rows
    out = pl.pallas_call(
        functools.partial(place_kernel, half=half, sizes=sizes),
        grid=(count,),
        in_specs=[CORE_SPEC, early, early, later, later],
        out_specs=pl.BlockSpec((1, devices, rows, D), lambda i: (i, 0, 0, 0)),
        out_shape=jax.ShapeDtypeStruct((count, devices, rows, D), bf16),
        compiler_params=params(),
        cost_estimate=cost(0, 4 * count * CH * D),
    )(own, *pieces)
    return out.reshape(count, CH, D)


def trade_rows(values):
    mine = lax.axis_index(("y", "x"))
    count = lax.axis_size(("y", "x"))
    cuts = [lax.dynamic_index_in_dim(values, mine ^ mask, 0, False) for mask in range(count)]
    return send(cuts, ("y", "x"))


def row_order_kernel(row_ref, *refs):
    at = pl.program_id(0) ^ row_ref[0]
    values = refs[0][...]
    for mask in range(1, len(refs) - 1):
        values = jnp.where(at == mask, refs[mask][...], values)
    refs[-1][0] = values.astype(f32)


def row_order(pieces):
    count = len(pieces)
    cells = pieces[0].size // CH
    return pl.pallas_call(
        row_order_kernel,
        grid=(count,),
        in_specs=[CORE_SPEC] + [pl.BlockSpec((cells, CH), lambda i: (0, 0))] * count,
        out_specs=pl.BlockSpec((1, cells, CH), lambda i: (i, 0, 0)),
        out_shape=jax.ShapeDtypeStruct((count, cells, CH), f32),
        compiler_params=params(),
        cost_estimate=cost(0, 6 * count * cells * CH),
    )(row_here(), *[piece.reshape(cells, CH) for piece in pieces])


def widen_kernel(row_ref, *refs):
    out_ref = refs[-1]
    cells = refs[0].shape[0]
    col = lax.broadcasted_iota(jnp.int32, (cells, CH), 0) % IMG
    out_ref[0:IMG, :] = jnp.zeros((IMG, 3 * CH), bf16)
    out_ref[CELLS + IMG :, :] = jnp.zeros((IMG, 3 * CH), bf16)
    for at in range(len(refs) - 1):
        values = refs[at][...]
        for mask in range(1, len(refs) - 1):
            values = jnp.where(row_ref[0] == mask, refs[at ^ mask][...], values)
        here = slice(IMG + at * cells, IMG + (at + 1) * cells)
        out_ref[here, CH : 2 * CH] = values
        values = values.astype(f32)
        left = jnp.where(col == 0, 0.0, pltpu.roll(values, 1, 0))
        right = jnp.where(col == IMG - 1, 0.0, pltpu.roll(values, cells - 1, 0))
        out_ref[here, 0:CH] = left.astype(bf16)
        out_ref[here, 2 * CH :] = right.astype(bf16)


def widen(pieces):
    cells = pieces[0].size // CH
    vmem = pl.BlockSpec(memory_space=pltpu.VMEM)
    return pl.pallas_call(
        widen_kernel,
        in_specs=[CORE_SPEC] + [vmem] * len(pieces),
        out_specs=vmem,
        out_shape=lasting((CELLS + 2 * IMG, 3 * CH), bf16),
        compiler_params=params(),
        cost_estimate=cost(0, 8 * CELLS * CH),
    )(row_here(), *[piece.reshape(cells, CH) for piece in pieces])


def slice_shape():
    z, c, y, x = [lax.axis_size(axis) for axis in AXES]
    return (z, y, x, CH // (z * c * y * x))


tie = lax.optimization_barrier


def to_tiles(slices, parts=1):
    blocks, rows, columns = slices.shape
    return (
        slices.reshape(parts, blocks // parts, rows, columns // CH, CH)
        .transpose(1, 0, 3, 2, 4)
        .reshape(-1, rows, CH)
    )


def from_tiles(tiles, row_blocks, parts):
    rows = tiles.shape[1]
    return (
        tiles.reshape(row_blocks, parts, D // CH, rows, CH)
        .transpose(1, 0, 3, 2, 4)
        .reshape(parts * row_blocks, rows, D)
    )


def dot_nt(a, b):
    return lax.dot_general(a, b, (((1,), (1,)), ((), ())), preferred_element_type=f32)


def dot_nn(a, b):
    return lax.dot_general(a, b, (((1,), (0,)), ((), ())), preferred_element_type=f32)


def dot_tn(a, b):
    return lax.dot_general(a, b, (((0,), (0,)), ((), ())), preferred_element_type=f32)


def head_mask(shape, head):
    return (lax.broadcasted_iota(jnp.int32, shape, len(shape) - 1) // HD) == head


def cost(flops, moved, transcendentals=0):
    return pl.CostEstimate(
        flops=int(flops), bytes_accessed=int(moved), transcendentals=int(transcendentals)
    )


def stay(values):
    return pltpu.with_memory_space_constraint(values, pltpu.HBM)


lasting = pltpu.HBM


def params():
    return pltpu.CompilerParams(vmem_limit_bytes=VMEM_BYTES)


def cross_forward_kernel(q_ref, k_ref, v_ref, o_ref, l_ref):
    rows = q_ref.shape[0]
    lane = lax.broadcasted_iota(jnp.int32, (rows, 128), 1)
    q = q_ref[...]
    mixed = jnp.zeros((rows, CH), f32)
    stat = jnp.zeros((rows, 128), f32)
    for head in range(TH):
        mask = head_mask((rows, CH), head)
        q_head = jnp.where(mask, q.astype(f32) * 0.125, 0.0).astype(bf16)
        scores = dot_nt(q_head, k_ref[...])
        peak = jnp.max(scores, -1, keepdims=True)
        shifted = jnp.exp(scores - peak)
        total = jnp.sum(shifted, -1, keepdims=True)
        part = dot_nn(shifted.astype(bf16), v_ref[...])
        mixed = jnp.where(mask, part / total, mixed)
        stat = jnp.where(lane == head, peak + jnp.log(total), stat)
    o_ref[...] = mixed.astype(bf16)
    l_ref[0] = stat.T[:8]


def cross_forward(query, kv):
    rows = query.shape[0] // 1
    cells = kv.shape[0]
    return pl.pallas_call(
        cross_forward_kernel,
        grid=(1,),
        in_specs=[
            pl.BlockSpec((rows, CH), lambda i: (i, 0)),
            pl.BlockSpec((cells, CH), lambda i: (0, 0)),
            pl.BlockSpec((cells, CH), lambda i: (0, 1)),
        ],
        out_specs=[
            pl.BlockSpec((rows, CH), lambda i: (i, 0)),
            pl.BlockSpec((1, 8, rows), lambda i: (i, 0, 0)),
        ],
        out_shape=[
            jax.ShapeDtypeStruct((rows, CH), bf16),
            jax.ShapeDtypeStruct((1, 8, rows), f32),
        ],
        compiler_params=params(),
        cost_estimate=cost(16 * TH * rows * cells * CH // 2, 8 * cells * CH, 2 * TH * rows * cells),
    )(query, kv, kv)


def delta_rows(d_out, out):
    product = d_out.astype(f32) * out.astype(f32)
    head = lax.broadcasted_iota(jnp.int32, (8, CH), 0)
    lane = lax.broadcasted_iota(jnp.int32, (8, CH), 1)
    pick = ((lane // HD) == head).astype(f32)
    return lax.dot_general(
        pick,
        product,
        (((1,), (1,)), ((), ())),
        precision=lax.Precision.HIGHEST,
        preferred_element_type=f32,
    )


def cross_backward_kernel(
    q_ref, k_ref, v_ref, do_ref, o_ref, l_ref, feats_ref, gupd_ref, query_w_ref,
    dkv_ref, query_g_ref, future_ref, q_s, do_s, delta_s, dq_s,
):
    step = pl.program_id(0)
    rows = q_ref.shape[0]

    @pl.when(step == 0)
    def _():
        for head in range(TH):
            mask = head_mask((rows, CH), head)
            q_s[head] = jnp.where(mask, q_ref[...].astype(f32) * 0.125, 0.0).astype(bf16)
            do_s[head] = jnp.where(mask, do_ref[...].astype(f32), 0.0).astype(bf16)
        delta_s[...] = delta_rows(do_ref[...], o_ref[...])
        dq_s[...] = jnp.zeros_like(dq_s)

    cells = k_ref.shape[0]
    dk = jnp.zeros((cells, CH), f32)
    dv = jnp.zeros((cells, CH), f32)
    dq = dq_s[...]
    k = k_ref[...]
    for head in range(TH):
        probs = jnp.exp(dot_nt(k, q_s[head]) - l_ref[head : head + 1, :])
        d_probs = dot_nt(v_ref[...], do_s[head])
        d_scores = (probs * (d_probs - delta_s[head : head + 1, :])).astype(bf16)
        dv = dv + dot_nn(probs.astype(bf16), do_s[head])
        dk = dk + dot_nn(d_scores, q_s[head])
        dq = dq + jnp.where(head_mask((rows, CH), head), dot_tn(d_scores, k), 0.0)
    dq_s[...] = dq
    dkv_ref[:, :CH] = dk.astype(bf16)
    dkv_ref[:, CH:] = dv.astype(bf16)

    @pl.when(step == pl.num_programs(0) - 1)
    def _():
        gq = (dq_s[...] * 0.125).astype(bf16)
        query_g_ref[...] = dot_tn(feats_ref[...], gq).astype(bf16)
        future_ref[...] = gupd_ref[...] + dot_nt(gq, query_w_ref[...])


def cross_backward(query, kv, d_out, out, log_rows, feats, gupd, to_query):
    rows = query.shape[0]
    cells = kv.shape[0]
    block = 1024
    whole = lambda i: (0, 0)
    return pl.pallas_call(
        cross_backward_kernel,
        grid=(cells // block,),
        in_specs=[
            pl.BlockSpec((rows, CH), whole),
            pl.BlockSpec((block, CH), lambda i: (i, 0)),
            pl.BlockSpec((block, CH), lambda i: (i, 1)),
            pl.BlockSpec((rows, CH), whole),
            pl.BlockSpec((rows, CH), whole),
            pl.BlockSpec((8, rows), whole),
            pl.BlockSpec((rows, CH), whole),
            pl.BlockSpec((rows, CH), whole),
            pl.BlockSpec((CH, CH), whole),
        ],
        out_specs=[
            pl.BlockSpec((block, 2 * CH), lambda i: (i, 0)),
            pl.BlockSpec((CH, CH), whole),
            pl.BlockSpec((rows, CH), whole),
        ],
        out_shape=[
            jax.ShapeDtypeStruct((cells, 2 * CH), bf16),
            jax.ShapeDtypeStruct((CH, CH), bf16),
            jax.ShapeDtypeStruct((rows, CH), f32),
        ],
        scratch_shapes=[
            pltpu.VMEM((TH, rows, CH), bf16),
            pltpu.VMEM((TH, rows, CH), bf16),
            pltpu.VMEM((8, rows), f32),
            pltpu.VMEM((rows, CH), f32),
        ],
        compiler_params=params(),
        cost_estimate=cost(10 * TH * rows * cells * CH, 8 * cells * CH, TH * rows * cells),
    )(query, kv, kv, d_out, out, log_rows, feats, gupd, to_query)


def self_forward_kernel(len_ref, q_ref, k_ref, v_ref, o_ref, l_ref):
    group = pl.program_id(0)
    length = len_ref[0]
    for start, count in ROW_BLOCKS:
        stop = start + count
        q = q_ref[0, start:stop, :].astype(f32) * 0.125
        row = lax.broadcasted_iota(jnp.int32, (count, 1), 0) + start
        bound = jnp.minimum(row, length - 1)
        allowed = lax.broadcasted_iota(jnp.int32, (count, stop), 1) <= bound
        mixed = jnp.zeros((count, CH), f32)
        stat = jnp.zeros((count, 128), f32)
        lane = lax.broadcasted_iota(jnp.int32, (count, 128), 1)
        for head in range(GROUP):
            mask = head_mask((count, CH), head)
            q_head = jnp.where(mask, q, 0.0).astype(bf16)
            scores = jnp.where(allowed, dot_nt(q_head, k_ref[0, :stop, :]), neg_large)
            peak = jnp.max(scores, -1, keepdims=True)
            shifted = jnp.exp(scores - peak)
            total = jnp.sum(shifted, -1, keepdims=True)
            part = dot_nn(shifted.astype(bf16), v_ref[0, :stop, :])
            mixed = jnp.where(mask, part / total, mixed)
            stat = jnp.where(lane == head, peak + jnp.log(total), stat)
        o_ref[start:stop, :] = mixed.astype(bf16)
        l_ref[0, :, start:stop] = stat.T[:8]


def self_forward(qkv, length):
    groups = D // CH
    at = lambda j: (lambda i, n: (j, 0, i))
    return pl.pallas_call(
        self_forward_kernel,
        grid_spec=pltpu.PrefetchScalarGridSpec(
            num_scalar_prefetch=1,
            grid=(groups,),
            in_specs=[pl.BlockSpec((1, SEQ, CH), at(j)) for j in range(3)],
            out_specs=[
                pl.BlockSpec((SEQ, CH), lambda i, n: (0, i)),
                pl.BlockSpec((1, 8, SEQ), lambda i, n: (i, 0, 0)),
            ],
        ),
        out_shape=[
            lasting((SEQ, D), bf16),
            jax.ShapeDtypeStruct((groups, 8, SEQ), f32),
        ],
        compiler_params=params(),
        cost_estimate=cost(4 * HEADS * SEQ * SEQ * CH, 8 * SEQ * D, HEADS * SEQ * SEQ),
    )(length, qkv, qkv, qkv)


def self_backward_kernel(
    len_ref, q_ref, k_ref, v_ref, do_ref, o_ref, l_ref, out_ref, dk_s, dv_s
):
    length = len_ref[0]
    dk_s[...] = jnp.zeros_like(dk_s)
    dv_s[...] = jnp.zeros_like(dv_s)
    delta = delta_rows(do_ref[...], o_ref[...])
    for start, count in ROW_BLOCKS:
        stop = start + count
        q = q_ref[0, start:stop, :].astype(f32) * 0.125
        d_out = do_ref[start:stop, :].astype(f32)
        row = lax.broadcasted_iota(jnp.int32, (1, count), 1) + start
        bound = jnp.minimum(row, length - 1)
        allowed = lax.broadcasted_iota(jnp.int32, (stop, count), 0) <= bound
        dq = jnp.zeros((count, CH), f32)
        k = k_ref[0, :stop, :]
        v = v_ref[0, :stop, :]
        dk = dk_s[:stop, :]
        dv = dv_s[:stop, :]
        for head in range(GROUP):
            mask = head_mask((count, CH), head)
            q_head = jnp.where(mask, q, 0.0).astype(bf16)
            d_head = jnp.where(mask, d_out, 0.0).astype(bf16)
            scores = dot_nt(k, q_head)
            logs = l_ref[0, head : head + 1, start:stop]
            probs = jnp.where(allowed, jnp.exp(scores - logs), 0.0)
            d_probs = dot_nt(v, d_head)
            d_scores = (probs * (d_probs - delta[head : head + 1, start:stop])).astype(bf16)
            dv = dv + dot_nn(probs.astype(bf16), d_head)
            dk = dk + dot_nn(d_scores, q_head)
            dq = dq + jnp.where(mask, dot_tn(d_scores, k), 0.0)
        dk_s[:stop, :] = dk
        dv_s[:stop, :] = dv
        out_ref[0, start:stop, :] = (dq * 0.125).astype(bf16)
    out_ref[1] = dk_s[...].astype(bf16)
    out_ref[2] = dv_s[...].astype(bf16)


def self_backward(qkv, d_out, out, log_rows, length, count):
    groups = D // CH
    at = lambda j: (lambda i, n: (j, 0, i))
    here = lambda i, n: (0, i)
    return pl.pallas_call(
        self_backward_kernel,
        grid_spec=pltpu.PrefetchScalarGridSpec(
            num_scalar_prefetch=1,
            grid=(count,),
            in_specs=[pl.BlockSpec((1, SEQ, CH), at(j)) for j in range(3)]
            + [
                pl.BlockSpec((SEQ, CH), here),
                pl.BlockSpec((SEQ, CH), here),
                pl.BlockSpec((1, 8, SEQ), lambda i, n: (i, 0, 0)),
            ],
            out_specs=pl.BlockSpec((3, SEQ, CH), lambda i, n: (0, 0, i)),
            scratch_shapes=[pltpu.VMEM((SEQ, CH), f32), pltpu.VMEM((SEQ, CH), f32)],
        ),
        out_shape=jax.ShapeDtypeStruct((3, SEQ, count * CH), bf16),
        compiler_params=params(),
        cost_estimate=cost(
            8 * HEADS * SEQ * SEQ * CH * count // groups, 16 * SEQ * D, HEADS * SEQ * SEQ
        ),
    )(length, stay(qkv), stay(qkv), stay(qkv), stay(d_out), stay(out), log_rows)


def full(*shape):
    return pl.BlockSpec(shape, lambda i: (0,) * len(shape))


def part_of(first):
    return pl.BlockSpec((3, CH, D), lambda i: (first + i, 0, 0))


def fixed_part(index):
    return pl.BlockSpec((3, CH, D), lambda i: (index, 0, 0))


def square(ref):
    return ref[...].reshape(D, D)


def write_cores(core, matrix, keep_refs, sizes, order, at=0):
    z, y, x, rows = sizes
    columns = matrix.shape[-1]
    if rows % 8:
        parts = matrix.reshape(-1, 2, y * x * rows, columns)
    else:
        parts = matrix.reshape(-1, 2, y, x, rows, columns)
    first, second = parts[:, 0], parts[:, 1]
    halves = (jnp.where(core == 0, first, second), jnp.where(core == 0, second, first))
    for ref, half in zip(keep_refs, halves):
        here = slice(at * z, at * z + half.shape[0])
        if rows % 8:
            ref[here] = half.astype(bf16)
            continue
        for row in range(y):
            for col in range(x):
                to = (col, row) if order == "xy" else (row, col)
                ref[to[0], to[1], here] = half[:, row, col].astype(bf16)


def core_shape(count, order, columns=D):
    z, y, x, rows = slice_shape()
    if rows % 8:
        return (count * z, y * x * rows, columns)
    cuts = (x, y) if order == "xy" else (y, x)
    return cuts + (count * z, rows, columns)


def core_block(count, order, at, columns=D):
    shape = core_shape(count, order, columns)
    return pl.BlockSpec(shape, lambda i: (0,) * (len(shape) - 3) + (at(i), 0, 0))


def core_cuts(parts, order):
    z, y, x, rows = slice_shape()
    if rows % 8 == 0:
        return list(parts)
    parts = [part.reshape(-1, y, x, rows, part.shape[-1]) for part in parts]
    dims = (2, 1, 0, 3, 4) if order == "xy" else (1, 2, 0, 3, 4)
    return [part.transpose(dims) for part in parts]


def split_z(slices):
    return slices.reshape((-1, lax.axis_size("z")) + slices.shape[1:])


def row_here():
    return lax.axis_index(("y", "x")).astype(jnp.int32).reshape(1)


def core_here():
    return lax.axis_index("c").astype(jnp.int32).reshape(1)


def row_scale(values):
    return lax.rsqrt(jnp.mean(values * values, -1, keepdims=True) + eps_norm)


def pull_norm(d_normed, values, gain):
    scale = row_scale(values)
    d_gain = jnp.sum(d_normed * values * scale, 0, keepdims=True)
    scaled = d_normed * gain
    inner = jnp.mean(scaled * values, -1, keepdims=True)
    return d_gain, scale * scaled - (scale * scale * scale) * values * inner


def embed_kernel(
    pool_ref, feats_ref, mixed_ref, out_w_ref, emb_ref, w_ref, gain_ref,
    seq_ref, embed_ref, normed_ref, qkv_ref,
):
    @pl.when(pl.program_id(0) == 0)
    def _():
        updated = feats_ref[...].astype(f32) + dot_nn(mixed_ref[...], out_w_ref[...])
        seq_ref[:CTX, :] = pool_ref[...]
        seq_ref[CTX:, :] = updated.astype(bf16)
        embed = dot_nn(seq_ref[...], emb_ref[0])
        embed_ref[...] = embed
        normed_ref[...] = (embed * row_scale(embed) * gain_ref[...]).astype(bf16)

    qkv_ref[0] = dot_nn(normed_ref[...], square(w_ref)).astype(bf16)


def embed_forward(pooled, feats, mixed, to_out, weights, gain):
    last = weights.shape[0] - 1
    return pl.pallas_call(
        embed_kernel,
        grid=(3,),
        in_specs=[
            full(CTX, CH),
            full(SEQ - CTX, CH),
            full(SEQ - CTX, CH),
            full(CH, CH),
            pl.BlockSpec((1, CH, D), lambda i: (last, 0, 0)),
            part_of(0),
            full(1, D),
        ],
        out_specs=[
            full(SEQ, CH),
            full(SEQ, D),
            full(SEQ, D),
            pl.BlockSpec((1, SEQ, D), lambda i: (i, 0, 0)),
        ],
        out_shape=[
            lasting((SEQ, CH), bf16),
            lasting((SEQ, D), f32),
            lasting((SEQ, D), bf16),
            lasting((3, SEQ, D), bf16),
        ],
        compiler_params=params(),
        cost_estimate=cost(2 * SEQ * D * (CH + 3 * D), 12 * SEQ * D),
    )(pooled, feats, mixed, to_out, stay(weights), stay(weights), gain)


def mlp_kernel(
    core_ref, mixed_ref, embed_ref, att_ref, up_ref, down_ref, gain_ref, gd_ref,
    out_ref, d_stream_ref, gog_ref, up_keep_ref, up_give_ref, down_keep_ref, down_give_ref,
    att_keep_ref, att_give_ref, gain_g_ref,
    stream_s, normed_s, turned_s, act_s, gpre_s, total_s, *, sizes
):
    step = pl.program_id(0)
    core = core_ref[0]

    @pl.when(step == 0)
    def _():
        stream = embed_ref[...] + dot_nn(mixed_ref[...], square(att_ref))
        stream_s[...] = stream
        out_ref[...] = stream
        total_s[...] = jnp.zeros_like(total_s)
        normed = stream * row_scale(stream) * gain_ref[...]
        normed_s[...] = normed.astype(bf16)
        turned_s[...] = normed.T.astype(bf16)

    factor = (2.0 / 3.141592653589793) ** 0.5
    cubic = 0.044715 * factor
    rows = SEQ // 2
    for start in range(0, SEQ, rows):
        here = slice(start, start + rows)
        v = dot_nn(normed_s[here, :], square(up_ref))
        v2 = v * v
        half = 0.5 + 0.5 * jnp.tanh(v * (factor + cubic * v2))
        act = (v * half).astype(bf16)
        act_s[here, :] = act
        slope = half + v * (2.0 * half * (1.0 - half) * (factor + 3.0 * cubic * v2))
        gpre = (dot_nt(gd_ref[here, :], square(down_ref)) * slope).astype(bf16)
        gpre_s[here, :] = gpre
        out_ref[here, :] += dot_nn(act, square(down_ref))
        total_s[here, :] += dot_nt(gpre, square(up_ref))
    down_refs, up_refs = (down_keep_ref, down_give_ref), (up_keep_ref, up_give_ref)
    write_cores(core, dot_tn(act_s[...], gd_ref[...]), down_refs, sizes, "xy")
    write_cores(core, dot_nn(turned_s[...], gpre_s[...]), up_refs, sizes, "yx")

    @pl.when(step == pl.num_programs(0) - 1)
    def _():
        d_gain, pulled = pull_norm(total_s[...], stream_s[...], gain_ref[...])
        gain_g_ref[...] = d_gain
        d_stream = gd_ref[...].astype(f32) + pulled
        d_stream_ref[...] = d_stream
        ga = d_stream.astype(bf16)
        gog_ref[...] = dot_nt(ga, square(att_ref)).astype(bf16)
        att_refs = (att_keep_ref, att_give_ref)
        write_cores(core, dot_tn(mixed_ref[...], ga), att_refs, sizes, "yx")


def mlp_block(mixed, embed, weights, mlp, gain, gd):
    up_part = core_block(3, "yx", lambda i: i)
    down_part = core_block(3, "xy", lambda i: i)
    att_part = core_block(3, "yx", lambda i: 0)
    return pl.pallas_call(
        functools.partial(mlp_kernel, sizes=slice_shape()),
        grid=(4,),
        in_specs=[
            CORE_SPEC,
            full(SEQ, D),
            full(SEQ, D),
            fixed_part(3),
            part_of(0),
            part_of(4),
            full(1, D),
            full(SEQ, D),
        ],
        out_specs=[full(SEQ, D)] * 3
        + [up_part] * 2
        + [down_part] * 2
        + [att_part] * 2
        + [full(1, D)],
        out_shape=[
            lasting((SEQ, D), f32),
            lasting((SEQ, D), f32),
            lasting((SEQ, D), bf16),
        ]
        + [jax.ShapeDtypeStruct(core_shape(12, "yx"), bf16)] * 2
        + [jax.ShapeDtypeStruct(core_shape(12, "xy"), bf16)] * 2
        + [lasting(core_shape(3, "yx"), bf16)] * 2
        + [jax.ShapeDtypeStruct((1, D), f32)],
        scratch_shapes=[
            pltpu.VMEM((SEQ, D), f32),
            pltpu.VMEM((SEQ, D), bf16),
            pltpu.VMEM((D, SEQ), bf16),
            pltpu.VMEM((SEQ, D), bf16),
            pltpu.VMEM((SEQ, D), bf16),
            pltpu.VMEM((SEQ, D), f32),
        ],
        compiler_params=pltpu.CompilerParams(vmem_limit_bytes=MLP_BYTES),
        cost_estimate=cost(54 * SEQ * D * D, 60 * SEQ * D, 4 * SEQ * D),
    )(
        core_here(), stay(mixed), stay(embed), stay(weights), stay(mlp), stay(mlp), gain, stay(gd)
    )


def embed_grad_kernel(
    core_ref, len_ref, q_ref, k_ref, v_ref, do_ref, o_ref, l_ref,
    g_ref, normed_ref, w_ref, emb_ref, embed_ref, d_stream_ref, seq_ref, mixed_ref, out_w_ref,
    gain_ref, gain_g_ref,
    qk_keep_ref, qk_give_ref, v_keep_ref, v_give_ref, keep_ref, give_ref,
    gupd_ref, pool_g_ref, out_g_ref, gox_ref,
    dk_s, dv_s, last_s, turned_s, total_s, *, sizes
):
    step = pl.program_id(0)
    core = core_ref[0]

    @pl.when(step == 0)
    def _():
        self_backward_kernel(
            len_ref, q_ref, k_ref, v_ref, do_ref, o_ref, l_ref, last_s, dk_s, dv_s
        )
        turned_s[...] = normed_ref[...].T
        total_s[...] = jnp.zeros_like(total_s)

    @pl.when(step > 0)
    def _():
        g = jnp.concatenate([g_ref[0], last_s[step - 1]], 1)
        total_s[...] += dot_nt(g, square(w_ref))
        grad = dot_nn(turned_s[...], g)

        @pl.when(step < 3)
        def _():
            write_cores(core, grad, (qk_keep_ref, qk_give_ref), sizes, "xy")

        @pl.when(step == 3)
        def _():
            write_cores(core, grad, (v_keep_ref, v_give_ref), sizes, "yx")

    @pl.when(step == 3)
    def _():
        d_gain, pulled = pull_norm(total_s[...], embed_ref[...], gain_ref[...])
        gembed = (d_stream_ref[...] + pulled).astype(bf16)
        at = lax.broadcasted_iota(jnp.int32, (CH, D), 0)
        gains = jnp.where(at == 0, d_gain, jnp.where(at == sizes[-1], gain_g_ref[...], 0.0))
        for index, values in enumerate((dot_tn(seq_ref[...], gembed), gains)):
            write_cores(core, values, (keep_ref, give_ref), sizes, "xy", index)
        gseq = dot_nt(gembed, emb_ref[0])
        gupd = gseq[CTX:]
        gb = gupd.astype(bf16)
        pool_g_ref[...] = gseq[:CTX].astype(bf16)
        gupd_ref[...] = gupd
        out_g_ref[...] = dot_tn(mixed_ref[...], gb).astype(bf16)
        gox_ref[...] = dot_nt(gb, out_w_ref[...]).astype(bf16)


def embed_grad(
    length, qkv, gog, out, log_rows, gqkv, normed, weights, embed, d_stream, seq, mixed, to_out,
    gain, gain_g,
):
    last = weights.shape[0] - 1
    group = D // CH - 1
    done = gqkv.shape[-1]
    part = lambda i: jnp.maximum(i - 1, 0)
    at = lambda j: pl.BlockSpec((1, SEQ, CH), lambda i: (j, 0, group))
    here = pl.BlockSpec((SEQ, CH), lambda i: (0, group))
    qk_part = core_block(3, "xy", lambda i: jnp.clip(i - 1, 0, 1))
    v_part = core_block(3, "yx", lambda i: 0)
    emb_part = core_block(2, "xy", lambda i: 0)
    return pl.pallas_call(
        functools.partial(embed_grad_kernel, sizes=slice_shape()),
        grid=(4,),
        in_specs=[
            CORE_SPEC,
            CORE_SPEC,
            at(0),
            at(1),
            at(2),
            here,
            here,
            pl.BlockSpec((1, 8, SEQ), lambda i: (group, 0, 0)),
            pl.BlockSpec((1, SEQ, done), lambda i: (part(i), 0, 0)),
            full(SEQ, D),
            pl.BlockSpec((3, CH, D), lambda i: (part(i), 0, 0)),
            pl.BlockSpec((1, CH, D), lambda i: (last, 0, 0)),
            full(SEQ, D),
            full(SEQ, D),
            full(SEQ, CH),
            full(SEQ - CTX, CH),
            full(CH, CH),
            full(1, D),
            full(1, D),
        ],
        out_specs=[
            qk_part,
            qk_part,
            v_part,
            v_part,
            emb_part,
            emb_part,
            full(SEQ - CTX, CH),
            full(CTX, CH),
            full(CH, CH),
            full(SEQ - CTX, CH),
        ],
        out_shape=[jax.ShapeDtypeStruct(core_shape(6, "xy"), bf16)] * 2
        + [jax.ShapeDtypeStruct(core_shape(3, "yx"), bf16)] * 2
        + [jax.ShapeDtypeStruct(core_shape(2, "xy"), bf16)] * 2
        + [
            jax.ShapeDtypeStruct((SEQ - CTX, CH), f32),
            jax.ShapeDtypeStruct((CTX, CH), bf16),
            jax.ShapeDtypeStruct((CH, CH), bf16),
            jax.ShapeDtypeStruct((SEQ - CTX, CH), bf16),
        ],
        scratch_shapes=[
            pltpu.VMEM((SEQ, CH), f32),
            pltpu.VMEM((SEQ, CH), f32),
            pltpu.VMEM((3, SEQ, CH), bf16),
            pltpu.VMEM((D, SEQ), bf16),
            pltpu.VMEM((SEQ, D), f32),
        ],
        compiler_params=pltpu.CompilerParams(vmem_limit_bytes=MLP_BYTES),
        cost_estimate=cost(2 * SEQ * D * (6 * D + 2 * CH) + 32 * SEQ * SEQ * CH, 50 * SEQ * D),
    )(
        core_here(), length, stay(qkv), stay(qkv), stay(qkv), stay(gog), stay(out), log_rows, gqkv, normed, stay(weights),
        stay(weights), stay(embed), stay(d_stream), stay(seq), stay(mixed), to_out, gain, gain_g,
    )


def patch_pick(rows, columns, patch_dim):
    patch = lax.broadcasted_iota(jnp.int32, (rows, columns), patch_dim)
    cell = lax.broadcasted_iota(jnp.int32, (rows, columns), 1 - patch_dim)
    inside = (cell // (PATCH * IMG)) * (IMG // PATCH) + (cell % IMG) // PATCH
    return jnp.where(patch == inside, 1.0 / (PATCH * PATCH), 0.0).astype(bf16)


def image_rows(step, row):
    return pl.ds(pl.multiple_of(step * BLOCK + row * IMG, IMG), BLOCK)


def token_forward_kernel(x_ref, conv_ref, kv_w_ref, slope_ref, hidden_ref, kv_ref, pool_ref):
    step = pl.program_id(0)
    z = jnp.zeros((BLOCK, CH), f32)
    for row in range(3):
        z = z + dot_nn(x_ref[image_rows(step, row), :], conv_ref[row])
    center = x_ref[image_rows(step, 1), CH : 2 * CH].astype(f32)
    gate = 1.0 / (1.0 + jnp.exp(-z))
    hidden = center + z * gate
    slope_ref[...] = (gate * (1.0 + z * (1.0 - gate))).astype(bf16)
    hidden_b = hidden.astype(bf16)
    hidden_ref[...] = hidden_b
    kv_ref[...] = dot_nn(hidden_b, kv_w_ref[...]).astype(bf16)
    rest = (hidden - hidden_b.astype(f32)).astype(bf16)
    pick = patch_pick(pool_ref.shape[0], BLOCK, 0)
    pool_ref[...] = (dot_nn(pick, hidden_b) + dot_nn(pick, rest)).astype(bf16)


def token_forward(wide, conv_rows, kv_weight):
    steps = CELLS // BLOCK
    whole = lambda i: (0, 0)
    block = lambda i: (i, 0)
    return pl.pallas_call(
        token_forward_kernel,
        grid=(steps,),
        in_specs=[
            pl.BlockSpec(wide.shape, whole),
            pl.BlockSpec((3, 3 * CH, CH), lambda i: (0, 0, 0)),
            pl.BlockSpec((CH, 2 * CH), whole),
        ],
        out_specs=[
            pl.BlockSpec((BLOCK, CH), block),
            pl.BlockSpec((BLOCK, CH), block),
            pl.BlockSpec((BLOCK, 2 * CH), block),
            pl.BlockSpec((CTX // steps, CH), block),
        ],
        out_shape=[
            lasting((CELLS, CH), bf16),
            lasting((CELLS, CH), bf16),
            jax.ShapeDtypeStruct((CELLS, 2 * CH), bf16),
            jax.ShapeDtypeStruct((CTX, CH), bf16),
        ],
        compiler_params=params(),
        cost_estimate=cost(22 * CELLS * CH * CH, 14 * CELLS * CH, CELLS * CH),
    )(stay(wide), conv_rows, kv_weight)


def token_backward_kernel(
    core_ref, dkv_ref, slope_ref, pool_ref, hidden_ref, x_ref, kv_w_ref, query_g_ref, out_g_ref,
    d_hidden_ref, gz_ref, keep_ref, give_ref, conv_s, kv_s, *, sizes
):
    step = pl.program_id(0)

    @pl.when(step == 0)
    def _():
        conv_s[...] = jnp.zeros_like(conv_s)
        kv_s[...] = jnp.zeros_like(kv_s)

    dkv = dkv_ref[...]
    d_hidden = dot_nt(dkv, kv_w_ref[...])
    d_hidden = d_hidden + dot_nn(patch_pick(BLOCK, pool_ref.shape[0], 1), pool_ref[...])
    gz = (d_hidden * slope_ref[...].astype(f32)).astype(bf16)
    d_hidden_ref[...] = d_hidden
    gz_ref[...] = gz
    kv_s[...] += dot_tn(hidden_ref[...], dkv)
    gz_t = gz.T
    for row in range(3):
        conv_s[row] += dot_nn(gz_t, x_ref[image_rows(step, row), :])

    @pl.when(step == pl.num_programs(0) - 1)
    def _():
        tiles = []
        for row in range(3):
            for col in range(3):
                tiles.append(conv_s[row, :, col * CH : (col + 1) * CH].T)
        tiles = tiles + [query_g_ref[...], kv_s[:, :CH], kv_s[:, CH:], out_g_ref[...]]
        for at, tile in enumerate(tiles):
            write_cores(core_ref[0], tile.astype(f32), (keep_ref, give_ref), sizes, "yx", at)


def token_backward(dkv, slope, d_pool, hidden_b, wide, kv_weight, query_g, out_g):
    steps = CELLS // BLOCK
    whole = lambda i: (0, 0)
    block = lambda i: (i, 0)
    return pl.pallas_call(
        functools.partial(token_backward_kernel, sizes=slice_shape()),
        grid=(steps,),
        in_specs=[
            CORE_SPEC,
            pl.BlockSpec((BLOCK, 2 * CH), block),
            pl.BlockSpec((BLOCK, CH), block),
            pl.BlockSpec((CTX // steps, CH), block),
            pl.BlockSpec((BLOCK, CH), block),
            pl.BlockSpec(wide.shape, whole),
            pl.BlockSpec((CH, 2 * CH), whole),
            pl.BlockSpec((CH, CH), whole),
            pl.BlockSpec((CH, CH), whole),
        ],
        out_specs=[
            pl.BlockSpec((BLOCK, CH), block),
            pl.BlockSpec((BLOCK, CH), block),
            core_block(EARLY, "yx", lambda i: 0, CH),
            core_block(EARLY, "yx", lambda i: 0, CH),
        ],
        out_shape=[
            jax.ShapeDtypeStruct((CELLS, CH), f32),
            jax.ShapeDtypeStruct((CELLS, CH), bf16),
            jax.ShapeDtypeStruct(core_shape(EARLY, "yx", CH), bf16),
            jax.ShapeDtypeStruct(core_shape(EARLY, "yx", CH), bf16),
        ],
        scratch_shapes=[pltpu.VMEM((3, CH, 3 * CH), f32), pltpu.VMEM((CH, 2 * CH), f32)],
        compiler_params=params(),
        cost_estimate=cost(26 * CELLS * CH * CH, 20 * CELLS * CH),
    )(core_here(), dkv, stay(slope), d_pool, stay(hidden_b), stay(wide), kv_weight, query_g, out_g)


def context_backward_kernel(gz_ref, d_hidden_ref, conv_ref, out_ref, wide_s):
    step = pl.program_id(0)
    steps = pl.num_programs(0)

    def widen(at):
        values = gz_ref[image_rows(at, 0), :].astype(f32)
        col = lax.broadcasted_iota(jnp.int32, (BLOCK, CH), 0) % IMG
        left = jnp.where(col == 0, 0.0, pltpu.roll(values, 1, 0))
        right = jnp.where(col == IMG - 1, 0.0, pltpu.roll(values, BLOCK - 1, 0))
        wide_s[image_rows(at, 1), 0:CH] = left.astype(bf16)
        wide_s[image_rows(at, 1), CH : 2 * CH] = values.astype(bf16)
        wide_s[image_rows(at, 1), 2 * CH :] = right.astype(bf16)

    @pl.when(step == 0)
    def _():
        wide_s[0:IMG, :] = jnp.zeros((IMG, 3 * CH), bf16)
        wide_s[CELLS + IMG :, :] = jnp.zeros((IMG, 3 * CH), bf16)
        widen(0)

    @pl.when(step < steps - 1)
    def _():
        widen(step + 1)

    total = d_hidden_ref[...]
    for row in range(3):
        values = wide_s[image_rows(step, row), :]
        for col in range(3):
            tap = conv_ref[3 * (2 - row) + (2 - col)]
            total = total + dot_nt(values[:, col * CH : (col + 1) * CH], tap)
    out_ref[...] = total.astype(bf16)


def context_backward(gz, d_hidden, conv_tiles):
    block = lambda i: (i, 0)
    return pl.pallas_call(
        context_backward_kernel,
        grid=(CELLS // BLOCK,),
        in_specs=[
            pl.BlockSpec((CELLS, CH), lambda i: (0, 0)),
            pl.BlockSpec((BLOCK, CH), block),
            pl.BlockSpec((9, CH, CH), lambda i: (0, 0, 0)),
        ],
        out_specs=pl.BlockSpec((BLOCK, CH), block),
        out_shape=jax.ShapeDtypeStruct((CELLS, CH), bf16),
        scratch_shapes=[pltpu.VMEM((CELLS + 2 * IMG, 3 * CH), bf16)],
        compiler_params=params(),
        cost_estimate=cost(18 * CELLS * CH * CH, 8 * CELLS * CH),
    )(gz, d_hidden, conv_tiles)


def local(
    context_map,
    future_feats,
    horizon,
    cotangent,
    tile_owner,
    master_tiles,
    moment_first,
    moment_second,
    norm_gains,
    gain_first,
    gain_second,
):
    slot_count = master_tiles.shape[0]
    devices = lax.axis_size(AXES)
    rows = CH // devices
    slot_of = slot_index(tile_owner, slot_count)

    length = CTX + FT * horizon
    valid = jnp.arange(SEQ) < length[0]
    gd = jnp.where(valid[:, None], cotangent[0], jnp.zeros((), bf16))

    slices = (
        master_tiles.astype(bf16)
        .reshape(slot_count, devices, rows, CH)
        .transpose(1, 0, 2, 3)
    )
    slices = lax.all_to_all(slices, AXES, split_axis=0, concat_axis=0, tiled=True)
    extra = max(1, 8 // rows)
    tiles = tile_owner.shape[0]
    span = slot_count + extra
    place = jnp.arange(devices * span)
    device, at = place // span, place % span
    found = slot_of[None, :] == jnp.where(at < slot_count, device * slot_count + at, -1)[:, None]
    tile_of = jnp.sum(jnp.where(found, jnp.arange(tiles)[None], 0), 1)
    tile_of = jnp.where(at < slot_count, tile_of, tiles + at - slot_count)
    mine_at = lax.axis_index(AXES) * slot_count + jnp.arange(slot_count)
    used = jnp.any(slot_of[None, :] == mine_at[:, None], 1).astype(f32)
    slices, gd, tile_of, used = tie((slices, gd, tile_of, used))
    slices = slices.reshape(devices * slot_count, rows, CH)
    slices = slices.at[slot_of].get(mode="promise_in_bounds")
    early, emb, qkv, att, up, down = jnp.split(slices, (13, 16, 43, 52, 88))
    mlp = jnp.concatenate([from_tiles(up, 3, 4), from_tiles(down, 12, 1)], 0)
    early = gather_axes(early, "z")
    core = jnp.concatenate([from_tiles(qkv, 3, 3), from_tiles(att, 3, 1), from_tiles(emb, 1, 1)], 0)
    core, early = tie((core, early))
    early = gather_axes(joined(early), ("y", "x"))
    core = gather_axes(core, "z")
    pieces = trade_rows(context_map)
    early = joined(gather_axes(joined(early), "c"))
    early = device_order(early, ("c", "y", "x", "z"))
    wide = widen(pieces)
    core = joined(core)
    low, high = gather_axes(core[:6], "x"), gather_axes(core[6:], "y")

    conv_tiles = early[:9]
    to_query, to_out = early[9], early[12]
    kv_weight = jnp.concatenate([early[10], early[11]], 1)

    wide, mlp, low, high = hold((wide, mlp), low, high)
    mlp = lax.all_gather(mlp, AXES, axis=1, tiled=True)
    low, high = joined(low), joined(high)
    wide, low, high = tie((wide, low, high))
    low, high = gather_axes(low, "y"), gather_axes(high, "x")
    slope_z, hidden_b, kv, pooled = token_forward(
        wide, conv_tiles.reshape(3, 3 * CH, CH), kv_weight
    )
    kv, low, high = hold((kv,), low, high)
    low, high = joined(low), joined(high)
    feats_b = future_feats[0]
    query = jnp.dot(feats_b, to_query, preferred_element_type=f32).astype(bf16)
    kv, low, high = tie((kv, low, high))
    low, high = gather_axes(low, "c"), gather_axes(high, "c")
    cross_mixed, cross_logs = cross_forward(query, kv)
    cross_mixed, low, high = hold((cross_mixed,), low, high)
    weights = place_rows(low, high)

    gain_one, gain_two = norm_gains[:1], norm_gains[1:]
    seq, embed, normed_one, qkv = embed_forward(
        pooled, feats_b, cross_mixed, to_out, weights, gain_one
    )
    mixed, logs = self_forward(qkv, length)
    (
        block_out, d_stream, gog, up_keep, up_give, down_keep, down_give, att_keep, att_give,
        gain_g_two,
    ) = mlp_block(mixed, embed, weights, mlp, gain_two, gd)
    up = core_cuts([up_keep, up_give], "yx")
    down = core_cuts([down_keep, down_give], "xy")
    att = core_cuts([att_keep, att_give], "yx")
    gog, up, down, att = tie((gog, up, down, att))
    up, down, att = send(up, "c"), send(down, "c"), send(att, "c")
    gqkv = self_backward(qkv, gog, mixed, logs, length, 2)
    gqkv, up, down, att = hold((gqkv,), up, down, att)
    up, down = advance(up, "y", 0), advance(down, "x", 0)
    gqkv, up, down = tie((gqkv, up, down))
    up, down = send(up, "y"), send(down, "x")
    (
        qk_keep, qk_give, v_keep, v_give, emb_keep, emb_give, gupd, pool_g, out_g, gox,
    ) = embed_grad(
        length, qkv, gog, mixed, logs, gqkv, normed_one, weights, embed, d_stream, seq,
        cross_mixed, to_out, gain_one, gain_g_two,
    )
    first = core_cuts([qk_keep, qk_give], "xy")
    second = core_cuts([v_keep, v_give], "yx")
    emb = core_cuts([emb_keep, emb_give], "xy")
    gox, gupd, first, second, emb, up, down = hold((gox, gupd, first, second, emb), up, down)
    up, down = advance(up, "x", 0), advance(down, "y", 0)
    gox, up, down, first, second, emb = tie((gox, up, down, first, second, emb))
    up, down, emb = send(up, "x"), send(down, "y"), send(emb, "c")
    first, second = send(first, "c"), send(second, "c")

    log_rows = cross_logs[0]
    gkv, query_g, future_grad = cross_backward(
        query, kv, gox, cross_mixed, log_rows, feats_b, gupd, to_query
    )
    gkv, up, down, first, second, emb = hold((gkv,), up, down, first, second, emb)
    mlp = advance_near([split_z(jnp.concatenate(part, 0)) for part in zip(up, down)])
    emb = advance(emb, "x", 0)
    second = [jnp.concatenate([p, q], 2) for p, q in zip(second, att)]
    first, second = advance(first, "x", 0), advance(second, "y", 0)
    gkv, mlp, first, second, emb = tie((gkv, mlp, first, second, emb))
    mlp, emb = send(mlp, "z"), send(emb, "x")
    first, second = send(first, "x"), send(second, "y")

    d_hidden, gz, early_keep, early_give = token_backward(
        gkv, slope_z, pool_g, hidden_b, wide, kv_weight, query_g, out_g
    )
    d_hidden, gz, early_keep, early_give, mlp, first, second, emb = hold(
        (d_hidden, gz, early_keep, early_give), mlp, first, second, emb
    )
    early = core_cuts([early_keep, early_give], "yx")
    early, mlp, first, second, emb = tie((early, mlp, first, second, emb))
    early = send(early, "c")
    first, second = advance(first, "y", 0), advance(second, "x", 0)
    emb, mlp = advance(emb, "y", 0), advance_far(mlp)
    first, second = send(first, "y"), send(second, "x")
    emb, mlp = send(emb, "y"), send(mlp, "z", 2)
    gz, early, first, second, emb = hold((gz,), early, first, second, emb)
    early = advance([p.reshape((-1,) + p.shape[2:]) for p in early], ("y", "x"), 0)
    att = advance_near([split_z(jnp.concatenate(part, 0)) for part in zip(first, second)])
    gz, early, att = tie((gz, early, att))
    early, att = send(early, ("y", "x")), send(att, "z")
    context_grad = context_backward(gz, d_hidden, conv_tiles)
    context_grad, early, att, mlp = hold((context_grad,), early, att, mlp)
    early = advance([split_z(part) for part in early], "z", 1)
    emb = advance([split_z(part) for part in emb], "z", 1)
    early = [jnp.concatenate([e, to_tiles(m)], 0) for e, m in zip(early, emb)]
    att = advance_far(att)
    context_grad, early, att = tie((context_grad, early, att))
    early, att = send(early, "z"), send(att, "z", 2)
    pieces = trade_rows(context_grad.reshape(context_map.shape))
    sum_mlp = add_up(mlp, keep_wide=True)
    square_mlp = jnp.sum(sum_mlp * sum_mlp)
    half = sum_mlp.shape[0] // 2
    mlp = jnp.concatenate([to_tiles(sum_mlp[:half], 4), to_tiles(sum_mlp[half:])], 0).astype(bf16)
    sum_early = add_up(early, keep_wide=True)
    sum_att = add_up(att, keep_wide=True)

    gains = sum_early[EARLY + 3 :, 0]
    square = square_mlp + jnp.sum(sum_att * sum_att) + jnp.sum(sum_early * sum_early)
    share = jnp.concatenate([gains, jnp.broadcast_to(square, (1, CH))], 0)
    share_high = share.astype(bf16)
    share_low = (share - share_high.astype(f32)).astype(bf16)
    share = jnp.concatenate([share_high, share_low], 0)
    share = jnp.pad(share, ((0, extra * rows - share.shape[0]), (0, 0)))
    sums = jnp.concatenate(
        [
            sum_early[: EARLY + 3].astype(bf16),
            to_tiles(sum_att[:9], 3).astype(bf16),
            to_tiles(sum_att[9:]).astype(bf16),
            mlp,
            share.reshape(extra, rows, CH),
        ],
        0,
    )
    mine = sums.at[tile_of].get(mode="promise_in_bounds")
    mine = mine.reshape(devices, slot_count + extra, rows, CH)
    mine, pieces[-1] = tie((mine, pieces[-1]))
    mine = lax.all_to_all(mine, AXES, split_axis=0, concat_axis=0, tiled=True)
    shares = mine[:, slot_count:].reshape(devices, -1, CH).astype(f32)
    shares = shares[:, :4] + shares[:, 4:8]
    gains = shares[:2, :3].reshape(2, D)
    mine = mine[:, :slot_count].transpose(1, 0, 2, 3).reshape(slot_count, CH, CH).astype(f32)

    used = used[:, None, None]
    grad_norm = jnp.sqrt(jnp.sum(shares[:, 3, 0]))
    factor = jnp.minimum(1.0, clip_level / (grad_norm + 1e-06))
    new_first, new_second, new_master = adam_step(
        master_tiles, mine * factor, moment_first, moment_second, learn_rate, decay_rate
    )
    new_gain_first, new_gain_second, new_gains = adam_step(
        norm_gains, gains * factor, gain_first, gain_second, gain_rate, 0.0
    )
    return (
        block_out[None],
        row_order(pieces).reshape(context_map.shape),
        future_grad[None],
        jnp.where(used > 0, new_first, 0.0),
        jnp.where(used > 0, new_second, 0.0),
        jnp.where(used > 0, new_master, 0.0),
        new_gain_first,
        new_gain_second,
        new_gains,
        grad_norm,
    )


def solution(mesh):
    groups, rows = mesh.devices.shape
    fine = jax.sharding.Mesh(mesh.devices.reshape(groups // 2, 2, rows // 2, 2), AXES)
    whole = P(AXES, None, None)
    image = P(("z", "c"), ("y", "x"), None, None)
    in_specs = (image, whole, P(AXES), whole, P(), whole, whole, whole, P(), P(), P())
    out_specs = (whole, image, whole, whole, whole, whole, P(), P(), P(), P())
    return jax.shard_map(local, mesh=fine, in_specs=in_specs, out_specs=out_specs, check_vma=False)
```

```python
import functools

import jax
import jax.numpy as jnp
from jax import lax
from jax.experimental import pallas as pl
from jax.experimental.pallas import tpu as pltpu
from jax.sharding import PartitionSpec as P

CH = 256
HD = 64
HEADS = 12
D = 768
FF = 3072
TH = 4
IMG = 64
PATCH = 4
FT = 16
CTX = 256
SEQ = 736
STEP = 10


eps_norm = 1e-05
beta_one = 0.9
beta_two = 0.999
learn_rate = 0.02
gain_rate = 0.6
decay_rate = 0.1
adam_eps = 1e-08
clip_level = 1.0
neg_large = -1e30
AXES = ("z", "c", "y", "x")
CELLS = IMG * IMG
BLOCK = 512
GROUP = 4
EARLY = 13
VMEM_BYTES = 28 * 1024 * 1024
MLP_BYTES = 40 * 1024 * 1024
ROW_BLOCKS = ((0, 256), (256, 256), (512, 224))
CORE_SPEC = pl.BlockSpec(memory_space=pltpu.SMEM)
bf16 = jnp.bfloat16
f32 = jnp.float32


def slot_index(tile_owner, slot_count):
    ordinal = jnp.arange(tile_owner.shape[0])
    earlier = (tile_owner[None, :] == tile_owner[:, None]) & (ordinal[None, :] < ordinal[:, None])
    return tile_owner * slot_count + jnp.sum(earlier.astype(jnp.int32), 1)


def adam_step(weight, grad_now, first, second, rate, decay):
    first_new = beta_one * first + (1.0 - beta_one) * grad_now
    second_new = beta_two * second + (1.0 - beta_two) * grad_now * grad_now
    corr_first = first_new / (1.0 - beta_one**STEP)
    corr_second = second_new / (1.0 - beta_two**STEP)
    weight_new = weight - rate * (corr_first / (jnp.sqrt(corr_second) + adam_eps) + decay * weight)
    return (first_new, second_new, weight_new)


def xor_permute(values, axes, mask):
    count = lax.axis_size(axes)
    return lax.ppermute(values, axes, [(i, i ^ mask) for i in range(count)])


def pick(parts, index, dim):
    if parts[0].shape[dim] == 2:
        total = add_up(parts)
        first, second = (lax.index_in_dim(total, at, dim, False) for at in range(2))
        return jnp.where(index == 0, first, second)
    return add_up([lax.dynamic_index_in_dim(part, index, dim, False) for part in parts])


def advance(parts, axes, dim):
    mine = lax.axis_index(axes)
    return [pick(parts, mine ^ mask, dim) for mask in range(lax.axis_size(axes))]


def advance_near(parts):
    mine = lax.axis_index("z") % 2
    shape = parts[0].shape
    parts = [p.reshape((shape[0], shape[1] // 2, 2) + shape[2:]) for p in parts]
    return [pick(parts, mine ^ mask, 2) for mask in range(2)]


def advance_far(parts):
    mine = lax.axis_index("z") // 2
    return [pick(parts, mine ^ mask, 1) for mask in range(parts[0].shape[1])]


def send(cuts, axes, unit=1):
    return [cuts[0]] + [
        xor_permute(cut, axes, unit * mask) for mask, cut in enumerate(cuts) if mask > 0
    ]


def add_up(parts, keep_wide=False):
    total = parts[0].astype(f32)
    for part in parts[1:]:
        total = total + part.astype(f32)
    return total if keep_wide else total.astype(parts[0].dtype)


def hold(values, *sums):
    tied = lax.optimization_barrier((tuple(values), tuple(tuple(parts) for parts in sums)))
    return tied[0] + tuple(list(parts) for parts in tied[1])


def gather_axes(values, axes):
    return [values] + [
        xor_permute(values, axes, mask) for mask in range(1, lax.axis_size(axes))
    ]


def joined(pieces):
    return jnp.stack(pieces, 1)


def device_order(values, axes):
    sizes = [lax.axis_size(axis) for axis in AXES]
    own = [lax.axis_index(axis) for axis in AXES]
    places = jnp.unravel_index(jnp.arange(lax.axis_size(AXES)), sizes)
    at = 0
    for axis in axes:
        which = AXES.index(axis)
        at = at * sizes[which] + (places[which] ^ own[which])
    values = values.reshape((values.shape[0], -1) + values.shape[-2:])
    values = values.at[:, at].get(mode="promise_in_bounds")
    return values.reshape(values.shape[0], -1, values.shape[-1])


def place_kernel(own_ref, low_ref, low_other_ref, high_ref, high_other_ref, out_ref, *, half, sizes):
    z_count, c_count, y_count, x_count = sizes
    own_z, own_c, own_y, own_x = (own_ref[axis] for axis in range(4))
    step = pl.program_id(0)

    def place(near_ref, far_ref, x_first):
        for z in range(z_count):
            for y in range(y_count):
                for x in range(x_count):
                    if x_first:
                        at = (x ^ own_x) * y_count + (y ^ own_y)
                    else:
                        at = (y ^ own_y) * x_count + (x ^ own_x)
                    at = at * z_count + (z ^ own_z)
                    near, far = near_ref[0, at], far_ref[0, at]
                    for c in range(c_count):
                        to = ((z * c_count + c) * y_count + y) * x_count + x
                        out_ref[0, to] = jnp.where(own_c == c, near, far)

    @pl.when(step < half)
    def _():
        place(low_ref, low_other_ref, False)

    @pl.when(step >= half)
    def _():
        place(high_ref, high_other_ref, True)


def place_rows(low, high):
    sizes = tuple(lax.axis_size(axis) for axis in AXES)
    half, rows = low[0].shape[0], low[0].shape[-2]
    count = half + high[0].shape[0]
    own = jnp.stack([lax.axis_index(axis) for axis in AXES]).astype(jnp.int32)
    pieces = [part.reshape(part.shape[0], -1, rows, D) for part in low + high]
    block = (1,) + pieces[0].shape[1:]
    early = pl.BlockSpec(block, lambda i: (jnp.minimum(i, half - 1), 0, 0, 0))
    later = pl.BlockSpec(block, lambda i: (jnp.maximum(i - half, 0), 0, 0, 0))
    devices = CH // rows
    out = pl.pallas_call(
        functools.partial(place_kernel, half=half, sizes=sizes),
        grid=(count,),
        in_specs=[CORE_SPEC, early, early, later, later],
        out_specs=pl.BlockSpec((1, devices, rows, D), lambda i: (i, 0, 0, 0)),
        out_shape=jax.ShapeDtypeStruct((count, devices, rows, D), bf16),
        compiler_params=params(),
        cost_estimate=cost(0, 4 * count * CH * D),
    )(own, *pieces)
    return out.reshape(count, CH, D)


def trade_rows(values):
    mine = lax.axis_index(("y", "x"))
    count = lax.axis_size(("y", "x"))
    cuts = [lax.dynamic_index_in_dim(values, mine ^ mask, 0, False) for mask in range(count)]
    return send(cuts, ("y", "x"))


def row_order_kernel(row_ref, *refs):
    at = pl.program_id(0) ^ row_ref[0]
    values = refs[0][...]
    for mask in range(1, len(refs) - 1):
        values = jnp.where(at == mask, refs[mask][...], values)
    refs[-1][0] = values.astype(f32)


def row_order(pieces):
    count = len(pieces)
    cells = pieces[0].size // CH
    return pl.pallas_call(
        row_order_kernel,
        grid=(count,),
        in_specs=[CORE_SPEC] + [pl.BlockSpec((cells, CH), lambda i: (0, 0))] * count,
        out_specs=pl.BlockSpec((1, cells, CH), lambda i: (i, 0, 0)),
        out_shape=jax.ShapeDtypeStruct((count, cells, CH), f32),
        compiler_params=params(),
        cost_estimate=cost(0, 6 * count * cells * CH),
    )(row_here(), *[piece.reshape(cells, CH) for piece in pieces])


def widen_kernel(row_ref, *refs):
    out_ref = refs[-1]
    cells = refs[0].shape[0]
    col = lax.broadcasted_iota(jnp.int32, (cells, CH), 0) % IMG
    out_ref[0:IMG, :] = jnp.zeros((IMG, 3 * CH), bf16)
    out_ref[CELLS + IMG :, :] = jnp.zeros((IMG, 3 * CH), bf16)
    for at in range(len(refs) - 1):
        values = refs[at][...]
        for mask in range(1, len(refs) - 1):
            values = jnp.where(row_ref[0] == mask, refs[at ^ mask][...], values)
        here = slice(IMG + at * cells, IMG + (at + 1) * cells)
        out_ref[here, CH : 2 * CH] = values
        values = values.astype(f32)
        left = jnp.where(col == 0, 0.0, pltpu.roll(values, 1, 0))
        right = jnp.where(col == IMG - 1, 0.0, pltpu.roll(values, cells - 1, 0))
        out_ref[here, 0:CH] = left.astype(bf16)
        out_ref[here, 2 * CH :] = right.astype(bf16)


def widen(pieces):
    cells = pieces[0].size // CH
    vmem = pl.BlockSpec(memory_space=pltpu.VMEM)
    return pl.pallas_call(
        widen_kernel,
        in_specs=[CORE_SPEC] + [vmem] * len(pieces),
        out_specs=vmem,
        out_shape=lasting((CELLS + 2 * IMG, 3 * CH), bf16),
        compiler_params=params(),
        cost_estimate=cost(0, 8 * CELLS * CH),
    )(row_here(), *[piece.reshape(cells, CH) for piece in pieces])


def slice_shape():
    z, c, y, x = [lax.axis_size(axis) for axis in AXES]
    return (z, y, x, CH // (z * c * y * x))


tie = lax.optimization_barrier


def to_tiles(slices, parts=1):
    blocks, rows, columns = slices.shape
    return (
        slices.reshape(parts, blocks // parts, rows, columns // CH, CH)
        .transpose(1, 0, 3, 2, 4)
        .reshape(-1, rows, CH)
    )


def from_tiles(tiles, row_blocks, parts):
    rows = tiles.shape[1]
    return (
        tiles.reshape(row_blocks, parts, D // CH, rows, CH)
        .transpose(1, 0, 3, 2, 4)
        .reshape(parts * row_blocks, rows, D)
    )


def dot_nt(a, b):
    return lax.dot_general(a, b, (((1,), (1,)), ((), ())), preferred_element_type=f32)


def dot_nn(a, b):
    return lax.dot_general(a, b, (((1,), (0,)), ((), ())), preferred_element_type=f32)


def dot_tn(a, b):
    return lax.dot_general(a, b, (((0,), (0,)), ((), ())), preferred_element_type=f32)


def head_mask(shape, head):
    return (lax.broadcasted_iota(jnp.int32, shape, len(shape) - 1) // HD) == head


def cost(flops, moved, transcendentals=0):
    return pl.CostEstimate(
        flops=int(flops), bytes_accessed=int(moved), transcendentals=int(transcendentals)
    )


def stay(values):
    return pltpu.with_memory_space_constraint(values, pltpu.HBM)


lasting = pltpu.HBM


def params():
    return pltpu.CompilerParams(vmem_limit_bytes=VMEM_BYTES)


def cross_forward_kernel(q_ref, k_ref, v_ref, o_ref, l_ref):
    rows = q_ref.shape[0]
    lane = lax.broadcasted_iota(jnp.int32, (rows, 128), 1)
    q = q_ref[...]
    mixed = jnp.zeros((rows, CH), f32)
    stat = jnp.zeros((rows, 128), f32)
    for head in range(TH):
        mask = head_mask((rows, CH), head)
        q_head = jnp.where(mask, q.astype(f32) * 0.125, 0.0).astype(bf16)
        scores = dot_nt(q_head, k_ref[...])
        peak = jnp.max(scores, -1, keepdims=True)
        shifted = jnp.exp(scores - peak)
        total = jnp.sum(shifted, -1, keepdims=True)
        part = dot_nn(shifted.astype(bf16), v_ref[...])
        mixed = jnp.where(mask, part / total, mixed)
        stat = jnp.where(lane == head, peak + jnp.log(total), stat)
    o_ref[...] = mixed.astype(bf16)
    l_ref[0] = stat.T[:8]


def cross_forward(query, kv):
    rows = query.shape[0] // 1
    cells = kv.shape[0]
    return pl.pallas_call(
        cross_forward_kernel,
        grid=(1,),
        in_specs=[
            pl.BlockSpec((rows, CH), lambda i: (i, 0)),
            pl.BlockSpec((cells, CH), lambda i: (0, 0)),
            pl.BlockSpec((cells, CH), lambda i: (0, 1)),
        ],
        out_specs=[
            pl.BlockSpec((rows, CH), lambda i: (i, 0)),
            pl.BlockSpec((1, 8, rows), lambda i: (i, 0, 0)),
        ],
        out_shape=[
            jax.ShapeDtypeStruct((rows, CH), bf16),
            jax.ShapeDtypeStruct((1, 8, rows), f32),
        ],
        compiler_params=params(),
        cost_estimate=cost(16 * TH * rows * cells * CH // 2, 8 * cells * CH, 2 * TH * rows * cells),
    )(query, kv, kv)


def delta_rows(d_out, out):
    product = d_out.astype(f32) * out.astype(f32)
    head = lax.broadcasted_iota(jnp.int32, (8, CH), 0)
    lane = lax.broadcasted_iota(jnp.int32, (8, CH), 1)
    pick = ((lane // HD) == head).astype(f32)
    return lax.dot_general(
        pick,
        product,
        (((1,), (1,)), ((), ())),
        precision=lax.Precision.HIGHEST,
        preferred_element_type=f32,
    )


def cross_probs_kernel(q_ref, k_ref, l_ref, p_ref):
    q = q_ref[...].astype(f32) * 0.125
    for head in range(TH):
        q_head = jnp.where(head_mask(q.shape, head), q, 0.0).astype(bf16)
        scores = dot_nt(k_ref[...], q_head)
        p_ref[head] = jnp.exp(scores - l_ref[head : head + 1, :]).astype(bf16)


def cross_probs(query, kv, log_rows):
    rows = query.shape[0]
    cells = kv.shape[0]
    block = 512
    return pl.pallas_call(
        cross_probs_kernel,
        grid=(cells // block,),
        in_specs=[
            pl.BlockSpec((rows, CH), lambda i: (0, 0)),
            pl.BlockSpec((block, CH), lambda i: (i, 0)),
            pl.BlockSpec((8, rows), lambda i: (0, 0)),
        ],
        out_specs=pl.BlockSpec((TH, block, rows), lambda i: (0, i, 0)),
        out_shape=lasting((TH, cells, rows), bf16),
        compiler_params=params(),
        cost_estimate=cost(2 * TH * rows * cells * CH, 2 * TH * rows * cells, TH * rows * cells),
    )(query, stay(kv), log_rows)


def cross_backward_kernel(
    q_ref, k_ref, v_ref, do_ref, o_ref, p_ref, feats_ref, gupd_ref, query_w_ref,
    dkv_ref, query_g_ref, future_ref, q_s, do_s, delta_s, dq_s,
):
    step = pl.program_id(0)
    rows = q_ref.shape[0]

    @pl.when(step == 0)
    def _():
        for head in range(TH):
            mask = head_mask((rows, CH), head)
            q_s[head] = jnp.where(mask, q_ref[...].astype(f32) * 0.125, 0.0).astype(bf16)
            do_s[head] = jnp.where(mask, do_ref[...].astype(f32), 0.0).astype(bf16)
        delta_s[...] = delta_rows(do_ref[...], o_ref[...])
        dq_s[...] = jnp.zeros_like(dq_s)

    cells = k_ref.shape[0]
    dk = jnp.zeros((cells, CH), f32)
    dv = jnp.zeros((cells, CH), f32)
    k_turned = k_ref[...].T
    for head in range(TH):
        probs = p_ref[head]
        d_probs = dot_nt(v_ref[...], do_s[head])
        d_scores = (probs.astype(f32) * (d_probs - delta_s[head : head + 1, :])).astype(bf16)
        dv = dv + dot_nn(probs, do_s[head])
        dk = dk + dot_nn(d_scores, q_s[head])
        here = slice(head * HD, (head + 1) * HD)
        dq_s[here, :] += dot_nn(k_turned[here, :], d_scores)
    dkv_ref[:, :CH] = dk.astype(bf16)
    dkv_ref[:, CH:] = dv.astype(bf16)

    @pl.when(step == pl.num_programs(0) - 1)
    def _():
        gq = (dq_s[...].T * 0.125).astype(bf16)
        query_g_ref[...] = dot_tn(feats_ref[...], gq).astype(bf16)
        future_ref[...] = gupd_ref[...] + dot_nt(gq, query_w_ref[...])


def cross_backward(query, kv, d_out, out, probs, feats, gupd, to_query):
    rows = query.shape[0]
    cells = kv.shape[0]
    block = 1024
    whole = lambda i: (0, 0)
    return pl.pallas_call(
        cross_backward_kernel,
        grid=(cells // block,),
        in_specs=[
            pl.BlockSpec((rows, CH), whole),
            pl.BlockSpec((block, CH), lambda i: (i, 0)),
            pl.BlockSpec((block, CH), lambda i: (i, 1)),
            pl.BlockSpec((rows, CH), whole),
            pl.BlockSpec((rows, CH), whole),
            pl.BlockSpec((TH, block, rows), lambda i: (0, i, 0)),
            pl.BlockSpec((rows, CH), whole),
            pl.BlockSpec((rows, CH), whole),
            pl.BlockSpec((CH, CH), whole),
        ],
        out_specs=[
            pl.BlockSpec((block, 2 * CH), lambda i: (i, 0)),
            pl.BlockSpec((CH, CH), whole),
            pl.BlockSpec((rows, CH), whole),
        ],
        out_shape=[
            jax.ShapeDtypeStruct((cells, 2 * CH), bf16),
            jax.ShapeDtypeStruct((CH, CH), bf16),
            jax.ShapeDtypeStruct((rows, CH), f32),
        ],
        scratch_shapes=[
            pltpu.VMEM((TH, rows, CH), bf16),
            pltpu.VMEM((TH, rows, CH), bf16),
            pltpu.VMEM((8, rows), f32),
            pltpu.VMEM((CH, rows), f32),
        ],
        compiler_params=pltpu.CompilerParams(vmem_limit_bytes=MLP_BYTES),
        cost_estimate=cost(10 * TH * rows * cells * CH, 8 * cells * CH, TH * rows * cells),
    )(query, kv, kv, d_out, out, stay(probs), feats, gupd, to_query)


def self_forward_kernel(len_ref, q_ref, k_ref, v_ref, o_ref, l_ref):
    group = pl.program_id(0)
    length = len_ref[0]
    for start, count in ROW_BLOCKS:
        stop = start + count
        q = q_ref[0, start:stop, :].astype(f32) * 0.125
        row = lax.broadcasted_iota(jnp.int32, (count, 1), 0) + start
        bound = jnp.minimum(row, length - 1)
        allowed = lax.broadcasted_iota(jnp.int32, (count, stop), 1) <= bound
        mixed = jnp.zeros((count, CH), f32)
        stat = jnp.zeros((count, 128), f32)
        lane = lax.broadcasted_iota(jnp.int32, (count, 128), 1)
        for head in range(GROUP):
            mask = head_mask((count, CH), head)
            q_head = jnp.where(mask, q, 0.0).astype(bf16)
            scores = jnp.where(allowed, dot_nt(q_head, k_ref[0, :stop, :]), neg_large)
            peak = jnp.max(scores, -1, keepdims=True)
            shifted = jnp.exp(scores - peak)
            total = jnp.sum(shifted, -1, keepdims=True)
            part = dot_nn(shifted.astype(bf16), v_ref[0, :stop, :])
            mixed = jnp.where(mask, part / total, mixed)
            stat = jnp.where(lane == head, peak + jnp.log(total), stat)
        o_ref[start:stop, :] = mixed.astype(bf16)
        l_ref[0, :, start:stop] = stat.T[:8]


def self_forward(qkv, length):
    groups = D // CH
    at = lambda j: (lambda i, n: (j, 0, i))
    return pl.pallas_call(
        self_forward_kernel,
        grid_spec=pltpu.PrefetchScalarGridSpec(
            num_scalar_prefetch=1,
            grid=(groups,),
            in_specs=[pl.BlockSpec((1, SEQ, CH), at(j)) for j in range(3)],
            out_specs=[
                pl.BlockSpec((SEQ, CH), lambda i, n: (0, i)),
                pl.BlockSpec((1, 8, SEQ), lambda i, n: (i, 0, 0)),
            ],
        ),
        out_shape=[
            lasting((SEQ, D), bf16),
            jax.ShapeDtypeStruct((groups, 8, SEQ), f32),
        ],
        compiler_params=params(),
        cost_estimate=cost(4 * HEADS * SEQ * SEQ * CH, 8 * SEQ * D, HEADS * SEQ * SEQ),
    )(length, qkv, qkv, qkv)


def self_backward_kernel(
    len_ref, q_ref, k_ref, v_ref, do_ref, o_ref, l_ref, out_ref, dk_s, dv_s
):
    length = len_ref[0]
    dk_s[...] = jnp.zeros_like(dk_s)
    dv_s[...] = jnp.zeros_like(dv_s)
    delta = delta_rows(do_ref[...], o_ref[...])
    k_turned = k_ref[0].T
    for start, count in ROW_BLOCKS:
        stop = start + count
        q = q_ref[0, start:stop, :].astype(f32) * 0.125
        d_out = do_ref[start:stop, :].astype(f32)
        row = lax.broadcasted_iota(jnp.int32, (1, count), 1) + start
        bound = jnp.minimum(row, length - 1)
        allowed = lax.broadcasted_iota(jnp.int32, (stop, count), 0) <= bound
        dq = []
        k = k_ref[0, :stop, :]
        v = v_ref[0, :stop, :]
        dk = dk_s[:stop, :]
        dv = dv_s[:stop, :]
        for head in range(GROUP):
            mask = head_mask((count, CH), head)
            q_head = jnp.where(mask, q, 0.0).astype(bf16)
            d_head = jnp.where(mask, d_out, 0.0).astype(bf16)
            scores = dot_nt(k, q_head)
            logs = l_ref[0, head : head + 1, start:stop]
            probs = jnp.where(allowed, jnp.exp(scores - logs), 0.0)
            d_probs = dot_nt(v, d_head)
            d_scores = (probs * (d_probs - delta[head : head + 1, start:stop])).astype(bf16)
            dv = dv + dot_nn(probs.astype(bf16), d_head)
            dk = dk + dot_nn(d_scores, q_head)
            dq.append(dot_nn(k_turned[head * HD : (head + 1) * HD, :stop], d_scores))
        dk_s[:stop, :] = dk
        dv_s[:stop, :] = dv
        out_ref[0, start:stop, :] = (jnp.concatenate(dq, 0).T * 0.125).astype(bf16)
    out_ref[1] = dk_s[...].astype(bf16)
    out_ref[2] = dv_s[...].astype(bf16)


def self_backward(qkv, d_out, out, log_rows, length, count):
    groups = D // CH
    at = lambda j: (lambda i, n: (j, 0, i))
    here = lambda i, n: (0, i)
    return pl.pallas_call(
        self_backward_kernel,
        grid_spec=pltpu.PrefetchScalarGridSpec(
            num_scalar_prefetch=1,
            grid=(count,),
            in_specs=[pl.BlockSpec((1, SEQ, CH), at(j)) for j in range(3)]
            + [
                pl.BlockSpec((SEQ, CH), here),
                pl.BlockSpec((SEQ, CH), here),
                pl.BlockSpec((1, 8, SEQ), lambda i, n: (i, 0, 0)),
            ],
            out_specs=pl.BlockSpec((3, SEQ, CH), lambda i, n: (0, 0, i)),
            scratch_shapes=[pltpu.VMEM((SEQ, CH), f32), pltpu.VMEM((SEQ, CH), f32)],
        ),
        out_shape=jax.ShapeDtypeStruct((3, SEQ, count * CH), bf16),
        compiler_params=params(),
        cost_estimate=cost(
            8 * HEADS * SEQ * SEQ * CH * count // groups, 16 * SEQ * D, HEADS * SEQ * SEQ
        ),
    )(length, stay(qkv), stay(qkv), stay(qkv), stay(d_out), stay(out), log_rows)


def full(*shape):
    return pl.BlockSpec(shape, lambda i: (0,) * len(shape))


def part_of(first):
    return pl.BlockSpec((3, CH, D), lambda i: (first + i, 0, 0))


def fixed_part(index):
    return pl.BlockSpec((3, CH, D), lambda i: (index, 0, 0))


def square(ref):
    return ref[...].reshape(D, D)


def write_cores(core, matrix, keep_refs, sizes, order, at=0):
    z, y, x, rows = sizes
    columns = matrix.shape[-1]
    if rows % 8:
        parts = matrix.reshape(-1, 2, y * x * rows, columns)
    else:
        parts = matrix.reshape(-1, 2, y, x, rows, columns)
    first, second = parts[:, 0], parts[:, 1]
    halves = (jnp.where(core == 0, first, second), jnp.where(core == 0, second, first))
    for ref, half in zip(keep_refs, halves):
        here = slice(at * z, at * z + half.shape[0])
        if rows % 8:
            ref[here] = half.astype(bf16)
            continue
        for row in range(y):
            for col in range(x):
                to = (col, row) if order == "xy" else (row, col)
                ref[to[0], to[1], here] = half[:, row, col].astype(bf16)


def core_shape(count, order, columns=D):
    z, y, x, rows = slice_shape()
    if rows % 8:
        return (count * z, y * x * rows, columns)
    cuts = (x, y) if order == "xy" else (y, x)
    return cuts + (count * z, rows, columns)


def core_block(count, order, at, columns=D):
    shape = core_shape(count, order, columns)
    return pl.BlockSpec(shape, lambda i: (0,) * (len(shape) - 3) + (at(i), 0, 0))


def core_cuts(parts, order):
    z, y, x, rows = slice_shape()
    if rows % 8 == 0:
        return list(parts)
    parts = [part.reshape(-1, y, x, rows, part.shape[-1]) for part in parts]
    dims = (2, 1, 0, 3, 4) if order == "xy" else (1, 2, 0, 3, 4)
    return [part.transpose(dims) for part in parts]


def split_z(slices):
    return slices.reshape((-1, lax.axis_size("z")) + slices.shape[1:])


def row_here():
    return lax.axis_index(("y", "x")).astype(jnp.int32).reshape(1)


def core_here():
    return lax.axis_index("c").astype(jnp.int32).reshape(1)


def row_scale(values):
    return lax.rsqrt(jnp.mean(values * values, -1, keepdims=True) + eps_norm)


def pull_norm(d_normed, values, gain):
    scale = row_scale(values)
    d_gain = jnp.sum(d_normed * values * scale, 0, keepdims=True)
    scaled = d_normed * gain
    inner = jnp.mean(scaled * values, -1, keepdims=True)
    return d_gain, scale * scaled - (scale * scale * scale) * values * inner


def embed_kernel(
    pool_ref, feats_ref, mixed_ref, out_w_ref, emb_ref, w_ref, gain_ref,
    seq_ref, embed_ref, normed_ref, qkv_ref,
):
    @pl.when(pl.program_id(0) == 0)
    def _():
        updated = feats_ref[...].astype(f32) + dot_nn(mixed_ref[...], out_w_ref[...])
        seq_ref[:CTX, :] = pool_ref[...]
        seq_ref[CTX:, :] = updated.astype(bf16)
        embed = dot_nn(seq_ref[...], emb_ref[0])
        embed_ref[...] = embed
        normed_ref[...] = (embed * row_scale(embed) * gain_ref[...]).astype(bf16)

    qkv_ref[0] = dot_nn(normed_ref[...], square(w_ref)).astype(bf16)


def embed_forward(pooled, feats, mixed, to_out, weights, gain):
    last = weights.shape[0] - 1
    return pl.pallas_call(
        embed_kernel,
        grid=(3,),
        in_specs=[
            full(CTX, CH),
            full(SEQ - CTX, CH),
            full(SEQ - CTX, CH),
            full(CH, CH),
            pl.BlockSpec((1, CH, D), lambda i: (last, 0, 0)),
            part_of(0),
            full(1, D),
        ],
        out_specs=[
            full(SEQ, CH),
            full(SEQ, D),
            full(SEQ, D),
            pl.BlockSpec((1, SEQ, D), lambda i: (i, 0, 0)),
        ],
        out_shape=[
            lasting((SEQ, CH), bf16),
            lasting((SEQ, D), f32),
            lasting((SEQ, D), bf16),
            lasting((3, SEQ, D), bf16),
        ],
        compiler_params=params(),
        cost_estimate=cost(2 * SEQ * D * (CH + 3 * D), 12 * SEQ * D),
    )(pooled, feats, mixed, to_out, stay(weights), stay(weights), gain)


def mlp_kernel(
    core_ref, mixed_ref, embed_ref, att_ref, up_ref, down_ref, gain_ref, gd_ref,
    out_ref, d_stream_ref, gog_ref, up_keep_ref, up_give_ref, down_keep_ref, down_give_ref,
    att_keep_ref, att_give_ref, gain_g_ref,
    stream_s, normed_s, turned_s, act_s, gpre_s, total_s, *, sizes
):
    step = pl.program_id(0)
    core = core_ref[0]

    @pl.when(step == 0)
    def _():
        stream = embed_ref[...] + dot_nn(mixed_ref[...], square(att_ref))
        stream_s[...] = stream
        out_ref[...] = stream
        total_s[...] = jnp.zeros_like(total_s)
        normed = stream * row_scale(stream) * gain_ref[...]
        normed_s[...] = normed.astype(bf16)
        turned_s[...] = normed.T.astype(bf16)

    factor = (2.0 / 3.141592653589793) ** 0.5
    cubic = 0.044715 * factor
    rows = SEQ // 2
    for start in range(0, SEQ, rows):
        here = slice(start, start + rows)
        v = dot_nn(normed_s[here, :], square(up_ref))
        v2 = v * v
        half = 0.5 + 0.5 * jnp.tanh(v * (factor + cubic * v2))
        act = (v * half).astype(bf16)
        act_s[here, :] = act
        slope = half + v * (2.0 * half * (1.0 - half) * (factor + 3.0 * cubic * v2))
        gpre = (dot_nt(gd_ref[here, :], square(down_ref)) * slope).astype(bf16)
        gpre_s[here, :] = gpre
        out_ref[here, :] += dot_nn(act, square(down_ref))
        total_s[here, :] += dot_nt(gpre, square(up_ref))
    down_refs, up_refs = (down_keep_ref, down_give_ref), (up_keep_ref, up_give_ref)
    write_cores(core, dot_tn(act_s[...], gd_ref[...]), down_refs, sizes, "xy")
    write_cores(core, dot_nn(turned_s[...], gpre_s[...]), up_refs, sizes, "yx")

    @pl.when(step == pl.num_programs(0) - 1)
    def _():
        d_gain, pulled = pull_norm(total_s[...], stream_s[...], gain_ref[...])
        gain_g_ref[...] = d_gain
        d_stream = gd_ref[...].astype(f32) + pulled
        d_stream_ref[...] = d_stream
        ga = d_stream.astype(bf16)
        gog_ref[...] = dot_nt(ga, square(att_ref)).astype(bf16)
        att_refs = (att_keep_ref, att_give_ref)
        write_cores(core, dot_tn(mixed_ref[...], ga), att_refs, sizes, "yx")


def mlp_block(mixed, embed, weights, mlp, gain, gd):
    up_part = core_block(3, "yx", lambda i: i)
    down_part = core_block(3, "xy", lambda i: i)
    att_part = core_block(3, "yx", lambda i: 0)
    return pl.pallas_call(
        functools.partial(mlp_kernel, sizes=slice_shape()),
        grid=(4,),
        in_specs=[
            CORE_SPEC,
            full(SEQ, D),
            full(SEQ, D),
            fixed_part(3),
            part_of(0),
            part_of(4),
            full(1, D),
            full(SEQ, D),
        ],
        out_specs=[full(SEQ, D)] * 3
        + [up_part] * 2
        + [down_part] * 2
        + [att_part] * 2
        + [full(1, D)],
        out_shape=[
            lasting((SEQ, D), f32),
            lasting((SEQ, D), f32),
            lasting((SEQ, D), bf16),
        ]
        + [jax.ShapeDtypeStruct(core_shape(12, "yx"), bf16)] * 2
        + [jax.ShapeDtypeStruct(core_shape(12, "xy"), bf16)] * 2
        + [lasting(core_shape(3, "yx"), bf16)] * 2
        + [jax.ShapeDtypeStruct((1, D), f32)],
        scratch_shapes=[
            pltpu.VMEM((SEQ, D), f32),
            pltpu.VMEM((SEQ, D), bf16),
            pltpu.VMEM((D, SEQ), bf16),
            pltpu.VMEM((SEQ, D), bf16),
            pltpu.VMEM((SEQ, D), bf16),
            pltpu.VMEM((SEQ, D), f32),
        ],
        compiler_params=pltpu.CompilerParams(vmem_limit_bytes=MLP_BYTES),
        cost_estimate=cost(54 * SEQ * D * D, 60 * SEQ * D, 4 * SEQ * D),
    )(
        core_here(), stay(mixed), stay(embed), stay(weights), stay(mlp), stay(mlp), gain, stay(gd)
    )


def embed_grad_kernel(
    core_ref, len_ref, q_ref, k_ref, v_ref, do_ref, o_ref, l_ref,
    g_ref, normed_ref, w_ref, emb_ref, embed_ref, d_stream_ref, seq_ref, mixed_ref, out_w_ref,
    gain_ref, gain_g_ref,
    qk_keep_ref, qk_give_ref, v_keep_ref, v_give_ref, keep_ref, give_ref,
    gupd_ref, pool_g_ref, out_g_ref, gox_ref,
    dk_s, dv_s, last_s, turned_s, total_s, *, sizes
):
    step = pl.program_id(0)
    core = core_ref[0]

    @pl.when(step == 0)
    def _():
        self_backward_kernel(
            len_ref, q_ref, k_ref, v_ref, do_ref, o_ref, l_ref, last_s, dk_s, dv_s
        )
        turned_s[...] = normed_ref[...].T
        total_s[...] = jnp.zeros_like(total_s)

    @pl.when(step > 0)
    def _():
        g = jnp.concatenate([g_ref[0], last_s[step - 1]], 1)
        total_s[...] += dot_nt(g, square(w_ref))
        grad = dot_nn(turned_s[...], g)

        @pl.when(step < 3)
        def _():
            write_cores(core, grad, (qk_keep_ref, qk_give_ref), sizes, "xy")

        @pl.when(step == 3)
        def _():
            write_cores(core, grad, (v_keep_ref, v_give_ref), sizes, "yx")

    @pl.when(step == 3)
    def _():
        d_gain, pulled = pull_norm(total_s[...], embed_ref[...], gain_ref[...])
        gembed = (d_stream_ref[...] + pulled).astype(bf16)
        at = lax.broadcasted_iota(jnp.int32, (CH, D), 0)
        gains = jnp.where(at == 0, d_gain, jnp.where(at == sizes[-1], gain_g_ref[...], 0.0))
        for index, values in enumerate((dot_tn(seq_ref[...], gembed), gains)):
            write_cores(core, values, (keep_ref, give_ref), sizes, "xy", index)
        gseq = dot_nt(gembed, emb_ref[0])
        gupd = gseq[CTX:]
        gb = gupd.astype(bf16)
        pool_g_ref[...] = gseq[:CTX].astype(bf16)
        gupd_ref[...] = gupd
        out_g_ref[...] = dot_tn(mixed_ref[...], gb).astype(bf16)
        gox_ref[...] = dot_nt(gb, out_w_ref[...]).astype(bf16)


def embed_grad(
    length, qkv, gog, out, log_rows, gqkv, normed, weights, embed, d_stream, seq, mixed, to_out,
    gain, gain_g,
):
    last = weights.shape[0] - 1
    group = D // CH - 1
    done = gqkv.shape[-1]
    part = lambda i: jnp.maximum(i - 1, 0)
    at = lambda j: pl.BlockSpec((1, SEQ, CH), lambda i: (j, 0, group))
    here = pl.BlockSpec((SEQ, CH), lambda i: (0, group))
    qk_part = core_block(3, "xy", lambda i: jnp.clip(i - 1, 0, 1))
    v_part = core_block(3, "yx", lambda i: 0)
    emb_part = core_block(2, "xy", lambda i: 0)
    return pl.pallas_call(
        functools.partial(embed_grad_kernel, sizes=slice_shape()),
        grid=(4,),
        in_specs=[
            CORE_SPEC,
            CORE_SPEC,
            at(0),
            at(1),
            at(2),
            here,
            here,
            pl.BlockSpec((1, 8, SEQ), lambda i: (group, 0, 0)),
            pl.BlockSpec((1, SEQ, done), lambda i: (part(i), 0, 0)),
            full(SEQ, D),
            pl.BlockSpec((3, CH, D), lambda i: (part(i), 0, 0)),
            pl.BlockSpec((1, CH, D), lambda i: (last, 0, 0)),
            full(SEQ, D),
            full(SEQ, D),
            full(SEQ, CH),
            full(SEQ - CTX, CH),
            full(CH, CH),
            full(1, D),
            full(1, D),
        ],
        out_specs=[
            qk_part,
            qk_part,
            v_part,
            v_part,
            emb_part,
            emb_part,
            full(SEQ - CTX, CH),
            full(CTX, CH),
            full(CH, CH),
            full(SEQ - CTX, CH),
        ],
        out_shape=[jax.ShapeDtypeStruct(core_shape(6, "xy"), bf16)] * 2
        + [jax.ShapeDtypeStruct(core_shape(3, "yx"), bf16)] * 2
        + [jax.ShapeDtypeStruct(core_shape(2, "xy"), bf16)] * 2
        + [
            jax.ShapeDtypeStruct((SEQ - CTX, CH), f32),
            jax.ShapeDtypeStruct((CTX, CH), bf16),
            jax.ShapeDtypeStruct((CH, CH), bf16),
            jax.ShapeDtypeStruct((SEQ - CTX, CH), bf16),
        ],
        scratch_shapes=[
            pltpu.VMEM((SEQ, CH), f32),
            pltpu.VMEM((SEQ, CH), f32),
            pltpu.VMEM((3, SEQ, CH), bf16),
            pltpu.VMEM((D, SEQ), bf16),
            pltpu.VMEM((SEQ, D), f32),
        ],
        compiler_params=pltpu.CompilerParams(vmem_limit_bytes=MLP_BYTES),
        cost_estimate=cost(2 * SEQ * D * (6 * D + 2 * CH) + 32 * SEQ * SEQ * CH, 50 * SEQ * D),
    )(
        core_here(), length, stay(qkv), stay(qkv), stay(qkv), stay(gog), stay(out), log_rows, gqkv, normed, stay(weights),
        stay(weights), stay(embed), stay(d_stream), stay(seq), stay(mixed), to_out, gain, gain_g,
    )


def patch_pick(rows, columns, patch_dim):
    patch = lax.broadcasted_iota(jnp.int32, (rows, columns), patch_dim)
    cell = lax.broadcasted_iota(jnp.int32, (rows, columns), 1 - patch_dim)
    inside = (cell // (PATCH * IMG)) * (IMG // PATCH) + (cell % IMG) // PATCH
    return jnp.where(patch == inside, 1.0 / (PATCH * PATCH), 0.0).astype(bf16)


def image_rows(step, row):
    return pl.ds(pl.multiple_of(step * BLOCK + row * IMG, IMG), BLOCK)


def token_forward_kernel(x_ref, conv_ref, kv_w_ref, slope_ref, hidden_ref, kv_ref, pool_ref):
    step = pl.program_id(0)
    z = jnp.zeros((BLOCK, CH), f32)
    for row in range(3):
        z = z + dot_nn(x_ref[image_rows(step, row), :], conv_ref[row])
    center = x_ref[image_rows(step, 1), CH : 2 * CH].astype(f32)
    gate = 1.0 / (1.0 + jnp.exp(-z))
    hidden = center + z * gate
    slope_ref[...] = (gate * (1.0 + z * (1.0 - gate))).astype(bf16)
    hidden_b = hidden.astype(bf16)
    hidden_ref[...] = hidden_b
    kv_ref[...] = dot_nn(hidden_b, kv_w_ref[...]).astype(bf16)
    rest = (hidden - hidden_b.astype(f32)).astype(bf16)
    pick = patch_pick(pool_ref.shape[0], BLOCK, 0)
    pool_ref[...] = (dot_nn(pick, hidden_b) + dot_nn(pick, rest)).astype(bf16)


def token_forward(wide, conv_rows, kv_weight):
    steps = CELLS // BLOCK
    whole = lambda i: (0, 0)
    block = lambda i: (i, 0)
    return pl.pallas_call(
        token_forward_kernel,
        grid=(steps,),
        in_specs=[
            pl.BlockSpec(wide.shape, whole),
            pl.BlockSpec((3, 3 * CH, CH), lambda i: (0, 0, 0)),
            pl.BlockSpec((CH, 2 * CH), whole),
        ],
        out_specs=[
            pl.BlockSpec((BLOCK, CH), block),
            pl.BlockSpec((BLOCK, CH), block),
            pl.BlockSpec((BLOCK, 2 * CH), block),
            pl.BlockSpec((CTX // steps, CH), block),
        ],
        out_shape=[
            lasting((CELLS, CH), bf16),
            lasting((CELLS, CH), bf16),
            jax.ShapeDtypeStruct((CELLS, 2 * CH), bf16),
            jax.ShapeDtypeStruct((CTX, CH), bf16),
        ],
        compiler_params=params(),
        cost_estimate=cost(22 * CELLS * CH * CH, 14 * CELLS * CH, CELLS * CH),
    )(stay(wide), conv_rows, kv_weight)


def token_backward_kernel(
    core_ref, dkv_ref, slope_ref, pool_ref, hidden_ref, x_ref, kv_w_ref, query_g_ref, out_g_ref,
    d_hidden_ref, gz_ref, keep_ref, give_ref, conv_s, kv_s, *, sizes
):
    step = pl.program_id(0)

    @pl.when(step == 0)
    def _():
        conv_s[...] = jnp.zeros_like(conv_s)
        kv_s[...] = jnp.zeros_like(kv_s)

    dkv = dkv_ref[...]
    d_hidden = dot_nt(dkv, kv_w_ref[...])
    d_hidden = d_hidden + dot_nn(patch_pick(BLOCK, pool_ref.shape[0], 1), pool_ref[...])
    gz = (d_hidden * slope_ref[...].astype(f32)).astype(bf16)
    d_hidden_ref[...] = d_hidden
    gz_ref[...] = gz
    kv_s[...] += dot_tn(hidden_ref[...], dkv)
    gz_t = gz.T
    for row in range(3):
        conv_s[row] += dot_nn(gz_t, x_ref[image_rows(step, row), :])

    @pl.when(step == pl.num_programs(0) - 1)
    def _():
        tiles = []
        for row in range(3):
            for col in range(3):
                tiles.append(conv_s[row, :, col * CH : (col + 1) * CH].T)
        tiles = tiles + [query_g_ref[...], kv_s[:, :CH], kv_s[:, CH:], out_g_ref[...]]
        for at, tile in enumerate(tiles):
            write_cores(core_ref[0], tile.astype(f32), (keep_ref, give_ref), sizes, "yx", at)


def token_backward(dkv, slope, d_pool, hidden_b, wide, kv_weight, query_g, out_g):
    steps = CELLS // BLOCK
    whole = lambda i: (0, 0)
    block = lambda i: (i, 0)
    return pl.pallas_call(
        functools.partial(token_backward_kernel, sizes=slice_shape()),
        grid=(steps,),
        in_specs=[
            CORE_SPEC,
            pl.BlockSpec((BLOCK, 2 * CH), block),
            pl.BlockSpec((BLOCK, CH), block),
            pl.BlockSpec((CTX // steps, CH), block),
            pl.BlockSpec((BLOCK, CH), block),
            pl.BlockSpec(wide.shape, whole),
            pl.BlockSpec((CH, 2 * CH), whole),
            pl.BlockSpec((CH, CH), whole),
            pl.BlockSpec((CH, CH), whole),
        ],
        out_specs=[
            pl.BlockSpec((BLOCK, CH), block),
            pl.BlockSpec((BLOCK, CH), block),
            core_block(EARLY, "yx", lambda i: 0, CH),
            core_block(EARLY, "yx", lambda i: 0, CH),
        ],
        out_shape=[
            jax.ShapeDtypeStruct((CELLS, CH), f32),
            jax.ShapeDtypeStruct((CELLS, CH), bf16),
            jax.ShapeDtypeStruct(core_shape(EARLY, "yx", CH), bf16),
            jax.ShapeDtypeStruct(core_shape(EARLY, "yx", CH), bf16),
        ],
        scratch_shapes=[pltpu.VMEM((3, CH, 3 * CH), f32), pltpu.VMEM((CH, 2 * CH), f32)],
        compiler_params=params(),
        cost_estimate=cost(26 * CELLS * CH * CH, 20 * CELLS * CH),
    )(core_here(), dkv, stay(slope), d_pool, stay(hidden_b), stay(wide), kv_weight, query_g, out_g)


def context_backward_kernel(gz_ref, d_hidden_ref, conv_ref, out_ref, wide_s):
    step = pl.program_id(0)
    steps = pl.num_programs(0)

    def widen(at):
        values = gz_ref[image_rows(at, 0), :].astype(f32)
        col = lax.broadcasted_iota(jnp.int32, (BLOCK, CH), 0) % IMG
        left = jnp.where(col == 0, 0.0, pltpu.roll(values, 1, 0))
        right = jnp.where(col == IMG - 1, 0.0, pltpu.roll(values, BLOCK - 1, 0))
        wide_s[image_rows(at, 1), 0:CH] = left.astype(bf16)
        wide_s[image_rows(at, 1), CH : 2 * CH] = values.astype(bf16)
        wide_s[image_rows(at, 1), 2 * CH :] = right.astype(bf16)

    @pl.when(step == 0)
    def _():
        wide_s[0:IMG, :] = jnp.zeros((IMG, 3 * CH), bf16)
        wide_s[CELLS + IMG :, :] = jnp.zeros((IMG, 3 * CH), bf16)
        widen(0)

    @pl.when(step < steps - 1)
    def _():
        widen(step + 1)

    total = d_hidden_ref[...]
    for row in range(3):
        values = wide_s[image_rows(step, row), :]
        for col in range(3):
            tap = conv_ref[3 * (2 - row) + (2 - col)]
            total = total + dot_nt(values[:, col * CH : (col + 1) * CH], tap)
    out_ref[...] = total.astype(bf16)


def context_backward(gz, d_hidden, conv_tiles):
    block = lambda i: (i, 0)
    return pl.pallas_call(
        context_backward_kernel,
        grid=(CELLS // BLOCK,),
        in_specs=[
            pl.BlockSpec((CELLS, CH), lambda i: (0, 0)),
            pl.BlockSpec((BLOCK, CH), block),
            pl.BlockSpec((9, CH, CH), lambda i: (0, 0, 0)),
        ],
        out_specs=pl.BlockSpec((BLOCK, CH), block),
        out_shape=jax.ShapeDtypeStruct((CELLS, CH), bf16),
        scratch_shapes=[pltpu.VMEM((CELLS + 2 * IMG, 3 * CH), bf16)],
        compiler_params=params(),
        cost_estimate=cost(18 * CELLS * CH * CH, 8 * CELLS * CH),
    )(gz, d_hidden, conv_tiles)


def local(
    context_map,
    future_feats,
    horizon,
    cotangent,
    tile_owner,
    master_tiles,
    moment_first,
    moment_second,
    norm_gains,
    gain_first,
    gain_second,
):
    slot_count = master_tiles.shape[0]
    devices = lax.axis_size(AXES)
    rows = CH // devices
    slot_of = slot_index(tile_owner, slot_count)

    length = CTX + FT * horizon
    valid = jnp.arange(SEQ) < length[0]
    gd = jnp.where(valid[:, None], cotangent[0], jnp.zeros((), bf16))

    slices = (
        master_tiles.astype(bf16)
        .reshape(slot_count, devices, rows, CH)
        .transpose(1, 0, 2, 3)
    )
    slices = lax.all_to_all(slices, AXES, split_axis=0, concat_axis=0, tiled=True)
    extra = max(1, 8 // rows)
    tiles = tile_owner.shape[0]
    span = slot_count + extra
    place = jnp.arange(devices * span)
    device, at = place // span, place % span
    found = slot_of[None, :] == jnp.where(at < slot_count, device * slot_count + at, -1)[:, None]
    tile_of = jnp.sum(jnp.where(found, jnp.arange(tiles)[None], 0), 1)
    tile_of = jnp.where(at < slot_count, tile_of, tiles + at - slot_count)
    mine_at = lax.axis_index(AXES) * slot_count + jnp.arange(slot_count)
    used = jnp.any(slot_of[None, :] == mine_at[:, None], 1).astype(f32)
    slices, gd, tile_of, used = tie((slices, gd, tile_of, used))
    slices = slices.reshape(devices * slot_count, rows, CH)
    slices = slices.at[slot_of].get(mode="promise_in_bounds")
    early, emb, qkv, att, up, down = jnp.split(slices, (13, 16, 43, 52, 88))
    mlp = jnp.concatenate([from_tiles(up, 3, 4), from_tiles(down, 12, 1)], 0)
    early = gather_axes(early, "z")
    core = jnp.concatenate([from_tiles(qkv, 3, 3), from_tiles(att, 3, 1), from_tiles(emb, 1, 1)], 0)
    core, early = tie((core, early))
    early = gather_axes(joined(early), ("y", "x"))
    core = gather_axes(core, "z")
    pieces = trade_rows(context_map)
    early = joined(gather_axes(joined(early), "c"))
    early = device_order(early, ("c", "y", "x", "z"))
    wide = widen(pieces)
    core = joined(core)
    low, high = gather_axes(core[:6], "x"), gather_axes(core[6:], "y")

    conv_tiles = early[:9]
    to_query, to_out = early[9], early[12]
    kv_weight = jnp.concatenate([early[10], early[11]], 1)

    wide, mlp, low, high = hold((wide, mlp), low, high)
    mlp = lax.all_gather(mlp, AXES, axis=1, tiled=True)
    low, high = joined(low), joined(high)
    wide, low, high = tie((wide, low, high))
    low, high = gather_axes(low, "y"), gather_axes(high, "x")
    slope_z, hidden_b, kv, pooled = token_forward(
        wide, conv_tiles.reshape(3, 3 * CH, CH), kv_weight
    )
    kv, low, high = hold((kv,), low, high)
    low, high = joined(low), joined(high)
    feats_b = future_feats[0]
    query = jnp.dot(feats_b, to_query, preferred_element_type=f32).astype(bf16)
    kv, low, high = tie((kv, low, high))
    low, high = gather_axes(low, "c"), gather_axes(high, "c")
    cross_mixed, cross_logs = cross_forward(query, kv)
    cross_mixed, low, high = hold((cross_mixed,), low, high)
    weights = place_rows(low, high)

    gain_one, gain_two = norm_gains[:1], norm_gains[1:]
    seq, embed, normed_one, qkv = embed_forward(
        pooled, feats_b, cross_mixed, to_out, weights, gain_one
    )
    mixed, logs = self_forward(qkv, length)
    mixed, log_rows = tie((mixed, cross_logs[0]))
    probs = cross_probs(query, kv, log_rows)
    mixed, probs = tie((mixed, probs))
    (
        block_out, d_stream, gog, up_keep, up_give, down_keep, down_give, att_keep, att_give,
        gain_g_two,
    ) = mlp_block(mixed, embed, weights, mlp, gain_two, gd)
    up = core_cuts([up_keep, up_give], "yx")
    down = core_cuts([down_keep, down_give], "xy")
    att = core_cuts([att_keep, att_give], "yx")
    gog, up, down, att = tie((gog, up, down, att))
    up, down, att = send(up, "c"), send(down, "c"), send(att, "c")
    gqkv = self_backward(qkv, gog, mixed, logs, length, 2)
    gqkv, up, down, att = hold((gqkv,), up, down, att)
    up, down = advance(up, "y", 0), advance(down, "x", 0)
    gqkv, up, down = tie((gqkv, up, down))
    up, down = send(up, "y"), send(down, "x")
    (
        qk_keep, qk_give, v_keep, v_give, emb_keep, emb_give, gupd, pool_g, out_g, gox,
    ) = embed_grad(
        length, qkv, gog, mixed, logs, gqkv, normed_one, weights, embed, d_stream, seq,
        cross_mixed, to_out, gain_one, gain_g_two,
    )
    first = core_cuts([qk_keep, qk_give], "xy")
    second = core_cuts([v_keep, v_give], "yx")
    emb = core_cuts([emb_keep, emb_give], "xy")
    gox, gupd, first, second, emb, up, down = hold((gox, gupd, first, second, emb), up, down)
    up, down = advance(up, "x", 0), advance(down, "y", 0)
    gox, up, down, first, second, emb = tie((gox, up, down, first, second, emb))
    up, down, emb = send(up, "x"), send(down, "y"), send(emb, "c")
    first, second = send(first, "c"), send(second, "c")

    gkv, query_g, future_grad = cross_backward(
        query, kv, gox, cross_mixed, probs, feats_b, gupd, to_query
    )
    gkv, up, down, first, second, emb = hold((gkv,), up, down, first, second, emb)
    mlp = advance_near([split_z(jnp.concatenate(part, 0)) for part in zip(up, down)])
    emb = advance(emb, "x", 0)
    second = [jnp.concatenate([p, q], 2) for p, q in zip(second, att)]
    first, second = advance(first, "x", 0), advance(second, "y", 0)
    gkv, mlp, first, second, emb = tie((gkv, mlp, first, second, emb))
    mlp, emb = send(mlp, "z"), send(emb, "x")
    first, second = send(first, "x"), send(second, "y")

    d_hidden, gz, early_keep, early_give = token_backward(
        gkv, slope_z, pool_g, hidden_b, wide, kv_weight, query_g, out_g
    )
    d_hidden, gz, early_keep, early_give, mlp, first, second, emb = hold(
        (d_hidden, gz, early_keep, early_give), mlp, first, second, emb
    )
    early = core_cuts([early_keep, early_give], "yx")
    early, mlp, first, second, emb = tie((early, mlp, first, second, emb))
    early = send(early, "c")
    first, second = advance(first, "y", 0), advance(second, "x", 0)
    emb, mlp = advance(emb, "y", 0), advance_far(mlp)
    first, second = send(first, "y"), send(second, "x")
    emb, mlp = send(emb, "y"), send(mlp, "z", 2)
    gz, early, first, second, emb = hold((gz,), early, first, second, emb)
    early = advance([p.reshape((-1,) + p.shape[2:]) for p in early], ("y", "x"), 0)
    att = advance_near([split_z(jnp.concatenate(part, 0)) for part in zip(first, second)])
    gz, early, att = tie((gz, early, att))
    early, att = send(early, ("y", "x")), send(att, "z")
    context_grad = context_backward(gz, d_hidden, conv_tiles)
    context_grad, early, att, mlp = hold((context_grad,), early, att, mlp)
    early = advance([split_z(part) for part in early], "z", 1)
    emb = advance([split_z(part) for part in emb], "z", 1)
    early = [jnp.concatenate([e, to_tiles(m)], 0) for e, m in zip(early, emb)]
    att = advance_far(att)
    context_grad, early, att = tie((context_grad, early, att))
    early, att = send(early, "z"), send(att, "z", 2)
    pieces = trade_rows(context_grad.reshape(context_map.shape))
    sum_mlp = add_up(mlp, keep_wide=True)
    square_mlp = jnp.sum(sum_mlp * sum_mlp)
    half = sum_mlp.shape[0] // 2
    mlp = jnp.concatenate([to_tiles(sum_mlp[:half], 4), to_tiles(sum_mlp[half:])], 0).astype(bf16)
    sum_early = add_up(early, keep_wide=True)
    sum_att = add_up(att, keep_wide=True)

    gains = sum_early[EARLY + 3 :, 0]
    square = square_mlp + jnp.sum(sum_att * sum_att) + jnp.sum(sum_early * sum_early)
    share = jnp.concatenate([gains, jnp.broadcast_to(square, (1, CH))], 0)
    share_high = share.astype(bf16)
    share_low = (share - share_high.astype(f32)).astype(bf16)
    share = jnp.concatenate([share_high, share_low], 0)
    share = jnp.pad(share, ((0, extra * rows - share.shape[0]), (0, 0)))
    sums = jnp.concatenate(
        [
            sum_early[: EARLY + 3].astype(bf16),
            to_tiles(sum_att[:9], 3).astype(bf16),
            to_tiles(sum_att[9:]).astype(bf16),
            mlp,
            share.reshape(extra, rows, CH),
        ],
        0,
    )
    mine = sums.at[tile_of].get(mode="promise_in_bounds")
    mine = mine.reshape(devices, slot_count + extra, rows, CH)
    mine, pieces[-1] = tie((mine, pieces[-1]))
    mine = lax.all_to_all(mine, AXES, split_axis=0, concat_axis=0, tiled=True)
    shares = mine[:, slot_count:].reshape(devices, -1, CH).astype(f32)
    shares = shares[:, :4] + shares[:, 4:8]
    gains = shares[:2, :3].reshape(2, D)
    mine = mine[:, :slot_count].transpose(1, 0, 2, 3).reshape(slot_count, CH, CH).astype(f32)

    used = used[:, None, None]
    grad_norm = jnp.sqrt(jnp.sum(shares[:, 3, 0]))
    factor = jnp.minimum(1.0, clip_level / (grad_norm + 1e-06))
    new_first, new_second, new_master = adam_step(
        master_tiles, mine * factor, moment_first, moment_second, learn_rate, decay_rate
    )
    new_gain_first, new_gain_second, new_gains = adam_step(
        norm_gains, gains * factor, gain_first, gain_second, gain_rate, 0.0
    )
    return (
        block_out[None],
        row_order(pieces).reshape(context_map.shape),
        future_grad[None],
        jnp.where(used > 0, new_first, 0.0),
        jnp.where(used > 0, new_second, 0.0),
        jnp.where(used > 0, new_master, 0.0),
        new_gain_first,
        new_gain_second,
        new_gains,
        grad_norm,
    )


def solution(mesh):
    groups, rows = mesh.devices.shape
    fine = jax.sharding.Mesh(mesh.devices.reshape(groups // 2, 2, rows // 2, 2), AXES)
    whole = P(AXES, None, None)
    image = P(("z", "c"), ("y", "x"), None, None)
    in_specs = (image, whole, P(AXES), whole, P(), whole, whole, whole, P(), P(), P())
    out_specs = (whole, image, whole, whole, whole, whole, P(), P(), P(), P())
    return jax.shard_map(local, mesh=fine, in_specs=in_specs, out_specs=out_specs, check_vma=False)
```

```python
import functools

import jax
import jax.numpy as jnp
from jax import lax
from jax.experimental import pallas as pl
from jax.experimental.pallas import tpu as pltpu
from jax.sharding import PartitionSpec as P

CH = 256
HD = 64
HEADS = 12
D = 768
FF = 3072
TH = 4
IMG = 64
PATCH = 4
FT = 16
CTX = 256
SEQ = 736
STEP = 10


eps_norm = 1e-05
beta_one = 0.9
beta_two = 0.999
learn_rate = 0.02
gain_rate = 0.6
decay_rate = 0.1
adam_eps = 1e-08
clip_level = 1.0
neg_large = -1e30
AXES = ("z", "c", "y", "x")
CELLS = IMG * IMG
BLOCK = 512
GROUP = 4
EARLY = 13
VMEM_BYTES = 28 * 1024 * 1024
MLP_BYTES = 40 * 1024 * 1024
ROW_BLOCKS = ((0, 256), (256, 256), (512, 224))
CORE_SPEC = pl.BlockSpec(memory_space=pltpu.SMEM)
bf16 = jnp.bfloat16
f32 = jnp.float32


def slot_index(tile_owner, slot_count):
    ordinal = jnp.arange(tile_owner.shape[0])
    earlier = (tile_owner[None, :] == tile_owner[:, None]) & (ordinal[None, :] < ordinal[:, None])
    return tile_owner * slot_count + jnp.sum(earlier.astype(jnp.int32), 1)


def adam_step(weight, grad_now, first, second, rate, decay):
    first_new = beta_one * first + (1.0 - beta_one) * grad_now
    second_new = beta_two * second + (1.0 - beta_two) * grad_now * grad_now
    corr_first = first_new / (1.0 - beta_one**STEP)
    corr_second = second_new / (1.0 - beta_two**STEP)
    weight_new = weight - rate * (corr_first / (jnp.sqrt(corr_second) + adam_eps) + decay * weight)
    return (first_new, second_new, weight_new)


def xor_permute(values, axes, mask):
    count = lax.axis_size(axes)
    return lax.ppermute(values, axes, [(i, i ^ mask) for i in range(count)])


def pick(parts, index, dim):
    if parts[0].shape[dim] == 2:
        total = add_up(parts)
        first, second = (lax.index_in_dim(total, at, dim, False) for at in range(2))
        return jnp.where(index == 0, first, second)
    return add_up([lax.dynamic_index_in_dim(part, index, dim, False) for part in parts])


def advance(parts, axes, dim):
    mine = lax.axis_index(axes)
    return [pick(parts, mine ^ mask, dim) for mask in range(lax.axis_size(axes))]


def advance_near(parts):
    mine = lax.axis_index("z") % 2
    shape = parts[0].shape
    parts = [p.reshape((shape[0], shape[1] // 2, 2) + shape[2:]) for p in parts]
    return [pick(parts, mine ^ mask, 2) for mask in range(2)]


def advance_far(parts):
    mine = lax.axis_index("z") // 2
    return [pick(parts, mine ^ mask, 1) for mask in range(parts[0].shape[1])]


def send(cuts, axes, unit=1):
    return [cuts[0]] + [
        xor_permute(cut, axes, unit * mask) for mask, cut in enumerate(cuts) if mask > 0
    ]


def add_up(parts, keep_wide=False):
    total = parts[0].astype(f32)
    for part in parts[1:]:
        total = total + part.astype(f32)
    return total if keep_wide else total.astype(parts[0].dtype)


def hold(values, *sums):
    tied = lax.optimization_barrier((tuple(values), tuple(tuple(parts) for parts in sums)))
    return tied[0] + tuple(list(parts) for parts in tied[1])


def gather_axes(values, axes):
    return [values] + [
        xor_permute(values, axes, mask) for mask in range(1, lax.axis_size(axes))
    ]


def joined(pieces):
    return jnp.stack(pieces, 1)


def device_order(values, axes):
    sizes = [lax.axis_size(axis) for axis in AXES]
    own = [lax.axis_index(axis) for axis in AXES]
    places = jnp.unravel_index(jnp.arange(lax.axis_size(AXES)), sizes)
    at = 0
    for axis in axes:
        which = AXES.index(axis)
        at = at * sizes[which] + (places[which] ^ own[which])
    values = values.reshape((values.shape[0], -1) + values.shape[-2:])
    values = values.at[:, at].get(mode="promise_in_bounds")
    return values.reshape(values.shape[0], -1, values.shape[-1])


def place_kernel(own_ref, low_ref, low_other_ref, high_ref, high_other_ref, out_ref, *, half, sizes):
    z_count, c_count, y_count, x_count = sizes
    own_z, own_c, own_y, own_x = (own_ref[axis] for axis in range(4))
    step = pl.program_id(0)

    def place(near_ref, far_ref, x_first):
        for z in range(z_count):
            for y in range(y_count):
                for x in range(x_count):
                    if x_first:
                        at = (x ^ own_x) * y_count + (y ^ own_y)
                    else:
                        at = (y ^ own_y) * x_count + (x ^ own_x)
                    at = at * z_count + (z ^ own_z)
                    near, far = near_ref[0, at], far_ref[0, at]
                    for c in range(c_count):
                        to = ((z * c_count + c) * y_count + y) * x_count + x
                        out_ref[0, to] = jnp.where(own_c == c, near, far)

    @pl.when(step < half)
    def _():
        place(low_ref, low_other_ref, False)

    @pl.when(step >= half)
    def _():
        place(high_ref, high_other_ref, True)


def place_rows(low, high):
    sizes = tuple(lax.axis_size(axis) for axis in AXES)
    half, rows = low[0].shape[0], low[0].shape[-2]
    count = half + high[0].shape[0]
    own = jnp.stack([lax.axis_index(axis) for axis in AXES]).astype(jnp.int32)
    pieces = [part.reshape(part.shape[0], -1, rows, D) for part in low + high]
    block = (1,) + pieces[0].shape[1:]
    early = pl.BlockSpec(block, lambda i: (jnp.minimum(i, half - 1), 0, 0, 0))
    later = pl.BlockSpec(block, lambda i: (jnp.maximum(i - half, 0), 0, 0, 0))
    devices = CH // rows
    out = pl.pallas_call(
        functools.partial(place_kernel, half=half, sizes=sizes),
        grid=(count,),
        in_specs=[CORE_SPEC, early, early, later, later],
        out_specs=pl.BlockSpec((1, devices, rows, D), lambda i: (i, 0, 0, 0)),
        out_shape=jax.ShapeDtypeStruct((count, devices, rows, D), bf16),
        compiler_params=params(),
        cost_estimate=cost(0, 4 * count * CH * D),
    )(own, *pieces)
    return out.reshape(count, CH, D)


def trade_rows(values):
    mine = lax.axis_index(("y", "x"))
    count = lax.axis_size(("y", "x"))
    cuts = [lax.dynamic_index_in_dim(values, mine ^ mask, 0, False) for mask in range(count)]
    return send(cuts, ("y", "x"))


def row_order_kernel(row_ref, *refs):
    at = pl.program_id(0) ^ row_ref[0]
    values = refs[0][...]
    for mask in range(1, len(refs) - 1):
        values = jnp.where(at == mask, refs[mask][...], values)
    refs[-1][0] = values.astype(f32)


def row_order(pieces):
    count = len(pieces)
    cells = pieces[0].size // CH
    return pl.pallas_call(
        row_order_kernel,
        grid=(count,),
        in_specs=[CORE_SPEC] + [pl.BlockSpec((cells, CH), lambda i: (0, 0))] * count,
        out_specs=pl.BlockSpec((1, cells, CH), lambda i: (i, 0, 0)),
        out_shape=jax.ShapeDtypeStruct((count, cells, CH), f32),
        compiler_params=params(),
        cost_estimate=cost(0, 6 * count * cells * CH),
    )(row_here(), *[piece.reshape(cells, CH) for piece in pieces])


def widen_kernel(row_ref, *refs):
    out_ref = refs[-1]
    cells = refs[0].shape[0]
    col = lax.broadcasted_iota(jnp.int32, (cells, CH), 0) % IMG
    out_ref[0:IMG, :] = jnp.zeros((IMG, 3 * CH), bf16)
    out_ref[CELLS + IMG :, :] = jnp.zeros((IMG, 3 * CH), bf16)
    for at in range(len(refs) - 1):
        values = refs[at][...]
        for mask in range(1, len(refs) - 1):
            values = jnp.where(row_ref[0] == mask, refs[at ^ mask][...], values)
        here = slice(IMG + at * cells, IMG + (at + 1) * cells)
        out_ref[here, CH : 2 * CH] = values
        values = values.astype(f32)
        left = jnp.where(col == 0, 0.0, pltpu.roll(values, 1, 0))
        right = jnp.where(col == IMG - 1, 0.0, pltpu.roll(values, cells - 1, 0))
        out_ref[here, 0:CH] = left.astype(bf16)
        out_ref[here, 2 * CH :] = right.astype(bf16)


def widen(pieces):
    cells = pieces[0].size // CH
    vmem = pl.BlockSpec(memory_space=pltpu.VMEM)
    return pl.pallas_call(
        widen_kernel,
        in_specs=[CORE_SPEC] + [vmem] * len(pieces),
        out_specs=vmem,
        out_shape=lasting((CELLS + 2 * IMG, 3 * CH), bf16),
        compiler_params=params(),
        cost_estimate=cost(0, 8 * CELLS * CH),
    )(row_here(), *[piece.reshape(cells, CH) for piece in pieces])


def slice_shape():
    z, c, y, x = [lax.axis_size(axis) for axis in AXES]
    return (z, y, x, CH // (z * c * y * x))


tie = lax.optimization_barrier


def to_tiles(slices, parts=1):
    blocks, rows, columns = slices.shape
    return (
        slices.reshape(parts, blocks // parts, rows, columns // CH, CH)
        .transpose(1, 0, 3, 2, 4)
        .reshape(-1, rows, CH)
    )


def from_tiles(tiles, row_blocks, parts):
    rows = tiles.shape[1]
    return (
        tiles.reshape(row_blocks, parts, D // CH, rows, CH)
        .transpose(1, 0, 3, 2, 4)
        .reshape(parts * row_blocks, rows, D)
    )


def dot_nt(a, b):
    return lax.dot_general(a, b, (((1,), (1,)), ((), ())), preferred_element_type=f32)


def dot_nn(a, b):
    return lax.dot_general(a, b, (((1,), (0,)), ((), ())), preferred_element_type=f32)


def dot_tn(a, b):
    return lax.dot_general(a, b, (((0,), (0,)), ((), ())), preferred_element_type=f32)


def head_mask(shape, head):
    return (lax.broadcasted_iota(jnp.int32, shape, len(shape) - 1) // HD) == head


def cost(flops, moved, transcendentals=0):
    return pl.CostEstimate(
        flops=int(flops), bytes_accessed=int(moved), transcendentals=int(transcendentals)
    )


def stay(values):
    return pltpu.with_memory_space_constraint(values, pltpu.HBM)


lasting = pltpu.HBM


def params():
    return pltpu.CompilerParams(vmem_limit_bytes=VMEM_BYTES)


def cross_forward_kernel(q_ref, k_ref, v_ref, o_ref, l_ref):
    rows = q_ref.shape[0]
    lane = lax.broadcasted_iota(jnp.int32, (rows, 128), 1)
    q = q_ref[...]
    mixed = jnp.zeros((rows, CH), f32)
    stat = jnp.zeros((rows, 128), f32)
    for head in range(TH):
        mask = head_mask((rows, CH), head)
        q_head = jnp.where(mask, q.astype(f32) * 0.125, 0.0).astype(bf16)
        scores = dot_nt(q_head, k_ref[...])
        peak = jnp.max(scores, -1, keepdims=True)
        shifted = jnp.exp(scores - peak)
        total = jnp.sum(shifted, -1, keepdims=True)
        part = dot_nn(shifted.astype(bf16), v_ref[...])
        mixed = jnp.where(mask, part * (1.0 / total), mixed)
        stat = jnp.where(lane == head, peak + jnp.log(total), stat)
    o_ref[...] = mixed.astype(bf16)
    l_ref[0] = stat.T[:8]


def cross_forward(query, kv):
    rows = query.shape[0] // 1
    cells = kv.shape[0]
    return pl.pallas_call(
        cross_forward_kernel,
        grid=(1,),
        in_specs=[
            pl.BlockSpec((rows, CH), lambda i: (i, 0)),
            pl.BlockSpec((cells, CH), lambda i: (0, 0)),
            pl.BlockSpec((cells, CH), lambda i: (0, 1)),
        ],
        out_specs=[
            pl.BlockSpec((rows, CH), lambda i: (i, 0)),
            pl.BlockSpec((1, 8, rows), lambda i: (i, 0, 0)),
        ],
        out_shape=[
            jax.ShapeDtypeStruct((rows, CH), bf16),
            jax.ShapeDtypeStruct((1, 8, rows), f32),
        ],
        compiler_params=params(),
        cost_estimate=cost(16 * TH * rows * cells * CH // 2, 8 * cells * CH, 2 * TH * rows * cells),
    )(query, kv, kv)


def delta_rows(d_out, out):
    product = d_out.astype(f32) * out.astype(f32)
    head = lax.broadcasted_iota(jnp.int32, (8, CH), 0)
    lane = lax.broadcasted_iota(jnp.int32, (8, CH), 1)
    pick = ((lane // HD) == head).astype(f32)
    return lax.dot_general(
        pick,
        product,
        (((1,), (1,)), ((), ())),
        precision=lax.Precision.HIGHEST,
        preferred_element_type=f32,
    )


def cross_probs_kernel(q_ref, k_ref, l_ref, p_ref):
    q = q_ref[...].astype(f32) * 0.125
    for head in range(TH):
        q_head = jnp.where(head_mask(q.shape, head), q, 0.0).astype(bf16)
        scores = dot_nt(k_ref[...], q_head)
        p_ref[head] = jnp.exp(scores - l_ref[head : head + 1, :]).astype(bf16)


def cross_probs(query, kv, log_rows):
    rows = query.shape[0]
    cells = kv.shape[0]
    block = 512
    return pl.pallas_call(
        cross_probs_kernel,
        grid=(cells // block,),
        in_specs=[
            pl.BlockSpec((rows, CH), lambda i: (0, 0)),
            pl.BlockSpec((block, CH), lambda i: (i, 0)),
            pl.BlockSpec((8, rows), lambda i: (0, 0)),
        ],
        out_specs=pl.BlockSpec((TH, block, rows), lambda i: (0, i, 0)),
        out_shape=lasting((TH, cells, rows), bf16),
        compiler_params=params(),
        cost_estimate=cost(2 * TH * rows * cells * CH, 2 * TH * rows * cells, TH * rows * cells),
    )(query, stay(kv), log_rows)


def cross_backward_kernel(
    q_ref, k_ref, v_ref, do_ref, o_ref, p_ref, feats_ref, gupd_ref, query_w_ref,
    dkv_ref, query_g_ref, future_ref, q_s, do_s, delta_s, dq_s,
):
    step = pl.program_id(0)
    rows = q_ref.shape[0]

    @pl.when(step == 0)
    def _():
        for head in range(TH):
            mask = head_mask((rows, CH), head)
            q_s[head] = jnp.where(mask, q_ref[...].astype(f32) * 0.125, 0.0).astype(bf16)
            do_s[head] = jnp.where(mask, do_ref[...].astype(f32), 0.0).astype(bf16)
        delta_s[...] = delta_rows(do_ref[...], o_ref[...])
        dq_s[...] = jnp.zeros_like(dq_s)

    cells = k_ref.shape[0]
    dk = jnp.zeros((cells, CH), f32)
    dv = jnp.zeros((cells, CH), f32)
    k_turned = k_ref[...].T
    for head in range(TH):
        probs = p_ref[head]
        d_probs = dot_nt(v_ref[...], do_s[head])
        d_scores = (probs.astype(f32) * (d_probs - delta_s[head : head + 1, :])).astype(bf16)
        dv = dv + dot_nn(probs, do_s[head])
        dk = dk + dot_nn(d_scores, q_s[head])
        here = slice(head * HD, (head + 1) * HD)
        dq_s[here, :] += dot_nn(k_turned[here, :], d_scores)
    dkv_ref[:, :CH] = dk.astype(bf16)
    dkv_ref[:, CH:] = dv.astype(bf16)

    @pl.when(step == pl.num_programs(0) - 1)
    def _():
        gq = (dq_s[...].T * 0.125).astype(bf16)
        query_g_ref[...] = dot_tn(feats_ref[...], gq).astype(bf16)
        future_ref[...] = gupd_ref[...] + dot_nt(gq, query_w_ref[...])


def cross_backward(query, kv, d_out, out, probs, feats, gupd, to_query):
    rows = query.shape[0]
    cells = kv.shape[0]
    block = 1024
    whole = lambda i: (0, 0)
    return pl.pallas_call(
        cross_backward_kernel,
        grid=(cells // block,),
        in_specs=[
            pl.BlockSpec((rows, CH), whole),
            pl.BlockSpec((block, CH), lambda i: (i, 0)),
            pl.BlockSpec((block, CH), lambda i: (i, 1)),
            pl.BlockSpec((rows, CH), whole),
            pl.BlockSpec((rows, CH), whole),
            pl.BlockSpec((TH, block, rows), lambda i: (0, i, 0)),
            pl.BlockSpec((rows, CH), whole),
            pl.BlockSpec((rows, CH), whole),
            pl.BlockSpec((CH, CH), whole),
        ],
        out_specs=[
            pl.BlockSpec((block, 2 * CH), lambda i: (i, 0)),
            pl.BlockSpec((CH, CH), whole),
            pl.BlockSpec((rows, CH), whole),
        ],
        out_shape=[
            jax.ShapeDtypeStruct((cells, 2 * CH), bf16),
            jax.ShapeDtypeStruct((CH, CH), bf16),
            jax.ShapeDtypeStruct((rows, CH), f32),
        ],
        scratch_shapes=[
            pltpu.VMEM((TH, rows, CH), bf16),
            pltpu.VMEM((TH, rows, CH), bf16),
            pltpu.VMEM((8, rows), f32),
            pltpu.VMEM((CH, rows), f32),
        ],
        compiler_params=pltpu.CompilerParams(vmem_limit_bytes=MLP_BYTES),
        cost_estimate=cost(10 * TH * rows * cells * CH, 8 * cells * CH, TH * rows * cells),
    )(query, kv, kv, d_out, out, stay(probs), feats, gupd, to_query)


def self_forward_kernel(len_ref, q_ref, k_ref, v_ref, o_ref, l_ref):
    group = pl.program_id(0)
    length = len_ref[0]
    for start, count in ROW_BLOCKS:
        stop = start + count
        q = q_ref[0, start:stop, :].astype(f32) * 0.125
        row = lax.broadcasted_iota(jnp.int32, (count, 1), 0) + start
        bound = jnp.minimum(row, length - 1)
        allowed = lax.broadcasted_iota(jnp.int32, (count, stop), 1) <= bound
        mixed = jnp.zeros((count, CH), f32)
        stat = jnp.zeros((count, 128), f32)
        lane = lax.broadcasted_iota(jnp.int32, (count, 128), 1)
        for head in range(GROUP):
            mask = head_mask((count, CH), head)
            q_head = jnp.where(mask, q, 0.0).astype(bf16)
            scores = jnp.where(allowed, dot_nt(q_head, k_ref[0, :stop, :]), neg_large)
            peak = jnp.max(scores, -1, keepdims=True)
            shifted = jnp.exp(scores - peak)
            total = jnp.sum(shifted, -1, keepdims=True)
            part = dot_nn(shifted.astype(bf16), v_ref[0, :stop, :])
            mixed = jnp.where(mask, part * (1.0 / total), mixed)
            stat = jnp.where(lane == head, peak + jnp.log(total), stat)
        o_ref[start:stop, :] = mixed.astype(bf16)
        l_ref[0, :, start:stop] = stat.T[:8]


def self_forward(qkv, length):
    groups = D // CH
    at = lambda j: (lambda i, n: (j, 0, i))
    return pl.pallas_call(
        self_forward_kernel,
        grid_spec=pltpu.PrefetchScalarGridSpec(
            num_scalar_prefetch=1,
            grid=(groups,),
            in_specs=[pl.BlockSpec((1, SEQ, CH), at(j)) for j in range(3)],
            out_specs=[
                pl.BlockSpec((SEQ, CH), lambda i, n: (0, i)),
                pl.BlockSpec((1, 8, SEQ), lambda i, n: (i, 0, 0)),
            ],
        ),
        out_shape=[
            lasting((SEQ, D), bf16),
            jax.ShapeDtypeStruct((groups, 8, SEQ), f32),
        ],
        compiler_params=params(),
        cost_estimate=cost(4 * HEADS * SEQ * SEQ * CH, 8 * SEQ * D, HEADS * SEQ * SEQ),
    )(length, qkv, qkv, qkv)


def self_backward_kernel(
    len_ref, q_ref, k_ref, v_ref, do_ref, o_ref, l_ref, out_ref, dk_s, dv_s
):
    length = len_ref[0]
    dk_s[...] = jnp.zeros_like(dk_s)
    dv_s[...] = jnp.zeros_like(dv_s)
    delta = delta_rows(do_ref[...], o_ref[...])
    k_turned = k_ref[0].T
    for start, count in ROW_BLOCKS:
        stop = start + count
        q = q_ref[0, start:stop, :].astype(f32) * 0.125
        d_out = do_ref[start:stop, :].astype(f32)
        row = lax.broadcasted_iota(jnp.int32, (1, count), 1) + start
        bound = jnp.minimum(row, length - 1)
        allowed = lax.broadcasted_iota(jnp.int32, (stop, count), 0) <= bound
        dq = []
        k = k_ref[0, :stop, :]
        v = v_ref[0, :stop, :]
        dk = dk_s[:stop, :]
        dv = dv_s[:stop, :]
        for head in range(GROUP):
            mask = head_mask((count, CH), head)
            q_head = jnp.where(mask, q, 0.0).astype(bf16)
            d_head = jnp.where(mask, d_out, 0.0).astype(bf16)
            scores = dot_nt(k, q_head)
            logs = l_ref[0, head : head + 1, start:stop]
            probs = jnp.where(allowed, jnp.exp(scores - logs), 0.0)
            d_probs = dot_nt(v, d_head)
            d_scores = (probs * (d_probs - delta[head : head + 1, start:stop])).astype(bf16)
            dv = dv + dot_nn(probs.astype(bf16), d_head)
            dk = dk + dot_nn(d_scores, q_head)
            dq.append(dot_nn(k_turned[head * HD : (head + 1) * HD, :stop], d_scores))
        dk_s[:stop, :] = dk
        dv_s[:stop, :] = dv
        out_ref[0, start:stop, :] = (jnp.concatenate(dq, 0).T * 0.125).astype(bf16)
    out_ref[1] = dk_s[...].astype(bf16)
    out_ref[2] = dv_s[...].astype(bf16)


def self_backward(qkv, d_out, out, log_rows, length, count):
    groups = D // CH
    at = lambda j: (lambda i, n: (j, 0, i))
    here = lambda i, n: (0, i)
    return pl.pallas_call(
        self_backward_kernel,
        grid_spec=pltpu.PrefetchScalarGridSpec(
            num_scalar_prefetch=1,
            grid=(count,),
            in_specs=[pl.BlockSpec((1, SEQ, CH), at(j)) for j in range(3)]
            + [
                pl.BlockSpec((SEQ, CH), here),
                pl.BlockSpec((SEQ, CH), here),
                pl.BlockSpec((1, 8, SEQ), lambda i, n: (i, 0, 0)),
            ],
            out_specs=pl.BlockSpec((3, SEQ, CH), lambda i, n: (0, 0, i)),
            scratch_shapes=[pltpu.VMEM((SEQ, CH), f32), pltpu.VMEM((SEQ, CH), f32)],
        ),
        out_shape=jax.ShapeDtypeStruct((3, SEQ, count * CH), bf16),
        compiler_params=params(),
        cost_estimate=cost(
            8 * HEADS * SEQ * SEQ * CH * count // groups, 16 * SEQ * D, HEADS * SEQ * SEQ
        ),
    )(length, stay(qkv), stay(qkv), stay(qkv), stay(d_out), stay(out), log_rows)


def full(*shape):
    return pl.BlockSpec(shape, lambda i: (0,) * len(shape))


def part_of(first):
    return pl.BlockSpec((3, CH, D), lambda i: (first + i, 0, 0))


def fixed_part(index):
    return pl.BlockSpec((3, CH, D), lambda i: (index, 0, 0))


def square(ref):
    return ref[...].reshape(D, D)


def write_cores(core, matrix, keep_refs, sizes, order, at=0):
    z, y, x, rows = sizes
    columns = matrix.shape[-1]
    if rows % 8:
        parts = matrix.reshape(-1, 2, y * x * rows, columns)
    else:
        parts = matrix.reshape(-1, 2, y, x, rows, columns)
    first, second = parts[:, 0], parts[:, 1]
    halves = (jnp.where(core == 0, first, second), jnp.where(core == 0, second, first))
    for ref, half in zip(keep_refs, halves):
        here = slice(at * z, at * z + half.shape[0])
        if rows % 8:
            ref[here] = half.astype(bf16)
            continue
        for row in range(y):
            for col in range(x):
                to = (col, row) if order == "xy" else (row, col)
                ref[to[0], to[1], here] = half[:, row, col].astype(bf16)


def core_shape(count, order, columns=D):
    z, y, x, rows = slice_shape()
    if rows % 8:
        return (count * z, y * x * rows, columns)
    cuts = (x, y) if order == "xy" else (y, x)
    return cuts + (count * z, rows, columns)


def core_block(count, order, at, columns=D):
    shape = core_shape(count, order, columns)
    return pl.BlockSpec(shape, lambda i: (0,) * (len(shape) - 3) + (at(i), 0, 0))


def core_cuts(parts, order):
    z, y, x, rows = slice_shape()
    if rows % 8 == 0:
        return list(parts)
    parts = [part.reshape(-1, y, x, rows, part.shape[-1]) for part in parts]
    dims = (2, 1, 0, 3, 4) if order == "xy" else (1, 2, 0, 3, 4)
    return [part.transpose(dims) for part in parts]


def split_z(slices):
    return slices.reshape((-1, lax.axis_size("z")) + slices.shape[1:])


def row_here():
    return lax.axis_index(("y", "x")).astype(jnp.int32).reshape(1)


def core_here():
    return lax.axis_index("c").astype(jnp.int32).reshape(1)


def row_scale(values):
    return lax.rsqrt(jnp.mean(values * values, -1, keepdims=True) + eps_norm)


def pull_norm(d_normed, values, gain):
    scale = row_scale(values)
    d_gain = jnp.sum(d_normed * values * scale, 0, keepdims=True)
    scaled = d_normed * gain
    inner = jnp.mean(scaled * values, -1, keepdims=True)
    return d_gain, scale * scaled - (scale * scale * scale) * values * inner


def embed_kernel(
    pool_ref, feats_ref, mixed_ref, out_w_ref, emb_ref, w_ref, gain_ref,
    seq_ref, embed_ref, normed_ref, qkv_ref,
):
    @pl.when(pl.program_id(0) == 0)
    def _():
        updated = feats_ref[...].astype(f32) + dot_nn(mixed_ref[...], out_w_ref[...])
        seq_ref[:CTX, :] = pool_ref[...]
        seq_ref[CTX:, :] = updated.astype(bf16)
        embed = dot_nn(seq_ref[...], emb_ref[0])
        embed_ref[...] = embed
        normed_ref[...] = (embed * row_scale(embed) * gain_ref[...]).astype(bf16)

    qkv_ref[0] = dot_nn(normed_ref[...], square(w_ref)).astype(bf16)


def embed_forward(pooled, feats, mixed, to_out, weights, gain):
    last = weights.shape[0] - 1
    return pl.pallas_call(
        embed_kernel,
        grid=(3,),
        in_specs=[
            full(CTX, CH),
            full(SEQ - CTX, CH),
            full(SEQ - CTX, CH),
            full(CH, CH),
            pl.BlockSpec((1, CH, D), lambda i: (last, 0, 0)),
            part_of(0),
            full(1, D),
        ],
        out_specs=[
            full(SEQ, CH),
            full(SEQ, D),
            full(SEQ, D),
            pl.BlockSpec((1, SEQ, D), lambda i: (i, 0, 0)),
        ],
        out_shape=[
            lasting((SEQ, CH), bf16),
            lasting((SEQ, D), f32),
            lasting((SEQ, D), bf16),
            lasting((3, SEQ, D), bf16),
        ],
        compiler_params=params(),
        cost_estimate=cost(2 * SEQ * D * (CH + 3 * D), 12 * SEQ * D),
    )(pooled, feats, mixed, to_out, stay(weights), stay(weights), gain)


def mlp_kernel(
    core_ref, mixed_ref, embed_ref, att_ref, up_ref, down_ref, gain_ref, gd_ref,
    out_ref, d_stream_ref, gog_ref, up_keep_ref, up_give_ref, down_keep_ref, down_give_ref,
    att_keep_ref, att_give_ref, gain_g_ref,
    stream_s, normed_s, turned_s, act_s, gpre_s, total_s, *, sizes
):
    step = pl.program_id(0)
    core = core_ref[0]

    @pl.when(step == 0)
    def _():
        stream = embed_ref[...] + dot_nn(mixed_ref[...], square(att_ref))
        stream_s[...] = stream
        out_ref[...] = stream
        total_s[...] = jnp.zeros_like(total_s)
        normed = stream * row_scale(stream) * gain_ref[...]
        normed_s[...] = normed.astype(bf16)
        turned_s[...] = normed.T.astype(bf16)

    factor = (2.0 / 3.141592653589793) ** 0.5
    cubic = 0.044715 * factor
    rows = SEQ // 2
    for start in range(0, SEQ, rows):
        here = slice(start, start + rows)
        v = dot_nn(normed_s[here, :], square(up_ref))
        v2 = v * v
        half = 0.5 + 0.5 * jnp.tanh(v * (factor + cubic * v2))
        act = (v * half).astype(bf16)
        act_s[here, :] = act
        slope = half + v * (2.0 * half * (1.0 - half) * (factor + 3.0 * cubic * v2))
        gpre = (dot_nt(gd_ref[here, :], square(down_ref)) * slope).astype(bf16)
        gpre_s[here, :] = gpre
        out_ref[here, :] += dot_nn(act, square(down_ref))
        total_s[here, :] += dot_nt(gpre, square(up_ref))
    down_refs, up_refs = (down_keep_ref, down_give_ref), (up_keep_ref, up_give_ref)
    write_cores(core, dot_tn(act_s[...], gd_ref[...]), down_refs, sizes, "xy")
    write_cores(core, dot_nn(turned_s[...], gpre_s[...]), up_refs, sizes, "yx")

    @pl.when(step == pl.num_programs(0) - 1)
    def _():
        d_gain, pulled = pull_norm(total_s[...], stream_s[...], gain_ref[...])
        gain_g_ref[...] = d_gain
        d_stream = gd_ref[...].astype(f32) + pulled
        d_stream_ref[...] = d_stream
        ga = d_stream.astype(bf16)
        gog_ref[...] = dot_nt(ga, square(att_ref)).astype(bf16)
        att_refs = (att_keep_ref, att_give_ref)
        write_cores(core, dot_tn(mixed_ref[...], ga), att_refs, sizes, "yx")


def mlp_block(mixed, embed, weights, mlp, gain, gd):
    up_part = core_block(3, "yx", lambda i: i)
    down_part = core_block(3, "xy", lambda i: i)
    att_part = core_block(3, "yx", lambda i: 0)
    return pl.pallas_call(
        functools.partial(mlp_kernel, sizes=slice_shape()),
        grid=(4,),
        in_specs=[
            CORE_SPEC,
            full(SEQ, D),
            full(SEQ, D),
            fixed_part(3),
            part_of(0),
            part_of(4),
            full(1, D),
            full(SEQ, D),
        ],
        out_specs=[full(SEQ, D)] * 3
        + [up_part] * 2
        + [down_part] * 2
        + [att_part] * 2
        + [full(1, D)],
        out_shape=[
            lasting((SEQ, D), f32),
            lasting((SEQ, D), f32),
            lasting((SEQ, D), bf16),
        ]
        + [jax.ShapeDtypeStruct(core_shape(12, "yx"), bf16)] * 2
        + [jax.ShapeDtypeStruct(core_shape(12, "xy"), bf16)] * 2
        + [lasting(core_shape(3, "yx"), bf16)] * 2
        + [jax.ShapeDtypeStruct((1, D), f32)],
        scratch_shapes=[
            pltpu.VMEM((SEQ, D), f32),
            pltpu.VMEM((SEQ, D), bf16),
            pltpu.VMEM((D, SEQ), bf16),
            pltpu.VMEM((SEQ, D), bf16),
            pltpu.VMEM((SEQ, D), bf16),
            pltpu.VMEM((SEQ, D), f32),
        ],
        compiler_params=pltpu.CompilerParams(vmem_limit_bytes=MLP_BYTES),
        cost_estimate=cost(54 * SEQ * D * D, 60 * SEQ * D, 4 * SEQ * D),
    )(
        core_here(), stay(mixed), stay(embed), stay(weights), stay(mlp), stay(mlp), gain, stay(gd)
    )


def embed_grad_kernel(
    core_ref, len_ref, q_ref, k_ref, v_ref, do_ref, o_ref, l_ref,
    g_ref, normed_ref, w_ref, emb_ref, embed_ref, d_stream_ref, seq_ref, mixed_ref, out_w_ref,
    gain_ref, gain_g_ref,
    qk_keep_ref, qk_give_ref, v_keep_ref, v_give_ref, keep_ref, give_ref,
    gupd_ref, pool_g_ref, out_g_ref, gox_ref,
    dk_s, dv_s, last_s, turned_s, total_s, *, sizes
):
    step = pl.program_id(0)
    core = core_ref[0]

    @pl.when(step == 0)
    def _():
        self_backward_kernel(
            len_ref, q_ref, k_ref, v_ref, do_ref, o_ref, l_ref, last_s, dk_s, dv_s
        )
        turned_s[...] = normed_ref[...].T
        total_s[...] = jnp.zeros_like(total_s)

    @pl.when(step > 0)
    def _():
        g = jnp.concatenate([g_ref[0], last_s[step - 1]], 1)
        total_s[...] += dot_nt(g, square(w_ref))
        grad = dot_nn(turned_s[...], g)

        @pl.when(step < 3)
        def _():
            write_cores(core, grad, (qk_keep_ref, qk_give_ref), sizes, "xy")

        @pl.when(step == 3)
        def _():
            write_cores(core, grad, (v_keep_ref, v_give_ref), sizes, "yx")

    @pl.when(step == 3)
    def _():
        d_gain, pulled = pull_norm(total_s[...], embed_ref[...], gain_ref[...])
        gembed = (d_stream_ref[...] + pulled).astype(bf16)
        at = lax.broadcasted_iota(jnp.int32, (CH, D), 0)
        gains = jnp.where(at == 0, d_gain, jnp.where(at == sizes[-1], gain_g_ref[...], 0.0))
        for index, values in enumerate((dot_tn(seq_ref[...], gembed), gains)):
            write_cores(core, values, (keep_ref, give_ref), sizes, "xy", index)
        gseq = dot_nt(gembed, emb_ref[0])
        gupd = gseq[CTX:]
        gb = gupd.astype(bf16)
        pool_g_ref[...] = gseq[:CTX].astype(bf16)
        gupd_ref[...] = gupd
        out_g_ref[...] = dot_tn(mixed_ref[...], gb).astype(bf16)
        gox_ref[...] = dot_nt(gb, out_w_ref[...]).astype(bf16)


def embed_grad(
    length, qkv, gog, out, log_rows, gqkv, normed, weights, embed, d_stream, seq, mixed, to_out,
    gain, gain_g,
):
    last = weights.shape[0] - 1
    group = D // CH - 1
    done = gqkv.shape[-1]
    part = lambda i: jnp.maximum(i - 1, 0)
    at = lambda j: pl.BlockSpec((1, SEQ, CH), lambda i: (j, 0, group))
    here = pl.BlockSpec((SEQ, CH), lambda i: (0, group))
    qk_part = core_block(3, "xy", lambda i: jnp.clip(i - 1, 0, 1))
    v_part = core_block(3, "yx", lambda i: 0)
    emb_part = core_block(2, "xy", lambda i: 0)
    return pl.pallas_call(
        functools.partial(embed_grad_kernel, sizes=slice_shape()),
        grid=(4,),
        in_specs=[
            CORE_SPEC,
            CORE_SPEC,
            at(0),
            at(1),
            at(2),
            here,
            here,
            pl.BlockSpec((1, 8, SEQ), lambda i: (group, 0, 0)),
            pl.BlockSpec((1, SEQ, done), lambda i: (part(i), 0, 0)),
            full(SEQ, D),
            pl.BlockSpec((3, CH, D), lambda i: (part(i), 0, 0)),
            pl.BlockSpec((1, CH, D), lambda i: (last, 0, 0)),
            full(SEQ, D),
            full(SEQ, D),
            full(SEQ, CH),
            full(SEQ - CTX, CH),
            full(CH, CH),
            full(1, D),
            full(1, D),
        ],
        out_specs=[
            qk_part,
            qk_part,
            v_part,
            v_part,
            emb_part,
            emb_part,
            full(SEQ - CTX, CH),
            full(CTX, CH),
            full(CH, CH),
            full(SEQ - CTX, CH),
        ],
        out_shape=[jax.ShapeDtypeStruct(core_shape(6, "xy"), bf16)] * 2
        + [jax.ShapeDtypeStruct(core_shape(3, "yx"), bf16)] * 2
        + [jax.ShapeDtypeStruct(core_shape(2, "xy"), bf16)] * 2
        + [
            jax.ShapeDtypeStruct((SEQ - CTX, CH), f32),
            jax.ShapeDtypeStruct((CTX, CH), bf16),
            jax.ShapeDtypeStruct((CH, CH), bf16),
            jax.ShapeDtypeStruct((SEQ - CTX, CH), bf16),
        ],
        scratch_shapes=[
            pltpu.VMEM((SEQ, CH), f32),
            pltpu.VMEM((SEQ, CH), f32),
            pltpu.VMEM((3, SEQ, CH), bf16),
            pltpu.VMEM((D, SEQ), bf16),
            pltpu.VMEM((SEQ, D), f32),
        ],
        compiler_params=pltpu.CompilerParams(vmem_limit_bytes=MLP_BYTES),
        cost_estimate=cost(2 * SEQ * D * (6 * D + 2 * CH) + 32 * SEQ * SEQ * CH, 50 * SEQ * D),
    )(
        core_here(), length, stay(qkv), stay(qkv), stay(qkv), stay(gog), stay(out), log_rows, gqkv, normed, stay(weights),
        stay(weights), stay(embed), stay(d_stream), stay(seq), stay(mixed), to_out, gain, gain_g,
    )


def patch_pick(rows, columns, patch_dim):
    patch = lax.broadcasted_iota(jnp.int32, (rows, columns), patch_dim)
    cell = lax.broadcasted_iota(jnp.int32, (rows, columns), 1 - patch_dim)
    inside = (cell // (PATCH * IMG)) * (IMG // PATCH) + (cell % IMG) // PATCH
    return jnp.where(patch == inside, 1.0 / (PATCH * PATCH), 0.0).astype(bf16)


def image_rows(step, row):
    return pl.ds(pl.multiple_of(step * BLOCK + row * IMG, IMG), BLOCK)


def token_forward_kernel(x_ref, conv_ref, kv_w_ref, slope_ref, hidden_ref, kv_ref, pool_ref):
    step = pl.program_id(0)
    z = jnp.zeros((BLOCK, CH), f32)
    for row in range(3):
        z = z + dot_nn(x_ref[image_rows(step, row), :], conv_ref[row])
    center = x_ref[image_rows(step, 1), CH : 2 * CH].astype(f32)
    gate = 1.0 / (1.0 + jnp.exp(-z))
    hidden = center + z * gate
    slope_ref[...] = (gate * (1.0 + z * (1.0 - gate))).astype(bf16)
    hidden_b = hidden.astype(bf16)
    hidden_ref[...] = hidden_b
    kv_ref[...] = dot_nn(hidden_b, kv_w_ref[...]).astype(bf16)
    rest = (hidden - hidden_b.astype(f32)).astype(bf16)
    pick = patch_pick(pool_ref.shape[0], BLOCK, 0)
    pool_ref[...] = (dot_nn(pick, hidden_b) + dot_nn(pick, rest)).astype(bf16)


def token_forward(wide, conv_rows, kv_weight):
    steps = CELLS // BLOCK
    whole = lambda i: (0, 0)
    block = lambda i: (i, 0)
    return pl.pallas_call(
        token_forward_kernel,
        grid=(steps,),
        in_specs=[
            pl.BlockSpec(wide.shape, whole),
            pl.BlockSpec((3, 3 * CH, CH), lambda i: (0, 0, 0)),
            pl.BlockSpec((CH, 2 * CH), whole),
        ],
        out_specs=[
            pl.BlockSpec((BLOCK, CH), block),
            pl.BlockSpec((BLOCK, CH), block),
            pl.BlockSpec((BLOCK, 2 * CH), block),
            pl.BlockSpec((CTX // steps, CH), block),
        ],
        out_shape=[
            lasting((CELLS, CH), bf16),
            lasting((CELLS, CH), bf16),
            jax.ShapeDtypeStruct((CELLS, 2 * CH), bf16),
            jax.ShapeDtypeStruct((CTX, CH), bf16),
        ],
        compiler_params=params(),
        cost_estimate=cost(22 * CELLS * CH * CH, 14 * CELLS * CH, CELLS * CH),
    )(stay(wide), conv_rows, kv_weight)


def token_backward_kernel(
    core_ref, dkv_ref, slope_ref, pool_ref, hidden_ref, x_ref, kv_w_ref, query_g_ref, out_g_ref,
    d_hidden_ref, gz_ref, keep_ref, give_ref, conv_s, kv_s, *, sizes
):
    step = pl.program_id(0)

    @pl.when(step == 0)
    def _():
        conv_s[...] = jnp.zeros_like(conv_s)
        kv_s[...] = jnp.zeros_like(kv_s)

    dkv = dkv_ref[...]
    d_hidden = dot_nt(dkv, kv_w_ref[...])
    d_hidden = d_hidden + dot_nn(patch_pick(BLOCK, pool_ref.shape[0], 1), pool_ref[...])
    gz = (d_hidden * slope_ref[...].astype(f32)).astype(bf16)
    d_hidden_ref[...] = d_hidden
    gz_ref[...] = gz
    kv_s[...] += dot_tn(hidden_ref[...], dkv)
    gz_t = gz.T
    for row in range(3):
        conv_s[row] += dot_nn(gz_t, x_ref[image_rows(step, row), :])

    @pl.when(step == pl.num_programs(0) - 1)
    def _():
        tiles = []
        for row in range(3):
            for col in range(3):
                tiles.append(conv_s[row, :, col * CH : (col + 1) * CH].T)
        tiles = tiles + [query_g_ref[...], kv_s[:, :CH], kv_s[:, CH:], out_g_ref[...]]
        for at, tile in enumerate(tiles):
            write_cores(core_ref[0], tile.astype(f32), (keep_ref, give_ref), sizes, "yx", at)


def token_backward(dkv, slope, d_pool, hidden_b, wide, kv_weight, query_g, out_g):
    steps = CELLS // BLOCK
    whole = lambda i: (0, 0)
    block = lambda i: (i, 0)
    return pl.pallas_call(
        functools.partial(token_backward_kernel, sizes=slice_shape()),
        grid=(steps,),
        in_specs=[
            CORE_SPEC,
            pl.BlockSpec((BLOCK, 2 * CH), block),
            pl.BlockSpec((BLOCK, CH), block),
            pl.BlockSpec((CTX // steps, CH), block),
            pl.BlockSpec((BLOCK, CH), block),
            pl.BlockSpec(wide.shape, whole),
            pl.BlockSpec((CH, 2 * CH), whole),
            pl.BlockSpec((CH, CH), whole),
            pl.BlockSpec((CH, CH), whole),
        ],
        out_specs=[
            pl.BlockSpec((BLOCK, CH), block),
            pl.BlockSpec((BLOCK, CH), block),
            core_block(EARLY, "yx", lambda i: 0, CH),
            core_block(EARLY, "yx", lambda i: 0, CH),
        ],
        out_shape=[
            jax.ShapeDtypeStruct((CELLS, CH), f32),
            jax.ShapeDtypeStruct((CELLS, CH), bf16),
            jax.ShapeDtypeStruct(core_shape(EARLY, "yx", CH), bf16),
            jax.ShapeDtypeStruct(core_shape(EARLY, "yx", CH), bf16),
        ],
        scratch_shapes=[pltpu.VMEM((3, CH, 3 * CH), f32), pltpu.VMEM((CH, 2 * CH), f32)],
        compiler_params=params(),
        cost_estimate=cost(26 * CELLS * CH * CH, 20 * CELLS * CH),
    )(core_here(), dkv, stay(slope), d_pool, stay(hidden_b), stay(wide), kv_weight, query_g, out_g)


def context_backward_kernel(gz_ref, d_hidden_ref, conv_ref, out_ref, wide_s):
    step = pl.program_id(0)
    steps = pl.num_programs(0)

    def widen(at):
        values = gz_ref[image_rows(at, 0), :].astype(f32)
        col = lax.broadcasted_iota(jnp.int32, (BLOCK, CH), 0) % IMG
        left = jnp.where(col == 0, 0.0, pltpu.roll(values, 1, 0))
        right = jnp.where(col == IMG - 1, 0.0, pltpu.roll(values, BLOCK - 1, 0))
        wide_s[image_rows(at, 1), 0:CH] = left.astype(bf16)
        wide_s[image_rows(at, 1), CH : 2 * CH] = values.astype(bf16)
        wide_s[image_rows(at, 1), 2 * CH :] = right.astype(bf16)

    @pl.when(step == 0)
    def _():
        wide_s[0:IMG, :] = jnp.zeros((IMG, 3 * CH), bf16)
        wide_s[CELLS + IMG :, :] = jnp.zeros((IMG, 3 * CH), bf16)
        widen(0)

    @pl.when(step < steps - 1)
    def _():
        widen(step + 1)

    total = d_hidden_ref[...]
    for row in range(3):
        values = wide_s[image_rows(step, row), :]
        for col in range(3):
            tap = conv_ref[3 * (2 - row) + (2 - col)]
            total = total + dot_nt(values[:, col * CH : (col + 1) * CH], tap)
    out_ref[...] = total.astype(bf16)


def context_backward(gz, d_hidden, conv_tiles):
    block = lambda i: (i, 0)
    return pl.pallas_call(
        context_backward_kernel,
        grid=(CELLS // BLOCK,),
        in_specs=[
            pl.BlockSpec((CELLS, CH), lambda i: (0, 0)),
            pl.BlockSpec((BLOCK, CH), block),
            pl.BlockSpec((9, CH, CH), lambda i: (0, 0, 0)),
        ],
        out_specs=pl.BlockSpec((BLOCK, CH), block),
        out_shape=jax.ShapeDtypeStruct((CELLS, CH), bf16),
        scratch_shapes=[pltpu.VMEM((CELLS + 2 * IMG, 3 * CH), bf16)],
        compiler_params=params(),
        cost_estimate=cost(18 * CELLS * CH * CH, 8 * CELLS * CH),
    )(gz, d_hidden, conv_tiles)


def local(
    context_map,
    future_feats,
    horizon,
    cotangent,
    tile_owner,
    master_tiles,
    moment_first,
    moment_second,
    norm_gains,
    gain_first,
    gain_second,
):
    slot_count = master_tiles.shape[0]
    devices = lax.axis_size(AXES)
    rows = CH // devices
    slot_of = slot_index(tile_owner, slot_count)

    length = CTX + FT * horizon
    valid = jnp.arange(SEQ) < length[0]
    gd = jnp.where(valid[:, None], cotangent[0], jnp.zeros((), bf16))

    slices = (
        master_tiles.astype(bf16)
        .reshape(slot_count, devices, rows, CH)
        .transpose(1, 0, 2, 3)
    )
    slices = lax.all_to_all(slices, AXES, split_axis=0, concat_axis=0, tiled=True)
    extra = max(1, 8 // rows)
    tiles = tile_owner.shape[0]
    span = slot_count + extra
    place = jnp.arange(devices * span)
    device, at = place // span, place % span
    found = slot_of[None, :] == jnp.where(at < slot_count, device * slot_count + at, -1)[:, None]
    tile_of = jnp.sum(jnp.where(found, jnp.arange(tiles)[None], 0), 1)
    tile_of = jnp.where(at < slot_count, tile_of, tiles + at - slot_count)
    mine_at = lax.axis_index(AXES) * slot_count + jnp.arange(slot_count)
    used = jnp.any(slot_of[None, :] == mine_at[:, None], 1).astype(f32)
    slices, gd, tile_of, used = tie((slices, gd, tile_of, used))
    slices = slices.reshape(devices * slot_count, rows, CH)
    slices = slices.at[slot_of].get(mode="promise_in_bounds")
    early, emb, qkv, att, up, down = jnp.split(slices, (13, 16, 43, 52, 88))
    mlp = jnp.concatenate([from_tiles(up, 3, 4), from_tiles(down, 12, 1)], 0)
    early = gather_axes(early, "z")
    core = jnp.concatenate([from_tiles(qkv, 3, 3), from_tiles(att, 3, 1), from_tiles(emb, 1, 1)], 0)
    core, early = tie((core, early))
    early = gather_axes(joined(early), ("y", "x"))
    core = gather_axes(core, "z")
    pieces = trade_rows(context_map)
    early = joined(gather_axes(joined(early), "c"))
    early = device_order(early, ("c", "y", "x", "z"))
    wide = widen(pieces)
    core = joined(core)
    low, high = gather_axes(core[:6], "x"), gather_axes(core[6:], "y")

    conv_tiles = early[:9]
    to_query, to_out = early[9], early[12]
    kv_weight = jnp.concatenate([early[10], early[11]], 1)

    wide, mlp, low, high = hold((wide, mlp), low, high)
    mlp = lax.all_gather(mlp, AXES, axis=1, tiled=True)
    low, high = joined(low), joined(high)
    wide, low, high = tie((wide, low, high))
    low, high = gather_axes(low, "y"), gather_axes(high, "x")
    slope_z, hidden_b, kv, pooled = token_forward(
        wide, conv_tiles.reshape(3, 3 * CH, CH), kv_weight
    )
    kv, low, high = hold((kv,), low, high)
    low, high = joined(low), joined(high)
    feats_b = future_feats[0]
    query = jnp.dot(feats_b, to_query, preferred_element_type=f32).astype(bf16)
    kv, low, high = tie((kv, low, high))
    low, high = gather_axes(low, "c"), gather_axes(high, "c")
    cross_mixed, cross_logs = cross_forward(query, kv)
    cross_mixed, low, high = hold((cross_mixed,), low, high)
    weights = place_rows(low, high)

    gain_one, gain_two = norm_gains[:1], norm_gains[1:]
    seq, embed, normed_one, qkv = embed_forward(
        pooled, feats_b, cross_mixed, to_out, weights, gain_one
    )
    mixed, logs = self_forward(qkv, length)
    mixed, log_rows = tie((mixed, cross_logs[0]))
    probs = cross_probs(query, kv, log_rows)
    mixed, probs = tie((mixed, probs))
    (
        block_out, d_stream, gog, up_keep, up_give, down_keep, down_give, att_keep, att_give,
        gain_g_two,
    ) = mlp_block(mixed, embed, weights, mlp, gain_two, gd)
    up = core_cuts([up_keep, up_give], "yx")
    down = core_cuts([down_keep, down_give], "xy")
    att = core_cuts([att_keep, att_give], "yx")
    gog, up, down, att = tie((gog, up, down, att))
    up, down, att = send(up, "c"), send(down, "c"), send(att, "c")
    gqkv = self_backward(qkv, gog, mixed, logs, length, 2)
    gqkv, up, down, att = hold((gqkv,), up, down, att)
    up, down = advance(up, "y", 0), advance(down, "x", 0)
    gqkv, up, down = tie((gqkv, up, down))
    up, down = send(up, "y"), send(down, "x")
    (
        qk_keep, qk_give, v_keep, v_give, emb_keep, emb_give, gupd, pool_g, out_g, gox,
    ) = embed_grad(
        length, qkv, gog, mixed, logs, gqkv, normed_one, weights, embed, d_stream, seq,
        cross_mixed, to_out, gain_one, gain_g_two,
    )
    first = core_cuts([qk_keep, qk_give], "xy")
    second = core_cuts([v_keep, v_give], "yx")
    emb = core_cuts([emb_keep, emb_give], "xy")
    gox, gupd, first, second, emb, up, down = hold((gox, gupd, first, second, emb), up, down)
    up, down = advance(up, "x", 0), advance(down, "y", 0)
    gox, up, down, first, second, emb = tie((gox, up, down, first, second, emb))
    up, down, emb = send(up, "x"), send(down, "y"), send(emb, "c")
    first, second = send(first, "c"), send(second, "c")

    gkv, query_g, future_grad = cross_backward(
        query, kv, gox, cross_mixed, probs, feats_b, gupd, to_query
    )
    gkv, up, down, first, second, emb = hold((gkv,), up, down, first, second, emb)
    mlp = advance_near([split_z(jnp.concatenate(part, 0)) for part in zip(up, down)])
    emb = advance(emb, "x", 0)
    second = [jnp.concatenate([p, q], 2) for p, q in zip(second, att)]
    first, second = advance(first, "x", 0), advance(second, "y", 0)
    gkv, mlp, first, second, emb = tie((gkv, mlp, first, second, emb))
    mlp, emb = send(mlp, "z"), send(emb, "x")
    first, second = send(first, "x"), send(second, "y")

    d_hidden, gz, early_keep, early_give = token_backward(
        gkv, slope_z, pool_g, hidden_b, wide, kv_weight, query_g, out_g
    )
    d_hidden, gz, early_keep, early_give, mlp, first, second, emb = hold(
        (d_hidden, gz, early_keep, early_give), mlp, first, second, emb
    )
    early = core_cuts([early_keep, early_give], "yx")
    early, mlp, first, second, emb = tie((early, mlp, first, second, emb))
    early = send(early, "c")
    first, second = advance(first, "y", 0), advance(second, "x", 0)
    emb, mlp = advance(emb, "y", 0), advance_far(mlp)
    first, second = send(first, "y"), send(second, "x")
    emb, mlp = send(emb, "y"), send(mlp, "z", 2)
    gz, early, first, second, emb = hold((gz,), early, first, second, emb)
    early = advance([p.reshape((-1,) + p.shape[2:]) for p in early], ("y", "x"), 0)
    att = advance_near([split_z(jnp.concatenate(part, 0)) for part in zip(first, second)])
    gz, early, att = tie((gz, early, att))
    early, att = send(early, ("y", "x")), send(att, "z")
    context_grad = context_backward(gz, d_hidden, conv_tiles)
    context_grad, early, att, mlp = hold((context_grad,), early, att, mlp)
    early = advance([split_z(part) for part in early], "z", 1)
    emb = advance([split_z(part) for part in emb], "z", 1)
    early = [jnp.concatenate([e, to_tiles(m)], 0) for e, m in zip(early, emb)]
    att = advance_far(att)
    context_grad, early, att = tie((context_grad, early, att))
    early, att = send(early, "z"), send(att, "z", 2)
    pieces = trade_rows(context_grad.reshape(context_map.shape))
    sum_mlp = add_up(mlp, keep_wide=True)
    square_mlp = jnp.sum(sum_mlp * sum_mlp)
    half = sum_mlp.shape[0] // 2
    mlp = jnp.concatenate([to_tiles(sum_mlp[:half], 4), to_tiles(sum_mlp[half:])], 0).astype(bf16)
    sum_early = add_up(early, keep_wide=True)
    sum_att = add_up(att, keep_wide=True)

    gains = sum_early[EARLY + 3 :, 0]
    square = square_mlp + jnp.sum(sum_att * sum_att) + jnp.sum(sum_early * sum_early)
    share = jnp.concatenate([gains, jnp.broadcast_to(square, (1, CH))], 0)
    share_high = share.astype(bf16)
    share_low = (share - share_high.astype(f32)).astype(bf16)
    share = jnp.concatenate([share_high, share_low], 0)
    share = jnp.pad(share, ((0, extra * rows - share.shape[0]), (0, 0)))
    sums = jnp.concatenate(
        [
            sum_early[: EARLY + 3].astype(bf16),
            to_tiles(sum_att[:9], 3).astype(bf16),
            to_tiles(sum_att[9:]).astype(bf16),
            mlp,
            share.reshape(extra, rows, CH),
        ],
        0,
    )
    mine = sums.at[tile_of].get(mode="promise_in_bounds")
    mine = mine.reshape(devices, slot_count + extra, rows, CH)
    mine, pieces[-1] = tie((mine, pieces[-1]))
    mine = lax.all_to_all(mine, AXES, split_axis=0, concat_axis=0, tiled=True)
    shares = mine[:, slot_count:].reshape(devices, -1, CH).astype(f32)
    shares = shares[:, :4] + shares[:, 4:8]
    gains = shares[:2, :3].reshape(2, D)
    mine = mine[:, :slot_count].transpose(1, 0, 2, 3).reshape(slot_count, CH, CH).astype(f32)

    used = used[:, None, None]
    grad_norm = jnp.sqrt(jnp.sum(shares[:, 3, 0]))
    factor = jnp.minimum(1.0, clip_level / (grad_norm + 1e-06))
    new_first, new_second, new_master = adam_step(
        master_tiles, mine * factor, moment_first, moment_second, learn_rate, decay_rate
    )
    new_gain_first, new_gain_second, new_gains = adam_step(
        norm_gains, gains * factor, gain_first, gain_second, gain_rate, 0.0
    )
    return (
        block_out[None],
        row_order(pieces).reshape(context_map.shape),
        future_grad[None],
        jnp.where(used > 0, new_first, 0.0),
        jnp.where(used > 0, new_second, 0.0),
        jnp.where(used > 0, new_master, 0.0),
        new_gain_first,
        new_gain_second,
        new_gains,
        grad_norm,
    )


def solution(mesh):
    groups, rows = mesh.devices.shape
    fine = jax.sharding.Mesh(mesh.devices.reshape(groups // 2, 2, rows // 2, 2), AXES)
    whole = P(AXES, None, None)
    image = P(("z", "c"), ("y", "x"), None, None)
    in_specs = (image, whole, P(AXES), whole, P(), whole, whole, whole, P(), P(), P())
    out_specs = (whole, image, whole, whole, whole, whole, P(), P(), P(), P())
    return jax.shard_map(local, mesh=fine, in_specs=in_specs, out_specs=out_specs, check_vma=False)
```
